32 devices in a mesh: gx: 8 (over y, x, core), gy: 4 (over z).
Axes of the slice: x: 2, y: 2, z: 4, core: 2. Of those that a mesh axis runs over, the one named last changes fastest.
Arguments:
- atm_state: float32 [6, 196608], P(None, ('gx', 'gy')), may hold values from -6 to 6
- pair_block: int32 [8192], P(('gx', 'gy')), may hold values from 0 to 47
- pair_owner: int32 [8192, 1], P(('gx', 'gy')), may hold values from 0 to 31; in each aligned block of 256 rows (0 to 255, 256 to 511, ...) at most 16 rows name the same one
- pair_row: int32 [8192], P(('gx', 'gy')), may hold values from 0 to 63
- pair_tile: int32 [8192], P(('gx', 'gy')), may hold values from 0 to 127
- remap_weight: bfloat16 [4096, 128, 128], P(('gx', 'gy')), may hold values from 0.0014953613 to 0.029907227
- wet_mask: int32 [512, 512], P('gx', 'gy'), may hold values 0 or 1
- ocean_state: float32 [4, 16, 512, 512], P(None, None, 'gx', 'gy'), may hold values from -6 to 6
- vert_kappa: float32 [16, 512, 512], P(None, 'gx', 'gy'), may hold values from 0.05 to 3
- horiz_kappa: float32 [512, 512], P('gx', 'gy'), may hold values from 0.02 to 0.24
Outputs:
- ocean_next: float32 [4, 16, 512, 512], P(None, None, 'gx', 'gy')
- atm_surface: float32 [4, 196608], P(None, ('gx', 'gy'))
The draws below stay inside these ranges and needn't reach their ends.
Inputs may be any that keep to these rules, and one draw needn't show every extreme that they name: `pair_owner`: the intersections of one device name one owner at most 16 times, and exactly 16 times for some owner.
All inputs are finite; a program needn't handle non-finite values. No bound on the sum of `wet_mask` on one device may be relied on, other than what follows from the above.
Results may differ from the reference program's by a relative error of at most 0.0039.
Values sent between devices are 32-bit elements; how exact they have to be, the bound alone decides.
No kernel may reach another device: no remote copies, remote signals or barrier semaphores. Data moves between devices by JAX's collectives and lax.ppermute only.
A program may use at most 64 MiB of HBM per device.

```python
import math
import jax
import jax.numpy as jnp
import numpy as np
from jax import lax

TX = 64
TY = 128
LEV = 16
ABLK = 128
NBLK_DEV = 48
NPAIR = 256
NTILE = 128
CAP = 16
NXO = 512
NYO = 512
ATM_COLS = 196608
N_GX = 8
N_GY = 4
DEVICES = 32


def place_ends(values, rng, smallest, high):
    dims = values.shape
    spot = [jax.random.randint(jax.random.fold_in(rng, axis), (), 0, dims[axis]) for axis in range(len(dims))]
    values = values.at[tuple(spot)].set(smallest)
    longest = dims.index(max(dims))
    spot[longest] = (spot[longest] + 1) % dims[longest]
    return values.at[tuple(spot)].set(high)


def steps_of(stream_key, extent, split, least, high):
    def one(axis_at, shards_of):
        heights = jax.random.uniform(jax.random.fold_in(jax.random.fold_in(stream_key, 6), axis_at), (shards_of,), jnp.float32, least / len(split), high / len(split))
        return jnp.repeat(jnp.exp(heights), extent[axis_at] // shards_of).reshape((-1,) + (1,) * (len(extent) - axis_at - 1))

    level = one(*split[0])
    for cut in split[1:]:
        level = level * one(*cut)
    return level


def assign_block(key, own, number, rows, count, top, limit, slope):
    sequence = jax.random.permutation(key, count)
    crowded, usual = load_shares(count, rows * top, limit, slope, True), load_shares(count, rows * top, limit, slope, False)
    places = jnp.arange(count)

    def named(sizes, offset_by):
        used = int((sizes > 0).sum())
        fixed = max(1, used // 4)
        moved = fixed + (places - fixed + offset_by * (used - fixed)) % max(1, count - fixed)
        return jnp.zeros((count,), jnp.int32).at[sequence[jnp.where(places < fixed, places, moved)]].set(jnp.asarray(sizes, jnp.int32))

    sizes = jnp.where(number % 4 == 0, named(crowded, number // 4), named(usual, number - number // 4 - 1))
    mixed = jax.random.permutation(jax.random.fold_in(own, 3), count)
    giver, receiver = mixed[0:count // 2 * 2:2], mixed[1:count // 2 * 2:2]
    margin = jnp.minimum(sizes[giver] - 1, limit - sizes[receiver]) // 2
    margin = jnp.where((giver == sequence[0]) | (receiver == sequence[0]) | (sizes[receiver] == 0), 0, jnp.maximum(margin, 0))
    moved = jax.random.randint(jax.random.fold_in(own, 4), (count // 2,), 0, 1 << 20) % (margin + 1)
    sizes = sizes.at[giver].add(-moved).at[receiver].add(moved)
    labels = jnp.searchsorted(jnp.cumsum(sizes), jnp.arange(rows * top), side="right").astype(jnp.int32)
    table = labels.reshape(top, rows).T
    table = table[jax.random.permutation(jax.random.fold_in(own, 1), rows)]
    offset_by = jax.random.randint(jax.random.fold_in(own, 2), (rows, 1), 0, top)
    return jnp.take_along_axis(table, (jnp.arange(top)[None, :] + offset_by) % top, axis=1)


def load_shares(count, total, most, skew, full):
    loads = [(1 << 20) // math.isqrt(grade ** skew) + 1 for grade in range(1, count + 1)]
    largest = most if full else min(most, max(-(-total // count), total * loads[0] // sum(loads)))
    least = 1 if total - largest >= count - 1 else 0
    counts, surplus = [largest] + [least] * (count - 1), total - largest - least * (count - 1)
    while surplus > 0:
        candidates = [i for i in range(1, count) if counts[i] < largest] or [i for i in range(1, count) if counts[i] < most]
        whole, remaining = sum([loads[i] for i in candidates]), surplus
        for i in candidates:
            addition = min(most - counts[i], max(1, remaining * loads[i] // whole), surplus)
            counts[i] = counts[i] + addition
            surplus = surplus - addition
    return np.array(counts)


def normal_values(rng, dims, spread, reach, shards=(), kind=jnp.bfloat16):
    values = jax.random.normal(rng, dims, jnp.float32) * spread
    if len(shards) > 0:
        values = steps_of(rng, dims, shards, -0.22, 0.18) * values
    return jnp.clip(values, min=-reach, max=reach).astype(kind)


def setup_inputs(seed: int = 0) -> dict:
    key_list = jax.random.split(jax.random.key(seed), 11)
    atm_state = normal_values(key_list[0], (6, ATM_COLS), 1.0, 6.0, ((1, 32),), jnp.float32)
    pair_block = place_ends(jax.random.randint(key_list[1], (DEVICES * NPAIR,), 0, NBLK_DEV), jax.random.fold_in(key_list[1], 1), 0, NBLK_DEV - 1).astype(jnp.int32)
    pair_owner_keys = jax.random.split(jax.random.fold_in(key_list[2], 1), (DEVICES * NPAIR) // NPAIR)
    pair_owner_turns = jax.random.permutation(jax.random.fold_in(key_list[2], 3), (DEVICES * NPAIR) // NPAIR)
    pair_owner = jax.vmap(lambda own, number: assign_block(jax.random.fold_in(key_list[2], 2), own, number, NPAIR, DEVICES, 1, CAP, 2))(pair_owner_keys, pair_owner_turns).reshape((DEVICES * NPAIR, 1))
    pair_row = place_ends(jax.random.randint(key_list[3], (DEVICES * NPAIR,), 0, TX), jax.random.fold_in(key_list[3], 1), 0, TX - 1).astype(jnp.int32)
    pair_tile = place_ends(jax.random.randint(key_list[4], (DEVICES * NPAIR,), 0, NTILE), jax.random.fold_in(key_list[4], 1), 0, NTILE - 1).astype(jnp.int32)
    remap_weight = jnp.clip(jnp.exp(math.log(0.029907227) - 2.9957323 * jax.random.uniform(key_list[5], (DEVICES * NTILE, ABLK, TY), jnp.float32) ** steps_of(key_list[5], (DEVICES * NTILE, ABLK, TY), ((0, 32),), -0.2, 0.2)), 0.0014953613, 0.029907227).astype(jnp.bfloat16)
    wet_mask = place_ends((jax.random.randint(key_list[6], (NXO, NYO), 0, 10) < 7).astype(jnp.int32), jax.random.fold_in(key_list[6], 1), 0, 1)
    ocean_state = normal_values(key_list[7], (4, LEV, NXO, NYO), 1.0, 6.0, ((2, 8), (3, 4)), jnp.float32)
    vert_kappa = jnp.clip(jnp.exp(math.log(3.0) - 4.0943445 * jax.random.uniform(key_list[8], (LEV, NXO, NYO), jnp.float32) ** steps_of(key_list[8], (LEV, NXO, NYO), ((1, 8), (2, 4)), -0.2, 0.2)), 0.05, 3.0)
    horiz_kappa = jnp.clip(jnp.exp(math.log(0.24) - 2.4849066 * jax.random.uniform(key_list[9], (NXO, NYO), jnp.float32) ** steps_of(key_list[9], (NXO, NYO), ((0, 8), (1, 4)), -0.2, 0.2)), 0.02, 0.24)
    return dict(atm_state=atm_state, pair_block=pair_block, pair_owner=pair_owner, pair_row=pair_row, pair_tile=pair_tile, remap_weight=remap_weight, wet_mask=wet_mask, ocean_state=ocean_state, vert_kappa=vert_kappa, horiz_kappa=horiz_kappa)


def surface_flux(atm_state):
    wind_u = atm_state[0]
    wind_v = atm_state[1]
    speed = jnp.sqrt(wind_u * wind_u + wind_v * wind_v + 0.25)
    heat_flux = 0.5 * speed * (atm_state[2] - atm_state[5])
    water_flux = atm_state[4] - 0.3 * speed * atm_state[3]
    return jnp.stack([heat_flux, water_flux, 0.2 * speed * wind_u, 0.2 * speed * wind_v]).astype(jnp.bfloat16)

def column_mix(fields, vert_kappa):
    levels = vert_kappa.shape[0]
    face_coef = 0.5 * (vert_kappa[:-1] + vert_kappa[1:])
    zero_plane = jnp.zeros_like(vert_kappa[:1])
    above = jnp.concatenate([zero_plane, face_coef], 0)
    below = jnp.concatenate([face_coef, zero_plane], 0)
    diagonal = 1.0 + above + below
    upper_list = []
    rhs_list = []
    for level_index in range(levels):
        if level_index == 0:
            pivot_inv = 1.0 / diagonal[0]
            rhs_now = fields[:, 0] * pivot_inv
        else:
            pivot_inv = 1.0 / (diagonal[level_index] + above[level_index] * upper_list[-1])
            rhs_now = (fields[:, level_index] + above[level_index] * rhs_list[-1]) * pivot_inv
        upper_list.append(-below[level_index] * pivot_inv)
        rhs_list.append(rhs_now)
    solved = [rhs_list[-1]]
    for level_index in range(levels - 2, -1, -1):
        solved.append(rhs_list[level_index] - upper_list[level_index] * solved[-1])
    return jnp.stack(solved[::-1], 1)

def shifted(array, step_x, step_y):
    size_x = array.shape[-2]
    size_y = array.shape[-1]
    return array[..., 1 + step_x:size_x - 1 + step_x, 1 + step_y:size_y - 1 + step_y]

def diffuse(padded, coefficients):
    kappa_pad = coefficients[0]
    wet_pad = coefficients[1]
    centre = shifted(padded, 0, 0)
    kappa_mid = shifted(kappa_pad, 0, 0)
    wet_mid = shifted(wet_pad, 0, 0)
    result = centre
    for step_x, step_y in ((1, 0), (-1, 0), (0, 1), (0, -1)):
        face_coef = 0.25 * (kappa_mid + shifted(kappa_pad, step_x, step_y)) * wet_mid * shifted(wet_pad, step_x, step_y)
        result = result + face_coef * (shifted(padded, step_x, step_y) - centre)
    return result

def reference(atm_state, pair_block, pair_owner, pair_row, pair_tile, remap_weight, wet_mask, ocean_state, vert_kappa, horiz_kappa):
    highest = lax.Precision.HIGHEST
    devices = N_GX * N_GY
    fluxes = surface_flux(atm_state)
    blocks_all = fluxes.reshape(4, devices, NBLK_DEV, ABLK).transpose(1, 2, 0, 3)
    blocks_of = pair_block.reshape(devices, NPAIR)
    tiles_of = pair_tile.reshape(devices, NPAIR)
    weights_all = remap_weight.reshape(devices, NTILE, ABLK, TY)

    def forward_one(inputs):
        device_blocks, block_ids, tile_ids, device_weights = inputs
        picked = device_blocks[block_ids].astype(jnp.float32)
        chosen = device_weights[tile_ids].astype(jnp.float32)
        return jnp.einsum('pca,pab->pcb', picked, chosen, precision=highest)
    contrib = lax.map(forward_one, (blocks_all, blocks_of, tiles_of, weights_all)).reshape(devices * NPAIR, 4, TY)
    owner_ids = pair_owner[:, 0]
    cell_x = owner_ids // N_GY * TX + pair_row
    cell_g = owner_ids % N_GY
    forcing = jnp.zeros((NXO, N_GY, 4, TY), jnp.float32).at[cell_x, cell_g].add(contrib)
    forcing = forcing.transpose(2, 0, 1, 3).reshape(4, NXO, NYO)
    wet_frac = wet_mask.astype(jnp.float32)
    forced = ocean_state.at[:, 0].add(forcing * wet_frac[None])
    mixed = column_mix(forced, vert_kappa)
    coefficients = jnp.pad(jnp.stack([horiz_kappa, wet_frac]), ((0, 0), (1, 1), (1, 1)))
    tracers = mixed[:2]
    for pass_index in range(2):
        tracers = diffuse(jnp.pad(tracers, ((0, 0), (0, 0), (1, 1), (1, 1))), coefficients)
    ocean_next = jnp.concatenate([tracers, mixed[2:]], 0)
    surface = jnp.concatenate([ocean_next[:, 0] * wet_frac[None], wet_frac[None]], 0)
    surface_cells = surface.reshape(5, NXO, N_GY, TY).transpose(1, 2, 0, 3)
    picks = surface_cells[cell_x, cell_g].reshape(devices, NPAIR, 5, TY)

    def backward_one(inputs):
        device_picks, block_ids, tile_ids, device_weights = inputs
        chosen = device_weights[tile_ids].astype(jnp.float32)
        back = jnp.einsum('pab,pcb->pca', chosen, device_picks, precision=highest)
        sums = jax.ops.segment_sum(back, block_ids, num_segments=NBLK_DEV)
        values = sums[:, :4] / jnp.maximum(sums[:, 4:5], 0.1)
        return values.transpose(1, 0, 2).reshape(4, NBLK_DEV * ABLK)
    per_device = lax.map(backward_one, (picks, blocks_of, tiles_of, weights_all))
    atm_surface = per_device.transpose(1, 0, 2).reshape(4, ATM_COLS)
    return (ocean_next, atm_surface)
```

```python
import functools

import jax
import jax.numpy as jnp
from jax import lax
from jax.experimental import pallas as pl
from jax.experimental.pallas import tpu as pltpu
from jax.sharding import PartitionSpec as P

F32 = jnp.float32
BF16 = jnp.bfloat16
VMEM = pltpu.VMEM
SMEM = pltpu.SMEM


def remap_out_kernel(capacity, block_s, owner_s, row_s, tile_s, atm, weights, out, slot_o, rows_o, flux, fill):
    npairs = block_s.shape[0]
    nblocks = flux.shape[0]
    devices = fill.shape[0]
    out[...] = jnp.zeros_like(out)

    def clear_rows(i, carry):
        rows_o[i] = -1
        return carry

    lax.fori_loop(0, rows_o.shape[0], clear_rows, 0, unroll=16)

    def clear_fill(i, carry):
        fill[i] = 0
        return carry

    lax.fori_loop(0, devices, clear_fill, 0, unroll=16)
    wind_u = atm[0:1, :]
    wind_v = atm[1:2, :]
    speed = jnp.sqrt(wind_u * wind_u + wind_v * wind_v + 0.25)
    heat = 0.5 * speed * (atm[2:3, :] - atm[5:6, :])
    water = atm[4:5, :] - 0.3 * speed * atm[3:4, :]
    planes = jnp.concatenate(
        [heat, water, 0.2 * speed * wind_u, 0.2 * speed * wind_v, jnp.zeros((12, wind_u.shape[1]), F32)], 0
    ).astype(BF16)
    for b in range(nblocks):
        flux[b] = planes[:, b * 128 : (b + 1) * 128]

    def pair(p, carry):
        owner = owner_s[p]
        rank = fill[owner]
        fill[owner] = rank + 1
        slot = owner * capacity + rank
        slot_o[p] = slot
        rows_o[slot] = row_s[p]
        value = jnp.dot(flux[block_s[p]], weights[tile_s[p]], preferred_element_type=F32)
        out[slot] = value[0:4]
        return carry

    lax.fori_loop(0, npairs, pair, 0, unroll=8)


def remap_out(capacity, devices, atm_state, pair_block, owner, pair_row, pair_tile, remap_weight):
    npairs = pair_block.shape[0]
    slots = devices * capacity
    nblocks = atm_state.shape[1] // 128
    smem = pl.BlockSpec(memory_space=SMEM)
    vmem = pl.BlockSpec(memory_space=VMEM)
    return pl.pallas_call(
        functools.partial(remap_out_kernel, capacity),
        out_shape=(
            jax.ShapeDtypeStruct((slots, 4, 128), F32),
            jax.ShapeDtypeStruct((npairs,), jnp.int32),
            jax.ShapeDtypeStruct((slots,), jnp.int32),
        ),
        in_specs=[smem] * 4 + [vmem] * 2,
        out_specs=(vmem, smem, smem),
        scratch_shapes=[pltpu.VMEM((nblocks, 16, 128), BF16), pltpu.SMEM((devices,), jnp.int32)],
        compiler_params=pltpu.CompilerParams(vmem_limit_bytes=24 * 1024 * 1024),
        cost_estimate=pl.CostEstimate(flops=2 * npairs * 16 * 128 * 128, bytes_accessed=6 << 20, transcendentals=0),
    )(pair_block, owner, pair_row, pair_tile, atm_state, remap_weight)


def remap_back_kernel(block_s, tile_s, slot_s, cell_s, returned, wet, weights, out, total):
    npairs = block_s.shape[0]
    nblocks = total.shape[0]
    total[...] = jnp.zeros_like(total)

    def pair(p, carry):
        rows = returned[slot_s[p]]
        mask = wet[pl.ds(cell_s[p], 1), :].astype(F32)
        full = jnp.concatenate([rows, mask, jnp.zeros((3, 128), F32)], 0)
        high = full.astype(BF16)
        low = (full - high.astype(F32)).astype(BF16)
        both = jnp.concatenate([high, low], 0)
        value = lax.dot_general(
            both, weights[tile_s[p]], (((1,), (1,)), ((), ())), preferred_element_type=F32
        )
        b = block_s[p]
        total[b] = total[b] + (value[0:8] + value[8:16])
        return carry

    lax.fori_loop(0, npairs, pair, 0, unroll=8)
    for b in range(nblocks):
        sums = total[b]
        out[:, b * 128 : (b + 1) * 128] = sums[0:4] / jnp.maximum(sums[4:5], 0.1)


def remap_back(pair_block, pair_tile, slot, cell, returned, wet_all, remap_weight, nblocks):
    npairs = pair_block.shape[0]
    smem = pl.BlockSpec(memory_space=SMEM)
    vmem = pl.BlockSpec(memory_space=VMEM)
    return pl.pallas_call(
        remap_back_kernel,
        out_shape=jax.ShapeDtypeStruct((4, nblocks * 128), F32),
        in_specs=[smem] * 4 + [vmem] * 3,
        out_specs=vmem,
        scratch_shapes=[pltpu.VMEM((nblocks, 8, 128), F32)],
        compiler_params=pltpu.CompilerParams(vmem_limit_bytes=24 * 1024 * 1024),
        cost_estimate=pl.CostEstimate(flops=2 * npairs * 16 * 128 * 128, bytes_accessed=6 << 20, transcendentals=0),
    )(pair_block, pair_tile, slot, cell, returned, wet_all, remap_weight)


def extended(shard, sides, width):
    for axis, dim in sides:
        count, length = (lax.axis_size(axis), shard.shape[dim])
        up = [(i, (i + 1) % count) for i in range(count - 1)]
        down = [(j, i) for i, j in up]
        last = lax.slice_in_dim(shard, length - width, length, axis=dim)
        leading = lax.slice_in_dim(shard, 0, width, axis=dim)
        before = lax.ppermute(last, axis, up)
        after = lax.ppermute(leading, axis, down)
        shard = jnp.concatenate([before, shard, after], axis=dim)
    return shard


def column_mix(fields, vert_kappa):
    levels = vert_kappa.shape[0]
    face_coef = 0.5 * (vert_kappa[:-1] + vert_kappa[1:])
    zero_plane = jnp.zeros_like(vert_kappa[:1])
    above = jnp.concatenate([zero_plane, face_coef], 0)
    below = jnp.concatenate([face_coef, zero_plane], 0)
    diagonal = 1.0 + above + below
    upper_list = []
    rhs_list = []
    for level_index in range(levels):
        if level_index == 0:
            pivot_inv = 1.0 / diagonal[0]
            rhs_now = fields[:, 0] * pivot_inv
        else:
            pivot_inv = 1.0 / (diagonal[level_index] + above[level_index] * upper_list[-1])
            rhs_now = (fields[:, level_index] + above[level_index] * rhs_list[-1]) * pivot_inv
        upper_list.append(-below[level_index] * pivot_inv)
        rhs_list.append(rhs_now)
    solved = [rhs_list[-1]]
    for level_index in range(levels - 2, -1, -1):
        solved.append(rhs_list[level_index] - upper_list[level_index] * solved[-1])
    return jnp.stack(solved[::-1], 1)


def shifted(array, step_x, step_y):
    size_x = array.shape[-2]
    size_y = array.shape[-1]
    return array[..., 1 + step_x : size_x - 1 + step_x, 1 + step_y : size_y - 1 + step_y]


def diffuse(padded, coefficients):
    kappa_pad = coefficients[0]
    wet_pad = coefficients[1]
    centre = shifted(padded, 0, 0)
    kappa_mid = shifted(kappa_pad, 0, 0)
    wet_mid = shifted(wet_pad, 0, 0)
    result = centre
    for step_x, step_y in ((1, 0), (-1, 0), (0, 1), (0, -1)):
        face_coef = (
            0.25
            * (kappa_mid + shifted(kappa_pad, step_x, step_y))
            * wet_mid
            * shifted(wet_pad, step_x, step_y)
        )
        result = result + face_coef * (shifted(padded, step_x, step_y) - centre)
    return result


def local(
    atm_state,
    pair_block,
    pair_owner,
    pair_row,
    pair_tile,
    remap_weight,
    wet_mask,
    ocean_state,
    vert_kappa,
    horiz_kappa,
):
    highest = lax.Precision.HIGHEST
    grid_x = lax.axis_size("gx")
    grid_y = lax.axis_size("gy")
    devices = grid_x * grid_y
    npairs = pair_block.shape[0]
    capacity = max(2, 2 * npairs // devices)
    slot_count = devices * capacity
    tile_rows = ocean_state.shape[2]
    nblocks = atm_state.shape[1] // 128
    me = lax.axis_index("gx") * grid_y + lax.axis_index("gy")
    owner = pair_owner.reshape(npairs)
    wet_all = lax.all_gather(wet_mask, ("gx", "gy"), axis=0, tiled=True)
    outgoing, slot, out_rows = remap_out(
        capacity, devices, atm_state, pair_block, owner, pair_row, pair_tile, remap_weight
    )
    arrived = lax.all_to_all(outgoing, ("gx", "gy"), split_axis=0, concat_axis=0, tiled=True)
    rows_all = lax.all_gather(out_rows, ("gx", "gy"), axis=0, tiled=True)
    in_rows = lax.dynamic_slice_in_dim(rows_all.reshape(devices, devices, capacity), me, 1, 1).reshape(slot_count)
    placing = (jnp.arange(tile_rows, dtype=jnp.int32)[:, None] == in_rows[None, :]).astype(F32)
    forcing = jnp.dot(
        placing,
        arrived.reshape(slot_count, 4 * 128),
        precision=highest,
        preferred_element_type=F32,
    )
    forcing = forcing.reshape(tile_rows, 4, 128).transpose(1, 0, 2)
    wet_frac = wet_mask.astype(F32)
    forced = ocean_state.at[:, 0].add(forcing * wet_frac[None])
    coef_pad = extended(jnp.stack([horiz_kappa, wet_frac]), (("gx", 1), ("gy", 2)), 2)
    mixed = column_mix(forced, vert_kappa)
    tracers = extended(mixed[:2], (("gx", 2), ("gy", 3)), 2)
    tracers = diffuse(tracers, coef_pad)
    tracers = diffuse(tracers, coef_pad[:, 1:-1, 1:-1])
    ocean_next = jnp.concatenate([tracers, mixed[2:]], 0)
    surface = ocean_next[:, 0] * wet_frac[None]
    sendback = surface.transpose(1, 0, 2)[jnp.maximum(in_rows, 0)]
    returned = lax.all_to_all(sendback, ("gx", "gy"), split_axis=0, concat_axis=0, tiled=True)
    atm_surface = remap_back(
        pair_block, pair_tile, slot, owner * tile_rows + pair_row, returned, wet_all, remap_weight, nblocks
    )
    return (ocean_next, atm_surface)


def solution(mesh):
    placed = (
        P(None, ("gx", "gy")),
        P(("gx", "gy")),
        P(("gx", "gy"), None),
        P(("gx", "gy")),
        P(("gx", "gy")),
        P(("gx", "gy"), None, None),
        P("gx", "gy"),
        P(None, None, "gx", "gy"),
        P(None, "gx", "gy"),
        P("gx", "gy"),
    )
    return jax.shard_map(
        local,
        mesh=mesh,
        in_specs=placed,
        out_specs=(P(None, None, "gx", "gy"), P(None, ("gx", "gy"))),
        check_vma=False,
    )
```

```python
import functools

import jax
import jax.numpy as jnp
from jax import lax
from jax.experimental import pallas as pl
from jax.experimental.pallas import tpu as pltpu
from jax.sharding import PartitionSpec as P

F32 = jnp.float32
BF16 = jnp.bfloat16
I32 = jnp.int32
VMEM = pltpu.VMEM
SMEM = pltpu.SMEM
LANES = 128
EDGE = 16
HALO = 8


def iota(shape, dim):
    return lax.broadcasted_iota(I32, shape, dim)


def pick(mask, value):
    return jnp.where(mask, value, 0.0)


def split(value):
    high = value.astype(BF16)
    return high, (value - high.astype(F32)).astype(BF16)


def back_rows(capacity):
    return 4 * capacity + max(8, capacity)


def remap_out_kernel(
    capacity, grid_y, tile_rows, block_h, owner_h, row_h, tile_h, atm_h, weights_h,
    out, field_o, wet_o, block_s, owner_s, row_s, tile_s, atm, weights, flux, fill, rows_acc, cols_acc, sems,
):
    devices = fill.shape[0]
    npairs = block_s.shape[0]
    nblocks = flux.shape[0]
    message = 4 * capacity + EDGE
    copies = [
        pltpu.make_async_copy(src, dst, sems.at[n])
        for n, (src, dst) in enumerate(
            [(atm_h, atm), (block_h, block_s), (owner_h, owner_s), (row_h, row_s), (tile_h, tile_s), (weights_h, weights)]
        )
    ]
    for copy in copies:
        copy.start()
    out[...] = jnp.zeros_like(out)
    rows_acc[...] = jnp.zeros_like(rows_acc)
    cols_acc[...] = jnp.zeros_like(cols_acc)

    def clear_fill(i, carry):
        fill[i] = 0
        return carry

    lax.fori_loop(0, devices, clear_fill, 0, unroll=16)
    copies[0].wait()
    wind_u = atm[0:1, :]
    wind_v = atm[1:2, :]
    speed = jnp.sqrt(wind_u * wind_u + wind_v * wind_v + 0.25)
    heat = 0.5 * speed * (atm[2:3, :] - atm[5:6, :])
    water = atm[4:5, :] - 0.3 * speed * atm[3:4, :]
    planes = jnp.concatenate(
        [heat, water, 0.2 * speed * wind_u, 0.2 * speed * wind_v, jnp.zeros((4, wind_u.shape[1]), F32)]
        + [heat] * 4
        + [water] * 4,
        0,
    ).astype(BF16)
    for b in range(nblocks):
        flux[b] = planes[:, b * LANES : (b + 1) * LANES]
    for copy in copies[1:]:
        copy.wait()

    sub = iota((8, LANES), 0)
    lane = iota((8, LANES), 1)
    part = sub % 4
    edge_row = jnp.where(part == 0, 0, jnp.where(part == 1, 1, tile_rows - 4 + part))
    edge_col = lane == jnp.where(part == 0, 0, jnp.where(part == 1, 1, LANES - 4 + part))
    col_lane = lane - 64 * (sub // 4)
    id_rank = jnp.where((sub == 0) & (lane >= 64), (lane - 64) // 4, -1)

    def pair(p, carry):
        owner = owner_s[p]
        row = row_s[p]
        rank = fill[owner]
        fill[owner] = rank + 1
        field_o[p] = owner * back_rows(capacity) + 4 * rank
        wet_o[p] = owner * back_rows(capacity) + 4 * capacity + rank
        value = jnp.dot(flux[block_s[p]], weights[tile_s[p]], preferred_element_type=F32)
        out[pl.ds(owner * message + 4 * rank, 4), :] = value[0:4]
        tracer = value[8:16]
        rows_acc[owner] = rows_acc[owner] + pick(edge_row == row, tracer)
        column = jnp.sum(pick(edge_col, tracer), axis=1, keepdims=True)
        number = (row + 1).astype(F32)
        cols_acc[owner] = cols_acc[owner] + (
            pick(col_lane == row, column) + pick(id_rank == rank, number)
        )
        return carry

    lax.fori_loop(0, npairs, pair, 0, unroll=8)

    grid_x = devices // grid_y
    zero = jnp.zeros((8, LANES), F32)
    inside = ((sub < 4) & (lane < 64)) | (sub >= 4)

    def folded(d):
        kept = pick(inside, cols_acc[d])
        return kept + pltpu.roll(kept, 4, 0)

    folds = {}

    def fold(i, j):
        if not (0 <= i < grid_x and 0 <= j < grid_y):
            return zero
        return folds_ref(i * grid_y + j)

    def folds_ref(d):
        if d not in folds:
            folds[d] = folded(d)
        return folds[d]

    last = (lane == tile_rows - 1) | (lane == 64 + tile_rows - 1)
    first = (lane == 0) | (lane == 64)
    for d in range(devices):
        i, j = d // grid_y, d % grid_y
        below = rows_acc[d + grid_y] if i < grid_x - 1 else zero
        above = rows_acc[d - grid_y] if i > 0 else zero
        base = d * message + 4 * capacity
        out[base : base + 8, :] = jnp.where(part < 2, below, above)
        if i > 1:
            folds.pop(d - 2 * grid_y, None)
        right, left = fold(i, j + 1), fold(i, j - 1)
        tile = pick(sub < 2, right) + pick((sub == 2) | (sub == 3), left)
        tile = tile + pick((sub == 4) & last, fold(i - 1, j + 1)) + pick((sub == 4) & first, fold(i + 1, j + 1))
        tile = tile + pick((sub == 7) & last, fold(i - 1, j - 1)) + pick((sub == 7) & first, fold(i + 1, j - 1))
        numbers = pltpu.roll(cols_acc[d], 5, 0)
        tile = tile + pick((sub == 5) & (lane >= 64), numbers)
        out[base + 8 : base + 16, :] = tile


def remap_out(capacity, grid_y, devices, tile_rows, atm_state, pair_block, owner, pair_row, pair_tile, remap_weight):
    npairs = pair_block.shape[0]
    nblocks = atm_state.shape[1] // LANES
    message = 4 * capacity + EDGE
    vmem = pl.BlockSpec(memory_space=VMEM)
    smem = pl.BlockSpec(memory_space=SMEM)
    return pl.pallas_call(
        functools.partial(remap_out_kernel, capacity, grid_y, tile_rows),
        out_shape=(
            jax.ShapeDtypeStruct((devices * message, LANES), F32),
            jax.ShapeDtypeStruct((npairs,), I32),
            jax.ShapeDtypeStruct((npairs,), I32),
        ),
        in_specs=[pl.BlockSpec(memory_space=pl.ANY)] * 6,
        out_specs=(vmem, smem, smem),
        scratch_shapes=[pltpu.SMEM((npairs,), I32)] * 4
        + [
            pltpu.VMEM(atm_state.shape, F32),
            pltpu.VMEM(remap_weight.shape, BF16),
            pltpu.VMEM((nblocks, 16, LANES), BF16),
            pltpu.SMEM((devices,), I32),
            pltpu.VMEM((devices, 8, LANES), F32),
            pltpu.VMEM((devices, 8, LANES), F32),
            pltpu.SemaphoreType.DMA((6,)),
        ],
        compiler_params=pltpu.CompilerParams(vmem_limit_bytes=24 << 20),
        cost_estimate=pl.CostEstimate(flops=2 * npairs * 16 * LANES * LANES, bytes_accessed=6 << 20, transcendentals=0),
    )(pair_block, owner, pair_row, pair_tile, atm_state, remap_weight)


def solve_kernel(state, kappa, horiz, wet, tracer, currents, edge_up, edge_down):
    levels = kappa.shape[0]
    rows_all = kappa.shape[1]
    planes = tracer.shape[0]

    def chunk(c, carry):
        rows = pl.ds(pl.multiple_of(c * 8, 8), 8)
        column = [kappa[l, rows, :] for l in range(levels)]
        face = [0.5 * (column[l] + column[l + 1]) for l in range(levels - 1)]
        upper = []
        now = None
        for l in range(levels):
            diagonal = 1.0
            if l > 0:
                diagonal = diagonal + face[l - 1]
            if l < levels - 1:
                diagonal = diagonal + face[l]
            if l > 0:
                diagonal = diagonal + face[l - 1] * upper[-1]
            inverse = 1.0 / diagonal
            if l == 0:
                now = [state[f, 0, rows, :] * inverse for f in range(4)] + [inverse]
            else:
                pull = face[l - 1] * inverse
                now = [state[f, l, rows, :] * inverse + pull * now[f] for f in range(4)] + [pull * now[4]]
            upper.append(-face[l] * inverse if l < levels - 1 else None)
            store(l, rows, now)
        for l in range(levels - 2, -1, -1):
            here = load(l, rows)
            now = [here[f] - upper[l] * now[f] for f in range(5)]
            store(l, rows, now)
        return carry

    def store(l, rows, now):
        tracer[l, rows, :] = now[0]
        tracer[levels + l, rows, :] = now[1]
        currents[0, l, rows, :] = now[2]
        currents[1, l, rows, :] = now[3]
        tracer[2 * levels + l, rows, :] = now[4]

    def load(l, rows):
        return [
            tracer[l, rows, :],
            tracer[levels + l, rows, :],
            currents[0, l, rows, :],
            currents[1, l, rows, :],
            tracer[2 * levels + l, rows, :],
        ]

    lax.fori_loop(0, rows_all // 8, chunk, 0)
    tracer[3 * levels] = horiz[...]
    tracer[3 * levels + 1] = wet[...].astype(F32)
    for k in range(planes):
        edge_up[k] = tracer[k, 0:8, :]
        edge_down[k] = tracer[k, rows_all - 8 : rows_all, :]


def solve(ocean_state, vert_kappa, horiz_kappa, wet_mask):
    levels, rows, _ = vert_kappa.shape
    planes = 3 * levels + 2
    vmem = pl.BlockSpec(memory_space=VMEM)
    return pl.pallas_call(
        solve_kernel,
        out_shape=(
            jax.ShapeDtypeStruct((planes, rows, LANES), F32),
            jax.ShapeDtypeStruct((2, levels, rows, LANES), F32),
            jax.ShapeDtypeStruct((planes, 8, LANES), F32),
            jax.ShapeDtypeStruct((planes, 8, LANES), F32),
        ),
        in_specs=[vmem] * 4,
        out_specs=(vmem,) * 4,
        compiler_params=pltpu.CompilerParams(vmem_limit_bytes=24 << 20),
        cost_estimate=pl.CostEstimate(flops=20 << 20, bytes_accessed=6 << 20, transcendentals=0),
    )(ocean_state, vert_kappa, horiz_kappa, wet_mask)


def pack_kernel(levels, tracer, above, below, wide, to_left, to_right):
    planes, rows, _ = tracer.shape
    for k in range(planes):
        wide[k, 0:HALO, :] = above[k]
        wide[k, HALO : HALO + rows, :] = tracer[k]
        wide[k, HALO + rows : 2 * HALO + rows, :] = below[k]
    lane = iota((8, LANES), 1)

    def chunk(c, carry):
        at = pl.ds(pl.multiple_of(c * 8, 8), 8)

        def place(values, lanes):
            left = [jnp.zeros((8, LANES), F32)] * 1
            left, right = jnp.zeros((8, LANES), F32), jnp.zeros((8, LANES), F32)
            for k, (near, far) in zip(values, lanes):
                value = wide[k, at, :]
                left = jnp.where(lane == near, pltpu.roll(value, near, 1), left)
                left = jnp.where(lane == far, pltpu.roll(value, far - 1, 1), left)
                right = jnp.where(lane == near + 1, pltpu.roll(value, (near + 2) % LANES, 1), right)
                right = jnp.where(lane == far + 1, pltpu.roll(value, (far + 3) % LANES, 1), right)
            return left, right

        left, right = place(range(2 * levels), [(2 * k, 64 + 2 * k) for k in range(2 * levels)])
        to_left[0, at, :] = left
        to_right[0, at, :] = right
        lanes = [(2 * l, 64 + 2 * l) for l in range(levels)]
        lanes += [(2 * levels, 2 * levels + 2), (2 * levels + 4, 2 * levels + 6)]
        left, right = place(range(2 * levels, 3 * levels + 2), lanes)
        to_left[1, at, :] = left
        to_right[1, at, :] = right
        return carry

    lax.fori_loop(0, (rows + 2 * HALO) // 8, chunk, 0)


def pack(levels, tracer, above, below):
    planes, rows, _ = tracer.shape
    tall = rows + 2 * HALO
    vmem = pl.BlockSpec(memory_space=VMEM)
    return pl.pallas_call(
        functools.partial(pack_kernel, levels),
        out_shape=(
            jax.ShapeDtypeStruct((planes, tall, LANES), F32),
            jax.ShapeDtypeStruct((2, tall, LANES), F32),
            jax.ShapeDtypeStruct((2, tall, LANES), F32),
        ),
        in_specs=[vmem] * 3,
        out_specs=(vmem,) * 3,
        compiler_params=pltpu.CompilerParams(vmem_limit_bytes=24 << 20),
        cost_estimate=pl.CostEstimate(flops=8 << 20, bytes_accessed=4 << 20, transcendentals=0),
    )(tracer, above, below)


def faces_kernel(levels, horiz, wet, own_left, own_right, from_left, from_right, faces, packed):
    tall = horiz.shape[0]
    lane = iota((tall, LANES), 1)
    odd = lane % 2 == 1
    twice = lane % 64 < 2 * levels
    tracer = jnp.where(odd, from_left[0], from_right[0])
    other = jnp.where(odd, from_left[1], from_right[1])
    at = 2 * levels

    def column(offset):
        return other[:, at + offset : at + offset + 1], other[:, at + offset + 1 : at + offset + 2]

    kappa_right, kappa_left = column(0)
    kappa_far_right, kappa_far_left = column(2)
    wet_right, wet_left = column(4)
    wet_far_right, wet_far_left = column(6)
    h = horiz[...]
    w = wet[...]

    kappa_near = jnp.where(odd, kappa_left, kappa_right)
    kappa_far = jnp.where(odd, kappa_far_left, kappa_far_right)
    wet_near = jnp.where(odd, wet_left, wet_right)
    wet_far = jnp.where(odd, wet_far_left, wet_far_right)
    kappa_own = jnp.where(odd, h[:, 0:1], h[:, LANES - 1 : LANES])
    wet_own = jnp.where(odd, w[:, 0:1], w[:, LANES - 1 : LANES])

    def face(kappa_a, wet_a, kappa_b, wet_b):
        return 0.25 * (kappa_a + kappa_b) * wet_a * wet_b

    unit = jnp.where(twice, other, pltpu.roll(other, 2 * levels, 1))
    packed[0] = tracer
    packed[1] = unit * jnp.where(lane < 64, wet_near, wet_far)
    packed[2] = jnp.where(odd, pltpu.roll(own_left[0], 1, 1), pltpu.roll(own_right[0], LANES - 1, 1))
    own = jnp.where(odd, pltpu.roll(own_left[1], 1, 1), pltpu.roll(own_right[1], LANES - 1, 1))
    packed[3] = jnp.where(twice, own, pltpu.roll(own, 2 * levels, 1)) * wet_own
    north = face(kappa_near, wet_near, pltpu.roll(kappa_near, 1, 0), pltpu.roll(wet_near, 1, 0))
    packed[4] = north
    packed[5] = pltpu.roll(north, tall - 1, 0)
    packed[6] = face(kappa_near, wet_near, kappa_far, wet_far)
    packed[7] = face(kappa_near, wet_near, kappa_own, wet_own)

    north = face(h, w, pltpu.roll(h, 1, 0), pltpu.roll(w, 1, 0))
    faces[0] = north
    faces[1] = pltpu.roll(north, tall - 1, 0)
    west = face(
        h, w, jnp.where(lane == 0, kappa_left, pltpu.roll(h, 1, 1)), jnp.where(lane == 0, wet_left, pltpu.roll(w, 1, 1))
    )
    faces[2] = west
    faces[3] = jnp.where(lane == LANES - 1, face(h, w, kappa_right, wet_right), pltpu.roll(west, LANES - 1, 1))


def face_values(levels, wide, own_left, own_right, from_left, from_right):
    tall = wide.shape[1]
    vmem = pl.BlockSpec(memory_space=VMEM)
    return pl.pallas_call(
        functools.partial(faces_kernel, levels),
        out_shape=(
            jax.ShapeDtypeStruct((4, tall, LANES), F32),
            jax.ShapeDtypeStruct((8, tall, LANES), F32),
        ),
        in_specs=[vmem] * 6,
        out_specs=(vmem,) * 2,
        cost_estimate=pl.CostEstimate(flops=1 << 20, bytes_accessed=1 << 20, transcendentals=0),
    )(wide[3 * levels], wide[3 * levels + 1], own_left, own_right, from_left, from_right)


def one_pass(value, faces, beside, shift):
    tall = value.shape[0]
    lane = iota(value.shape, 1)
    moved = pltpu.roll(beside, shift, 1)
    west = jnp.where(lane == 0, moved, pltpu.roll(value, 1, 1))
    east = jnp.where(lane == LANES - 1, moved, pltpu.roll(value, LANES - 1, 1))
    result = value + faces[1] * (pltpu.roll(value, tall - 1, 0) - value)
    result = result + faces[0] * (pltpu.roll(value, 1, 0) - value)
    result = result + faces[3] * (east - value)
    return result + faces[2] * (west - value)


def middle_kernel(
    capacity, levels, arrived, top, currents, wet_wide, faces, packed, sent, forcing, near_o,
    placing, values, number_t,
):
    devices, message, _ = arrived.shape
    rows_all = currents.shape[1]
    tall = rows_all + 2 * HALO
    span = 4 * capacity
    group = LANES // span
    groups = devices // group
    sub8 = iota((8, LANES), 0)
    lane8 = iota((8, LANES), 1)

    lane1 = iota((1, LANES), 1)
    numbers = []
    for m in range(groups):
        line = jnp.zeros((1, LANES), F32)
        for g in range(group):
            ids = arrived[m * group + g, span + 13 : span + 14, :]
            moved = pltpu.roll(ids, (g * span - 64) % LANES, 1)
            line = jnp.where(lane1 // span == g, moved, line)
        numbers.append(line)
    number_t[...] = jnp.transpose(
        jnp.concatenate(numbers + [jnp.zeros((LANES - groups, LANES), F32)], 0)
    )

    row_number = iota((rows_all, LANES), 0).astype(F32) + 1.0
    lane_field = iota((rows_all, LANES), 1) % 4
    for m in range(groups):
        hit = numbers[m] == row_number
        for f in range(4):
            placing[f * rows_all : (f + 1) * rows_all, m * LANES : (m + 1) * LANES] = jnp.where(
                hit & (lane_field == f), 1.0, 0.0
            ).astype(BF16)
    edge_rows = jnp.zeros((8, LANES), F32)
    edge_cols = jnp.zeros((8, LANES), F32)
    for s in range(devices):
        high, low = split(arrived[s, 0:span, :])
        values[s * span : (s + 1) * span, 0:LANES] = high
        values[s * span : (s + 1) * span, LANES : 2 * LANES] = low
        edge_rows = edge_rows + arrived[s, span : span + 8, :]
        edge_cols = edge_cols + arrived[s, span + 8 : span + 16, :]
    total = jnp.dot(placing[...], values[...], preferred_element_type=F32)
    total = total[:, 0:LANES] + total[:, LANES : 2 * LANES]

    def plane(f):
        return total[f * rows_all : (f + 1) * rows_all]

    wide = []
    for f in range(2):
        before = pick(sub8 >= 6, edge_rows if f == 1 else pltpu.roll(edge_rows, 4, 0))
        after = pick(sub8 < 2, edge_rows if f == 0 else pltpu.roll(edge_rows, 4, 0))
        wide.append(jnp.concatenate([before, plane(f), after], 0))
        forcing[f] = wide[f]
    wet = wet_wide[HALO : HALO + rows_all, :]
    for f in range(2, 4):
        forcing[f, 0:HALO, :] = jnp.zeros((HALO, LANES), F32)
        forcing[f, HALO : HALO + rows_all, :] = plane(f) * wet
        forcing[f, HALO + rows_all : tall, :] = jnp.zeros((HALO, LANES), F32)

    corner = pick((sub8 == 0) | (sub8 == 3), pltpu.roll(edge_cols, 4, 0))
    side = pick(sub8 < 4, edge_cols)
    within = (lane8 >= HALO) & (lane8 < HALO + rows_all)
    ends = (lane8 == HALO - 1) | (lane8 == HALO + rows_all)
    halves = []
    for f in range(2):
        body = pltpu.roll(side, (HALO - 64 * f) % LANES, 1)
        tips = pltpu.roll(corner, (HALO + rows_all - 64 * f) % LANES, 1)
        halves.append((pick(within, body) + pick(ends, tips))[0:4])
    columns = jnp.concatenate(halves, 0)
    upright = jnp.transpose(jnp.concatenate([columns, jnp.zeros((LANES - 8, LANES), F32)], 0))[0:tall]
    lane = iota((tall, LANES), 1)
    odd = lane % 2 == 1
    heat = lane % 64 < 2 * levels
    close = lane < 64

    def chosen(right_near, left_near, right_far, left_far):
        near = jnp.where(odd, left_near, right_near)
        far = jnp.where(odd, left_far, right_far)
        return jnp.where(close, near, far)

    def of_field(f):
        return [upright[:, 4 * f + e : 4 * f + e + 1] for e in (0, 3, 1, 2)]

    beside = jnp.where(heat, chosen(*of_field(0)), chosen(*of_field(1)))
    both = packed[0] + packed[1] * beside
    far = pltpu.roll(both, 64, 1)
    ends_of = [jnp.where(odd, w[:, 0:1], w[:, LANES - 1 : LANES]) for w in wide]
    own = packed[2] + packed[3] * jnp.where(heat, ends_of[0], ends_of[1])
    near = both + packed[5] * (pltpu.roll(both, tall - 1, 0) - both)
    near = near + packed[4] * (pltpu.roll(both, 1, 0) - both)
    near = near + packed[6] * (far - both)
    near = near + packed[7] * (own - both)
    near_o[0] = both
    near_o[1] = near

    surface = []
    unit = top[2] * wet_wide[...]
    for f in range(2):
        value = top[f] + unit * wide[f]
        shift = LANES - (2 * levels * f + 1)
        value = one_pass(value, faces, both, shift)
        value = one_pass(value, faces, near, shift)
        surface.append(value[HALO : HALO + rows_all] * wet)
    for f in range(2):
        surface.append(
            (currents[f] + top[2, HALO : HALO + rows_all, :] * forcing[2 + f, HALO : HALO + rows_all, :]) * wet
        )
    high, low = split(jnp.concatenate(surface, 0))
    source = jnp.concatenate([high, low], 1)
    lane_t = iota((LANES, 4 * rows_all), 1)
    sub_t = iota((LANES, 4 * rows_all), 0)
    target = jnp.where(sub_t % 4 == lane_t // rows_all, lane_t % rows_all + 1, -1).astype(F32)
    mask = jnp.concatenate([wet, jnp.zeros((LANES - rows_all, LANES), F32)], 0).astype(BF16)
    per = LANES // 4
    slot_number = number_t[pl.ds(0, per, stride=4), :]
    lane_s = (iota((per, LANES), 1) + 1).astype(F32)
    height = back_rows(capacity)
    for m in range(groups):
        chosen_rows = jnp.where(number_t[:, m : m + 1] == target, 1.0, 0.0).astype(BF16)
        rows = jnp.dot(chosen_rows, source, preferred_element_type=F32)
        rows = rows[:, 0:LANES] + rows[:, LANES : 2 * LANES]
        slots = jnp.where(slot_number[:, m : m + 1] == lane_s, 1.0, 0.0).astype(BF16)
        masks = jnp.dot(slots, mask, preferred_element_type=F32)
        for g in range(group):
            s = m * group + g
            sent[s, 0:span, :] = rows[g * span : (g + 1) * span]
            sent[s, span : span + capacity, :] = masks[g * capacity : (g + 1) * capacity]
            if height > span + capacity:
                sent[s, span + capacity : height, :] = jnp.zeros((height - span - capacity, LANES), F32)


def middle(capacity, levels, arrived, top, currents, wet_wide, faces, packed):
    devices = arrived.shape[0]
    rows = currents.shape[1]
    tall = rows + 2 * HALO
    vmem = pl.BlockSpec(memory_space=VMEM)
    return pl.pallas_call(
        functools.partial(middle_kernel, capacity, levels),
        out_shape=(
            jax.ShapeDtypeStruct((devices, back_rows(capacity), LANES), F32),
            jax.ShapeDtypeStruct((4, tall, LANES), F32),
            jax.ShapeDtypeStruct((2, tall, LANES), F32),
        ),
        in_specs=[vmem] * 6,
        out_specs=(vmem,) * 3,
        scratch_shapes=[
            pltpu.VMEM((4 * rows, 4 * capacity * devices), BF16),
            pltpu.VMEM((4 * capacity * devices, 2 * LANES), BF16),
            pltpu.VMEM((LANES, LANES), F32),
        ],
        compiler_params=pltpu.CompilerParams(vmem_limit_bytes=24 << 20),
        cost_estimate=pl.CostEstimate(flops=200 << 20, bytes_accessed=4 << 20, transcendentals=0),
    )(arrived, top, currents, wet_wide, faces, packed)


def finish_kernel(levels, wide, currents, faces, forcing, near, ocean):
    rows_all = currents.shape[2]
    inner = slice(HALO, HALO + rows_all)

    def level(l, carry):
        unit = wide[2 * levels + l]
        masked = unit * wide[3 * levels + 1]
        for f in range(2):
            value = wide[f * levels + l] + masked * forcing[f]
            shift = LANES - 1 - 2 * (levels * f + l)
            value = one_pass(value, faces, near[0], shift)
            value = one_pass(value, faces, near[1], shift)
            ocean[f, l] = value[inner]
            ocean[2 + f, l] = currents[f, l] + unit[inner] * forcing[2 + f][inner]
        return carry

    lax.fori_loop(0, levels, level, 0)


def finish(levels, wide, currents, faces, forcing, near):
    rows = currents.shape[2]
    vmem = pl.BlockSpec(memory_space=VMEM)
    return pl.pallas_call(
        functools.partial(finish_kernel, levels),
        out_shape=jax.ShapeDtypeStruct((4, levels, rows, LANES), F32),
        in_specs=[vmem] * 5,
        out_specs=vmem,
        compiler_params=pltpu.CompilerParams(vmem_limit_bytes=24 << 20),
        cost_estimate=pl.CostEstimate(flops=40 << 20, bytes_accessed=6 << 20, transcendentals=0),
    )(wide, currents, faces, forcing, near)


def remap_back_kernel(block_h, tile_h, field_h, wet_h, returned, weights, out, block_s, tile_s, field_s, wet_s, total, sems):
    npairs = block_s.shape[0]
    nblocks = total.shape[0]
    copies = [
        pltpu.make_async_copy(src, dst, sems.at[n])
        for n, (src, dst) in enumerate([(block_h, block_s), (tile_h, tile_s), (field_h, field_s), (wet_h, wet_s)])
    ]
    for copy in copies:
        copy.start()
    total[...] = jnp.zeros_like(total)
    for copy in copies:
        copy.wait()

    def pair(p, carry):
        rows = returned[pl.ds(field_s[p], 4), :]
        mask = returned[pl.ds(wet_s[p], 1), :]
        full = jnp.concatenate([rows, mask, jnp.zeros((3, LANES), F32)], 0)
        high, low = split(full)
        value = lax.dot_general(
            jnp.concatenate([high, low], 0),
            weights[tile_s[p]],
            (((1,), (1,)), ((), ())),
            preferred_element_type=F32,
        )
        b = block_s[p]
        total[b] = total[b] + (value[0:8] + value[8:16])
        return carry

    lax.fori_loop(0, npairs, pair, 0, unroll=8)
    for b in range(nblocks):
        sums = total[b]
        out[:, b * LANES : (b + 1) * LANES] = sums[0:4] / jnp.maximum(sums[4:5], 0.1)


def remap_back(pair_block, pair_tile, field_at, wet_at, returned, remap_weight, nblocks):
    npairs = pair_block.shape[0]
    vmem = pl.BlockSpec(memory_space=VMEM)
    return pl.pallas_call(
        remap_back_kernel,
        out_shape=jax.ShapeDtypeStruct((4, nblocks * LANES), F32),
        in_specs=[pl.BlockSpec(memory_space=pl.ANY)] * 4 + [vmem] * 2,
        out_specs=vmem,
        scratch_shapes=[pltpu.SMEM((npairs,), I32)] * 4
        + [pltpu.VMEM((nblocks, 8, LANES), F32), pltpu.SemaphoreType.DMA((4,))],
        compiler_params=pltpu.CompilerParams(vmem_limit_bytes=24 << 20),
        cost_estimate=pl.CostEstimate(flops=2 * npairs * 16 * LANES * LANES, bytes_accessed=6 << 20, transcendentals=0),
    )(pair_block, pair_tile, field_at, wet_at, returned, remap_weight)


def local(
    atm_state,
    pair_block,
    pair_owner,
    pair_row,
    pair_tile,
    remap_weight,
    wet_mask,
    ocean_state,
    vert_kappa,
    horiz_kappa,
):
    grid_x = lax.axis_size("gx")
    grid_y = lax.axis_size("gy")
    devices = grid_x * grid_y
    npairs = pair_block.shape[0]
    capacity = max(2, 2 * npairs // devices)
    levels, tile_rows, _ = vert_kappa.shape
    nblocks = atm_state.shape[1] // LANES
    owner = pair_owner.reshape(npairs)
    message = 4 * capacity + EDGE
    outgoing, field_at, wet_at = remap_out(
        capacity, grid_y, devices, tile_rows, atm_state, pair_block, owner, pair_row, pair_tile, remap_weight
    )
    arrived = lax.all_to_all(
        outgoing.reshape(devices, message, LANES), ("gx", "gy"), split_axis=0, concat_axis=0, tiled=True
    )
    tracer, currents, edge_up, edge_down = solve(ocean_state, vert_kappa, horiz_kappa, wet_mask)
    rise_x = [(i, i + 1) for i in range(grid_x - 1)]
    fall_x = [(b, a) for a, b in rise_x]
    rise_y = [(i, i + 1) for i in range(grid_y - 1)]
    fall_y = [(b, a) for a, b in rise_y]
    above = lax.ppermute(edge_down, "gx", rise_x)
    below = lax.ppermute(edge_up, "gx", fall_x)
    wide, to_left, to_right = pack(levels, tracer, above, below)
    from_left = lax.ppermute(to_right, "gy", rise_y)
    from_right = lax.ppermute(to_left, "gy", fall_y)
    faces, packed = face_values(levels, wide, to_left, to_right, from_left, from_right)
    top = jnp.stack([wide[0], wide[levels], wide[2 * levels]])
    sent, forcing, near = middle(
        capacity, levels, arrived, top, currents[:, 0], wide[3 * levels + 1], faces, packed
    )
    returned = lax.all_to_all(sent, ("gx", "gy"), split_axis=0, concat_axis=0, tiled=True)
    ocean_next = finish(levels, wide, currents, faces, forcing, near)
    atm_surface = remap_back(
        pair_block, pair_tile, field_at, wet_at, returned.reshape(-1, LANES), remap_weight, nblocks
    )
    return (ocean_next, atm_surface)


def solution(mesh):
    placed = (
        P(None, ("gx", "gy")),
        P(("gx", "gy")),
        P(("gx", "gy"), None),
        P(("gx", "gy")),
        P(("gx", "gy")),
        P(("gx", "gy"), None, None),
        P("gx", "gy"),
        P(None, None, "gx", "gy"),
        P(None, "gx", "gy"),
        P("gx", "gy"),
    )
    return jax.shard_map(
        local,
        mesh=mesh,
        in_specs=placed,
        out_specs=(P(None, None, "gx", "gy"), P(None, ("gx", "gy"))),
        check_vma=False,
    )
```

```python
import functools

import jax
import jax.numpy as jnp
from jax import lax
from jax.experimental import pallas as pl
from jax.experimental.pallas import tpu as pltpu
from jax.sharding import PartitionSpec as P

F32 = jnp.float32
BF16 = jnp.bfloat16
I32 = jnp.int32
VMEM = pltpu.VMEM
SMEM = pltpu.SMEM
LANES = 128
EDGE = 16
HALO = 8
PARTS = 8


def hbm():
    return pl.BlockSpec(memory_space=pltpu.HBM)


def vmem():
    return pl.BlockSpec(memory_space=VMEM)


def pin(*arrays):
    return [pltpu.with_memory_space_constraint(a, pltpu.HBM) for a in arrays]


def start_all(pairs, sems, first=0):
    copies = [pltpu.make_async_copy(src, dst, sems.at[first + n]) for n, (src, dst) in enumerate(pairs)]
    for copy in copies:
        copy.start()
    return copies


def wait_all(copies):
    for copy in copies:
        copy.wait()


def iota(shape, dim):
    return lax.broadcasted_iota(I32, shape, dim)


def pick(mask, value):
    return jnp.where(mask, value, 0.0)


def split(value):
    high = value.astype(BF16)
    return high, (value - high.astype(F32)).astype(BF16)


def back_rows(capacity):
    return 4 * capacity + max(8, capacity)


def remap_out_kernel(
    capacity, grid_y, tile_rows, block_h, owner_h, row_h, tile_h, atm_h, weights_h, out_h,
    out, block_s, owner_s, row_s, tile_s, atm, weights, flux, every, fill, rows_acc, cols_acc, sems, weight_sems, out_sems,
):
    devices = fill.shape[0]
    npairs = block_s.shape[0]
    tiles = weights.shape[0]
    four = flux.shape[0]
    nblocks = four // 4
    message = 4 * capacity + EDGE
    copies = [
        pltpu.make_async_copy(src, dst, sems.at[n])
        for n, (src, dst) in enumerate(
            [(atm_h, atm), (block_h, block_s), (owner_h, owner_s), (row_h, row_s), (tile_h, tile_s)]
        )
    ]
    for copy in copies:
        copy.start()
    part_tiles = tiles // PARTS
    parts = [pl.ds(n * part_tiles, part_tiles) for n in range(PARTS)]
    loads = [pltpu.make_async_copy(weights_h.at[at], weights.at[at], weight_sems.at[n]) for n, at in enumerate(parts)]
    for load in loads:
        load.start()
    out[...] = jnp.zeros_like(out)
    rows_acc[...] = jnp.zeros_like(rows_acc)
    cols_acc[...] = jnp.zeros_like(cols_acc)

    def clear_fill(i, carry):
        fill[i] = 0
        return carry

    lax.fori_loop(0, devices, clear_fill, 0, unroll=16)
    copies[0].wait()
    wind_u = atm[0:1, :]
    wind_v = atm[1:2, :]
    speed = jnp.sqrt(wind_u * wind_u + wind_v * wind_v + 0.25)
    heat = 0.5 * speed * (atm[2:3, :] - atm[5:6, :])
    water = atm[4:5, :] - 0.3 * speed * atm[3:4, :]
    for f, plane in enumerate([heat, water, 0.2 * speed * wind_u, 0.2 * speed * wind_v]):
        for b in range(nblocks):
            flux[f * nblocks + b : f * nblocks + b + 1, :] = plane[:, b * LANES : (b + 1) * LANES]
    source = flux[...].astype(BF16)

    for n in range(PARTS):
        loads[n].wait()

        def tile_step(t, carry):
            every[pl.ds(pl.multiple_of(t * four, 8), four), :] = jnp.dot(
                source, weights[t], preferred_element_type=F32
            )
            return carry

        lax.fori_loop(n * part_tiles, (n + 1) * part_tiles, tile_step, 0, unroll=4)
    for copy in copies[1:]:
        copy.wait()

    sub = iota((8, LANES), 0)
    lane = iota((8, LANES), 1)
    part = sub % 4
    edge_row = jnp.where(part == 0, 0, jnp.where(part == 1, 1, tile_rows - 4 + part))
    edge_col = lane == jnp.where(part == 0, 0, jnp.where(part == 1, 1, LANES - 4 + part))
    col_lane = lane - 64 * (sub // 4)
    id_rank = jnp.where((sub == 0) & (lane >= 64), (lane - 64) // 4, -1)

    def pair(p, carry):
        owner = owner_s[p]
        row = row_s[p]
        rank = fill[owner]
        fill[owner] = rank + 1
        first = tile_s[p] * four + block_s[p]
        lines = [every[pl.ds(first + f * nblocks, 1), :] for f in range(4)]
        for f in range(4):
            out[pl.ds(owner * message + 4 * rank + f, 1), :] = lines[f]
        tracer = jnp.where(sub < 4, lines[0], lines[1])
        rows_acc[owner] = rows_acc[owner] + pick(edge_row == row, tracer)
        column = jnp.sum(pick(edge_col, tracer), axis=1, keepdims=True)
        number = (row + 1).astype(F32)
        cols_acc[owner] = cols_acc[owner] + (
            pick(col_lane == row, column) + pick(id_rank == rank, number)
        )
        return carry

    lax.fori_loop(0, npairs, pair, 0, unroll=8)

    grid_x = devices // grid_y
    zero = jnp.zeros((8, LANES), F32)
    inside = ((sub < 4) & (lane < 64)) | (sub >= 4)
    folds = {}

    def fold(i, j):
        if not (0 <= i < grid_x and 0 <= j < grid_y):
            return zero
        d = i * grid_y + j
        if d not in folds:
            kept = pick(inside, cols_acc[d])
            folds[d] = kept + pltpu.roll(kept, 4, 0)
        return folds[d]

    last = (lane == tile_rows - 1) | (lane == 64 + tile_rows - 1)
    first = (lane == 0) | (lane == 64)
    send = devices // 4
    stores = []
    for d in range(devices):
        i, j = d // grid_y, d % grid_y
        below = rows_acc[d + grid_y] if i < grid_x - 1 else zero
        above = rows_acc[d - grid_y] if i > 0 else zero
        base = d * message + 4 * capacity
        out[base : base + 8, :] = jnp.where(part < 2, below, above)
        if i > 1:
            folds.pop(d - 2 * grid_y, None)
        right, left = fold(i, j + 1), fold(i, j - 1)
        tile = pick(sub < 2, right) + pick((sub == 2) | (sub == 3), left)
        tile = tile + pick((sub == 4) & last, fold(i - 1, j + 1)) + pick((sub == 4) & first, fold(i + 1, j + 1))
        tile = tile + pick((sub == 7) & last, fold(i - 1, j - 1)) + pick((sub == 7) & first, fold(i + 1, j - 1))
        numbers = pltpu.roll(cols_acc[d], 5, 0)
        tile = tile + pick((sub == 5) & (lane >= 64), numbers)
        out[base + 8 : base + 16, :] = tile
        if d % send == send - 1:
            n = d // send
            at = pl.ds(n * send * message, send * message)
            stores.append(pltpu.make_async_copy(out.at[at], out_h.at[at], out_sems.at[n]))
            stores[-1].start()
    for store in stores:
        store.wait()


def remap_out(capacity, grid_y, devices, tile_rows, atm_state, pair_block, owner, pair_row, pair_tile, remap_weight):
    npairs = pair_block.shape[0]
    nblocks = atm_state.shape[1] // LANES
    message = 4 * capacity + EDGE
    tiles = remap_weight.shape[0]
    return pl.pallas_call(
        functools.partial(remap_out_kernel, capacity, grid_y, tile_rows),
        out_shape=pltpu.HBM((devices * message, LANES), F32),
        in_specs=[hbm()] * 6,
        out_specs=hbm(),
        scratch_shapes=[pltpu.VMEM((devices * message, LANES), F32)]
        + [pltpu.SMEM((npairs,), I32)] * 4
        + [
            pltpu.VMEM(atm_state.shape, F32),
            pltpu.VMEM(remap_weight.shape, BF16),
            pltpu.VMEM((4 * nblocks, LANES), F32),
            pltpu.VMEM((tiles * 4 * nblocks, LANES), F32),
            pltpu.SMEM((devices,), I32),
            pltpu.VMEM((devices, 8, LANES), F32),
            pltpu.VMEM((devices, 8, LANES), F32),
            pltpu.SemaphoreType.DMA((5,)),
            pltpu.SemaphoreType.DMA((PARTS,)),
            pltpu.SemaphoreType.DMA((4,)),
        ],
        compiler_params=pltpu.CompilerParams(vmem_limit_bytes=40 << 20),
        cost_estimate=pl.CostEstimate(
            flops=2 * tiles * 4 * nblocks * LANES * LANES, bytes_accessed=6 << 20, transcendentals=0
        ),
    )(*pin(pair_block, owner, pair_row, pair_tile, atm_state, remap_weight))


def solve_kernel(state, kappa, horiz, wet, tracer, currents_h, edge_up, edge_down, currents, sems):
    levels = kappa.shape[0]
    rows_all = kappa.shape[1]
    planes = tracer.shape[0]

    def chunk(c, carry):
        rows = pl.ds(pl.multiple_of(c * 8, 8), 8)
        column = [kappa[l, rows, :] for l in range(levels)]
        face = [0.5 * (column[l] + column[l + 1]) for l in range(levels - 1)]
        upper = []
        now = None
        for l in range(levels):
            diagonal = 1.0
            if l > 0:
                diagonal = diagonal + face[l - 1]
            if l < levels - 1:
                diagonal = diagonal + face[l]
            if l > 0:
                diagonal = diagonal + face[l - 1] * upper[-1]
            inverse = 1.0 / diagonal
            if l == 0:
                now = [state[f, 0, rows, :] * inverse for f in range(4)] + [inverse]
            else:
                pull = face[l - 1] * inverse
                now = [state[f, l, rows, :] * inverse + pull * now[f] for f in range(4)] + [pull * now[4]]
            upper.append(-face[l] * inverse if l < levels - 1 else None)
            store(l, rows, now)
        for l in range(levels - 2, -1, -1):
            here = load(l, rows)
            now = [here[f] - upper[l] * now[f] for f in range(5)]
            store(l, rows, now)
        return carry

    def store(l, rows, now):
        tracer[l, rows, :] = now[0]
        tracer[levels + l, rows, :] = now[1]
        currents[0, l, rows, :] = now[2]
        currents[1, l, rows, :] = now[3]
        tracer[2 * levels + l, rows, :] = now[4]

    def load(l, rows):
        return [
            tracer[l, rows, :],
            tracer[levels + l, rows, :],
            currents[0, l, rows, :],
            currents[1, l, rows, :],
            tracer[2 * levels + l, rows, :],
        ]

    lax.fori_loop(0, rows_all // 8, chunk, 0)
    out = start_all([(currents, currents_h)], sems)
    tracer[3 * levels] = horiz[...]
    tracer[3 * levels + 1] = wet[...].astype(F32)
    for k in range(planes):
        edge_up[k] = tracer[k, 0:8, :]
        edge_down[k] = tracer[k, rows_all - 8 : rows_all, :]
    wait_all(out)


def solve(ocean_state, vert_kappa, horiz_kappa, wet_mask):
    levels, rows, _ = vert_kappa.shape
    planes = 3 * levels + 2
    return pl.pallas_call(
        solve_kernel,
        out_shape=(
            jax.ShapeDtypeStruct((planes, rows, LANES), F32),
            pltpu.HBM((2, levels, rows, LANES), F32),
            jax.ShapeDtypeStruct((planes, 8, LANES), F32),
            jax.ShapeDtypeStruct((planes, 8, LANES), F32),
        ),
        in_specs=[vmem()] * 4,
        out_specs=(vmem(), hbm(), vmem(), vmem()),
        scratch_shapes=[pltpu.VMEM((2, levels, rows, LANES), F32), pltpu.SemaphoreType.DMA((1,))],
        compiler_params=pltpu.CompilerParams(vmem_limit_bytes=24 << 20),
        cost_estimate=pl.CostEstimate(flops=20 << 20, bytes_accessed=6 << 20, transcendentals=0),
    )(ocean_state, vert_kappa, horiz_kappa, wet_mask)


def pack_kernel(levels, tracer, above, below, wide_h, to_left, to_right, wide, sems):
    planes, rows, _ = tracer.shape
    for k in range(planes):
        wide[k, 0:HALO, :] = above[k]
        wide[k, HALO : HALO + rows, :] = tracer[k]
        wide[k, HALO + rows : 2 * HALO + rows, :] = below[k]
    out = start_all([(wide, wide_h)], sems)
    lane = iota((8, LANES), 1)

    def chunk(c, carry):
        at = pl.ds(pl.multiple_of(c * 8, 8), 8)

        def place(values, lanes):
            left, right = jnp.zeros((8, LANES), F32), jnp.zeros((8, LANES), F32)
            for k, (near, far) in zip(values, lanes):
                value = wide[k, at, :]
                left = jnp.where(lane == near, pltpu.roll(value, near, 1), left)
                left = jnp.where(lane == far, pltpu.roll(value, far - 1, 1), left)
                right = jnp.where(lane == near + 1, pltpu.roll(value, (near + 2) % LANES, 1), right)
                right = jnp.where(lane == far + 1, pltpu.roll(value, (far + 3) % LANES, 1), right)
            return left, right

        left, right = place(range(2 * levels), [(2 * k, 64 + 2 * k) for k in range(2 * levels)])
        to_left[0, at, :] = left
        to_right[0, at, :] = right
        lanes = [(2 * l, 64 + 2 * l) for l in range(levels)]
        lanes += [(2 * levels, 2 * levels + 2), (2 * levels + 4, 2 * levels + 6)]
        left, right = place(range(2 * levels, 3 * levels + 2), lanes)
        to_left[1, at, :] = left
        to_right[1, at, :] = right
        return carry

    lax.fori_loop(0, (rows + 2 * HALO) // 8, chunk, 0)
    wait_all(out)


def pack(levels, tracer, above, below):
    planes, rows, _ = tracer.shape
    tall = rows + 2 * HALO
    return pl.pallas_call(
        functools.partial(pack_kernel, levels),
        out_shape=(
            pltpu.HBM((planes, tall, LANES), F32),
            jax.ShapeDtypeStruct((2, tall, LANES), F32),
            jax.ShapeDtypeStruct((2, tall, LANES), F32),
        ),
        in_specs=[vmem()] * 3,
        out_specs=(hbm(), vmem(), vmem()),
        scratch_shapes=[pltpu.VMEM((planes, tall, LANES), F32), pltpu.SemaphoreType.DMA((1,))],
        compiler_params=pltpu.CompilerParams(vmem_limit_bytes=24 << 20),
        cost_estimate=pl.CostEstimate(flops=8 << 20, bytes_accessed=4 << 20, transcendentals=0),
    )(tracer, above, below)


def faces_kernel(
    levels, wide_h, own_left_h, own_right_h, from_left_h, from_right_h, faces_h, packed_h,
    coef, own_left, own_right, from_left, from_right, faces, packed, sems,
):
    wait_all(
        start_all(
            [
                (wide_h.at[pl.ds(3 * levels, 2)], coef),
                (own_left_h, own_left),
                (own_right_h, own_right),
                (from_left_h, from_left),
                (from_right_h, from_right),
            ],
            sems,
        )
    )
    horiz, wet = coef.at[0], coef.at[1]
    tall = horiz.shape[0]
    lane = iota((tall, LANES), 1)
    odd = lane % 2 == 1
    twice = lane % 64 < 2 * levels
    tracer = jnp.where(odd, from_left[0], from_right[0])
    other = jnp.where(odd, from_left[1], from_right[1])
    at = 2 * levels

    def column(offset):
        return other[:, at + offset : at + offset + 1], other[:, at + offset + 1 : at + offset + 2]

    kappa_right, kappa_left = column(0)
    kappa_far_right, kappa_far_left = column(2)
    wet_right, wet_left = column(4)
    wet_far_right, wet_far_left = column(6)
    h = horiz[...]
    w = wet[...]

    kappa_near = jnp.where(odd, kappa_left, kappa_right)
    kappa_far = jnp.where(odd, kappa_far_left, kappa_far_right)
    wet_near = jnp.where(odd, wet_left, wet_right)
    wet_far = jnp.where(odd, wet_far_left, wet_far_right)
    kappa_own = jnp.where(odd, h[:, 0:1], h[:, LANES - 1 : LANES])
    wet_own = jnp.where(odd, w[:, 0:1], w[:, LANES - 1 : LANES])

    def face(kappa_a, wet_a, kappa_b, wet_b):
        return 0.25 * (kappa_a + kappa_b) * wet_a * wet_b

    unit = jnp.where(twice, other, pltpu.roll(other, 2 * levels, 1))
    packed[0] = tracer
    packed[1] = unit * jnp.where(lane < 64, wet_near, wet_far)
    packed[2] = jnp.where(odd, pltpu.roll(own_left[0], 1, 1), pltpu.roll(own_right[0], LANES - 1, 1))
    own = jnp.where(odd, pltpu.roll(own_left[1], 1, 1), pltpu.roll(own_right[1], LANES - 1, 1))
    packed[3] = jnp.where(twice, own, pltpu.roll(own, 2 * levels, 1)) * wet_own
    north = face(kappa_near, wet_near, pltpu.roll(kappa_near, 1, 0), pltpu.roll(wet_near, 1, 0))
    packed[4] = north
    packed[5] = pltpu.roll(north, tall - 1, 0)
    packed[6] = face(kappa_near, wet_near, kappa_far, wet_far)
    packed[7] = face(kappa_near, wet_near, kappa_own, wet_own)

    north = face(h, w, pltpu.roll(h, 1, 0), pltpu.roll(w, 1, 0))
    faces[0] = north
    faces[1] = pltpu.roll(north, tall - 1, 0)
    west = face(
        h, w, jnp.where(lane == 0, kappa_left, pltpu.roll(h, 1, 1)), jnp.where(lane == 0, wet_left, pltpu.roll(w, 1, 1))
    )
    faces[2] = west
    faces[3] = jnp.where(lane == LANES - 1, face(h, w, kappa_right, wet_right), pltpu.roll(west, LANES - 1, 1))
    wait_all(start_all([(faces, faces_h), (packed, packed_h)], sems, 5))


def face_values(levels, wide, own_left, own_right, from_left, from_right):
    tall = wide.shape[1]
    return pl.pallas_call(
        functools.partial(faces_kernel, levels),
        out_shape=(
            pltpu.HBM((4, tall, LANES), F32),
            pltpu.HBM((8, tall, LANES), F32),
        ),
        in_specs=[hbm()] + [pl.BlockSpec(memory_space=pl.ANY)] * 4,
        out_specs=(hbm(),) * 2,
        scratch_shapes=[pltpu.VMEM((2, tall, LANES), F32)] * 5
        + [pltpu.VMEM((4, tall, LANES), F32), pltpu.VMEM((8, tall, LANES), F32), pltpu.SemaphoreType.DMA((7,))],
        compiler_params=pltpu.CompilerParams(vmem_limit_bytes=24 << 20),
        cost_estimate=pl.CostEstimate(flops=1 << 20, bytes_accessed=1 << 20, transcendentals=0),
    )(*pin(wide), own_left, own_right, from_left, from_right)


def one_pass(value, faces, beside, shift):
    tall = value.shape[0]
    lane = iota(value.shape, 1)
    moved = pltpu.roll(beside, shift, 1)
    west = jnp.where(lane == 0, moved, pltpu.roll(value, 1, 1))
    east = jnp.where(lane == LANES - 1, moved, pltpu.roll(value, LANES - 1, 1))
    result = value + faces[1] * (pltpu.roll(value, tall - 1, 0) - value)
    result = result + faces[0] * (pltpu.roll(value, 1, 0) - value)
    result = result + faces[3] * (east - value)
    return result + faces[2] * (west - value)


def middle_kernel(
    capacity, levels, arrived, wide_h, currents_h, faces_h, packed_h, sent_h, forcing_h, near_h,
    placing, values, number_t, top, currents, faces, packed, sent, forcing, near_o, sems, sent_sems,
):
    devices, message, _ = arrived.shape
    rows_all = currents.shape[1]
    tall = rows_all + 2 * HALO
    loads = start_all(
        [(wide_h.at[levels * k], top.at[k]) for k in range(3)]
        + [
            (wide_h.at[3 * levels + 1], top.at[3]),
            (currents_h.at[0, 0], currents.at[0]),
            (currents_h.at[1, 0], currents.at[1]),
            (faces_h, faces),
            (packed_h, packed),
        ],
        sems,
    )
    span = 4 * capacity
    group = LANES // span
    groups = devices // group
    sub8 = iota((8, LANES), 0)
    lane8 = iota((8, LANES), 1)

    lane1 = iota((1, LANES), 1)
    numbers = []
    for m in range(groups):
        line = jnp.zeros((1, LANES), F32)
        for g in range(group):
            ids = arrived[m * group + g, span + 13 : span + 14, :]
            moved = pltpu.roll(ids, (g * span - 64) % LANES, 1)
            line = jnp.where(lane1 // span == g, moved, line)
        numbers.append(line)
    number_t[...] = jnp.transpose(
        jnp.concatenate(numbers + [jnp.zeros((LANES - groups, LANES), F32)], 0)
    )

    row_number = iota((rows_all, LANES), 0).astype(F32) + 1.0
    lane_field = iota((rows_all, LANES), 1) % 4
    for m in range(groups):
        hit = numbers[m] == row_number
        for f in range(4):
            placing[f * rows_all : (f + 1) * rows_all, m * LANES : (m + 1) * LANES] = jnp.where(
                hit & (lane_field == f), 1.0, 0.0
            ).astype(BF16)
    edge_rows = jnp.zeros((8, LANES), F32)
    edge_cols = jnp.zeros((8, LANES), F32)
    for s in range(devices):
        high, low = split(arrived[s, 0:span, :])
        values[s * span : (s + 1) * span, 0:LANES] = high
        values[s * span : (s + 1) * span, LANES : 2 * LANES] = low
        edge_rows = edge_rows + arrived[s, span : span + 8, :]
        edge_cols = edge_cols + arrived[s, span + 8 : span + 16, :]
    total = jnp.dot(placing[...], values[...], preferred_element_type=F32)
    total = total[:, 0:LANES] + total[:, LANES : 2 * LANES]

    wait_all(loads)
    wet_wide = top[3]

    def plane(f):
        return total[f * rows_all : (f + 1) * rows_all]

    wide = []
    for f in range(2):
        before = pick(sub8 >= 6, edge_rows if f == 1 else pltpu.roll(edge_rows, 4, 0))
        after = pick(sub8 < 2, edge_rows if f == 0 else pltpu.roll(edge_rows, 4, 0))
        wide.append(jnp.concatenate([before, plane(f), after], 0))
        forcing[f] = wide[f]
    wet = wet_wide[HALO : HALO + rows_all]
    for f in range(2, 4):
        forcing[f, 0:HALO, :] = jnp.zeros((HALO, LANES), F32)
        forcing[f, HALO : HALO + rows_all, :] = plane(f) * wet
        forcing[f, HALO + rows_all : tall, :] = jnp.zeros((HALO, LANES), F32)

    corner = pick((sub8 == 0) | (sub8 == 3), pltpu.roll(edge_cols, 4, 0))
    side = pick(sub8 < 4, edge_cols)
    within = (lane8 >= HALO) & (lane8 < HALO + rows_all)
    ends = (lane8 == HALO - 1) | (lane8 == HALO + rows_all)
    halves = []
    for f in range(2):
        body = pltpu.roll(side, (HALO - 64 * f) % LANES, 1)
        tips = pltpu.roll(corner, (HALO + rows_all - 64 * f) % LANES, 1)
        halves.append((pick(within, body) + pick(ends, tips))[0:4])
    columns = jnp.concatenate(halves, 0)
    upright = jnp.transpose(jnp.concatenate([columns, jnp.zeros((LANES - 8, LANES), F32)], 0))[0:tall]
    lane = iota((tall, LANES), 1)
    odd = lane % 2 == 1
    heat = lane % 64 < 2 * levels
    close = lane < 64

    def chosen(right_near, left_near, right_far, left_far):
        near = jnp.where(odd, left_near, right_near)
        far = jnp.where(odd, left_far, right_far)
        return jnp.where(close, near, far)

    def of_field(f):
        return [upright[:, 4 * f + e : 4 * f + e + 1] for e in (0, 3, 1, 2)]

    beside = jnp.where(heat, chosen(*of_field(0)), chosen(*of_field(1)))
    both = packed[0] + packed[1] * beside
    far = pltpu.roll(both, 64, 1)
    ends_of = [jnp.where(odd, w[:, 0:1], w[:, LANES - 1 : LANES]) for w in wide]
    own = packed[2] + packed[3] * jnp.where(heat, ends_of[0], ends_of[1])
    near = both + packed[5] * (pltpu.roll(both, tall - 1, 0) - both)
    near = near + packed[4] * (pltpu.roll(both, 1, 0) - both)
    near = near + packed[6] * (far - both)
    near = near + packed[7] * (own - both)
    near_o[0] = both
    near_o[1] = near
    stores = start_all([(forcing, forcing_h), (near_o, near_h)], sems, 8)

    surface = []
    unit = top[2] * wet_wide
    for f in range(2):
        value = top[f] + unit * wide[f]
        shift = LANES - (2 * levels * f + 1)
        value = one_pass(value, faces, both, shift)
        value = one_pass(value, faces, near, shift)
        surface.append(value[HALO : HALO + rows_all] * wet)
    for f in range(2):
        surface.append(
            (currents[f] + top[2, HALO : HALO + rows_all, :] * forcing[2 + f, HALO : HALO + rows_all, :]) * wet
        )
    high, low = split(jnp.concatenate(surface, 0))
    source = jnp.concatenate([high, low], 1)
    lane_t = iota((LANES, 4 * rows_all), 1)
    sub_t = iota((LANES, 4 * rows_all), 0)
    target = jnp.where(sub_t % 4 == lane_t // rows_all, lane_t % rows_all + 1, -1).astype(F32)
    mask = jnp.concatenate([wet, jnp.zeros((LANES - rows_all, LANES), F32)], 0).astype(BF16)
    per = LANES // 4
    slot_number = number_t[pl.ds(0, per, stride=4), :]
    lane_s = (iota((per, LANES), 1) + 1).astype(F32)
    height = back_rows(capacity)
    for m in range(groups):
        chosen_rows = jnp.where(number_t[:, m : m + 1] == target, 1.0, 0.0).astype(BF16)
        rows = jnp.dot(chosen_rows, source, preferred_element_type=F32)
        rows = rows[:, 0:LANES] + rows[:, LANES : 2 * LANES]
        slots = jnp.where(slot_number[:, m : m + 1] == lane_s, 1.0, 0.0).astype(BF16)
        masks = jnp.dot(slots, mask, preferred_element_type=F32)
        for g in range(group):
            s = m * group + g
            sent[s, 0:span, :] = rows[g * span : (g + 1) * span]
            sent[s, span : span + capacity, :] = masks[g * capacity : (g + 1) * capacity]
            if height > span + capacity:
                sent[s, span + capacity : height, :] = jnp.zeros((height - span - capacity, LANES), F32)
        at = pl.ds(m * group, group)
        stores += start_all([(sent.at[at], sent_h.at[at])], sent_sems, m)
    wait_all(stores)


def middle(capacity, levels, arrived, wide, currents, faces, packed):
    devices = arrived.shape[0]
    rows = currents.shape[2]
    tall = rows + 2 * HALO
    height = back_rows(capacity)
    return pl.pallas_call(
        functools.partial(middle_kernel, capacity, levels),
        out_shape=(
            pltpu.HBM((devices, height, LANES), F32),
            pltpu.HBM((4, tall, LANES), F32),
            pltpu.HBM((2, tall, LANES), F32),
        ),
        in_specs=[vmem()] + [hbm()] * 4,
        out_specs=(hbm(),) * 3,
        scratch_shapes=[
            pltpu.VMEM((4 * rows, 4 * capacity * devices), BF16),
            pltpu.VMEM((4 * capacity * devices, 2 * LANES), BF16),
            pltpu.VMEM((LANES, LANES), F32),
            pltpu.VMEM((4, tall, LANES), F32),
            pltpu.VMEM((2, rows, LANES), F32),
            pltpu.VMEM((4, tall, LANES), F32),
            pltpu.VMEM((8, tall, LANES), F32),
            pltpu.VMEM((devices, height, LANES), F32),
            pltpu.VMEM((4, tall, LANES), F32),
            pltpu.VMEM((2, tall, LANES), F32),
            pltpu.SemaphoreType.DMA((10,)),
            pltpu.SemaphoreType.DMA((4 * capacity * devices // LANES,)),
        ],
        compiler_params=pltpu.CompilerParams(vmem_limit_bytes=24 << 20),
        cost_estimate=pl.CostEstimate(flops=200 << 20, bytes_accessed=4 << 20, transcendentals=0),
    )(arrived, *pin(wide, currents, faces, packed))


def finish_kernel(
    levels, wide_h, currents_h, faces_h, forcing_h, near_h, ocean, wide, currents, faces, forcing, near, sems
):
    rows_all = currents.shape[2]
    wait_all(
        start_all(
            [(wide_h, wide), (currents_h, currents), (faces_h, faces), (forcing_h, forcing), (near_h, near)], sems
        )
    )
    inner = slice(HALO, HALO + rows_all)

    def level(l, carry):
        unit = wide[2 * levels + l]
        masked = unit * wide[3 * levels + 1]
        for f in range(2):
            value = wide[f * levels + l] + masked * forcing[f]
            shift = LANES - 1 - 2 * (levels * f + l)
            value = one_pass(value, faces, near[0], shift)
            value = one_pass(value, faces, near[1], shift)
            ocean[f, l] = value[inner]
            ocean[2 + f, l] = currents[f, l] + unit[inner] * forcing[2 + f][inner]
        return carry

    lax.fori_loop(0, levels, level, 0)


def finish(levels, wide, currents, faces, forcing, near):
    rows = currents.shape[2]
    return pl.pallas_call(
        functools.partial(finish_kernel, levels),
        out_shape=jax.ShapeDtypeStruct((4, levels, rows, LANES), F32),
        in_specs=[hbm()] * 5,
        out_specs=vmem(),
        scratch_shapes=[pltpu.VMEM(a.shape, F32) for a in (wide, currents, faces, forcing, near)]
        + [pltpu.SemaphoreType.DMA((5,))],
        compiler_params=pltpu.CompilerParams(vmem_limit_bytes=24 << 20),
        cost_estimate=pl.CostEstimate(flops=40 << 20, bytes_accessed=6 << 20, transcendentals=0),
    )(*pin(wide, currents, faces, forcing, near))


def remap_back_kernel(
    capacity, block_h, tile_h, owner_h, returned, weights_h, out,
    block_s, tile_s, owner_s, fill, weights, picked, total, sems, weight_sems,
):
    npairs = block_s.shape[0]
    nblocks = total.shape[0]
    devices = fill.shape[0]
    height = back_rows(capacity)
    scalars = start_all([(owner_h, owner_s), (block_h, block_s), (tile_h, tile_s)], sems)
    part_tiles = weights.shape[0] // PARTS
    parts = [pl.ds(n * part_tiles, part_tiles) for n in range(PARTS)]
    loads = start_all([(weights_h.at[at], weights.at[at]) for at in parts], weight_sems)
    total[...] = jnp.zeros_like(total)

    def clear_fill(i, carry):
        fill[i] = 0
        return carry

    lax.fori_loop(0, devices, clear_fill, 0, unroll=16)
    wait_all(scalars)

    def gather(p, carry):
        owner = owner_s[p]
        rank = fill[owner]
        fill[owner] = rank + 1
        rows = returned[pl.ds(owner * height + 4 * rank, 4), :]
        mask = returned[pl.ds(owner * height + 4 * capacity + rank, 1), :]
        high, low = split(jnp.concatenate([rows, mask, jnp.zeros((3, LANES), F32)], 0))
        picked[p] = jnp.concatenate([high, low], 0)
        return carry

    lax.fori_loop(0, npairs, gather, 0, unroll=8)
    wait_all(loads)

    def pair(p, carry):
        value = lax.dot_general(
            picked[p], weights[tile_s[p]], (((1,), (1,)), ((), ())), preferred_element_type=F32
        )
        b = block_s[p]
        total[b] = total[b] + (value[0:8] + value[8:16])
        return carry

    lax.fori_loop(0, npairs, pair, 0, unroll=16)
    for b in range(nblocks):
        sums = total[b]
        out[:, b * LANES : (b + 1) * LANES] = sums[0:4] / jnp.maximum(sums[4:5], 0.1)


def remap_back(capacity, devices, pair_block, pair_tile, owner, returned, remap_weight, nblocks):
    npairs = pair_block.shape[0]
    return pl.pallas_call(
        functools.partial(remap_back_kernel, capacity),
        out_shape=jax.ShapeDtypeStruct((4, nblocks * LANES), F32),
        in_specs=[hbm()] * 3 + [vmem(), hbm()],
        out_specs=vmem(),
        scratch_shapes=[pltpu.SMEM((npairs,), I32)] * 3
        + [
            pltpu.SMEM((devices,), I32),
            pltpu.VMEM(remap_weight.shape, BF16),
            pltpu.VMEM((npairs, 16, LANES), BF16),
            pltpu.VMEM((nblocks, 8, LANES), F32),
            pltpu.SemaphoreType.DMA((3,)),
            pltpu.SemaphoreType.DMA((PARTS,)),
        ],
        compiler_params=pltpu.CompilerParams(vmem_limit_bytes=24 << 20),
        cost_estimate=pl.CostEstimate(flops=2 * npairs * 16 * LANES * LANES, bytes_accessed=6 << 20, transcendentals=0),
    )(*pin(pair_block, pair_tile, owner), returned, *pin(remap_weight))


def local(
    atm_state,
    pair_block,
    pair_owner,
    pair_row,
    pair_tile,
    remap_weight,
    wet_mask,
    ocean_state,
    vert_kappa,
    horiz_kappa,
):
    grid_x = lax.axis_size("gx")
    grid_y = lax.axis_size("gy")
    devices = grid_x * grid_y
    npairs = pair_block.shape[0]
    capacity = max(2, 2 * npairs // devices)
    levels, tile_rows, _ = vert_kappa.shape
    nblocks = atm_state.shape[1] // LANES
    owner = pair_owner.reshape(npairs)
    message = 4 * capacity + EDGE
    outgoing = remap_out(
        capacity, grid_y, devices, tile_rows, atm_state, pair_block, owner, pair_row, pair_tile, remap_weight
    )
    arrived = lax.all_to_all(
        outgoing.reshape(devices, message, LANES), ("gx", "gy"), split_axis=0, concat_axis=0, tiled=True
    )
    tracer, currents, edge_up, edge_down = solve(ocean_state, vert_kappa, horiz_kappa, wet_mask)
    rise_x = [(i, i + 1) for i in range(grid_x - 1)]
    fall_x = [(b, a) for a, b in rise_x]
    rise_y = [(i, i + 1) for i in range(grid_y - 1)]
    fall_y = [(b, a) for a, b in rise_y]
    above = lax.ppermute(edge_down, "gx", rise_x)
    below = lax.ppermute(edge_up, "gx", fall_x)
    wide, to_left, to_right = pack(levels, tracer, above, below)
    from_left = lax.ppermute(to_right, "gy", rise_y)
    from_right = lax.ppermute(to_left, "gy", fall_y)
    faces, packed = face_values(levels, wide, to_left, to_right, from_left, from_right)
    sent, forcing, near = middle(capacity, levels, arrived, wide, currents, faces, packed)
    returned = lax.all_to_all(sent, ("gx", "gy"), split_axis=0, concat_axis=0, tiled=True)
    ocean_next = finish(levels, wide, currents, faces, forcing, near)
    atm_surface = remap_back(
        capacity, devices, pair_block, pair_tile, owner, returned.reshape(-1, LANES), remap_weight, nblocks
    )
    return (ocean_next, atm_surface)


def solution(mesh):
    placed = (
        P(None, ("gx", "gy")),
        P(("gx", "gy")),
        P(("gx", "gy"), None),
        P(("gx", "gy")),
        P(("gx", "gy")),
        P(("gx", "gy"), None, None),
        P("gx", "gy"),
        P(None, None, "gx", "gy"),
        P(None, "gx", "gy"),
        P("gx", "gy"),
    )
    return jax.shard_map(
        local,
        mesh=mesh,
        in_specs=placed,
        out_specs=(P(None, None, "gx", "gy"), P(None, ("gx", "gy"))),
        check_vma=False,
    )
```

```python
import functools

import jax
import jax.numpy as jnp
from jax import lax
from jax.experimental import pallas as pl
from jax.experimental.pallas import tpu as pltpu
from jax.sharding import PartitionSpec as P

F32 = jnp.float32
BF16 = jnp.bfloat16
I32 = jnp.int32
VMEM = pltpu.VMEM
SMEM = pltpu.SMEM
LANES = 128
EDGE = 16
HALO = 8
PARTS = 8


def hbm():
    return pl.BlockSpec(memory_space=pltpu.HBM)


def vmem():
    return pl.BlockSpec(memory_space=VMEM)


def pin(*arrays):
    return [pltpu.with_memory_space_constraint(a, pltpu.HBM) for a in arrays]


def start_all(pairs, sems, first=0):
    copies = [pltpu.make_async_copy(src, dst, sems.at[first + n]) for n, (src, dst) in enumerate(pairs)]
    for copy in copies:
        copy.start()
    return copies


def wait_all(copies):
    for copy in copies:
        copy.wait()


def iota(shape, dim):
    return lax.broadcasted_iota(I32, shape, dim)


def pick(mask, value):
    return jnp.where(mask, value, 0.0)


def split(value):
    high = value.astype(BF16)
    return high, (value - high.astype(F32)).astype(BF16)


def back_rows(capacity):
    return 2 * capacity + max(8, capacity)


def remap_out_kernel(
    capacity, grid_y, tile_rows, block_h, owner_h, row_h, tile_h, atm_h, weights_h, out_h, winds_h,
    out, winds, block_s, owner_s, row_s, tile_s, atm, weights, flux, every, fill, rows_acc, cols_acc, sems, weight_sems, out_sems,
):
    devices = fill.shape[0]
    npairs = block_s.shape[0]
    tiles = weights.shape[0]
    four = flux.shape[0]
    nblocks = four // 4
    span = 2 * capacity
    message = span + EDGE
    copies = [
        pltpu.make_async_copy(src, dst, sems.at[n])
        for n, (src, dst) in enumerate(
            [(atm_h, atm), (block_h, block_s), (owner_h, owner_s), (row_h, row_s), (tile_h, tile_s)]
        )
    ]
    for copy in copies:
        copy.start()
    part_tiles = tiles // PARTS
    parts = [pl.ds(n * part_tiles, part_tiles) for n in range(PARTS)]
    loads = [pltpu.make_async_copy(weights_h.at[at], weights.at[at], weight_sems.at[n]) for n, at in enumerate(parts)]
    for load in loads:
        load.start()
    out[...] = jnp.zeros_like(out)
    winds[...] = jnp.zeros_like(winds)
    rows_acc[...] = jnp.zeros_like(rows_acc)
    cols_acc[...] = jnp.zeros_like(cols_acc)

    def clear_fill(i, carry):
        fill[i] = 0
        return carry

    lax.fori_loop(0, devices, clear_fill, 0, unroll=16)
    copies[0].wait()
    wind_u = atm[0:1, :]
    wind_v = atm[1:2, :]
    speed = jnp.sqrt(wind_u * wind_u + wind_v * wind_v + 0.25)
    heat = 0.5 * speed * (atm[2:3, :] - atm[5:6, :])
    water = atm[4:5, :] - 0.3 * speed * atm[3:4, :]
    for f, plane in enumerate([heat, water, 0.2 * speed * wind_u, 0.2 * speed * wind_v]):
        for b in range(nblocks):
            flux[f * nblocks + b : f * nblocks + b + 1, :] = plane[:, b * LANES : (b + 1) * LANES]
    source = flux[...].astype(BF16)

    for n in range(PARTS):
        loads[n].wait()

        def tile_step(t, carry):
            every[pl.ds(pl.multiple_of(t * four, 8), four), :] = jnp.dot(
                source, weights[t], preferred_element_type=F32
            )
            return carry

        lax.fori_loop(n * part_tiles, (n + 1) * part_tiles, tile_step, 0, unroll=4)
    for copy in copies[1:]:
        copy.wait()

    sub = iota((8, LANES), 0)
    lane = iota((8, LANES), 1)
    part = sub % 4
    edge_row = jnp.where(part == 0, 0, jnp.where(part == 1, 1, tile_rows - 4 + part))
    edge_col = lane == jnp.where(part == 0, 0, jnp.where(part == 1, 1, LANES - 4 + part))
    col_lane = lane - 64 * (sub // 4)
    id_rank = jnp.where((sub == 0) & (lane >= 64), (lane - 64) // 2, -1)

    def pair(p, carry):
        owner = owner_s[p]
        row = row_s[p]
        rank = fill[owner]
        fill[owner] = rank + 1
        first = tile_s[p] * four + block_s[p]
        lines = [every[pl.ds(first + f * nblocks, 1), :] for f in range(4)]
        for f in range(2):
            out[pl.ds(owner * message + 2 * rank + f, 1), :] = lines[f]
            winds[pl.ds(owner * span + 2 * rank + f, 1), :] = lines[2 + f]
        tracer = jnp.where(sub < 4, lines[0], lines[1])
        rows_acc[owner] = rows_acc[owner] + pick(edge_row == row, tracer)
        column = jnp.sum(pick(edge_col, tracer), axis=1, keepdims=True)
        number = (row + 1).astype(F32)
        cols_acc[owner] = cols_acc[owner] + (
            pick(col_lane == row, column) + pick(id_rank == rank, number)
        )
        return carry

    lax.fori_loop(0, npairs, pair, 0, unroll=8)
    stores = start_all([(winds, winds_h)], out_sems, 4)

    grid_x = devices // grid_y
    zero = jnp.zeros((8, LANES), F32)
    inside = ((sub < 4) & (lane < 64)) | (sub >= 4)
    folds = {}

    def fold(i, j):
        if not (0 <= i < grid_x and 0 <= j < grid_y):
            return zero
        d = i * grid_y + j
        if d not in folds:
            kept = pick(inside, cols_acc[d])
            folds[d] = kept + pltpu.roll(kept, 4, 0)
        return folds[d]

    last = (lane == tile_rows - 1) | (lane == 64 + tile_rows - 1)
    first = (lane == 0) | (lane == 64)
    send = devices // 4
    for d in range(devices):
        i, j = d // grid_y, d % grid_y
        below = rows_acc[d + grid_y] if i < grid_x - 1 else zero
        above = rows_acc[d - grid_y] if i > 0 else zero
        base = d * message + span
        out[base : base + 8, :] = jnp.where(part < 2, below, above)
        if i > 1:
            folds.pop(d - 2 * grid_y, None)
        right, left = fold(i, j + 1), fold(i, j - 1)
        tile = pick(sub < 2, right) + pick((sub == 2) | (sub == 3), left)
        tile = tile + pick((sub == 4) & last, fold(i - 1, j + 1)) + pick((sub == 4) & first, fold(i + 1, j + 1))
        tile = tile + pick((sub == 7) & last, fold(i - 1, j - 1)) + pick((sub == 7) & first, fold(i + 1, j - 1))
        numbers = pltpu.roll(cols_acc[d], 5, 0)
        tile = tile + pick((sub == 5) & (lane >= 64), numbers)
        out[base + 8 : base + 16, :] = tile
        if d % send == send - 1:
            n = d // send
            at = pl.ds(n * send * message, send * message)
            stores.append(pltpu.make_async_copy(out.at[at], out_h.at[at], out_sems.at[n]))
            stores[-1].start()
    for store in stores:
        store.wait()


def remap_out(capacity, grid_y, devices, tile_rows, atm_state, pair_block, owner, pair_row, pair_tile, remap_weight):
    npairs = pair_block.shape[0]
    nblocks = atm_state.shape[1] // LANES
    span = 2 * capacity
    message = span + EDGE
    tiles = remap_weight.shape[0]
    return pl.pallas_call(
        functools.partial(remap_out_kernel, capacity, grid_y, tile_rows),
        out_shape=(pltpu.HBM((devices * message, LANES), F32), pltpu.HBM((devices * span, LANES), F32)),
        in_specs=[hbm()] * 6,
        out_specs=(hbm(), hbm()),
        scratch_shapes=[pltpu.VMEM((devices * message, LANES), F32), pltpu.VMEM((devices * span, LANES), F32)]
        + [pltpu.SMEM((npairs,), I32)] * 4
        + [
            pltpu.VMEM(atm_state.shape, F32),
            pltpu.VMEM(remap_weight.shape, BF16),
            pltpu.VMEM((4 * nblocks, LANES), F32),
            pltpu.VMEM((tiles * 4 * nblocks, LANES), F32),
            pltpu.SMEM((devices,), I32),
            pltpu.VMEM((devices, 8, LANES), F32),
            pltpu.VMEM((devices, 8, LANES), F32),
            pltpu.SemaphoreType.DMA((5,)),
            pltpu.SemaphoreType.DMA((PARTS,)),
            pltpu.SemaphoreType.DMA((5,)),
        ],
        compiler_params=pltpu.CompilerParams(vmem_limit_bytes=40 << 20),
        cost_estimate=pl.CostEstimate(
            flops=2 * tiles * 4 * nblocks * LANES * LANES, bytes_accessed=6 << 20, transcendentals=0
        ),
    )(*pin(pair_block, owner, pair_row, pair_tile, atm_state, remap_weight))


def solve_kernel(
    state, kappa, horiz, wet, tracer, top, currents_h, edge_up, edge_down, top_up, top_down, currents, sems
):
    levels = kappa.shape[0]
    rows_all = kappa.shape[1]
    planes = tracer.shape[0]

    def chunk(c, carry):
        rows = pl.ds(pl.multiple_of(c * 8, 8), 8)
        column = [kappa[l, rows, :] for l in range(levels)]
        face = [0.5 * (column[l] + column[l + 1]) for l in range(levels - 1)]
        upper = []
        now = None
        for l in range(levels):
            diagonal = 1.0
            if l > 0:
                diagonal = diagonal + face[l - 1]
            if l < levels - 1:
                diagonal = diagonal + face[l]
            if l > 0:
                diagonal = diagonal + face[l - 1] * upper[-1]
            inverse = 1.0 / diagonal
            if l == 0:
                now = [state[f, 0, rows, :] * inverse for f in range(4)] + [inverse]
            else:
                pull = face[l - 1] * inverse
                now = [state[f, l, rows, :] * inverse + pull * now[f] for f in range(4)] + [pull * now[4]]
            upper.append(-face[l] * inverse if l < levels - 1 else None)
            store(l, rows, now)
        for l in range(levels - 2, -1, -1):
            here = load(l, rows)
            now = [here[f] - upper[l] * now[f] for f in range(5)]
            store(l, rows, now)
        return carry

    def store(l, rows, now):
        tracer[l, rows, :] = now[0]
        tracer[levels + l, rows, :] = now[1]
        currents[0, l, rows, :] = now[2]
        currents[1, l, rows, :] = now[3]
        tracer[2 * levels + l, rows, :] = now[4]

    def load(l, rows):
        return [
            tracer[l, rows, :],
            tracer[levels + l, rows, :],
            currents[0, l, rows, :],
            currents[1, l, rows, :],
            tracer[2 * levels + l, rows, :],
        ]

    lax.fori_loop(0, rows_all // 8, chunk, 0)
    out = start_all([(currents, currents_h)], sems)
    tracer[3 * levels] = horiz[...]
    tracer[3 * levels + 1] = wet[...].astype(F32)
    for k in range(planes):
        edge_up[k] = tracer[k, 0:8, :]
        edge_down[k] = tracer[k, rows_all - 8 : rows_all, :]
    for n, k in enumerate([0, levels, 2 * levels, 3 * levels, 3 * levels + 1]):
        top[n] = tracer[k]
        top_up[n] = edge_up[k]
        top_down[n] = edge_down[k]
    wait_all(out)


def solve(ocean_state, vert_kappa, horiz_kappa, wet_mask):
    levels, rows, _ = vert_kappa.shape
    planes = 3 * levels + 2
    return pl.pallas_call(
        solve_kernel,
        out_shape=(
            jax.ShapeDtypeStruct((planes, rows, LANES), F32),
            jax.ShapeDtypeStruct((5, rows, LANES), F32),
            pltpu.HBM((2, levels, rows, LANES), F32),
            jax.ShapeDtypeStruct((planes, 8, LANES), F32),
            jax.ShapeDtypeStruct((planes, 8, LANES), F32),
            jax.ShapeDtypeStruct((5, 8, LANES), F32),
            jax.ShapeDtypeStruct((5, 8, LANES), F32),
        ),
        in_specs=[vmem()] * 4,
        out_specs=(vmem(), vmem(), hbm()) + (vmem(),) * 4,
        scratch_shapes=[pltpu.VMEM((2, levels, rows, LANES), F32), pltpu.SemaphoreType.DMA((1,))],
        compiler_params=pltpu.CompilerParams(vmem_limit_bytes=24 << 20),
        cost_estimate=pl.CostEstimate(flops=20 << 20, bytes_accessed=6 << 20, transcendentals=0),
    )(ocean_state, vert_kappa, horiz_kappa, wet_mask)


def pack_kernel(levels, tracer, above, below, wide_h, to_left, to_right, wide, sems):
    planes, rows, _ = tracer.shape
    for k in range(planes):
        wide[k, 0:HALO, :] = above[k]
        wide[k, HALO : HALO + rows, :] = tracer[k]
        wide[k, HALO + rows : 2 * HALO + rows, :] = below[k]
    out = start_all([(wide, wide_h)], sems)
    lane = iota((8, LANES), 1)

    def chunk(c, carry):
        at = pl.ds(pl.multiple_of(c * 8, 8), 8)

        def place(values, lanes):
            left, right = jnp.zeros((8, LANES), F32), jnp.zeros((8, LANES), F32)
            for k, (near, far) in zip(values, lanes):
                value = wide[k, at, :]
                left = jnp.where(lane == near, pltpu.roll(value, near, 1), left)
                left = jnp.where(lane == far, pltpu.roll(value, far - 1, 1), left)
                right = jnp.where(lane == near + 1, pltpu.roll(value, (near + 2) % LANES, 1), right)
                right = jnp.where(lane == far + 1, pltpu.roll(value, (far + 3) % LANES, 1), right)
            return left, right

        left, right = place(range(2 * levels), [(2 * k, 64 + 2 * k) for k in range(2 * levels)])
        lanes = [(2 * l, 64 + 2 * l) for l in range(levels)]
        lanes += [(2 * levels, 2 * levels + 2), (2 * levels + 4, 2 * levels + 6)]
        left_unit, right_unit = place(range(2 * levels, 3 * levels + 2), lanes)
        if to_left.shape[0] == 1:
            to_left[0, at, :] = left + pltpu.roll(left_unit, 32, 1)
            to_right[0, at, :] = right + pltpu.roll(right_unit, 32, 1)
        else:
            to_left[0, at, :], to_left[1, at, :] = left, left_unit
            to_right[0, at, :], to_right[1, at, :] = right, right_unit
        return carry

    lax.fori_loop(0, (rows + 2 * HALO) // 8, chunk, 0)
    wait_all(out)


def pack(levels, tracer, above, below):
    planes, rows, _ = tracer.shape
    tall = rows + 2 * HALO
    arrays = 1 if levels == 1 else 2
    return pl.pallas_call(
        functools.partial(pack_kernel, levels),
        out_shape=(
            pltpu.HBM((planes, tall, LANES), F32),
            jax.ShapeDtypeStruct((arrays, tall, LANES), F32),
            jax.ShapeDtypeStruct((arrays, tall, LANES), F32),
        ),
        in_specs=[vmem()] * 3,
        out_specs=(hbm(), vmem(), vmem()),
        scratch_shapes=[pltpu.VMEM((planes, tall, LANES), F32), pltpu.SemaphoreType.DMA((1,))],
        compiler_params=pltpu.CompilerParams(vmem_limit_bytes=24 << 20),
        cost_estimate=pl.CostEstimate(flops=8 << 20, bytes_accessed=4 << 20, transcendentals=0),
    )(tracer, above, below)


def packed_pair(ref):
    value = ref[0]
    if ref.shape[0] > 1:
        return value, ref[1]
    return value, pltpu.roll(value, LANES - 32, 1)


def set_faces(levels, h, w, own_left, own_right, from_left, from_right, faces, packed):
    tall = h.shape[0]
    lane = iota((tall, LANES), 1)
    odd = lane % 2 == 1
    twice = lane % 64 < 2 * levels
    (left, left_unit), (right, right_unit) = packed_pair(from_left), packed_pair(from_right)
    other = jnp.where(odd, left_unit, right_unit)
    at = 2 * levels

    def column(offset):
        return other[:, at + offset : at + offset + 1], other[:, at + offset + 1 : at + offset + 2]

    kappa_right, kappa_left = column(0)
    kappa_far_right, kappa_far_left = column(2)
    wet_right, wet_left = column(4)
    wet_far_right, wet_far_left = column(6)

    kappa_near = jnp.where(odd, kappa_left, kappa_right)
    kappa_far = jnp.where(odd, kappa_far_left, kappa_far_right)
    wet_near = jnp.where(odd, wet_left, wet_right)
    wet_far = jnp.where(odd, wet_far_left, wet_far_right)
    kappa_own = jnp.where(odd, h[:, 0:1], h[:, LANES - 1 : LANES])
    wet_own = jnp.where(odd, w[:, 0:1], w[:, LANES - 1 : LANES])

    def face(kappa_a, wet_a, kappa_b, wet_b):
        return 0.25 * (kappa_a + kappa_b) * wet_a * wet_b

    unit = jnp.where(twice, other, pltpu.roll(other, 2 * levels, 1))
    packed[0] = jnp.where(odd, left, right)
    packed[1] = unit * jnp.where(lane < 64, wet_near, wet_far)
    (left, left_unit), (right, right_unit) = packed_pair(own_left), packed_pair(own_right)
    packed[2] = jnp.where(odd, pltpu.roll(left, 1, 1), pltpu.roll(right, LANES - 1, 1))
    own = jnp.where(odd, pltpu.roll(left_unit, 1, 1), pltpu.roll(right_unit, LANES - 1, 1))
    packed[3] = jnp.where(twice, own, pltpu.roll(own, 2 * levels, 1)) * wet_own
    north = face(kappa_near, wet_near, pltpu.roll(kappa_near, 1, 0), pltpu.roll(wet_near, 1, 0))
    packed[4] = north
    packed[5] = pltpu.roll(north, tall - 1, 0)
    packed[6] = face(kappa_near, wet_near, kappa_far, wet_far)
    packed[7] = face(kappa_near, wet_near, kappa_own, wet_own)

    north = face(h, w, pltpu.roll(h, 1, 0), pltpu.roll(w, 1, 0))
    faces[0] = north
    faces[1] = pltpu.roll(north, tall - 1, 0)
    west = face(
        h, w, jnp.where(lane == 0, kappa_left, pltpu.roll(h, 1, 1)), jnp.where(lane == 0, wet_left, pltpu.roll(w, 1, 1))
    )
    faces[2] = west
    faces[3] = jnp.where(lane == LANES - 1, face(h, w, kappa_right, wet_right), pltpu.roll(west, LANES - 1, 1))


def set_beside(levels, upright, wide, packed, beside):
    tall = upright.shape[0]
    lane = iota((tall, LANES), 1)
    odd = lane % 2 == 1
    heat = lane % 64 < 2 * levels

    def chosen(f):
        right_near, right_far, left_far, left_near = [upright[:, 4 * f + e : 4 * f + e + 1] for e in range(4)]
        near = jnp.where(odd, left_near, right_near)
        return jnp.where(lane < 64, near, jnp.where(odd, left_far, right_far))

    both = packed[0] + packed[1] * jnp.where(heat, chosen(0), chosen(1))
    far = pltpu.roll(both, 64, 1)
    ends_of = [jnp.where(odd, w[:, 0:1], w[:, LANES - 1 : LANES]) for w in wide]
    own = packed[2] + packed[3] * jnp.where(heat, ends_of[0], ends_of[1])
    near = both + packed[5] * (pltpu.roll(both, tall - 1, 0) - both)
    near = near + packed[4] * (pltpu.roll(both, 1, 0) - both)
    near = near + packed[6] * (far - both)
    near = near + packed[7] * (own - both)
    beside[0] = both
    beside[1] = near


def one_pass(value, faces, beside, shift):
    tall = value.shape[0]
    lane = iota(value.shape, 1)
    moved = pltpu.roll(beside, shift, 1)
    west = jnp.where(lane == 0, moved, pltpu.roll(value, 1, 1))
    east = jnp.where(lane == LANES - 1, moved, pltpu.roll(value, LANES - 1, 1))
    result = value + faces[1] * (pltpu.roll(value, tall - 1, 0) - value)
    result = result + faces[0] * (pltpu.roll(value, 1, 0) - value)
    result = result + faces[3] * (east - value)
    return result + faces[2] * (west - value)


def set_forcing(span, numbers, rows_all, arrived, placing, values):
    devices = arrived.shape[0]
    row_number = iota((rows_all, LANES), 0).astype(F32) + 1.0
    lane_field = iota((rows_all, LANES), 1) % 2
    for m, line in enumerate(numbers):
        hit = line == row_number
        for f in range(2):
            placing[f * rows_all : (f + 1) * rows_all, m * LANES : (m + 1) * LANES] = jnp.where(
                hit & (lane_field == f), 1.0, 0.0
            ).astype(BF16)
    for s in range(0, devices, 16 // min(16, span)):
        many = 16 // min(16, span)
        high, low = split(jnp.concatenate([arrived[s + n, 0:span, :] for n in range(many)], 0))
        values[s * span : (s + many) * span, 0:LANES] = high
        values[s * span : (s + many) * span, LANES : 2 * LANES] = low
    total = jnp.dot(placing[...], values[...], preferred_element_type=F32)
    total = total[:, 0:LANES] + total[:, LANES : 2 * LANES]
    return [total[f * rows_all : (f + 1) * rows_all] for f in range(2)]


def wanted(rows_all):
    lane_t = iota((LANES, 2 * rows_all), 1)
    sub_t = iota((LANES, 2 * rows_all), 0)
    return jnp.where(sub_t % 2 == lane_t // rows_all, lane_t % rows_all + 1, -1).astype(F32)


def picked_rows(column, target, source):
    rows = jnp.dot(jnp.where(column == target, 1.0, 0.0).astype(BF16), source, preferred_element_type=F32)
    return rows[:, 0:LANES] + rows[:, LANES : 2 * LANES]


def two_parts(surface):
    high, low = split(jnp.concatenate(surface, 0))
    return jnp.concatenate([high, low], 1)


def tracer_kernel(
    capacity, arrived, wide_h, own_left, own_right, from_left, from_right,
    sent_h, forcing_h, upright_h, numbers_h, number_t_h,
    placing, values, number_t, lines, top, faces, packed, beside, sent, forcing, upright, sems, sent_sems,
):
    devices = arrived.shape[0]
    tall = top.shape[1]
    rows_all = tall - 2 * HALO
    span = 2 * capacity
    group = LANES // span
    groups = devices // group
    sub8 = iota((8, LANES), 0)
    lane8 = iota((8, LANES), 1)
    loads = start_all([(wide_h, top)], sems)

    lane1 = iota((1, LANES), 1)
    numbers = []
    for m in range(groups):
        line = jnp.zeros((1, LANES), F32)
        for g in range(group):
            ids = arrived[m * group + g, span + 13 : span + 14, :]
            moved = pltpu.roll(ids, (g * span - 64) % LANES, 1)
            line = jnp.where(lane1 // span == g, moved, line)
        numbers.append(line)
        lines[m : m + 1, :] = line
    number_t[...] = jnp.transpose(
        jnp.concatenate(numbers + [jnp.zeros((LANES - groups, LANES), F32)], 0)
    )
    stores = start_all([(lines, numbers_h), (number_t, number_t_h)], sems, 1)

    planes = set_forcing(span, numbers, rows_all, arrived, placing, values)
    edge_rows = jnp.zeros((8, LANES), F32)
    edge_cols = jnp.zeros((8, LANES), F32)
    for s in range(devices):
        edge_rows = edge_rows + arrived[s, span : span + 8, :]
        edge_cols = edge_cols + arrived[s, span + 8 : span + 16, :]
    wide = []
    for f in range(2):
        before = pick(sub8 >= 6, edge_rows if f == 1 else pltpu.roll(edge_rows, 4, 0))
        after = pick(sub8 < 2, edge_rows if f == 0 else pltpu.roll(edge_rows, 4, 0))
        wide.append(jnp.concatenate([before, planes[f], after], 0))
        forcing[f] = wide[f]

    corner = pick((sub8 == 0) | (sub8 == 3), pltpu.roll(edge_cols, 4, 0))
    side = pick(sub8 < 4, edge_cols)
    within = (lane8 >= HALO) & (lane8 < HALO + rows_all)
    ends = (lane8 == HALO - 1) | (lane8 == HALO + rows_all)
    halves = []
    for f in range(2):
        body = pltpu.roll(side, (HALO - 64 * f) % LANES, 1)
        tips = pltpu.roll(corner, (HALO + rows_all - 64 * f) % LANES, 1)
        halves.append((pick(within, body) + pick(ends, tips))[0:4])
    columns = jnp.concatenate(halves, 0)
    upright[...] = jnp.transpose(jnp.concatenate([columns, jnp.zeros((LANES - 8, LANES), F32)], 0))[0:tall]
    stores += start_all([(forcing, forcing_h), (upright, upright_h)], sems, 3)

    wait_all(loads)
    set_faces(1, top[3], top[4], own_left, own_right, from_left, from_right, faces, packed)
    set_beside(1, upright[...], wide, packed, beside)
    wet = top[4, HALO : HALO + rows_all, :]
    unit = top[2] * top[4]
    surface = []
    for f in range(2):
        value = top[f] + unit * wide[f]
        shift = LANES - (2 * f + 1)
        value = one_pass(value, faces, beside[0], shift)
        value = one_pass(value, faces, beside[1], shift)
        surface.append(value[HALO : HALO + rows_all] * wet)
    source = two_parts(surface)
    target = wanted(rows_all)
    mask = jnp.concatenate([wet, jnp.zeros((LANES - rows_all, LANES), F32)], 0).astype(BF16)
    per = LANES // 2
    slot_number = number_t[pl.ds(0, per, stride=2), :]
    lane_s = (iota((per, LANES), 1) + 1).astype(F32)
    height = back_rows(capacity)
    for m in range(groups):
        rows = picked_rows(number_t[:, m : m + 1], target, source)
        slots = jnp.where(slot_number[:, m : m + 1] == lane_s, 1.0, 0.0).astype(BF16)
        masks = jnp.dot(slots, mask, preferred_element_type=F32)
        for g in range(group):
            s = m * group + g
            sent[s, 0:span, :] = rows[g * span : (g + 1) * span]
            sent[s, span : span + capacity, :] = masks[g * capacity : (g + 1) * capacity]
            if height > span + capacity:
                sent[s, span + capacity : height, :] = jnp.zeros((height - span - capacity, LANES), F32)
        at = pl.ds(m * group, group)
        stores += start_all([(sent.at[at], sent_h.at[at])], sent_sems, m)
    wait_all(stores)


def tracer_surface(capacity, arrived, wide, own_left, own_right, from_left, from_right):
    devices = arrived.shape[0]
    tall = wide.shape[1]
    rows = tall - 2 * HALO
    height = back_rows(capacity)
    slots = 2 * capacity * devices
    groups = slots // LANES
    return pl.pallas_call(
        functools.partial(tracer_kernel, capacity),
        out_shape=(
            pltpu.HBM((devices, height, LANES), F32),
            pltpu.HBM((2, tall, LANES), F32),
            pltpu.HBM((tall, LANES), F32),
            pltpu.HBM((groups, LANES), F32),
            pltpu.HBM((LANES, LANES), F32),
        ),
        in_specs=[vmem(), hbm()] + [vmem()] * 4,
        out_specs=(hbm(),) * 5,
        scratch_shapes=[
            pltpu.VMEM((2 * rows, slots), BF16),
            pltpu.VMEM((slots, 2 * LANES), BF16),
            pltpu.VMEM((LANES, LANES), F32),
            pltpu.VMEM((groups, LANES), F32),
            pltpu.VMEM((5, tall, LANES), F32),
            pltpu.VMEM((4, tall, LANES), F32),
            pltpu.VMEM((8, tall, LANES), F32),
            pltpu.VMEM((2, tall, LANES), F32),
            pltpu.VMEM((devices, height, LANES), F32),
            pltpu.VMEM((2, tall, LANES), F32),
            pltpu.VMEM((tall, LANES), F32),
            pltpu.SemaphoreType.DMA((5,)),
            pltpu.SemaphoreType.DMA((groups,)),
        ],
        compiler_params=pltpu.CompilerParams(vmem_limit_bytes=24 << 20),
        cost_estimate=pl.CostEstimate(flops=100 << 20, bytes_accessed=4 << 20, transcendentals=0),
    )(arrived, *pin(wide), own_left, own_right, from_left, from_right)


def current_kernel(
    capacity, arrived, wide_h, currents_h, numbers_h, number_t_h, sent_h, forcing_h,
    placing, values, lines, number_t, top, base, sent, forcing, sems, sent_sems,
):
    devices = arrived.shape[0]
    rows_all = base.shape[1]
    span = 2 * capacity
    group = LANES // span
    groups = devices // group
    loads = start_all(
        [
            (numbers_h, lines),
            (number_t_h, number_t),
            (wide_h.at[pl.ds(2, 3)], top),
            (currents_h.at[0, 0], base.at[0]),
            (currents_h.at[1, 0], base.at[1]),
        ],
        sems,
    )
    wait_all(loads)
    planes = set_forcing(span, [lines[m : m + 1, :] for m in range(groups)], rows_all, arrived, placing, values)
    wet = top[2, HALO : HALO + rows_all, :]
    unit = top[0, HALO : HALO + rows_all, :]
    surface = []
    for f in range(2):
        forcing[f] = planes[f] * wet
        surface.append((base[f] + unit * forcing[f]) * wet)
    stores = start_all([(forcing, forcing_h)], sems, 5)
    source = two_parts(surface)
    target = wanted(rows_all)
    for m in range(groups):
        rows = picked_rows(number_t[:, m : m + 1], target, source)
        for g in range(group):
            sent[m * group + g] = rows[g * span : (g + 1) * span]
        at = pl.ds(m * group, group)
        stores += start_all([(sent.at[at], sent_h.at[at])], sent_sems, m)
    wait_all(stores)


def current_surface(capacity, arrived, wide, currents, numbers, number_t):
    devices, span, _ = arrived.shape
    rows = currents.shape[2]
    tall = rows + 2 * HALO
    slots = span * devices
    groups = slots // LANES
    return pl.pallas_call(
        functools.partial(current_kernel, capacity),
        out_shape=(pltpu.HBM((devices, span, LANES), F32), pltpu.HBM((2, rows, LANES), F32)),
        in_specs=[vmem()] + [hbm()] * 4,
        out_specs=(hbm(),) * 2,
        scratch_shapes=[
            pltpu.VMEM((2 * rows, slots), BF16),
            pltpu.VMEM((slots, 2 * LANES), BF16),
            pltpu.VMEM((groups, LANES), F32),
            pltpu.VMEM((LANES, LANES), F32),
            pltpu.VMEM((3, tall, LANES), F32),
            pltpu.VMEM((2, rows, LANES), F32),
            pltpu.VMEM((devices, span, LANES), F32),
            pltpu.VMEM((2, rows, LANES), F32),
            pltpu.SemaphoreType.DMA((6,)),
            pltpu.SemaphoreType.DMA((groups,)),
        ],
        compiler_params=pltpu.CompilerParams(vmem_limit_bytes=24 << 20),
        cost_estimate=pl.CostEstimate(flops=100 << 20, bytes_accessed=3 << 20, transcendentals=0),
    )(arrived, *pin(wide, currents, numbers, number_t))


def finish_kernel(
    levels, wide_h, currents_h, forcing_h, push_h, upright_h, own_left, own_right, from_left, from_right, ocean,
    wide, currents, forcing, push, upright, faces, packed, beside, sems,
):
    rows_all = currents.shape[2]
    inner = slice(HALO, HALO + rows_all)
    wait_all(
        start_all(
            [(wide_h, wide), (currents_h, currents), (forcing_h, forcing), (push_h, push), (upright_h, upright)], sems
        )
    )
    set_faces(
        levels, wide[3 * levels], wide[3 * levels + 1], own_left, own_right, from_left, from_right, faces, packed
    )
    set_beside(levels, upright[...], [forcing[0], forcing[1]], packed, beside)

    def level(l, carry):
        unit = wide[2 * levels + l]
        masked = unit * wide[3 * levels + 1]
        for f in range(2):
            value = wide[f * levels + l] + masked * forcing[f]
            shift = LANES - 1 - 2 * (levels * f + l)
            value = one_pass(value, faces, beside[0], shift)
            value = one_pass(value, faces, beside[1], shift)
            ocean[f, l] = value[inner]
            ocean[2 + f, l] = currents[f, l] + unit[inner] * push[f]
        return carry

    lax.fori_loop(0, levels, level, 0)


def finish(levels, wide, currents, forcing, push, upright, own_left, own_right, from_left, from_right):
    rows = currents.shape[2]
    tall = rows + 2 * HALO
    return pl.pallas_call(
        functools.partial(finish_kernel, levels),
        out_shape=jax.ShapeDtypeStruct((4, levels, rows, LANES), F32),
        in_specs=[hbm()] * 5 + [vmem()] * 4,
        out_specs=vmem(),
        scratch_shapes=[pltpu.VMEM(a.shape, F32) for a in (wide, currents, forcing, push, upright)]
        + [pltpu.VMEM((n, tall, LANES), F32) for n in (4, 8, 2)]
        + [pltpu.SemaphoreType.DMA((5,))],
        compiler_params=pltpu.CompilerParams(vmem_limit_bytes=24 << 20),
        cost_estimate=pl.CostEstimate(flops=40 << 20, bytes_accessed=6 << 20, transcendentals=0),
    )(*pin(wide, currents, forcing, push, upright), own_left, own_right, from_left, from_right)


def remap_back_kernel(
    capacity, last, block_h, tile_h, owner_h, returned, weights_h, *refs
):
    if last:
        before_h, out, before = refs[0], refs[1], refs[-1]
        refs = refs[2:-1]
    else:
        out, refs = refs[0], refs[1:]
    block_s, tile_s, owner_s, fill, weights, picked, total, sems, weight_sems = refs
    npairs = block_s.shape[0]
    nblocks = total.shape[0]
    devices = fill.shape[0]
    span = 2 * capacity
    height = span if last else back_rows(capacity)
    scalars = start_all([(owner_h, owner_s), (block_h, block_s), (tile_h, tile_s)], sems)
    part_tiles = weights.shape[0] // PARTS
    parts = [pl.ds(n * part_tiles, part_tiles) for n in range(PARTS)]
    loads = start_all([(weights_h.at[at], weights.at[at]) for at in parts], weight_sems)
    if last:
        loads += start_all([(before_h, before)], sems, 3)
    total[...] = jnp.zeros_like(total)

    def clear_fill(i, carry):
        fill[i] = 0
        return carry

    lax.fori_loop(0, devices, clear_fill, 0, unroll=16)
    wait_all(scalars)

    def gather(p, carry):
        owner = owner_s[p]
        rank = fill[owner]
        fill[owner] = rank + 1
        rows = [returned[pl.ds(owner * height + 2 * rank, 2), :]]
        if not last:
            rows.append(returned[pl.ds(owner * height + span + rank, 1), :])
        rows.append(jnp.zeros((6 if last else 5, LANES), F32))
        high, low = split(jnp.concatenate(rows, 0))
        picked[p] = jnp.concatenate([high, low], 0)
        return carry

    lax.fori_loop(0, npairs, gather, 0, unroll=8)
    wait_all(loads)

    def pair(p, carry):
        value = lax.dot_general(
            picked[p], weights[tile_s[p]], (((1,), (1,)), ((), ())), preferred_element_type=F32
        )
        b = block_s[p]
        total[b] = total[b] + (value[0:8] + value[8:16])
        return carry

    lax.fori_loop(0, npairs, pair, 0, unroll=16)
    if not last:
        wait_all(start_all([(total, out)], sems, 3))
        return
    for b in range(nblocks):
        sums = jnp.concatenate([before[b, 0:2, :], total[b, 0:2, :]], 0)
        out[:, b * LANES : (b + 1) * LANES] = sums / jnp.maximum(before[b, 2:3, :], 0.1)


def remap_back(capacity, devices, pair_block, pair_tile, owner, returned, remap_weight, nblocks, before=None):
    npairs = pair_block.shape[0]
    last = before is not None
    sums = (nblocks, 8, LANES)
    return pl.pallas_call(
        functools.partial(remap_back_kernel, capacity, last),
        out_shape=jax.ShapeDtypeStruct((4, nblocks * LANES), F32) if last else pltpu.HBM(sums, F32),
        in_specs=[hbm()] * 3 + [vmem(), hbm()] + [hbm()] * last,
        out_specs=vmem() if last else hbm(),
        scratch_shapes=[pltpu.SMEM((npairs,), I32)] * 3
        + [
            pltpu.SMEM((devices,), I32),
            pltpu.VMEM(remap_weight.shape, BF16),
            pltpu.VMEM((npairs, 16, LANES), BF16),
            pltpu.VMEM(sums, F32),
            pltpu.SemaphoreType.DMA((4,)),
            pltpu.SemaphoreType.DMA((PARTS,)),
        ]
        + [pltpu.VMEM(sums, F32)] * last,
        compiler_params=pltpu.CompilerParams(vmem_limit_bytes=24 << 20),
        cost_estimate=pl.CostEstimate(flops=2 * npairs * 16 * LANES * LANES, bytes_accessed=6 << 20, transcendentals=0),
    )(*pin(pair_block, pair_tile, owner), returned, *pin(remap_weight), *(pin(before) if last else []))


def local(
    atm_state,
    pair_block,
    pair_owner,
    pair_row,
    pair_tile,
    remap_weight,
    wet_mask,
    ocean_state,
    vert_kappa,
    horiz_kappa,
):
    grid_x = lax.axis_size("gx")
    grid_y = lax.axis_size("gy")
    devices = grid_x * grid_y
    npairs = pair_block.shape[0]
    capacity = max(2, 2 * npairs // devices)
    levels, tile_rows, _ = vert_kappa.shape
    nblocks = atm_state.shape[1] // LANES
    owner = pair_owner.reshape(npairs)
    span = 2 * capacity

    def exchange(array, rows):
        array = array.reshape(devices, rows, LANES)
        return lax.all_to_all(array, ("gx", "gy"), split_axis=0, concat_axis=0, tiled=True)

    def both_ways(axis, count, backward, forward):
        rise = [(i, i + 1) for i in range(count - 1)]
        return lax.ppermute(forward, axis, rise), lax.ppermute(backward, axis, [(b, a) for a, b in rise])

    outgoing, outgoing_winds = remap_out(
        capacity, grid_y, devices, tile_rows, atm_state, pair_block, owner, pair_row, pair_tile, remap_weight
    )
    arrived = exchange(outgoing, span + EDGE)
    arrived_winds = exchange(outgoing_winds, span)
    tracer, top, currents, edge_up, edge_down, top_up, top_down = solve(
        ocean_state, vert_kappa, horiz_kappa, wet_mask
    )
    above, below = both_ways("gx", grid_x, top_up, top_down)
    top_wide, *top_own = pack(1, top, above, below)
    top_beside = both_ways("gy", grid_y, *top_own)
    sent, forcing, upright, numbers, number_t = tracer_surface(capacity, arrived, top_wide, *top_own, *top_beside)
    returned = exchange(sent, back_rows(capacity))
    above, below = both_ways("gx", grid_x, edge_up, edge_down)
    wide, *own = pack(levels, tracer, above, below)
    beside = both_ways("gy", grid_y, *own)
    sent_winds, push = current_surface(capacity, arrived_winds, top_wide, currents, numbers, number_t)
    returned_winds = exchange(sent_winds, span)
    ocean_next = finish(levels, wide, currents, forcing, push, upright, *own, *beside)
    pairs = (capacity, devices, pair_block, pair_tile, owner)
    sums = remap_back(*pairs, returned.reshape(-1, LANES), remap_weight, nblocks)
    atm_surface = remap_back(*pairs, returned_winds.reshape(-1, LANES), remap_weight, nblocks, sums)
    return (ocean_next, atm_surface)


def solution(mesh):
    placed = (
        P(None, ("gx", "gy")),
        P(("gx", "gy")),
        P(("gx", "gy"), None),
        P(("gx", "gy")),
        P(("gx", "gy")),
        P(("gx", "gy"), None, None),
        P("gx", "gy"),
        P(None, None, "gx", "gy"),
        P(None, "gx", "gy"),
        P("gx", "gy"),
    )
    return jax.shard_map(
        local,
        mesh=mesh,
        in_specs=placed,
        out_specs=(P(None, None, "gx", "gy"), P(None, ("gx", "gy"))),
        check_vma=False,
    )
```

```python
import functools

import jax
import jax.numpy as jnp
from jax import lax
from jax.experimental import pallas as pl
from jax.experimental.pallas import tpu as pltpu
from jax.sharding import PartitionSpec as P

F32 = jnp.float32
BF16 = jnp.bfloat16
I32 = jnp.int32
VMEM = pltpu.VMEM
SMEM = pltpu.SMEM
LANES = 128
EDGE = 16
HALO = 8
NUMBERS = 72
CORNERS = 112
PARTS = 8


def hbm():
    return pl.BlockSpec(memory_space=pltpu.HBM)


def vmem():
    return pl.BlockSpec(memory_space=VMEM)


def pin(*arrays):
    return [pltpu.with_memory_space_constraint(a, pltpu.HBM) for a in arrays]


def start_all(pairs, sems, first=0):
    copies = [pltpu.make_async_copy(src, dst, sems.at[first + n]) for n, (src, dst) in enumerate(pairs)]
    for copy in copies:
        copy.start()
    return copies


def wait_all(copies):
    for copy in copies:
        copy.wait()


def iota(shape, dim):
    return lax.broadcasted_iota(I32, shape, dim)


def pick(mask, value):
    return jnp.where(mask, value, 0.0)


def split(value):
    high = value.astype(BF16)
    return high, (value - high.astype(F32)).astype(BF16)


def back_rows(capacity):
    return 4 * capacity + max(8, capacity)


def remap_out_kernel(
    capacity, grid_y, tile_rows, block_h, owner_h, row_h, tile_h, atm_h, weights_h, out_h,
    out, block_s, owner_s, row_s, tile_s, atm, weights, flux, every, fill, row_slots, col_slots, rows_acc, cols_acc, sems, weight_sems, out_sems,
):
    devices = fill.shape[0]
    npairs = block_s.shape[0]
    tiles = weights.shape[0]
    four = flux.shape[0]
    nblocks = four // 4
    message = 4 * capacity + EDGE
    copies = [
        pltpu.make_async_copy(src, dst, sems.at[n])
        for n, (src, dst) in enumerate(
            [(atm_h, atm), (block_h, block_s), (owner_h, owner_s), (row_h, row_s), (tile_h, tile_s)]
        )
    ]
    for copy in copies:
        copy.start()
    part_tiles = tiles // PARTS
    parts = [pl.ds(n * part_tiles, part_tiles) for n in range(PARTS)]
    loads = [pltpu.make_async_copy(weights_h.at[at], weights.at[at], weight_sems.at[n]) for n, at in enumerate(parts)]
    for load in loads:
        load.start()
    out[...] = jnp.zeros_like(out)
    row_slots[...] = jnp.zeros_like(row_slots)
    col_slots[...] = jnp.zeros_like(col_slots)

    def clear_fill(i, carry):
        fill[i] = 0
        return carry

    lax.fori_loop(0, devices, clear_fill, 0, unroll=16)
    copies[0].wait()
    wind_u = atm[0:1, :]
    wind_v = atm[1:2, :]
    speed = jnp.sqrt(wind_u * wind_u + wind_v * wind_v + 0.25)
    heat = 0.5 * speed * (atm[2:3, :] - atm[5:6, :])
    water = atm[4:5, :] - 0.3 * speed * atm[3:4, :]
    for f, plane in enumerate([heat, water, 0.2 * speed * wind_u, 0.2 * speed * wind_v]):
        for b in range(nblocks):
            flux[f * nblocks + b : f * nblocks + b + 1, :] = plane[:, b * LANES : (b + 1) * LANES]
    source = flux[...].astype(BF16)

    for n in range(PARTS):
        loads[n].wait()

        def tile_step(t, carry):
            every[pl.ds(pl.multiple_of(t * four, 8), four), :] = jnp.dot(
                source, weights[t], preferred_element_type=F32
            )
            return carry

        lax.fori_loop(n * part_tiles, (n + 1) * part_tiles, tile_step, 0, unroll=16)
    for copy in copies[1:]:
        copy.wait()

    sub = iota((8, LANES), 0)
    lane = iota((8, LANES), 1)
    part = sub % 4
    edge_row = jnp.where(part == 0, 0, jnp.where(part == 1, 1, tile_rows - 4 + part))
    band = ((lane - part) >> 2) * 4 + part
    id_rank = jnp.where(sub == 0, lane - NUMBERS, -1)

    def pair(p, carry):
        owner = owner_s[p]
        row = row_s[p]
        rank = fill[owner]
        fill[owner] = rank + 1
        first = tile_s[p] * four + block_s[p]
        lines = [every[pl.ds(first + f * nblocks, 1), :] for f in range(4)]
        for f in range(4):
            out[pl.ds(owner * message + 4 * rank + f, 1), :] = lines[f]
        tracer = jnp.where(sub < 4, lines[0], lines[1])
        slot = owner * capacity + rank
        row_slots[slot] = pick(edge_row == row, tracer)
        number = (row + 1).astype(F32)
        col_slots[slot] = pick(band == row, pltpu.roll(tracer, row + 2, 1)) + pick(id_rank == rank, number)
        return carry

    lax.fori_loop(0, npairs, pair, 0, unroll=32)

    def owner_step(d, carry):
        rows = row_slots[d * capacity]
        cols = col_slots[d * capacity]
        for r in range(1, capacity):
            rows = rows + row_slots[d * capacity + r]
            cols = cols + col_slots[d * capacity + r]
        rows_acc[d] = rows
        cols_acc[d] = cols
        return carry

    lax.fori_loop(0, devices, owner_step, 0, unroll=8)

    grid_x = devices // grid_y
    zero = jnp.zeros((8, LANES), F32)

    def columns_of(i, j):
        if not (0 <= i < grid_x and 0 <= j < grid_y):
            return zero
        return cols_acc[i * grid_y + j]

    from_left = (lane - sub) % 4 < 2
    in_band = lane < tile_rows + 4
    in_ids = (sub == 0) & (lane >= NUMBERS) & (lane < NUMBERS + capacity)
    last, first = part == 3, part == 0
    send = devices // 4
    stores = []
    for d in range(devices):
        i, j = d // grid_y, d % grid_y
        below = rows_acc[d + grid_y] if i < grid_x - 1 else zero
        above = rows_acc[d - grid_y] if i > 0 else zero
        base = d * message + 4 * capacity
        out[base : base + 8, :] = jnp.where(part < 2, below, above)
        tile = pick(in_band, jnp.where(from_left, columns_of(i, j - 1), columns_of(i, j + 1)))
        upper = pick(last & (lane == tile_rows), columns_of(i - 1, j - 1))
        upper = upper + pick(last & (lane == tile_rows + 1), columns_of(i - 1, j + 1))
        lower = pick(first & (lane == 1), columns_of(i + 1, j - 1))
        lower = lower + pick(first & (lane == 2), columns_of(i + 1, j + 1))
        tile = tile + pltpu.roll(upper, CORNERS - tile_rows, 1) + pltpu.roll(lower, CORNERS + 1, 1)
        tile = tile + pick(in_ids, cols_acc[d])
        out[base + 8 : base + 16, :] = tile
        if d % send == send - 1:
            n = d // send
            at = pl.ds(n * send * message, send * message)
            stores.append(pltpu.make_async_copy(out.at[at], out_h.at[at], out_sems.at[n]))
            stores[-1].start()
    for store in stores:
        store.wait()


def remap_out(capacity, grid_y, devices, tile_rows, atm_state, pair_block, owner, pair_row, pair_tile, remap_weight):
    npairs = pair_block.shape[0]
    nblocks = atm_state.shape[1] // LANES
    message = 4 * capacity + EDGE
    tiles = remap_weight.shape[0]
    return pl.pallas_call(
        functools.partial(remap_out_kernel, capacity, grid_y, tile_rows),
        out_shape=pltpu.HBM((devices * message, LANES), F32),
        in_specs=[hbm()] * 6,
        out_specs=hbm(),
        scratch_shapes=[pltpu.VMEM((devices * message, LANES), F32)]
        + [pltpu.SMEM((npairs,), I32)] * 4
        + [
            pltpu.VMEM(atm_state.shape, F32),
            pltpu.VMEM(remap_weight.shape, BF16),
            pltpu.VMEM((4 * nblocks, LANES), F32),
            pltpu.VMEM((tiles * 4 * nblocks, LANES), F32),
            pltpu.SMEM((devices,), I32),
            pltpu.VMEM((devices * capacity, 8, LANES), F32),
            pltpu.VMEM((devices * capacity, 8, LANES), F32),
            pltpu.VMEM((devices, 8, LANES), F32),
            pltpu.VMEM((devices, 8, LANES), F32),
            pltpu.SemaphoreType.DMA((5,)),
            pltpu.SemaphoreType.DMA((PARTS,)),
            pltpu.SemaphoreType.DMA((4,)),
        ],
        compiler_params=pltpu.CompilerParams(vmem_limit_bytes=40 << 20),
        cost_estimate=pl.CostEstimate(
            flops=2 * tiles * 4 * nblocks * LANES * LANES, bytes_accessed=6 << 20, transcendentals=0
        ),
    )(*pin(pair_block, owner, pair_row, pair_tile, atm_state, remap_weight))


def solve_kernel(state, kappa, horiz, wet, tracer, currents_h, edge_up, edge_down, currents, sems):
    levels = kappa.shape[0]
    rows_all = kappa.shape[1]
    planes = tracer.shape[0]

    def chunk(c, carry):
        rows = pl.ds(pl.multiple_of(c * 8, 8), 8)
        column = [kappa[l, rows, :] for l in range(levels)]
        face = [0.5 * (column[l] + column[l + 1]) for l in range(levels - 1)]
        upper = []
        now = None
        for l in range(levels):
            diagonal = 1.0
            if l > 0:
                diagonal = diagonal + face[l - 1]
            if l < levels - 1:
                diagonal = diagonal + face[l]
            if l > 0:
                diagonal = diagonal + face[l - 1] * upper[-1]
            inverse = 1.0 / diagonal
            if l == 0:
                now = [state[f, 0, rows, :] * inverse for f in range(4)] + [inverse]
            else:
                pull = face[l - 1] * inverse
                now = [state[f, l, rows, :] * inverse + pull * now[f] for f in range(4)] + [pull * now[4]]
            upper.append(-face[l] * inverse if l < levels - 1 else None)
            store(l, rows, now)
        for l in range(levels - 2, -1, -1):
            here = load(l, rows)
            now = [here[f] - upper[l] * now[f] for f in range(5)]
            store(l, rows, now)
        return carry

    def store(l, rows, now):
        tracer[l, rows, :] = now[0]
        tracer[levels + l, rows, :] = now[1]
        currents[0, l, rows, :] = now[2]
        currents[1, l, rows, :] = now[3]
        tracer[2 * levels + l, rows, :] = now[4]

    def load(l, rows):
        return [
            tracer[l, rows, :],
            tracer[levels + l, rows, :],
            currents[0, l, rows, :],
            currents[1, l, rows, :],
            tracer[2 * levels + l, rows, :],
        ]

    lax.fori_loop(0, rows_all // 8, chunk, 0)
    out = start_all([(currents, currents_h)], sems)
    tracer[3 * levels] = horiz[...]
    tracer[3 * levels + 1] = wet[...].astype(F32)
    for k in range(planes):
        edge_up[k] = tracer[k, 0:8, :]
        edge_down[k] = tracer[k, rows_all - 8 : rows_all, :]
    wait_all(out)


def solve(ocean_state, vert_kappa, horiz_kappa, wet_mask):
    levels, rows, _ = vert_kappa.shape
    planes = 3 * levels + 2
    return pl.pallas_call(
        solve_kernel,
        out_shape=(
            jax.ShapeDtypeStruct((planes, rows, LANES), F32),
            pltpu.HBM((2, levels, rows, LANES), F32),
            jax.ShapeDtypeStruct((planes, 8, LANES), F32),
            jax.ShapeDtypeStruct((planes, 8, LANES), F32),
        ),
        in_specs=[vmem()] * 4,
        out_specs=(vmem(), hbm(), vmem(), vmem()),
        scratch_shapes=[pltpu.VMEM((2, levels, rows, LANES), F32), pltpu.SemaphoreType.DMA((1,))],
        compiler_params=pltpu.CompilerParams(vmem_limit_bytes=24 << 20),
        cost_estimate=pl.CostEstimate(flops=20 << 20, bytes_accessed=6 << 20, transcendentals=0),
    )(ocean_state, vert_kappa, horiz_kappa, wet_mask)


def pack_kernel(levels, tracer, above, below, wide_h, to_left, to_right, wide, sems):
    planes, rows, _ = tracer.shape
    for k in range(planes):
        wide[k, 0:HALO, :] = above[k]
        wide[k, HALO : HALO + rows, :] = tracer[k]
        wide[k, HALO + rows : 2 * HALO + rows, :] = below[k]
    out = start_all([(wide, wide_h)], sems)
    lane = iota((8, LANES), 1)

    def chunk(c, carry):
        at = pl.ds(pl.multiple_of(c * 8, 8), 8)

        def place(values, lanes):
            left, right = jnp.zeros((8, LANES), F32), jnp.zeros((8, LANES), F32)
            for k, (near, far) in zip(values, lanes):
                value = wide[k, at, :]
                left = jnp.where(lane == near, pltpu.roll(value, near, 1), left)
                left = jnp.where(lane == far, pltpu.roll(value, far - 1, 1), left)
                right = jnp.where(lane == near + 1, pltpu.roll(value, (near + 2) % LANES, 1), right)
                right = jnp.where(lane == far + 1, pltpu.roll(value, (far + 3) % LANES, 1), right)
            return left, right

        left, right = place(range(2 * levels), [(2 * k, 64 + 2 * k) for k in range(2 * levels)])
        to_left[0, at, :] = left
        to_right[0, at, :] = right
        lanes = [(2 * l, 64 + 2 * l) for l in range(levels)]
        lanes += [(2 * levels, 2 * levels + 2), (2 * levels + 4, 2 * levels + 6)]
        left, right = place(range(2 * levels, 3 * levels + 2), lanes)
        to_left[1, at, :] = left
        to_right[1, at, :] = right
        return carry

    lax.fori_loop(0, (rows + 2 * HALO) // 8, chunk, 0)
    wait_all(out)


def pack(levels, tracer, above, below):
    planes, rows, _ = tracer.shape
    tall = rows + 2 * HALO
    return pl.pallas_call(
        functools.partial(pack_kernel, levels),
        out_shape=(
            pltpu.HBM((planes, tall, LANES), F32),
            jax.ShapeDtypeStruct((2, tall, LANES), F32),
            jax.ShapeDtypeStruct((2, tall, LANES), F32),
        ),
        in_specs=[vmem()] * 3,
        out_specs=(hbm(), vmem(), vmem()),
        scratch_shapes=[pltpu.VMEM((planes, tall, LANES), F32), pltpu.SemaphoreType.DMA((1,))],
        compiler_params=pltpu.CompilerParams(vmem_limit_bytes=24 << 20),
        cost_estimate=pl.CostEstimate(flops=8 << 20, bytes_accessed=4 << 20, transcendentals=0),
    )(tracer, above, below)


def set_faces(levels, h, w, own_left, own_right, from_left, from_right, faces, packed):
    tall = h.shape[0]
    lane = iota((tall, LANES), 1)
    odd = lane % 2 == 1
    twice = lane % 64 < 2 * levels
    left, left_unit, right, right_unit = from_left[0], from_left[1], from_right[0], from_right[1]
    other = jnp.where(odd, left_unit, right_unit)
    at = 2 * levels

    def column(offset):
        return other[:, at + offset : at + offset + 1], other[:, at + offset + 1 : at + offset + 2]

    kappa_right, kappa_left = column(0)
    kappa_far_right, kappa_far_left = column(2)
    wet_right, wet_left = column(4)
    wet_far_right, wet_far_left = column(6)

    kappa_near = jnp.where(odd, kappa_left, kappa_right)
    kappa_far = jnp.where(odd, kappa_far_left, kappa_far_right)
    wet_near = jnp.where(odd, wet_left, wet_right)
    wet_far = jnp.where(odd, wet_far_left, wet_far_right)
    kappa_own = jnp.where(odd, h[:, 0:1], h[:, LANES - 1 : LANES])
    wet_own = jnp.where(odd, w[:, 0:1], w[:, LANES - 1 : LANES])

    def face(kappa_a, wet_a, kappa_b, wet_b):
        return 0.25 * (kappa_a + kappa_b) * wet_a * wet_b

    unit = jnp.where(twice, other, pltpu.roll(other, 2 * levels, 1))
    packed[0] = jnp.where(odd, left, right)
    packed[1] = unit * jnp.where(lane < 64, wet_near, wet_far)
    left, left_unit, right, right_unit = own_left[0], own_left[1], own_right[0], own_right[1]
    packed[2] = jnp.where(odd, pltpu.roll(left, 1, 1), pltpu.roll(right, LANES - 1, 1))
    own = jnp.where(odd, pltpu.roll(left_unit, 1, 1), pltpu.roll(right_unit, LANES - 1, 1))
    packed[3] = jnp.where(twice, own, pltpu.roll(own, 2 * levels, 1)) * wet_own
    north = face(kappa_near, wet_near, pltpu.roll(kappa_near, 1, 0), pltpu.roll(wet_near, 1, 0))
    packed[4] = north
    packed[5] = pltpu.roll(north, tall - 1, 0)
    packed[6] = face(kappa_near, wet_near, kappa_far, wet_far)
    packed[7] = face(kappa_near, wet_near, kappa_own, wet_own)

    north = face(h, w, pltpu.roll(h, 1, 0), pltpu.roll(w, 1, 0))
    faces[0] = north
    faces[1] = pltpu.roll(north, tall - 1, 0)
    west = face(
        h, w, jnp.where(lane == 0, kappa_left, pltpu.roll(h, 1, 1)), jnp.where(lane == 0, wet_left, pltpu.roll(w, 1, 1))
    )
    faces[2] = west
    faces[3] = jnp.where(lane == LANES - 1, face(h, w, kappa_right, wet_right), pltpu.roll(west, LANES - 1, 1))


def set_beside(levels, upright, wide, packed, beside):
    tall = upright.shape[0]
    lane = iota((tall, LANES), 1)
    odd = lane % 2 == 1
    heat = lane % 64 < 2 * levels

    def chosen(f):
        left_far, left_near, right_near, right_far = [upright[:, 4 * f + e : 4 * f + e + 1] for e in range(4)]
        near = jnp.where(odd, left_near, right_near)
        return jnp.where(lane < 64, near, jnp.where(odd, left_far, right_far))

    both = packed[0] + packed[1] * jnp.where(heat, chosen(0), chosen(1))
    far = pltpu.roll(both, 64, 1)
    ends_of = [jnp.where(odd, w[:, 0:1], w[:, LANES - 1 : LANES]) for w in wide]
    own = packed[2] + packed[3] * jnp.where(heat, ends_of[0], ends_of[1])
    near = both + packed[5] * (pltpu.roll(both, tall - 1, 0) - both)
    near = near + packed[4] * (pltpu.roll(both, 1, 0) - both)
    near = near + packed[6] * (far - both)
    near = near + packed[7] * (own - both)
    beside[0] = both
    beside[1] = near


def one_pass(value, faces, beside, shift):
    tall = value.shape[0]
    lane = iota(value.shape, 1)
    moved = pltpu.roll(beside, shift, 1)
    west = jnp.where(lane == 0, moved, pltpu.roll(value, 1, 1))
    east = jnp.where(lane == LANES - 1, moved, pltpu.roll(value, LANES - 1, 1))
    result = value + faces[1] * (pltpu.roll(value, tall - 1, 0) - value)
    result = result + faces[0] * (pltpu.roll(value, 1, 0) - value)
    result = result + faces[3] * (east - value)
    return result + faces[2] * (west - value)


def middle_kernel(
    capacity, levels, arrived, wide_h, currents_h, own_left_h, own_right_h, from_left_h, from_right_h,
    sent_h, forcing_h, near_h, faces_h,
    placing, values, number_t, top, currents, own_left, own_right, from_left, from_right,
    faces, packed, sent, forcing, near_o, sems, sent_sems,
):
    devices, message, _ = arrived.shape
    rows_all = currents.shape[1]
    tall = rows_all + 2 * HALO
    loads = start_all(
        [(wide_h.at[levels * k], top.at[k]) for k in range(3)]
        + [
            (wide_h.at[pl.ds(3 * levels, 2)], top.at[pl.ds(3, 2)]),
            (currents_h.at[0, 0], currents.at[0]),
            (currents_h.at[1, 0], currents.at[1]),
            (own_left_h, own_left),
            (own_right_h, own_right),
            (from_left_h, from_left),
            (from_right_h, from_right),
        ],
        sems,
    )
    span = 4 * capacity
    group = LANES // span
    groups = devices // group
    sub8 = iota((8, LANES), 0)
    lane8 = iota((8, LANES), 1)

    lane1 = iota((1, LANES), 1)
    spread = (iota((LANES, LANES), 0) - NUMBERS) == iota((LANES, LANES), 1) % span // 4
    every = jnp.concatenate([arrived[s, span + 8 : span + 9, :] for s in range(devices)], 0).astype(BF16)
    every = jnp.dot(every, jnp.where(spread, 1.0, 0.0).astype(BF16), preferred_element_type=F32)
    numbers = []
    for m in range(groups):
        line = jnp.zeros((1, LANES), F32)
        for g in range(group):
            s = m * group + g
            line = jnp.where(lane1 // span == g, every[s : s + 1], line)
        numbers.append(line)
    number_t[...] = jnp.transpose(
        jnp.concatenate(numbers + [jnp.zeros((LANES - groups, LANES), F32)], 0)
    )

    row_number = iota((rows_all, LANES), 0).astype(F32) + 1.0
    lane_field = iota((rows_all, LANES), 1) % 4
    for m in range(groups):
        hit = numbers[m] == row_number
        for f in range(4):
            placing[f * rows_all : (f + 1) * rows_all, m * LANES : (m + 1) * LANES] = jnp.where(
                hit & (lane_field == f), 1.0, 0.0
            ).astype(BF16)
    edge_rows = jnp.zeros((8, LANES), F32)
    edge_cols = jnp.zeros((8, LANES), F32)
    for s in range(devices):
        high, low = split(arrived[s, 0:span, :])
        values[s * span : (s + 1) * span, 0:LANES] = high
        values[s * span : (s + 1) * span, LANES : 2 * LANES] = low
        edge_rows = edge_rows + arrived[s, span : span + 8, :]
        edge_cols = edge_cols + arrived[s, span + 8 : span + 16, :]
    total = jnp.dot(placing[...], values[...], preferred_element_type=F32)
    total = total[:, 0:LANES] + total[:, LANES : 2 * LANES]

    wait_all(loads)
    set_faces(levels, top[3], top[4], own_left, own_right, from_left, from_right, faces, packed)
    wet_wide = top[4]

    def plane(f):
        return total[f * rows_all : (f + 1) * rows_all]

    wide = []
    for f in range(2):
        before = pick(sub8 >= 6, edge_rows if f == 1 else pltpu.roll(edge_rows, 4, 0))
        after = pick(sub8 < 2, edge_rows if f == 0 else pltpu.roll(edge_rows, 4, 0))
        wide.append(jnp.concatenate([before, plane(f), after], 0))
        forcing[f] = wide[f]
    wet = wet_wide[HALO : HALO + rows_all]
    for f in range(2, 4):
        forcing[f, 0:HALO, :] = jnp.zeros((HALO, LANES), F32)
        forcing[f, HALO : HALO + rows_all, :] = plane(f) * wet
        forcing[f, HALO + rows_all : tall, :] = jnp.zeros((HALO, LANES), F32)

    part8 = sub8 % 4
    within = (part8 == lane8 % 4) & (lane8 >= HALO) & (lane8 < HALO + rows_all)
    upper = (part8 == 3) & (lane8 == HALO - 1)
    lower = (part8 == 0) & (lane8 == HALO + rows_all)
    halves = [[], []]
    for k in range(4):
        column = pick(within, pltpu.roll(edge_cols, HALO - k, 1))
        if k in (1, 2):
            column = column + pick(upper, pltpu.roll(edge_cols, (HALO - CORNERS - k) % LANES, 1))
            column = column + pick(lower, pltpu.roll(edge_cols, (HALO + rows_all - CORNERS - 1 - k) % LANES, 1))
        for f in range(2):
            halves[f].append(jnp.sum(column[4 * f : 4 * f + 4], axis=0, keepdims=True))
    columns = jnp.concatenate(halves[0] + halves[1], 0)
    upright = jnp.transpose(jnp.concatenate([columns, jnp.zeros((LANES - 8, LANES), F32)], 0))[0:tall]
    set_beside(levels, upright, wide, packed, near_o)
    stores = start_all([(forcing, forcing_h), (near_o, near_h), (faces, faces_h)], sems, 10)

    surface = []
    unit = top[2] * wet_wide
    for f in range(2):
        value = top[f] + unit * wide[f]
        shift = LANES - (2 * levels * f + 1)
        value = one_pass(value, faces, near_o[0], shift)
        value = one_pass(value, faces, near_o[1], shift)
        surface.append(value[HALO : HALO + rows_all] * wet)
    for f in range(2):
        surface.append(
            (currents[f] + top[2, HALO : HALO + rows_all, :] * forcing[2 + f, HALO : HALO + rows_all, :]) * wet
        )
    high, low = split(jnp.concatenate(surface, 0))
    source = jnp.concatenate([high, low], 1)
    lane_t = iota((LANES, 4 * rows_all), 1)
    sub_t = iota((LANES, 4 * rows_all), 0)
    target = jnp.where(sub_t % 4 == lane_t // rows_all, lane_t % rows_all + 1, -1).astype(F32)
    mask = jnp.concatenate([wet, jnp.zeros((LANES - rows_all, LANES), F32)], 0).astype(BF16)
    per = LANES // 4
    slot_number = number_t[pl.ds(0, per, stride=4), :]
    lane_s = (iota((per, LANES), 1) + 1).astype(F32)
    height = back_rows(capacity)
    for m in range(groups):
        chosen_rows = jnp.where(number_t[:, m : m + 1] == target, 1.0, 0.0).astype(BF16)
        rows = jnp.dot(chosen_rows, source, preferred_element_type=F32)
        rows = rows[:, 0:LANES] + rows[:, LANES : 2 * LANES]
        slots = jnp.where(slot_number[:, m : m + 1] == lane_s, 1.0, 0.0).astype(BF16)
        masks = jnp.dot(slots, mask, preferred_element_type=F32)
        for g in range(group):
            s = m * group + g
            sent[s, 0:span, :] = rows[g * span : (g + 1) * span]
            sent[s, span : span + capacity, :] = masks[g * capacity : (g + 1) * capacity]
            if height > span + capacity:
                sent[s, span + capacity : height, :] = jnp.zeros((height - span - capacity, LANES), F32)
        at = pl.ds(m * group, group)
        stores += start_all([(sent.at[at], sent_h.at[at])], sent_sems, m)
    wait_all(stores)


def middle(capacity, levels, arrived, wide, currents, *columns):
    devices = arrived.shape[0]
    rows = currents.shape[2]
    tall = rows + 2 * HALO
    height = back_rows(capacity)
    return pl.pallas_call(
        functools.partial(middle_kernel, capacity, levels),
        out_shape=(
            pltpu.HBM((devices, height, LANES), F32),
            pltpu.HBM((4, tall, LANES), F32),
            pltpu.HBM((2, tall, LANES), F32),
            pltpu.HBM((4, tall, LANES), F32),
        ),
        in_specs=[vmem()] + [hbm()] * 2 + [pl.BlockSpec(memory_space=pl.ANY)] * 4,
        out_specs=(hbm(),) * 4,
        scratch_shapes=[
            pltpu.VMEM((4 * rows, 4 * capacity * devices), BF16),
            pltpu.VMEM((4 * capacity * devices, 2 * LANES), BF16),
            pltpu.VMEM((LANES, LANES), F32),
            pltpu.VMEM((5, tall, LANES), F32),
            pltpu.VMEM((2, rows, LANES), F32),
        ]
        + [pltpu.VMEM((2, tall, LANES), F32)] * 4
        + [
            pltpu.VMEM((4, tall, LANES), F32),
            pltpu.VMEM((8, tall, LANES), F32),
            pltpu.VMEM((devices, height, LANES), F32),
            pltpu.VMEM((4, tall, LANES), F32),
            pltpu.VMEM((2, tall, LANES), F32),
            pltpu.SemaphoreType.DMA((13,)),
            pltpu.SemaphoreType.DMA((4 * capacity * devices // LANES,)),
        ],
        compiler_params=pltpu.CompilerParams(vmem_limit_bytes=24 << 20),
        cost_estimate=pl.CostEstimate(flops=200 << 20, bytes_accessed=4 << 20, transcendentals=0),
    )(arrived, *pin(wide, currents), *columns)


def finish_kernel(
    levels, wide_h, currents_h, faces_h, forcing_h, near_h, ocean, wide, currents, faces, forcing, near, sems
):
    rows_all = currents.shape[2]
    wait_all(
        start_all(
            [(wide_h, wide), (currents_h, currents), (faces_h, faces), (forcing_h, forcing), (near_h, near)], sems
        )
    )
    inner = slice(HALO, HALO + rows_all)

    def level(l, carry):
        unit = wide[2 * levels + l]
        masked = unit * wide[3 * levels + 1]
        for f in range(2):
            value = wide[f * levels + l] + masked * forcing[f]
            shift = LANES - 1 - 2 * (levels * f + l)
            value = one_pass(value, faces, near[0], shift)
            value = one_pass(value, faces, near[1], shift)
            ocean[f, l] = value[inner]
            ocean[2 + f, l] = currents[f, l] + unit[inner] * forcing[2 + f][inner]
        return carry

    lax.fori_loop(0, levels, level, 0)


def finish(levels, wide, currents, faces, forcing, near):
    rows = currents.shape[2]
    return pl.pallas_call(
        functools.partial(finish_kernel, levels),
        out_shape=jax.ShapeDtypeStruct((4, levels, rows, LANES), F32),
        in_specs=[hbm()] * 5,
        out_specs=vmem(),
        scratch_shapes=[pltpu.VMEM(a.shape, F32) for a in (wide, currents, faces, forcing, near)]
        + [pltpu.SemaphoreType.DMA((5,))],
        compiler_params=pltpu.CompilerParams(vmem_limit_bytes=24 << 20),
        cost_estimate=pl.CostEstimate(flops=40 << 20, bytes_accessed=6 << 20, transcendentals=0),
    )(*pin(wide, currents, faces, forcing, near))


def remap_back_kernel(
    capacity, block_h, tile_h, owner_h, returned, weights_h, out,
    block_s, tile_s, owner_s, fill, weights, picked, total, sems, weight_sems,
):
    npairs = block_s.shape[0]
    nblocks = total.shape[0]
    devices = fill.shape[0]
    height = back_rows(capacity)
    scalars = start_all([(owner_h, owner_s), (block_h, block_s), (tile_h, tile_s)], sems)
    part_tiles = weights.shape[0] // PARTS
    parts = [pl.ds(n * part_tiles, part_tiles) for n in range(PARTS)]
    loads = start_all([(weights_h.at[at], weights.at[at]) for at in parts], weight_sems)
    total[...] = jnp.zeros_like(total)

    def clear_fill(i, carry):
        fill[i] = 0
        return carry

    lax.fori_loop(0, devices, clear_fill, 0, unroll=16)
    wait_all(scalars)

    def gather(p, carry):
        owner = owner_s[p]
        rank = fill[owner]
        fill[owner] = rank + 1
        rows = returned[pl.ds(owner * height + 4 * rank, 4), :]
        mask = returned[pl.ds(owner * height + 4 * capacity + rank, 1), :]
        high, low = split(jnp.concatenate([rows, mask, jnp.zeros((3, LANES), F32)], 0))
        picked[p] = jnp.concatenate([high, low], 0)
        return carry

    lax.fori_loop(0, npairs, gather, 0, unroll=32)
    wait_all(loads)

    def pair(p, carry):
        value = lax.dot_general(
            picked[p], weights[tile_s[p]], (((1,), (1,)), ((), ())), preferred_element_type=F32
        )
        b = block_s[p]
        total[b] = total[b] + (value[0:8] + value[8:16])
        return carry

    lax.fori_loop(0, npairs, pair, 0, unroll=64)
    for b in range(nblocks):
        sums = total[b]
        out[:, b * LANES : (b + 1) * LANES] = sums[0:4] / jnp.maximum(sums[4:5], 0.1)


def remap_back(capacity, devices, pair_block, pair_tile, owner, returned, remap_weight, nblocks):
    npairs = pair_block.shape[0]
    return pl.pallas_call(
        functools.partial(remap_back_kernel, capacity),
        out_shape=jax.ShapeDtypeStruct((4, nblocks * LANES), F32),
        in_specs=[hbm()] * 3 + [vmem(), hbm()],
        out_specs=vmem(),
        scratch_shapes=[pltpu.SMEM((npairs,), I32)] * 3
        + [
            pltpu.SMEM((devices,), I32),
            pltpu.VMEM(remap_weight.shape, BF16),
            pltpu.VMEM((npairs, 16, LANES), BF16),
            pltpu.VMEM((nblocks, 8, LANES), F32),
            pltpu.SemaphoreType.DMA((3,)),
            pltpu.SemaphoreType.DMA((PARTS,)),
        ],
        compiler_params=pltpu.CompilerParams(vmem_limit_bytes=24 << 20),
        cost_estimate=pl.CostEstimate(flops=2 * npairs * 16 * LANES * LANES, bytes_accessed=6 << 20, transcendentals=0),
    )(*pin(pair_block, pair_tile, owner), returned, *pin(remap_weight))


def local(
    atm_state,
    pair_block,
    pair_owner,
    pair_row,
    pair_tile,
    remap_weight,
    wet_mask,
    ocean_state,
    vert_kappa,
    horiz_kappa,
):
    grid_x = lax.axis_size("gx")
    grid_y = lax.axis_size("gy")
    devices = grid_x * grid_y
    npairs = pair_block.shape[0]
    capacity = max(2, 2 * npairs // devices)
    levels, tile_rows, _ = vert_kappa.shape
    nblocks = atm_state.shape[1] // LANES
    owner = pair_owner.reshape(npairs)
    message = 4 * capacity + EDGE
    outgoing = remap_out(
        capacity, grid_y, devices, tile_rows, atm_state, pair_block, owner, pair_row, pair_tile, remap_weight
    )
    arrived = lax.all_to_all(
        outgoing.reshape(devices, message, LANES), ("gx", "gy"), split_axis=0, concat_axis=0, tiled=True
    )
    tracer, currents, edge_up, edge_down = solve(ocean_state, vert_kappa, horiz_kappa, wet_mask)
    rise_x = [(i, i + 1) for i in range(grid_x - 1)]
    fall_x = [(b, a) for a, b in rise_x]
    rise_y = [(i, i + 1) for i in range(grid_y - 1)]
    fall_y = [(b, a) for a, b in rise_y]
    above = lax.ppermute(edge_down, "gx", rise_x)
    below = lax.ppermute(edge_up, "gx", fall_x)
    wide, to_left, to_right = pack(levels, tracer, above, below)
    from_left = lax.ppermute(to_right, "gy", rise_y)
    from_right = lax.ppermute(to_left, "gy", fall_y)
    sent, forcing, near, faces = middle(
        capacity, levels, arrived, wide, currents, to_left, to_right, from_left, from_right
    )
    returned = lax.all_to_all(sent, ("gx", "gy"), split_axis=0, concat_axis=0, tiled=True)
    ocean_next = finish(levels, wide, currents, faces, forcing, near)
    atm_surface = remap_back(
        capacity, devices, pair_block, pair_tile, owner, returned.reshape(-1, LANES), remap_weight, nblocks
    )
    return (ocean_next, atm_surface)


def solution(mesh):
    placed = (
        P(None, ("gx", "gy")),
        P(("gx", "gy")),
        P(("gx", "gy"), None),
        P(("gx", "gy")),
        P(("gx", "gy")),
        P(("gx", "gy"), None, None),
        P("gx", "gy"),
        P(None, None, "gx", "gy"),
        P(None, "gx", "gy"),
        P("gx", "gy"),
    )
    return jax.shard_map(
        local,
        mesh=mesh,
        in_specs=placed,
        out_specs=(P(None, None, "gx", "gy"), P(None, ("gx", "gy"))),
        check_vma=False,
    )
```

```python
import functools

import jax
import jax.numpy as jnp
from jax import lax
from jax.experimental import pallas as pl
from jax.experimental.pallas import tpu as pltpu
from jax.sharding import PartitionSpec as P

F32 = jnp.float32
BF16 = jnp.bfloat16
I32 = jnp.int32
VMEM = pltpu.VMEM
SMEM = pltpu.SMEM
LANES = 128
EDGE = 16
HALO = 8
NUMBERS = 72
CORNERS = 112
PARTS = 8


def hbm():
    return pl.BlockSpec(memory_space=pltpu.HBM)


def vmem():
    return pl.BlockSpec(memory_space=VMEM)


def pin(*arrays):
    return [pltpu.with_memory_space_constraint(a, pltpu.HBM) for a in arrays]


def start_all(pairs, sems, first=0):
    copies = [pltpu.make_async_copy(src, dst, sems.at[first + n]) for n, (src, dst) in enumerate(pairs)]
    for copy in copies:
        copy.start()
    return copies


def wait_all(copies):
    for copy in copies:
        copy.wait()


def iota(shape, dim):
    return lax.broadcasted_iota(I32, shape, dim)


def pick(mask, value):
    return jnp.where(mask, value, 0.0)


def split(value):
    high = value.astype(BF16)
    return high, (value - high.astype(F32)).astype(BF16)


def remap_out_kernel(
    capacity, grid_y, tile_rows, block_h, owner_h, row_h, tile_h, atm_h, weights_h, out_h,
    out, block_s, owner_s, row_s, tile_s, atm, weights, flux, every, fill, row_slots, col_slots, rows_acc, cols_acc, sems, weight_sems, out_sems,
):
    devices = fill.shape[0]
    npairs = block_s.shape[0]
    tiles = weights.shape[0]
    four = flux.shape[0]
    nblocks = four // 4
    message = 4 * capacity + EDGE
    copies = [
        pltpu.make_async_copy(src, dst, sems.at[n])
        for n, (src, dst) in enumerate(
            [(atm_h, atm), (block_h, block_s), (owner_h, owner_s), (row_h, row_s), (tile_h, tile_s)]
        )
    ]
    for copy in copies:
        copy.start()
    part_tiles = tiles // PARTS
    parts = [pl.ds(n * part_tiles, part_tiles) for n in range(PARTS)]
    loads = [pltpu.make_async_copy(weights_h.at[at], weights.at[at], weight_sems.at[n]) for n, at in enumerate(parts)]
    for load in loads:
        load.start()
    out[...] = jnp.zeros_like(out)
    row_slots[...] = jnp.zeros_like(row_slots)
    col_slots[...] = jnp.zeros_like(col_slots)

    def clear_fill(i, carry):
        fill[i] = 0
        return carry

    lax.fori_loop(0, devices, clear_fill, 0, unroll=16)
    copies[0].wait()
    wind_u = atm[0:1, :]
    wind_v = atm[1:2, :]
    speed = jnp.sqrt(wind_u * wind_u + wind_v * wind_v + 0.25)
    heat = 0.5 * speed * (atm[2:3, :] - atm[5:6, :])
    water = atm[4:5, :] - 0.3 * speed * atm[3:4, :]
    for f, plane in enumerate([heat, water, 0.2 * speed * wind_u, 0.2 * speed * wind_v]):
        for b in range(nblocks):
            flux[f * nblocks + b : f * nblocks + b + 1, :] = plane[:, b * LANES : (b + 1) * LANES]
    source = flux[...].astype(BF16)

    for n in range(PARTS):
        loads[n].wait()

        def tile_step(t, carry):
            every[pl.ds(pl.multiple_of(t * four, 8), four), :] = jnp.dot(
                source, weights[t], preferred_element_type=F32
            )
            return carry

        lax.fori_loop(n * part_tiles, (n + 1) * part_tiles, tile_step, 0, unroll=16)
    for copy in copies[1:]:
        copy.wait()

    sub = iota((8, LANES), 0)
    lane = iota((8, LANES), 1)
    part = sub % 4
    edge_row = jnp.where(part == 0, 0, jnp.where(part == 1, 1, tile_rows - 4 + part))
    band = ((lane - part) >> 2) * 4 + part
    id_rank = jnp.where(sub == 0, lane - NUMBERS, -1)

    def pair(p, carry):
        owner = owner_s[p]
        row = row_s[p]
        rank = fill[owner]
        fill[owner] = rank + 1
        first = tile_s[p] * four + block_s[p]
        lines = [every[pl.ds(first + f * nblocks, 1), :] for f in range(4)]
        for f in range(4):
            out[pl.ds(owner * message + 4 * rank + f, 1), :] = lines[f]
        tracer = jnp.where(sub < 4, lines[0], lines[1])
        slot = owner * capacity + rank
        row_slots[slot] = pick(edge_row == row, tracer)
        number = (row + 1).astype(F32)
        col_slots[slot] = pick(band == row, pltpu.roll(tracer, row + 2, 1)) + pick(id_rank == rank, number)
        return carry

    lax.fori_loop(0, npairs, pair, 0, unroll=32)

    def owner_step(d, carry):
        rows = row_slots[d * capacity]
        cols = col_slots[d * capacity]
        for r in range(1, capacity):
            rows = rows + row_slots[d * capacity + r]
            cols = cols + col_slots[d * capacity + r]
        rows_acc[d] = rows
        cols_acc[d] = cols
        return carry

    lax.fori_loop(0, devices, owner_step, 0, unroll=8)

    grid_x = devices // grid_y
    zero = jnp.zeros((8, LANES), F32)

    def columns_of(i, j):
        if not (0 <= i < grid_x and 0 <= j < grid_y):
            return zero
        return cols_acc[i * grid_y + j]

    from_left = (lane - sub) % 4 < 2
    in_band = lane < tile_rows + 4
    in_ids = (sub == 0) & (lane >= NUMBERS) & (lane < NUMBERS + capacity)
    last, first = part == 3, part == 0
    send = devices // 4
    stores = []
    for d in range(devices):
        i, j = d // grid_y, d % grid_y
        below = rows_acc[d + grid_y] if i < grid_x - 1 else zero
        above = rows_acc[d - grid_y] if i > 0 else zero
        base = d * message + 4 * capacity
        out[base : base + 8, :] = jnp.where(part < 2, below, above)
        tile = pick(in_band, jnp.where(from_left, columns_of(i, j - 1), columns_of(i, j + 1)))
        upper = pick(last & (lane == tile_rows), columns_of(i - 1, j - 1))
        upper = upper + pick(last & (lane == tile_rows + 1), columns_of(i - 1, j + 1))
        lower = pick(first & (lane == 1), columns_of(i + 1, j - 1))
        lower = lower + pick(first & (lane == 2), columns_of(i + 1, j + 1))
        tile = tile + pltpu.roll(upper, CORNERS - tile_rows, 1) + pltpu.roll(lower, CORNERS + 1, 1)
        tile = tile + pick(in_ids, cols_acc[d])
        out[base + 8 : base + 16, :] = tile
        if d % send == send - 1:
            n = d // send
            at = pl.ds(n * send * message, send * message)
            stores.append(pltpu.make_async_copy(out.at[at], out_h.at[at], out_sems.at[n]))
            stores[-1].start()
    for store in stores:
        store.wait()


def remap_out(capacity, grid_y, devices, tile_rows, atm_state, pair_block, owner, pair_row, pair_tile, remap_weight):
    npairs = pair_block.shape[0]
    nblocks = atm_state.shape[1] // LANES
    message = 4 * capacity + EDGE
    tiles = remap_weight.shape[0]
    return pl.pallas_call(
        functools.partial(remap_out_kernel, capacity, grid_y, tile_rows),
        out_shape=pltpu.HBM((devices * message, LANES), F32),
        in_specs=[hbm()] * 6,
        out_specs=hbm(),
        scratch_shapes=[pltpu.VMEM((devices * message, LANES), F32)]
        + [pltpu.SMEM((npairs,), I32)] * 4
        + [
            pltpu.VMEM(atm_state.shape, F32),
            pltpu.VMEM(remap_weight.shape, BF16),
            pltpu.VMEM((4 * nblocks, LANES), F32),
            pltpu.VMEM((tiles * 4 * nblocks, LANES), F32),
            pltpu.SMEM((devices,), I32),
            pltpu.VMEM((devices * capacity, 8, LANES), F32),
            pltpu.VMEM((devices * capacity, 8, LANES), F32),
            pltpu.VMEM((devices, 8, LANES), F32),
            pltpu.VMEM((devices, 8, LANES), F32),
            pltpu.SemaphoreType.DMA((5,)),
            pltpu.SemaphoreType.DMA((PARTS,)),
            pltpu.SemaphoreType.DMA((4,)),
        ],
        compiler_params=pltpu.CompilerParams(vmem_limit_bytes=40 << 20),
        cost_estimate=pl.CostEstimate(
            flops=2 * tiles * 4 * nblocks * LANES * LANES, bytes_accessed=6 << 20, transcendentals=0
        ),
    )(*pin(pair_block, owner, pair_row, pair_tile, atm_state, remap_weight))


def solve_kernel(state, kappa, horiz, wet, tracer, currents_h, edge_up, edge_down, currents, sems):
    levels = kappa.shape[0]
    rows_all = kappa.shape[1]
    planes = tracer.shape[0]

    def chunk(c, carry):
        rows = pl.ds(pl.multiple_of(c * 8, 8), 8)
        column = [kappa[l, rows, :] for l in range(levels)]
        face = [0.5 * (column[l] + column[l + 1]) for l in range(levels - 1)]
        upper = []
        now = None
        for l in range(levels):
            diagonal = 1.0
            if l > 0:
                diagonal = diagonal + face[l - 1]
            if l < levels - 1:
                diagonal = diagonal + face[l]
            if l > 0:
                diagonal = diagonal + face[l - 1] * upper[-1]
            inverse = 1.0 / diagonal
            if l == 0:
                now = [state[f, 0, rows, :] * inverse for f in range(4)] + [inverse]
            else:
                pull = face[l - 1] * inverse
                now = [state[f, l, rows, :] * inverse + pull * now[f] for f in range(4)] + [pull * now[4]]
            upper.append(-face[l] * inverse if l < levels - 1 else None)
            store(l, rows, now)
        for l in range(levels - 2, -1, -1):
            here = load(l, rows)
            now = [here[f] - upper[l] * now[f] for f in range(5)]
            store(l, rows, now)
        return carry

    def store(l, rows, now):
        tracer[l, rows, :] = now[0]
        tracer[levels + l, rows, :] = now[1]
        currents[0, l, rows, :] = now[2]
        currents[1, l, rows, :] = now[3]
        tracer[2 * levels + l, rows, :] = now[4]

    def load(l, rows):
        return [
            tracer[l, rows, :],
            tracer[levels + l, rows, :],
            currents[0, l, rows, :],
            currents[1, l, rows, :],
            tracer[2 * levels + l, rows, :],
        ]

    lax.fori_loop(0, rows_all // 8, chunk, 0)
    out = start_all([(currents, currents_h)], sems)
    tracer[3 * levels] = horiz[...]
    tracer[3 * levels + 1] = wet[...].astype(F32)
    for k in range(planes):
        edge_up[k] = tracer[k, 0:8, :]
        edge_down[k] = tracer[k, rows_all - 8 : rows_all, :]
    wait_all(out)


def solve(ocean_state, vert_kappa, horiz_kappa, wet_mask):
    levels, rows, _ = vert_kappa.shape
    planes = 3 * levels + 2
    return pl.pallas_call(
        solve_kernel,
        out_shape=(
            jax.ShapeDtypeStruct((planes, rows, LANES), F32),
            pltpu.HBM((2, levels, rows, LANES), F32),
            jax.ShapeDtypeStruct((planes, 8, LANES), F32),
            jax.ShapeDtypeStruct((planes, 8, LANES), F32),
        ),
        in_specs=[vmem()] * 4,
        out_specs=(vmem(), hbm(), vmem(), vmem()),
        scratch_shapes=[pltpu.VMEM((2, levels, rows, LANES), F32), pltpu.SemaphoreType.DMA((1,))],
        compiler_params=pltpu.CompilerParams(vmem_limit_bytes=24 << 20),
        cost_estimate=pl.CostEstimate(flops=20 << 20, bytes_accessed=6 << 20, transcendentals=0),
    )(ocean_state, vert_kappa, horiz_kappa, wet_mask)


def pack_kernel(levels, tracer, above, below, wide_h, to_left, to_right, wide, sems):
    planes, rows, _ = tracer.shape
    for k in range(planes):
        wide[k, 0:HALO, :] = above[k]
        wide[k, HALO : HALO + rows, :] = tracer[k]
        wide[k, HALO + rows : 2 * HALO + rows, :] = below[k]
    out = start_all([(wide, wide_h)], sems)
    lane = iota((8, LANES), 1)

    def chunk(c, carry):
        at = pl.ds(pl.multiple_of(c * 8, 8), 8)

        def place(values, lanes):
            left, right = jnp.zeros((8, LANES), F32), jnp.zeros((8, LANES), F32)
            for k, (near, far) in zip(values, lanes):
                value = wide[k, at, :]
                left = jnp.where(lane == near, pltpu.roll(value, near, 1), left)
                left = jnp.where(lane == far, pltpu.roll(value, far - 1, 1), left)
                right = jnp.where(lane == near + 1, pltpu.roll(value, (near + 2) % LANES, 1), right)
                right = jnp.where(lane == far + 1, pltpu.roll(value, (far + 3) % LANES, 1), right)
            return left, right

        left, right = place(range(2 * levels), [(2 * k, 64 + 2 * k) for k in range(2 * levels)])
        to_left[0, at, :] = left
        to_right[0, at, :] = right
        lanes = [(2 * l, 64 + 2 * l) for l in range(levels)]
        lanes += [(2 * levels, 2 * levels + 2), (2 * levels + 4, 2 * levels + 6)]
        left, right = place(range(2 * levels, 3 * levels + 2), lanes)
        to_left[1, at, :] = left
        to_right[1, at, :] = right
        return carry

    lax.fori_loop(0, (rows + 2 * HALO) // 8, chunk, 0)
    wait_all(out)


def pack(levels, tracer, above, below):
    planes, rows, _ = tracer.shape
    tall = rows + 2 * HALO
    return pl.pallas_call(
        functools.partial(pack_kernel, levels),
        out_shape=(
            pltpu.HBM((planes, tall, LANES), F32),
            jax.ShapeDtypeStruct((2, tall, LANES), F32),
            jax.ShapeDtypeStruct((2, tall, LANES), F32),
        ),
        in_specs=[vmem()] * 3,
        out_specs=(hbm(), vmem(), vmem()),
        scratch_shapes=[pltpu.VMEM((planes, tall, LANES), F32), pltpu.SemaphoreType.DMA((1,))],
        compiler_params=pltpu.CompilerParams(vmem_limit_bytes=24 << 20),
        cost_estimate=pl.CostEstimate(flops=8 << 20, bytes_accessed=4 << 20, transcendentals=0),
    )(tracer, above, below)


def set_faces(levels, h, w, own_left, own_right, from_left, from_right, faces, packed):
    tall = h.shape[0]
    lane = iota((tall, LANES), 1)
    odd = lane % 2 == 1
    twice = lane % 64 < 2 * levels
    left, left_unit, right, right_unit = from_left[0], from_left[1], from_right[0], from_right[1]
    other = jnp.where(odd, left_unit, right_unit)
    at = 2 * levels

    def column(offset):
        return other[:, at + offset : at + offset + 1], other[:, at + offset + 1 : at + offset + 2]

    kappa_right, kappa_left = column(0)
    kappa_far_right, kappa_far_left = column(2)
    wet_right, wet_left = column(4)
    wet_far_right, wet_far_left = column(6)

    kappa_near = jnp.where(odd, kappa_left, kappa_right)
    kappa_far = jnp.where(odd, kappa_far_left, kappa_far_right)
    wet_near = jnp.where(odd, wet_left, wet_right)
    wet_far = jnp.where(odd, wet_far_left, wet_far_right)
    kappa_own = jnp.where(odd, h[:, 0:1], h[:, LANES - 1 : LANES])
    wet_own = jnp.where(odd, w[:, 0:1], w[:, LANES - 1 : LANES])

    def face(kappa_a, wet_a, kappa_b, wet_b):
        return 0.25 * (kappa_a + kappa_b) * wet_a * wet_b

    unit = jnp.where(twice, other, pltpu.roll(other, 2 * levels, 1))
    packed[0] = jnp.where(odd, left, right)
    packed[1] = unit * jnp.where(lane < 64, wet_near, wet_far)
    left, left_unit, right, right_unit = own_left[0], own_left[1], own_right[0], own_right[1]
    packed[2] = jnp.where(odd, pltpu.roll(left, 1, 1), pltpu.roll(right, LANES - 1, 1))
    own = jnp.where(odd, pltpu.roll(left_unit, 1, 1), pltpu.roll(right_unit, LANES - 1, 1))
    packed[3] = jnp.where(twice, own, pltpu.roll(own, 2 * levels, 1)) * wet_own
    north = face(kappa_near, wet_near, pltpu.roll(kappa_near, 1, 0), pltpu.roll(wet_near, 1, 0))
    packed[4] = north
    packed[5] = pltpu.roll(north, tall - 1, 0)
    packed[6] = face(kappa_near, wet_near, kappa_far, wet_far)
    packed[7] = face(kappa_near, wet_near, kappa_own, wet_own)

    north = face(h, w, pltpu.roll(h, 1, 0), pltpu.roll(w, 1, 0))
    faces[0] = north
    faces[1] = pltpu.roll(north, tall - 1, 0)
    west = face(
        h, w, jnp.where(lane == 0, kappa_left, pltpu.roll(h, 1, 1)), jnp.where(lane == 0, wet_left, pltpu.roll(w, 1, 1))
    )
    faces[2] = west
    faces[3] = jnp.where(lane == LANES - 1, face(h, w, kappa_right, wet_right), pltpu.roll(west, LANES - 1, 1))


def set_beside(levels, upright, wide, packed, beside):
    tall = upright.shape[0]
    lane = iota((tall, LANES), 1)
    odd = lane % 2 == 1
    heat = lane % 64 < 2 * levels

    def chosen(f):
        left_far, left_near, right_near, right_far = [upright[:, 4 * f + e : 4 * f + e + 1] for e in range(4)]
        near = jnp.where(odd, left_near, right_near)
        return jnp.where(lane < 64, near, jnp.where(odd, left_far, right_far))

    both = packed[0] + packed[1] * jnp.where(heat, chosen(0), chosen(1))
    far = pltpu.roll(both, 64, 1)
    ends_of = [jnp.where(odd, w[:, 0:1], w[:, LANES - 1 : LANES]) for w in wide]
    own = packed[2] + packed[3] * jnp.where(heat, ends_of[0], ends_of[1])
    near = both + packed[5] * (pltpu.roll(both, tall - 1, 0) - both)
    near = near + packed[4] * (pltpu.roll(both, 1, 0) - both)
    near = near + packed[6] * (far - both)
    near = near + packed[7] * (own - both)
    beside[0] = both
    beside[1] = near


def one_pass(value, faces, beside, shift):
    tall = value.shape[0]
    lane = iota(value.shape, 1)
    moved = pltpu.roll(beside, shift, 1)
    west = jnp.where(lane == 0, moved, pltpu.roll(value, 1, 1))
    east = jnp.where(lane == LANES - 1, moved, pltpu.roll(value, LANES - 1, 1))
    result = value + faces[1] * (pltpu.roll(value, tall - 1, 0) - value)
    result = result + faces[0] * (pltpu.roll(value, 1, 0) - value)
    result = result + faces[3] * (east - value)
    return result + faces[2] * (west - value)


def middle_kernel(
    capacity, levels, arrived, wide_h, currents_h, own_left_h, own_right_h, from_left_h, from_right_h,
    sent_h, forcing_h, near_h, faces_h,
    placing, values, number_t, top, currents, own_left, own_right, from_left, from_right,
    faces, packed, sent, forcing, near_o, sems, sent_sems,
):
    devices, message, _ = arrived.shape
    rows_all = currents.shape[1]
    tall = rows_all + 2 * HALO
    loads = start_all(
        [(wide_h.at[levels * k], top.at[k]) for k in range(3)]
        + [
            (wide_h.at[pl.ds(3 * levels, 2)], top.at[pl.ds(3, 2)]),
            (currents_h.at[0, 0], currents.at[0]),
            (currents_h.at[1, 0], currents.at[1]),
            (own_left_h, own_left),
            (own_right_h, own_right),
            (from_left_h, from_left),
            (from_right_h, from_right),
        ],
        sems,
    )
    span = 4 * capacity
    group = LANES // span
    groups = devices // group
    sub8 = iota((8, LANES), 0)
    lane8 = iota((8, LANES), 1)

    lane1 = iota((1, LANES), 1)
    spread = (iota((LANES, LANES), 0) - NUMBERS) == iota((LANES, LANES), 1) % span // 4
    every = jnp.concatenate([arrived[s, span + 8 : span + 9, :] for s in range(devices)], 0).astype(BF16)
    every = jnp.dot(every, jnp.where(spread, 1.0, 0.0).astype(BF16), preferred_element_type=F32)
    numbers = []
    for m in range(groups):
        line = jnp.zeros((1, LANES), F32)
        for g in range(group):
            s = m * group + g
            line = jnp.where(lane1 // span == g, every[s : s + 1], line)
        numbers.append(line)
    number_t[...] = jnp.transpose(
        jnp.concatenate(numbers + [jnp.zeros((LANES - groups, LANES), F32)], 0)
    )

    row_number = iota((rows_all, LANES), 0).astype(F32) + 1.0
    lane_field = iota((rows_all, LANES), 1) % 4
    for m in range(groups):
        hit = numbers[m] == row_number
        for f in range(4):
            placing[f * rows_all : (f + 1) * rows_all, m * LANES : (m + 1) * LANES] = jnp.where(
                hit & (lane_field == f), 1.0, 0.0
            ).astype(BF16)
    edge_rows = jnp.zeros((8, LANES), F32)
    edge_cols = jnp.zeros((8, LANES), F32)
    for s in range(devices):
        high, low = split(arrived[s, 0:span, :])
        values[s * span : (s + 1) * span, 0:LANES] = high
        values[s * span : (s + 1) * span, LANES : 2 * LANES] = low
        edge_rows = edge_rows + arrived[s, span : span + 8, :]
        edge_cols = edge_cols + arrived[s, span + 8 : span + 16, :]
    total = jnp.dot(placing[...], values[...], preferred_element_type=F32)
    total = total[:, 0:LANES] + total[:, LANES : 2 * LANES]

    wait_all(loads)
    set_faces(levels, top[3], top[4], own_left, own_right, from_left, from_right, faces, packed)
    wet_wide = top[4]

    def plane(f):
        return total[f * rows_all : (f + 1) * rows_all]

    wide = []
    for f in range(2):
        before = pick(sub8 >= 6, edge_rows if f == 1 else pltpu.roll(edge_rows, 4, 0))
        after = pick(sub8 < 2, edge_rows if f == 0 else pltpu.roll(edge_rows, 4, 0))
        wide.append(jnp.concatenate([before, plane(f), after], 0))
        forcing[f] = wide[f]
    wet = wet_wide[HALO : HALO + rows_all]
    for f in range(2, 4):
        forcing[f, 0:HALO, :] = jnp.zeros((HALO, LANES), F32)
        forcing[f, HALO : HALO + rows_all, :] = plane(f) * wet
        forcing[f, HALO + rows_all : tall, :] = jnp.zeros((HALO, LANES), F32)

    part8 = sub8 % 4
    within = (part8 == lane8 % 4) & (lane8 >= HALO) & (lane8 < HALO + rows_all)
    upper = (part8 == 3) & (lane8 == HALO - 1)
    lower = (part8 == 0) & (lane8 == HALO + rows_all)
    halves = [[], []]
    for k in range(4):
        column = pick(within, pltpu.roll(edge_cols, HALO - k, 1))
        if k in (1, 2):
            column = column + pick(upper, pltpu.roll(edge_cols, (HALO - CORNERS - k) % LANES, 1))
            column = column + pick(lower, pltpu.roll(edge_cols, (HALO + rows_all - CORNERS - 1 - k) % LANES, 1))
        for f in range(2):
            halves[f].append(jnp.sum(column[4 * f : 4 * f + 4], axis=0, keepdims=True))
    columns = jnp.concatenate(halves[0] + halves[1], 0)
    upright = jnp.transpose(jnp.concatenate([columns, jnp.zeros((LANES - 8, LANES), F32)], 0))[0:tall]
    set_beside(levels, upright, wide, packed, near_o)
    stores = start_all([(forcing, forcing_h), (near_o, near_h), (faces, faces_h)], sems, 10)

    surface = []
    unit = top[2] * wet_wide
    for f in range(2):
        value = top[f] + unit * wide[f]
        shift = LANES - (2 * levels * f + 1)
        value = one_pass(value, faces, near_o[0], shift)
        value = one_pass(value, faces, near_o[1], shift)
        surface.append(value[HALO : HALO + rows_all] * wet)
    for f in range(2):
        surface.append(
            (currents[f] + top[2, HALO : HALO + rows_all, :] * forcing[2 + f, HALO : HALO + rows_all, :]) * wet
        )
    high, low = split(jnp.concatenate(surface, 0))
    source = jnp.concatenate([high, low], 1)
    lane_t = iota((LANES, 4 * rows_all), 1)
    sub_t = iota((LANES, 4 * rows_all), 0)
    target = jnp.where(sub_t % 4 == lane_t // rows_all, lane_t % rows_all + 1, -1).astype(F32)
    for m in range(groups):
        chosen_rows = jnp.where(number_t[:, m : m + 1] == target, 1.0, 0.0).astype(BF16)
        rows = jnp.dot(chosen_rows, source, preferred_element_type=F32)
        rows = rows[:, 0:LANES] + rows[:, LANES : 2 * LANES]
        for g in range(group):
            sent[m * group + g] = rows[g * span : (g + 1) * span]
        at = pl.ds(m * group, group)
        stores += start_all([(sent.at[at], sent_h.at[at])], sent_sems, m)
    wait_all(stores)


def middle(capacity, levels, arrived, wide, currents, *columns):
    devices = arrived.shape[0]
    rows = currents.shape[2]
    tall = rows + 2 * HALO
    height = 4 * capacity
    return pl.pallas_call(
        functools.partial(middle_kernel, capacity, levels),
        out_shape=(
            pltpu.HBM((devices, height, LANES), F32),
            pltpu.HBM((4, tall, LANES), F32),
            pltpu.HBM((2, tall, LANES), F32),
            pltpu.HBM((4, tall, LANES), F32),
        ),
        in_specs=[vmem()] + [hbm()] * 2 + [pl.BlockSpec(memory_space=pl.ANY)] * 4,
        out_specs=(hbm(),) * 4,
        scratch_shapes=[
            pltpu.VMEM((4 * rows, 4 * capacity * devices), BF16),
            pltpu.VMEM((4 * capacity * devices, 2 * LANES), BF16),
            pltpu.VMEM((LANES, LANES), F32),
            pltpu.VMEM((5, tall, LANES), F32),
            pltpu.VMEM((2, rows, LANES), F32),
        ]
        + [pltpu.VMEM((2, tall, LANES), F32)] * 4
        + [
            pltpu.VMEM((4, tall, LANES), F32),
            pltpu.VMEM((8, tall, LANES), F32),
            pltpu.VMEM((devices, height, LANES), F32),
            pltpu.VMEM((4, tall, LANES), F32),
            pltpu.VMEM((2, tall, LANES), F32),
            pltpu.SemaphoreType.DMA((13,)),
            pltpu.SemaphoreType.DMA((4 * capacity * devices // LANES,)),
        ],
        compiler_params=pltpu.CompilerParams(vmem_limit_bytes=24 << 20),
        cost_estimate=pl.CostEstimate(flops=200 << 20, bytes_accessed=4 << 20, transcendentals=0),
    )(arrived, *pin(wide, currents), *columns)


def finish_kernel(
    levels, wide_h, currents_h, faces_h, forcing_h, near_h, ocean, wide, currents, faces, forcing, near, sems
):
    rows_all = currents.shape[2]
    wait_all(
        start_all(
            [(wide_h, wide), (currents_h, currents), (faces_h, faces), (forcing_h, forcing), (near_h, near)], sems
        )
    )
    inner = slice(HALO, HALO + rows_all)

    def level(l, carry):
        unit = wide[2 * levels + l]
        masked = unit * wide[3 * levels + 1]
        for f in range(2):
            value = wide[f * levels + l] + masked * forcing[f]
            shift = LANES - 1 - 2 * (levels * f + l)
            value = one_pass(value, faces, near[0], shift)
            value = one_pass(value, faces, near[1], shift)
            ocean[f, l] = value[inner]
            ocean[2 + f, l] = currents[f, l] + unit[inner] * forcing[2 + f][inner]
        return carry

    lax.fori_loop(0, levels, level, 0)


def finish(levels, wide, currents, faces, forcing, near):
    rows = currents.shape[2]
    return pl.pallas_call(
        functools.partial(finish_kernel, levels),
        out_shape=jax.ShapeDtypeStruct((4, levels, rows, LANES), F32),
        in_specs=[hbm()] * 5,
        out_specs=vmem(),
        scratch_shapes=[pltpu.VMEM(a.shape, F32) for a in (wide, currents, faces, forcing, near)]
        + [pltpu.SemaphoreType.DMA((5,))],
        compiler_params=pltpu.CompilerParams(vmem_limit_bytes=24 << 20),
        cost_estimate=pl.CostEstimate(flops=40 << 20, bytes_accessed=6 << 20, transcendentals=0),
    )(*pin(wide, currents, faces, forcing, near))


def remap_back_kernel(
    capacity, tile_rows, block_h, tile_h, owner_h, row_h, returned, wet_h, weights_h, out,
    block_s, tile_s, owner_s, row_s, fill, wet, weights, picked, total, sems, weight_sems,
):
    npairs = block_s.shape[0]
    nblocks = total.shape[0]
    devices = fill.shape[0]
    height = 4 * capacity
    scalars = start_all(
        [(owner_h, owner_s), (row_h, row_s), (block_h, block_s), (tile_h, tile_s), (wet_h, wet)], sems
    )
    part_tiles = weights.shape[0] // PARTS
    parts = [pl.ds(n * part_tiles, part_tiles) for n in range(PARTS)]
    loads = start_all([(weights_h.at[at], weights.at[at]) for at in parts], weight_sems)
    total[...] = jnp.zeros_like(total)

    def clear_fill(i, carry):
        fill[i] = 0
        return carry

    lax.fori_loop(0, devices, clear_fill, 0, unroll=16)
    wait_all(scalars)

    def gather(p, carry):
        owner = owner_s[p]
        rank = fill[owner]
        fill[owner] = rank + 1
        rows = returned[pl.ds(owner * height + 4 * rank, 4), :]
        mask = wet[pl.ds(owner * tile_rows + row_s[p], 1), :].astype(F32)
        high, low = split(jnp.concatenate([rows, mask, jnp.zeros((3, LANES), F32)], 0))
        picked[p] = jnp.concatenate([high, low], 0)
        return carry

    lax.fori_loop(0, npairs, gather, 0, unroll=32)
    wait_all(loads)

    def pair(p, carry):
        value = lax.dot_general(
            picked[p], weights[tile_s[p]], (((1,), (1,)), ((), ())), preferred_element_type=F32
        )
        b = block_s[p]
        total[b] = total[b] + (value[0:8] + value[8:16])
        return carry

    lax.fori_loop(0, npairs, pair, 0, unroll=64)
    for b in range(nblocks):
        sums = total[b]
        out[:, b * LANES : (b + 1) * LANES] = sums[0:4] / jnp.maximum(sums[4:5], 0.1)


def remap_back(capacity, devices, tile_rows, pair_block, pair_tile, owner, pair_row, returned, wet, remap_weight, nblocks):
    npairs = pair_block.shape[0]
    return pl.pallas_call(
        functools.partial(remap_back_kernel, capacity, tile_rows),
        out_shape=jax.ShapeDtypeStruct((4, nblocks * LANES), F32),
        in_specs=[hbm()] * 4 + [vmem(), hbm(), hbm()],
        out_specs=vmem(),
        scratch_shapes=[pltpu.SMEM((npairs,), I32)] * 4
        + [
            pltpu.SMEM((devices,), I32),
            pltpu.VMEM(wet.shape, I32),
            pltpu.VMEM(remap_weight.shape, BF16),
            pltpu.VMEM((npairs, 16, LANES), BF16),
            pltpu.VMEM((nblocks, 8, LANES), F32),
            pltpu.SemaphoreType.DMA((5,)),
            pltpu.SemaphoreType.DMA((PARTS,)),
        ],
        compiler_params=pltpu.CompilerParams(vmem_limit_bytes=24 << 20),
        cost_estimate=pl.CostEstimate(flops=2 * npairs * 16 * LANES * LANES, bytes_accessed=6 << 20, transcendentals=0),
    )(*pin(pair_block, pair_tile, owner, pair_row), returned, *pin(wet, remap_weight))


def local(
    atm_state,
    pair_block,
    pair_owner,
    pair_row,
    pair_tile,
    remap_weight,
    wet_mask,
    ocean_state,
    vert_kappa,
    horiz_kappa,
):
    grid_x = lax.axis_size("gx")
    grid_y = lax.axis_size("gy")
    devices = grid_x * grid_y
    npairs = pair_block.shape[0]
    capacity = max(2, 2 * npairs // devices)
    levels, tile_rows, _ = vert_kappa.shape
    nblocks = atm_state.shape[1] // LANES
    owner = pair_owner.reshape(npairs)
    message = 4 * capacity + EDGE
    wet_all = lax.all_gather(wet_mask, "gy", axis=0, tiled=True)
    wet_all = lax.all_gather(wet_all, "gx", axis=0, tiled=True)
    outgoing = remap_out(
        capacity, grid_y, devices, tile_rows, atm_state, pair_block, owner, pair_row, pair_tile, remap_weight
    )
    arrived = lax.all_to_all(
        outgoing.reshape(devices, message, LANES), ("gx", "gy"), split_axis=0, concat_axis=0, tiled=True
    )
    tracer, currents, edge_up, edge_down = solve(ocean_state, vert_kappa, horiz_kappa, wet_mask)
    rise_x = [(i, i + 1) for i in range(grid_x - 1)]
    fall_x = [(b, a) for a, b in rise_x]
    rise_y = [(i, i + 1) for i in range(grid_y - 1)]
    fall_y = [(b, a) for a, b in rise_y]
    above = lax.ppermute(edge_down, "gx", rise_x)
    below = lax.ppermute(edge_up, "gx", fall_x)
    wide, to_left, to_right = pack(levels, tracer, above, below)
    from_left = lax.ppermute(to_right, "gy", rise_y)
    from_right = lax.ppermute(to_left, "gy", fall_y)
    sent, forcing, near, faces = middle(
        capacity, levels, arrived, wide, currents, to_left, to_right, from_left, from_right
    )
    returned = lax.all_to_all(sent, ("gx", "gy"), split_axis=0, concat_axis=0, tiled=True)
    ocean_next = finish(levels, wide, currents, faces, forcing, near)
    atm_surface = remap_back(
        capacity, devices, tile_rows, pair_block, pair_tile, owner, pair_row,
        returned.reshape(-1, LANES), wet_all, remap_weight, nblocks,
    )
    return (ocean_next, atm_surface)


def solution(mesh):
    placed = (
        P(None, ("gx", "gy")),
        P(("gx", "gy")),
        P(("gx", "gy"), None),
        P(("gx", "gy")),
        P(("gx", "gy")),
        P(("gx", "gy"), None, None),
        P("gx", "gy"),
        P(None, None, "gx", "gy"),
        P(None, "gx", "gy"),
        P("gx", "gy"),
    )
    return jax.shard_map(
        local,
        mesh=mesh,
        in_specs=placed,
        out_specs=(P(None, None, "gx", "gy"), P(None, ("gx", "gy"))),
        check_vma=False,
    )
```

```python
import functools

import jax
import jax.numpy as jnp
from jax import lax
from jax.experimental import pallas as pl
from jax.experimental.pallas import tpu as pltpu
from jax.sharding import PartitionSpec as P

F32 = jnp.float32
BF16 = jnp.bfloat16
I32 = jnp.int32
VMEM = pltpu.VMEM
SMEM = pltpu.SMEM
LANES = 128
EDGE = 16
HALO = 8
NUMBERS = 72
CORNERS = 112
PARTS = 8


def hbm():
    return pl.BlockSpec(memory_space=pltpu.HBM)


def vmem():
    return pl.BlockSpec(memory_space=VMEM)


def pin(*arrays):
    return [pltpu.with_memory_space_constraint(a, pltpu.HBM) for a in arrays]


def start_all(pairs, sems, first=0):
    copies = [pltpu.make_async_copy(src, dst, sems.at[first + n]) for n, (src, dst) in enumerate(pairs)]
    for copy in copies:
        copy.start()
    return copies


def wait_all(copies):
    for copy in copies:
        copy.wait()


def iota(shape, dim):
    return lax.broadcasted_iota(I32, shape, dim)


def pick(mask, value):
    return jnp.where(mask, value, 0.0)


def split(value):
    high = value.astype(BF16)
    return high, (value - high.astype(F32)).astype(BF16)


def back_rows(capacity):
    return 4 * capacity + max(8, capacity)


def remap_out_kernel(
    capacity, grid_y, tile_rows, block_h, owner_h, row_h, tile_h, atm_h, weights_h, out_h,
    out, block_s, owner_s, row_s, tile_s, atm, weights, flux, fill, row_slots, col_slots, rows_acc, cols_acc, sems, weight_sems, out_sems,
):
    devices = fill.shape[0]
    npairs = block_s.shape[0]
    tiles = weights.shape[0]
    nblocks = flux.shape[0]
    message = 4 * capacity + EDGE
    copies = [
        pltpu.make_async_copy(src, dst, sems.at[n])
        for n, (src, dst) in enumerate(
            [(atm_h, atm), (block_h, block_s), (owner_h, owner_s), (row_h, row_s), (tile_h, tile_s)]
        )
    ]
    for copy in copies:
        copy.start()
    part_tiles = tiles // PARTS
    parts = [pl.ds(n * part_tiles, part_tiles) for n in range(PARTS)]
    loads = [pltpu.make_async_copy(weights_h.at[at], weights.at[at], weight_sems.at[n]) for n, at in enumerate(parts)]
    for load in loads:
        load.start()
    out[...] = jnp.zeros_like(out)
    row_slots[...] = jnp.zeros_like(row_slots)
    col_slots[...] = jnp.zeros_like(col_slots)

    def clear_fill(i, carry):
        fill[i] = 0
        return carry

    lax.fori_loop(0, devices, clear_fill, 0, unroll=16)
    copies[0].wait()
    wind_u = atm[0:1, :]
    wind_v = atm[1:2, :]
    speed = jnp.sqrt(wind_u * wind_u + wind_v * wind_v + 0.25)
    heat = 0.5 * speed * (atm[2:3, :] - atm[5:6, :])
    water = atm[4:5, :] - 0.3 * speed * atm[3:4, :]
    planes = jnp.concatenate(
        [heat, water, 0.2 * speed * wind_u, 0.2 * speed * wind_v, jnp.zeros((4, wind_u.shape[1]), F32)]
        + [heat] * 4
        + [water] * 4,
        0,
    ).astype(BF16)
    for b in range(nblocks):
        flux[b] = planes[:, b * LANES : (b + 1) * LANES]
    wait_all(loads)
    for copy in copies[1:]:
        copy.wait()

    sub = iota((8, LANES), 0)
    lane = iota((8, LANES), 1)
    part = sub % 4
    edge_row = jnp.where(part == 0, 0, jnp.where(part == 1, 1, tile_rows - 4 + part))
    band = ((lane - part) >> 2) * 4 + part
    id_rank = jnp.where(sub == 0, lane - NUMBERS, -1)

    def pair(p, carry):
        owner = owner_s[p]
        row = row_s[p]
        rank = fill[owner]
        fill[owner] = rank + 1
        value = jnp.dot(flux[block_s[p]], weights[tile_s[p]], preferred_element_type=F32)
        out[pl.ds(owner * message + 4 * rank, 4), :] = value[0:4]
        tracer = value[8:16]
        slot = owner * capacity + rank
        row_slots[slot] = pick(edge_row == row, tracer)
        number = (row + 1).astype(F32)
        col_slots[slot] = pick(band == row, pltpu.roll(tracer, row + 2, 1)) + pick(id_rank == rank, number)
        return carry

    lax.fori_loop(0, npairs, pair, 0, unroll=32)

    def owner_step(d, carry):
        rows = row_slots[d * capacity]
        cols = col_slots[d * capacity]
        for r in range(1, capacity):
            rows = rows + row_slots[d * capacity + r]
            cols = cols + col_slots[d * capacity + r]
        rows_acc[d] = rows
        cols_acc[d] = cols
        return carry

    lax.fori_loop(0, devices, owner_step, 0, unroll=8)

    grid_x = devices // grid_y
    zero = jnp.zeros((8, LANES), F32)

    def columns_of(i, j):
        if not (0 <= i < grid_x and 0 <= j < grid_y):
            return zero
        return cols_acc[i * grid_y + j]

    from_left = (lane - sub) % 4 < 2
    in_band = lane < tile_rows + 4
    in_ids = (sub == 0) & (lane >= NUMBERS) & (lane < NUMBERS + capacity)
    last, first = part == 3, part == 0
    send = devices // 4
    stores = []
    for d in range(devices):
        i, j = d // grid_y, d % grid_y
        below = rows_acc[d + grid_y] if i < grid_x - 1 else zero
        above = rows_acc[d - grid_y] if i > 0 else zero
        base = d * message + 4 * capacity
        out[base : base + 8, :] = jnp.where(part < 2, below, above)
        tile = pick(in_band, jnp.where(from_left, columns_of(i, j - 1), columns_of(i, j + 1)))
        upper = pick(last & (lane == tile_rows), columns_of(i - 1, j - 1))
        upper = upper + pick(last & (lane == tile_rows + 1), columns_of(i - 1, j + 1))
        lower = pick(first & (lane == 1), columns_of(i + 1, j - 1))
        lower = lower + pick(first & (lane == 2), columns_of(i + 1, j + 1))
        tile = tile + pltpu.roll(upper, CORNERS - tile_rows, 1) + pltpu.roll(lower, CORNERS + 1, 1)
        tile = tile + pick(in_ids, cols_acc[d])
        out[base + 8 : base + 16, :] = tile
        if d % send == send - 1:
            n = d // send
            at = pl.ds(n * send * message, send * message)
            stores.append(pltpu.make_async_copy(out.at[at], out_h.at[at], out_sems.at[n]))
            stores[-1].start()
    for store in stores:
        store.wait()


def remap_out(capacity, grid_y, devices, tile_rows, atm_state, pair_block, owner, pair_row, pair_tile, remap_weight):
    npairs = pair_block.shape[0]
    nblocks = atm_state.shape[1] // LANES
    message = 4 * capacity + EDGE
    return pl.pallas_call(
        functools.partial(remap_out_kernel, capacity, grid_y, tile_rows),
        out_shape=pltpu.HBM((devices * message, LANES), F32),
        in_specs=[hbm()] * 6,
        out_specs=hbm(),
        scratch_shapes=[pltpu.VMEM((devices * message, LANES), F32)]
        + [pltpu.SMEM((npairs,), I32)] * 4
        + [
            pltpu.VMEM(atm_state.shape, F32),
            pltpu.VMEM(remap_weight.shape, BF16),
            pltpu.VMEM((nblocks, 16, LANES), BF16),
            pltpu.SMEM((devices,), I32),
            pltpu.VMEM((devices * capacity, 8, LANES), F32),
            pltpu.VMEM((devices * capacity, 8, LANES), F32),
            pltpu.VMEM((devices, 8, LANES), F32),
            pltpu.VMEM((devices, 8, LANES), F32),
            pltpu.SemaphoreType.DMA((5,)),
            pltpu.SemaphoreType.DMA((PARTS,)),
            pltpu.SemaphoreType.DMA((4,)),
        ],
        compiler_params=pltpu.CompilerParams(vmem_limit_bytes=40 << 20),
        cost_estimate=pl.CostEstimate(
            flops=2 * npairs * 16 * LANES * LANES, bytes_accessed=6 << 20, transcendentals=0
        ),
    )(*pin(pair_block, owner, pair_row, pair_tile, atm_state, remap_weight))


def solve_kernel(state, kappa, horiz, wet, tracer, currents_h, edge_up, edge_down, currents, sems):
    levels = kappa.shape[0]
    rows_all = kappa.shape[1]
    planes = tracer.shape[0]

    def chunk(c, carry):
        rows = pl.ds(pl.multiple_of(c * 8, 8), 8)
        column = [kappa[l, rows, :] for l in range(levels)]
        face = [0.5 * (column[l] + column[l + 1]) for l in range(levels - 1)]
        upper = []
        now = None
        for l in range(levels):
            diagonal = 1.0
            if l > 0:
                diagonal = diagonal + face[l - 1]
            if l < levels - 1:
                diagonal = diagonal + face[l]
            if l > 0:
                diagonal = diagonal + face[l - 1] * upper[-1]
            inverse = 1.0 / diagonal
            if l == 0:
                now = [state[f, 0, rows, :] * inverse for f in range(4)] + [inverse]
            else:
                pull = face[l - 1] * inverse
                now = [state[f, l, rows, :] * inverse + pull * now[f] for f in range(4)] + [pull * now[4]]
            upper.append(-face[l] * inverse if l < levels - 1 else None)
            store(l, rows, now)
        for l in range(levels - 2, -1, -1):
            here = load(l, rows)
            now = [here[f] - upper[l] * now[f] for f in range(5)]
            store(l, rows, now)
        return carry

    def store(l, rows, now):
        tracer[l, rows, :] = now[0]
        tracer[levels + l, rows, :] = now[1]
        currents[0, l, rows, :] = now[2]
        currents[1, l, rows, :] = now[3]
        tracer[2 * levels + l, rows, :] = now[4]

    def load(l, rows):
        return [
            tracer[l, rows, :],
            tracer[levels + l, rows, :],
            currents[0, l, rows, :],
            currents[1, l, rows, :],
            tracer[2 * levels + l, rows, :],
        ]

    lax.fori_loop(0, rows_all // 8, chunk, 0)
    out = start_all([(currents, currents_h)], sems)
    tracer[3 * levels] = horiz[...]
    tracer[3 * levels + 1] = wet[...].astype(F32)
    for k in range(planes):
        edge_up[k] = tracer[k, 0:8, :]
        edge_down[k] = tracer[k, rows_all - 8 : rows_all, :]
    wait_all(out)


def solve(ocean_state, vert_kappa, horiz_kappa, wet_mask):
    levels, rows, _ = vert_kappa.shape
    planes = 3 * levels + 2
    return pl.pallas_call(
        solve_kernel,
        out_shape=(
            jax.ShapeDtypeStruct((planes, rows, LANES), F32),
            pltpu.HBM((2, levels, rows, LANES), F32),
            jax.ShapeDtypeStruct((planes, 8, LANES), F32),
            jax.ShapeDtypeStruct((planes, 8, LANES), F32),
        ),
        in_specs=[vmem()] * 4,
        out_specs=(vmem(), hbm(), vmem(), vmem()),
        scratch_shapes=[pltpu.VMEM((2, levels, rows, LANES), F32), pltpu.SemaphoreType.DMA((1,))],
        compiler_params=pltpu.CompilerParams(vmem_limit_bytes=24 << 20),
        cost_estimate=pl.CostEstimate(flops=20 << 20, bytes_accessed=6 << 20, transcendentals=0),
    )(ocean_state, vert_kappa, horiz_kappa, wet_mask)


def pack_kernel(levels, tracer, above, below, wide_h, to_left, to_right, wide, sems):
    planes, rows, _ = tracer.shape
    for k in range(planes):
        wide[k, 0:HALO, :] = above[k]
        wide[k, HALO : HALO + rows, :] = tracer[k]
        wide[k, HALO + rows : 2 * HALO + rows, :] = below[k]
    out = start_all([(wide, wide_h)], sems)
    lane = iota((8, LANES), 1)

    def chunk(c, carry):
        at = pl.ds(pl.multiple_of(c * 8, 8), 8)

        def place(values, lanes):
            left, right = jnp.zeros((8, LANES), F32), jnp.zeros((8, LANES), F32)
            for k, (near, far) in zip(values, lanes):
                value = wide[k, at, :]
                left = jnp.where(lane == near, pltpu.roll(value, near, 1), left)
                left = jnp.where(lane == far, pltpu.roll(value, far - 1, 1), left)
                right = jnp.where(lane == near + 1, pltpu.roll(value, (near + 2) % LANES, 1), right)
                right = jnp.where(lane == far + 1, pltpu.roll(value, (far + 3) % LANES, 1), right)
            return left, right

        left, right = place(range(2 * levels), [(2 * k, 64 + 2 * k) for k in range(2 * levels)])
        to_left[0, at, :] = left
        to_right[0, at, :] = right
        lanes = [(2 * l, 64 + 2 * l) for l in range(levels)]
        lanes += [(2 * levels, 2 * levels + 2), (2 * levels + 4, 2 * levels + 6)]
        left, right = place(range(2 * levels, 3 * levels + 2), lanes)
        to_left[1, at, :] = left
        to_right[1, at, :] = right
        return carry

    lax.fori_loop(0, (rows + 2 * HALO) // 8, chunk, 0)
    wait_all(out)


def pack(levels, tracer, above, below):
    planes, rows, _ = tracer.shape
    tall = rows + 2 * HALO
    return pl.pallas_call(
        functools.partial(pack_kernel, levels),
        out_shape=(
            pltpu.HBM((planes, tall, LANES), F32),
            jax.ShapeDtypeStruct((2, tall, LANES), F32),
            jax.ShapeDtypeStruct((2, tall, LANES), F32),
        ),
        in_specs=[vmem()] * 3,
        out_specs=(hbm(), vmem(), vmem()),
        scratch_shapes=[pltpu.VMEM((planes, tall, LANES), F32), pltpu.SemaphoreType.DMA((1,))],
        compiler_params=pltpu.CompilerParams(vmem_limit_bytes=24 << 20),
        cost_estimate=pl.CostEstimate(flops=8 << 20, bytes_accessed=4 << 20, transcendentals=0),
    )(tracer, above, below)


def set_faces(levels, h, w, own_left, own_right, from_left, from_right, faces, packed):
    tall = h.shape[0]
    lane = iota((tall, LANES), 1)
    odd = lane % 2 == 1
    twice = lane % 64 < 2 * levels
    left, left_unit, right, right_unit = from_left[0], from_left[1], from_right[0], from_right[1]
    other = jnp.where(odd, left_unit, right_unit)
    at = 2 * levels

    def column(offset):
        return other[:, at + offset : at + offset + 1], other[:, at + offset + 1 : at + offset + 2]

    kappa_right, kappa_left = column(0)
    kappa_far_right, kappa_far_left = column(2)
    wet_right, wet_left = column(4)
    wet_far_right, wet_far_left = column(6)

    kappa_near = jnp.where(odd, kappa_left, kappa_right)
    kappa_far = jnp.where(odd, kappa_far_left, kappa_far_right)
    wet_near = jnp.where(odd, wet_left, wet_right)
    wet_far = jnp.where(odd, wet_far_left, wet_far_right)
    kappa_own = jnp.where(odd, h[:, 0:1], h[:, LANES - 1 : LANES])
    wet_own = jnp.where(odd, w[:, 0:1], w[:, LANES - 1 : LANES])

    def face(kappa_a, wet_a, kappa_b, wet_b):
        return 0.25 * (kappa_a + kappa_b) * wet_a * wet_b

    unit = jnp.where(twice, other, pltpu.roll(other, 2 * levels, 1))
    packed[0] = jnp.where(odd, left, right)
    packed[1] = unit * jnp.where(lane < 64, wet_near, wet_far)
    left, left_unit, right, right_unit = own_left[0], own_left[1], own_right[0], own_right[1]
    packed[2] = jnp.where(odd, pltpu.roll(left, 1, 1), pltpu.roll(right, LANES - 1, 1))
    own = jnp.where(odd, pltpu.roll(left_unit, 1, 1), pltpu.roll(right_unit, LANES - 1, 1))
    packed[3] = jnp.where(twice, own, pltpu.roll(own, 2 * levels, 1)) * wet_own
    north = face(kappa_near, wet_near, pltpu.roll(kappa_near, 1, 0), pltpu.roll(wet_near, 1, 0))
    packed[4] = north
    packed[5] = pltpu.roll(north, tall - 1, 0)
    packed[6] = face(kappa_near, wet_near, kappa_far, wet_far)
    packed[7] = face(kappa_near, wet_near, kappa_own, wet_own)

    north = face(h, w, pltpu.roll(h, 1, 0), pltpu.roll(w, 1, 0))
    faces[0] = north
    faces[1] = pltpu.roll(north, tall - 1, 0)
    west = face(
        h, w, jnp.where(lane == 0, kappa_left, pltpu.roll(h, 1, 1)), jnp.where(lane == 0, wet_left, pltpu.roll(w, 1, 1))
    )
    faces[2] = west
    faces[3] = jnp.where(lane == LANES - 1, face(h, w, kappa_right, wet_right), pltpu.roll(west, LANES - 1, 1))


def set_beside(levels, upright, wide, packed, beside):
    tall = upright.shape[0]
    lane = iota((tall, LANES), 1)
    odd = lane % 2 == 1
    heat = lane % 64 < 2 * levels

    def chosen(f):
        left_far, left_near, right_near, right_far = [upright[:, 4 * f + e : 4 * f + e + 1] for e in range(4)]
        near = jnp.where(odd, left_near, right_near)
        return jnp.where(lane < 64, near, jnp.where(odd, left_far, right_far))

    both = packed[0] + packed[1] * jnp.where(heat, chosen(0), chosen(1))
    far = pltpu.roll(both, 64, 1)
    ends_of = [jnp.where(odd, w[:, 0:1], w[:, LANES - 1 : LANES]) for w in wide]
    own = packed[2] + packed[3] * jnp.where(heat, ends_of[0], ends_of[1])
    near = both + packed[5] * (pltpu.roll(both, tall - 1, 0) - both)
    near = near + packed[4] * (pltpu.roll(both, 1, 0) - both)
    near = near + packed[6] * (far - both)
    near = near + packed[7] * (own - both)
    beside[0] = both
    beside[1] = near


def one_pass(value, faces, beside, shift):
    tall = value.shape[0]
    lane = iota(value.shape, 1)
    moved = pltpu.roll(beside, shift, 1)
    west = jnp.where(lane == 0, moved, pltpu.roll(value, 1, 1))
    east = jnp.where(lane == LANES - 1, moved, pltpu.roll(value, LANES - 1, 1))
    result = value + faces[1] * (pltpu.roll(value, tall - 1, 0) - value)
    result = result + faces[0] * (pltpu.roll(value, 1, 0) - value)
    result = result + faces[3] * (east - value)
    return result + faces[2] * (west - value)


def middle_kernel(
    capacity, levels, arrived, wide_h, currents_h, own_left_h, own_right_h, from_left_h, from_right_h,
    sent_h, forcing_h, near_h, faces_h,
    placing, values, number_t, top, currents, own_left, own_right, from_left, from_right,
    faces, packed, sent, forcing, near_o, sems, sent_sems,
):
    devices, message, _ = arrived.shape
    rows_all = currents.shape[1]
    tall = rows_all + 2 * HALO
    loads = start_all(
        [(wide_h.at[levels * k], top.at[k]) for k in range(3)]
        + [
            (wide_h.at[pl.ds(3 * levels, 2)], top.at[pl.ds(3, 2)]),
            (currents_h.at[0, 0], currents.at[0]),
            (currents_h.at[1, 0], currents.at[1]),
            (own_left_h, own_left),
            (own_right_h, own_right),
            (from_left_h, from_left),
            (from_right_h, from_right),
        ],
        sems,
    )
    span = 4 * capacity
    group = LANES // span
    groups = devices // group
    sub8 = iota((8, LANES), 0)
    lane8 = iota((8, LANES), 1)

    lane1 = iota((1, LANES), 1)
    spread = (iota((LANES, LANES), 0) - NUMBERS) == iota((LANES, LANES), 1) % span // 4
    every = jnp.concatenate([arrived[s, span + 8 : span + 9, :] for s in range(devices)], 0).astype(BF16)
    every = jnp.dot(every, jnp.where(spread, 1.0, 0.0).astype(BF16), preferred_element_type=F32)
    numbers = []
    for m in range(groups):
        line = jnp.zeros((1, LANES), F32)
        for g in range(group):
            s = m * group + g
            line = jnp.where(lane1 // span == g, every[s : s + 1], line)
        numbers.append(line)
    number_t[...] = jnp.transpose(
        jnp.concatenate(numbers + [jnp.zeros((LANES - groups, LANES), F32)], 0)
    )

    row_number = iota((rows_all, LANES), 0).astype(F32) + 1.0
    lane_field = iota((rows_all, LANES), 1) % 4
    for m in range(groups):
        hit = numbers[m] == row_number
        for f in range(4):
            placing[f * rows_all : (f + 1) * rows_all, m * LANES : (m + 1) * LANES] = jnp.where(
                hit & (lane_field == f), 1.0, 0.0
            ).astype(BF16)
    edge_rows = jnp.zeros((8, LANES), F32)
    edge_cols = jnp.zeros((8, LANES), F32)
    for s in range(devices):
        high, low = split(arrived[s, 0:span, :])
        values[s * span : (s + 1) * span, 0:LANES] = high
        values[s * span : (s + 1) * span, LANES : 2 * LANES] = low
        edge_rows = edge_rows + arrived[s, span : span + 8, :]
        edge_cols = edge_cols + arrived[s, span + 8 : span + 16, :]
    total = jnp.dot(placing[...], values[...], preferred_element_type=F32)
    total = total[:, 0:LANES] + total[:, LANES : 2 * LANES]

    wait_all(loads)
    set_faces(levels, top[3], top[4], own_left, own_right, from_left, from_right, faces, packed)
    wet_wide = top[4]

    def plane(f):
        return total[f * rows_all : (f + 1) * rows_all]

    wide = []
    for f in range(2):
        before = pick(sub8 >= 6, edge_rows if f == 1 else pltpu.roll(edge_rows, 4, 0))
        after = pick(sub8 < 2, edge_rows if f == 0 else pltpu.roll(edge_rows, 4, 0))
        wide.append(jnp.concatenate([before, plane(f), after], 0))
        forcing[f] = wide[f]
    wet = wet_wide[HALO : HALO + rows_all]
    for f in range(2, 4):
        forcing[f, 0:HALO, :] = jnp.zeros((HALO, LANES), F32)
        forcing[f, HALO : HALO + rows_all, :] = plane(f) * wet
        forcing[f, HALO + rows_all : tall, :] = jnp.zeros((HALO, LANES), F32)

    part8 = sub8 % 4
    within = (part8 == lane8 % 4) & (lane8 >= HALO) & (lane8 < HALO + rows_all)
    upper = (part8 == 3) & (lane8 == HALO - 1)
    lower = (part8 == 0) & (lane8 == HALO + rows_all)
    halves = [[], []]
    for k in range(4):
        column = pick(within, pltpu.roll(edge_cols, HALO - k, 1))
        if k in (1, 2):
            column = column + pick(upper, pltpu.roll(edge_cols, (HALO - CORNERS - k) % LANES, 1))
            column = column + pick(lower, pltpu.roll(edge_cols, (HALO + rows_all - CORNERS - 1 - k) % LANES, 1))
        for f in range(2):
            halves[f].append(jnp.sum(column[4 * f : 4 * f + 4], axis=0, keepdims=True))
    columns = jnp.concatenate(halves[0] + halves[1], 0)
    upright = jnp.transpose(jnp.concatenate([columns, jnp.zeros((LANES - 8, LANES), F32)], 0))[0:tall]
    set_beside(levels, upright, wide, packed, near_o)
    stores = start_all([(forcing, forcing_h), (near_o, near_h), (faces, faces_h)], sems, 10)

    surface = []
    unit = top[2] * wet_wide
    for f in range(2):
        value = top[f] + unit * wide[f]
        shift = LANES - (2 * levels * f + 1)
        value = one_pass(value, faces, near_o[0], shift)
        value = one_pass(value, faces, near_o[1], shift)
        surface.append(value[HALO : HALO + rows_all] * wet)
    for f in range(2):
        surface.append(
            (currents[f] + top[2, HALO : HALO + rows_all, :] * forcing[2 + f, HALO : HALO + rows_all, :]) * wet
        )
    high, low = split(jnp.concatenate(surface, 0))
    source = jnp.concatenate([high, low], 1)
    lane_t = iota((LANES, 4 * rows_all), 1)
    sub_t = iota((LANES, 4 * rows_all), 0)
    target = jnp.where(sub_t % 4 == lane_t // rows_all, lane_t % rows_all + 1, -1).astype(F32)
    mask = jnp.concatenate([wet, jnp.zeros((LANES - rows_all, LANES), F32)], 0).astype(BF16)
    per = LANES // 4
    slot_number = number_t[pl.ds(0, per, stride=4), :]
    lane_s = (iota((per, LANES), 1) + 1).astype(F32)
    height = back_rows(capacity)
    for m in range(groups):
        chosen_rows = jnp.where(number_t[:, m : m + 1] == target, 1.0, 0.0).astype(BF16)
        rows = jnp.dot(chosen_rows, source, preferred_element_type=F32)
        rows = rows[:, 0:LANES] + rows[:, LANES : 2 * LANES]
        slots = jnp.where(slot_number[:, m : m + 1] == lane_s, 1.0, 0.0).astype(BF16)
        masks = jnp.dot(slots, mask, preferred_element_type=F32)
        for g in range(group):
            s = m * group + g
            sent[s, 0:span, :] = rows[g * span : (g + 1) * span]
            sent[s, span : span + capacity, :] = masks[g * capacity : (g + 1) * capacity]
            if height > span + capacity:
                sent[s, span + capacity : height, :] = jnp.zeros((height - span - capacity, LANES), F32)
        at = pl.ds(m * group, group)
        stores += start_all([(sent.at[at], sent_h.at[at])], sent_sems, m)
    wait_all(stores)


def middle(capacity, levels, arrived, wide, currents, *columns):
    devices = arrived.shape[0]
    rows = currents.shape[2]
    tall = rows + 2 * HALO
    height = back_rows(capacity)
    return pl.pallas_call(
        functools.partial(middle_kernel, capacity, levels),
        out_shape=(
            pltpu.HBM((devices, height, LANES), F32),
            pltpu.HBM((4, tall, LANES), F32),
            pltpu.HBM((2, tall, LANES), F32),
            pltpu.HBM((4, tall, LANES), F32),
        ),
        in_specs=[vmem()] + [hbm()] * 2 + [pl.BlockSpec(memory_space=pl.ANY)] * 4,
        out_specs=(hbm(),) * 4,
        scratch_shapes=[
            pltpu.VMEM((4 * rows, 4 * capacity * devices), BF16),
            pltpu.VMEM((4 * capacity * devices, 2 * LANES), BF16),
            pltpu.VMEM((LANES, LANES), F32),
            pltpu.VMEM((5, tall, LANES), F32),
            pltpu.VMEM((2, rows, LANES), F32),
        ]
        + [pltpu.VMEM((2, tall, LANES), F32)] * 4
        + [
            pltpu.VMEM((4, tall, LANES), F32),
            pltpu.VMEM((8, tall, LANES), F32),
            pltpu.VMEM((devices, height, LANES), F32),
            pltpu.VMEM((4, tall, LANES), F32),
            pltpu.VMEM((2, tall, LANES), F32),
            pltpu.SemaphoreType.DMA((13,)),
            pltpu.SemaphoreType.DMA((4 * capacity * devices // LANES,)),
        ],
        compiler_params=pltpu.CompilerParams(vmem_limit_bytes=24 << 20),
        cost_estimate=pl.CostEstimate(flops=200 << 20, bytes_accessed=4 << 20, transcendentals=0),
    )(arrived, *pin(wide, currents), *columns)


def finish_kernel(
    levels, wide_h, currents_h, faces_h, forcing_h, near_h, ocean, wide, currents, faces, forcing, near, sems
):
    rows_all = currents.shape[2]
    wait_all(
        start_all(
            [(wide_h, wide), (currents_h, currents), (faces_h, faces), (forcing_h, forcing), (near_h, near)], sems
        )
    )
    inner = slice(HALO, HALO + rows_all)

    def level(l, carry):
        unit = wide[2 * levels + l]
        masked = unit * wide[3 * levels + 1]
        for f in range(2):
            value = wide[f * levels + l] + masked * forcing[f]
            shift = LANES - 1 - 2 * (levels * f + l)
            value = one_pass(value, faces, near[0], shift)
            value = one_pass(value, faces, near[1], shift)
            ocean[f, l] = value[inner]
            ocean[2 + f, l] = currents[f, l] + unit[inner] * forcing[2 + f][inner]
        return carry

    lax.fori_loop(0, levels, level, 0)


def finish(levels, wide, currents, faces, forcing, near):
    rows = currents.shape[2]
    return pl.pallas_call(
        functools.partial(finish_kernel, levels),
        out_shape=jax.ShapeDtypeStruct((4, levels, rows, LANES), F32),
        in_specs=[hbm()] * 5,
        out_specs=vmem(),
        scratch_shapes=[pltpu.VMEM(a.shape, F32) for a in (wide, currents, faces, forcing, near)]
        + [pltpu.SemaphoreType.DMA((5,))],
        compiler_params=pltpu.CompilerParams(vmem_limit_bytes=24 << 20),
        cost_estimate=pl.CostEstimate(flops=40 << 20, bytes_accessed=6 << 20, transcendentals=0),
    )(*pin(wide, currents, faces, forcing, near))


def turn_kernel(weights_h, turned_h, weights, turned, sems, out_sems):
    part_tiles = weights.shape[0] // PARTS
    parts = [pl.ds(n * part_tiles, part_tiles) for n in range(PARTS)]
    loads = start_all([(weights_h.at[at], weights.at[at]) for at in parts], sems)
    stores = []
    for n, at in enumerate(parts):
        loads[n].wait()

        def tile_step(t, carry):
            turned[t] = weights[t].T
            return carry

        lax.fori_loop(n * part_tiles, (n + 1) * part_tiles, tile_step, 0, unroll=4)
        stores += start_all([(turned.at[at], turned_h.at[at])], out_sems, n)
    wait_all(stores)


def turn(remap_weight):
    return pl.pallas_call(
        turn_kernel,
        out_shape=pltpu.HBM(remap_weight.shape, BF16),
        in_specs=[hbm()],
        out_specs=hbm(),
        scratch_shapes=[pltpu.VMEM(remap_weight.shape, BF16)] * 2 + [pltpu.SemaphoreType.DMA((PARTS,))] * 2,
        compiler_params=pltpu.CompilerParams(vmem_limit_bytes=24 << 20),
        cost_estimate=pl.CostEstimate(flops=8 << 20, bytes_accessed=8 << 20, transcendentals=0),
    )(*pin(remap_weight))


def remap_back_kernel(
    capacity, block_h, tile_h, owner_h, returned, weights_h, out,
    block_s, tile_s, owner_s, fill, weights, picked_a, picked_b, total, sems, weight_sems,
):
    npairs = block_s.shape[0]
    nblocks = total.shape[0]
    devices = fill.shape[0]
    height = back_rows(capacity)
    scalars = start_all([(owner_h, owner_s), (block_h, block_s), (tile_h, tile_s)], sems)
    part_tiles = weights.shape[0] // PARTS
    parts = [pl.ds(n * part_tiles, part_tiles) for n in range(PARTS)]
    loads = start_all([(weights_h.at[at], weights.at[at]) for at in parts], weight_sems)
    total[...] = jnp.zeros_like(total)

    def clear_fill(i, carry):
        fill[i] = 0
        return carry

    lax.fori_loop(0, devices, clear_fill, 0, unroll=16)
    wait_all(scalars)

    def gather(p, picked, at):
        owner = owner_s[p]
        rank = fill[owner]
        fill[owner] = rank + 1
        rows = returned[pl.ds(owner * height + 4 * rank, 4), :]
        mask = returned[pl.ds(owner * height + 4 * capacity + rank - 4, 5), :]
        high, low = split(jnp.concatenate([rows, mask[4:5], jnp.zeros((3, LANES), F32)], 0))
        picked[at] = jnp.concatenate([high, low], 0)

    def product(p, picked, at):
        value = jnp.dot(picked[at], weights[tile_s[p]], preferred_element_type=F32)
        b = block_s[p]
        total[b] = total[b] + (value[0:8] + value[8:16])

    half = npairs // 2

    def first(p, carry):
        gather(p, picked_a, p)
        return carry

    def both(p, carry):
        gather(half + p, picked_b, p)
        product(p, picked_a, p)
        return carry

    def last(p, carry):
        product(half + p, picked_b, p)
        return carry

    lax.fori_loop(0, half, first, 0, unroll=32)
    wait_all(loads)
    lax.fori_loop(0, half, both, 0, unroll=64)
    lax.fori_loop(0, half, last, 0, unroll=64)
    for b in range(nblocks):
        sums = total[b]
        out[:, b * LANES : (b + 1) * LANES] = sums[0:4] / jnp.maximum(sums[4:5], 0.1)


def remap_back(capacity, devices, pair_block, pair_tile, owner, returned, remap_weight, nblocks):
    npairs = pair_block.shape[0]
    return pl.pallas_call(
        functools.partial(remap_back_kernel, capacity),
        out_shape=jax.ShapeDtypeStruct((4, nblocks * LANES), F32),
        in_specs=[hbm()] * 3 + [vmem(), hbm()],
        out_specs=vmem(),
        scratch_shapes=[pltpu.SMEM((npairs,), I32)] * 3
        + [
            pltpu.SMEM((devices,), I32),
            pltpu.VMEM(remap_weight.shape, BF16),
            pltpu.VMEM((npairs // 2, 16, LANES), BF16),
            pltpu.VMEM((npairs // 2, 16, LANES), BF16),
            pltpu.VMEM((nblocks, 8, LANES), F32),
            pltpu.SemaphoreType.DMA((3,)),
            pltpu.SemaphoreType.DMA((PARTS,)),
        ],
        compiler_params=pltpu.CompilerParams(vmem_limit_bytes=24 << 20),
        cost_estimate=pl.CostEstimate(flops=2 * npairs * 16 * LANES * LANES, bytes_accessed=6 << 20, transcendentals=0),
    )(*pin(pair_block, pair_tile, owner), returned, *pin(remap_weight))


def local(
    atm_state,
    pair_block,
    pair_owner,
    pair_row,
    pair_tile,
    remap_weight,
    wet_mask,
    ocean_state,
    vert_kappa,
    horiz_kappa,
):
    grid_x = lax.axis_size("gx")
    grid_y = lax.axis_size("gy")
    devices = grid_x * grid_y
    npairs = pair_block.shape[0]
    capacity = max(2, 2 * npairs // devices)
    levels, tile_rows, _ = vert_kappa.shape
    nblocks = atm_state.shape[1] // LANES
    owner = pair_owner.reshape(npairs)
    message = 4 * capacity + EDGE
    outgoing = remap_out(
        capacity, grid_y, devices, tile_rows, atm_state, pair_block, owner, pair_row, pair_tile, remap_weight
    )
    arrived = lax.all_to_all(
        outgoing.reshape(devices, message, LANES), ("gx", "gy"), split_axis=0, concat_axis=0, tiled=True
    )
    tracer, currents, edge_up, edge_down = solve(ocean_state, vert_kappa, horiz_kappa, wet_mask)
    rise_x = [(i, i + 1) for i in range(grid_x - 1)]
    fall_x = [(b, a) for a, b in rise_x]
    rise_y = [(i, i + 1) for i in range(grid_y - 1)]
    fall_y = [(b, a) for a, b in rise_y]
    above = lax.ppermute(edge_down, "gx", rise_x)
    below = lax.ppermute(edge_up, "gx", fall_x)
    wide, to_left, to_right = pack(levels, tracer, above, below)
    from_left = lax.ppermute(to_right, "gy", rise_y)
    from_right = lax.ppermute(to_left, "gy", fall_y)
    sent, forcing, near, faces = middle(
        capacity, levels, arrived, wide, currents, to_left, to_right, from_left, from_right
    )
    returned = lax.all_to_all(sent, ("gx", "gy"), split_axis=0, concat_axis=0, tiled=True)
    ocean_next = finish(levels, wide, currents, faces, forcing, near)
    weights, _ = lax.optimization_barrier((remap_weight, near))
    atm_surface = remap_back(
        capacity, devices, pair_block, pair_tile, owner, returned.reshape(-1, LANES), turn(weights), nblocks
    )
    return (ocean_next, atm_surface)


def solution(mesh):
    placed = (
        P(None, ("gx", "gy")),
        P(("gx", "gy")),
        P(("gx", "gy"), None),
        P(("gx", "gy")),
        P(("gx", "gy")),
        P(("gx", "gy"), None, None),
        P("gx", "gy"),
        P(None, None, "gx", "gy"),
        P(None, "gx", "gy"),
        P("gx", "gy"),
    )
    return jax.shard_map(
        local,
        mesh=mesh,
        in_specs=placed,
        out_specs=(P(None, None, "gx", "gy"), P(None, ("gx", "gy"))),
        check_vma=False,
    )
```

```python
import functools

import jax
import jax.numpy as jnp
from jax import lax
from jax.experimental import pallas as pl
from jax.experimental.pallas import tpu as pltpu
from jax.sharding import PartitionSpec as P

F32 = jnp.float32
BF16 = jnp.bfloat16
I32 = jnp.int32
VMEM = pltpu.VMEM
SMEM = pltpu.SMEM
LANES = 128
EDGE = 16
HALO = 8
NUMBERS = 72
CORNERS = 112
SENDS = 8
PARTS = 8


def hbm():
    return pl.BlockSpec(memory_space=pltpu.HBM)


def vmem():
    return pl.BlockSpec(memory_space=VMEM)


def pin(*arrays):
    return [pltpu.with_memory_space_constraint(a, pltpu.HBM) for a in arrays]


def start_all(pairs, sems, first=0):
    copies = [pltpu.make_async_copy(src, dst, sems.at[first + n]) for n, (src, dst) in enumerate(pairs)]
    for copy in copies:
        copy.start()
    return copies


def wait_all(copies):
    for copy in copies:
        copy.wait()


def iota(shape, dim):
    return lax.broadcasted_iota(I32, shape, dim)


def pick(mask, value):
    return jnp.where(mask, value, 0.0)


def split(value):
    high = value.astype(BF16)
    return high, (value - high.astype(F32)).astype(BF16)


def back_rows(capacity):
    return 4 * capacity + max(8, capacity)


def remap_out_kernel(
    capacity, grid_y, tile_rows, block_h, owner_h, row_h, tile_h, atm_h, weights_h, out_h, field_h, wet_h,
    out, block_s, owner_s, row_s, tile_s, slot_s, rank_s, field_s, wet_s, atm, weights, flux, fill, row_slots, col_slots, rows_acc, cols_acc, sems, weight_sems, out_sems,
):
    devices = fill.shape[0]
    npairs = block_s.shape[0]
    tiles = weights.shape[0]
    nblocks = flux.shape[0]
    message = 4 * capacity + EDGE
    copies = [
        pltpu.make_async_copy(src, dst, sems.at[n])
        for n, (src, dst) in enumerate(
            [(atm_h, atm), (block_h, block_s), (owner_h, owner_s), (row_h, row_s), (tile_h, tile_s)]
        )
    ]
    for copy in copies:
        copy.start()
    part_tiles = tiles // PARTS
    parts = [pl.ds(n * part_tiles, part_tiles) for n in range(PARTS)]
    loads = [pltpu.make_async_copy(weights_h.at[at], weights.at[at], weight_sems.at[n]) for n, at in enumerate(parts)]
    for load in loads:
        load.start()
    out[...] = jnp.zeros_like(out)
    row_slots[...] = jnp.zeros_like(row_slots)
    col_slots[...] = jnp.zeros_like(col_slots)

    def clear_fill(i, carry):
        fill[i] = 0
        return carry

    lax.fori_loop(0, devices, clear_fill, 0, unroll=16)
    copies[0].wait()
    wind_u = atm[0:1, :]
    wind_v = atm[1:2, :]
    speed = jnp.sqrt(wind_u * wind_u + wind_v * wind_v + 0.25)
    heat = 0.5 * speed * (atm[2:3, :] - atm[5:6, :])
    water = atm[4:5, :] - 0.3 * speed * atm[3:4, :]
    planes = jnp.concatenate(
        [heat, water, 0.2 * speed * wind_u, 0.2 * speed * wind_v, jnp.zeros((4, wind_u.shape[1]), F32)]
        + [heat] * 4
        + [water] * 4,
        0,
    ).astype(BF16)
    for b in range(nblocks):
        flux[b] = planes[:, b * LANES : (b + 1) * LANES]
    wait_all(copies[1:])

    height = back_rows(capacity)

    def place(p, carry):
        owner = owner_s[p]
        rank = fill[owner]
        fill[owner] = rank + 1
        field_s[p] = owner * height + 4 * rank
        wet_s[p] = owner * height + 4 * capacity + rank
        slot_s[p] = owner * capacity + rank
        rank_s[p] = rank
        return carry

    lax.fori_loop(0, npairs, place, 0, unroll=32)
    stores = start_all([(field_s, field_h), (wet_s, wet_h)], out_sems, SENDS)
    wait_all(loads)

    sub = iota((8, LANES), 0)
    lane = iota((8, LANES), 1)
    part = sub % 4
    edge_row = jnp.where(part == 0, 0, jnp.where(part == 1, 1, tile_rows - 4 + part))
    band = ((lane - part) >> 2) * 4 + part
    id_rank = jnp.where(sub == 0, lane - NUMBERS, -1)

    def pair(p, carry):
        slot = slot_s[p]
        row = row_s[p]
        rank = rank_s[p]
        value = jnp.dot(flux[block_s[p]], weights[tile_s[p]], preferred_element_type=F32)
        out[pl.ds(owner_s[p] * message + 4 * rank, 4), :] = value[0:4]
        tracer = value[8:16]
        row_slots[slot] = pick(edge_row == row, tracer)
        number = (row + 1).astype(F32)
        col_slots[slot] = pick(band == row, pltpu.roll(tracer, row + 2, 1)) + pick(id_rank == rank, number)
        return carry

    lax.fori_loop(0, npairs, pair, 0, unroll=64)

    def owner_step(d, carry):
        rows = row_slots[d * capacity]
        cols = col_slots[d * capacity]
        for r in range(1, capacity):
            rows = rows + row_slots[d * capacity + r]
            cols = cols + col_slots[d * capacity + r]
        rows_acc[d] = rows
        cols_acc[d] = cols
        return carry

    lax.fori_loop(0, devices, owner_step, 0, unroll=8)

    grid_x = devices // grid_y
    zero = jnp.zeros((8, LANES), F32)

    def columns_of(i, j):
        if not (0 <= i < grid_x and 0 <= j < grid_y):
            return zero
        return cols_acc[i * grid_y + j]

    from_left = (lane - sub) % 4 < 2
    in_band = lane < tile_rows + 4
    in_ids = (sub == 0) & (lane >= NUMBERS) & (lane < NUMBERS + capacity)
    last, first = part == 3, part == 0
    send = devices // SENDS
    for d in range(devices):
        i, j = d // grid_y, d % grid_y
        below = rows_acc[d + grid_y] if i < grid_x - 1 else zero
        above = rows_acc[d - grid_y] if i > 0 else zero
        base = d * message + 4 * capacity
        out[base : base + 8, :] = jnp.where(part < 2, below, above)
        tile = pick(in_band, jnp.where(from_left, columns_of(i, j - 1), columns_of(i, j + 1)))
        upper = pick(last & (lane == tile_rows), columns_of(i - 1, j - 1))
        upper = upper + pick(last & (lane == tile_rows + 1), columns_of(i - 1, j + 1))
        lower = pick(first & (lane == 1), columns_of(i + 1, j - 1))
        lower = lower + pick(first & (lane == 2), columns_of(i + 1, j + 1))
        tile = tile + pltpu.roll(upper, CORNERS - tile_rows, 1) + pltpu.roll(lower, CORNERS + 1, 1)
        tile = tile + pick(in_ids, cols_acc[d])
        out[base + 8 : base + 16, :] = tile
        if d % send == send - 1:
            n = d // send
            at = pl.ds(n * send * message, send * message)
            stores.append(pltpu.make_async_copy(out.at[at], out_h.at[at], out_sems.at[n]))
            stores[-1].start()
    for store in stores:
        store.wait()


def remap_out(capacity, grid_y, devices, tile_rows, atm_state, pair_block, owner, pair_row, pair_tile, remap_weight):
    npairs = pair_block.shape[0]
    nblocks = atm_state.shape[1] // LANES
    message = 4 * capacity + EDGE
    return pl.pallas_call(
        functools.partial(remap_out_kernel, capacity, grid_y, tile_rows),
        out_shape=(
            pltpu.HBM((devices * message, LANES), F32),
            pltpu.HBM((npairs,), I32),
            pltpu.HBM((npairs,), I32),
        ),
        in_specs=[hbm()] * 6,
        out_specs=(hbm(),) * 3,
        scratch_shapes=[pltpu.VMEM((devices * message, LANES), F32)]
        + [pltpu.SMEM((npairs,), I32)] * 8
        + [
            pltpu.VMEM(atm_state.shape, F32),
            pltpu.VMEM(remap_weight.shape, BF16),
            pltpu.VMEM((nblocks, 16, LANES), BF16),
            pltpu.SMEM((devices,), I32),
            pltpu.VMEM((devices * capacity, 8, LANES), F32),
            pltpu.VMEM((devices * capacity, 8, LANES), F32),
            pltpu.VMEM((devices, 8, LANES), F32),
            pltpu.VMEM((devices, 8, LANES), F32),
            pltpu.SemaphoreType.DMA((5,)),
            pltpu.SemaphoreType.DMA((PARTS,)),
            pltpu.SemaphoreType.DMA((SENDS + 2,)),
        ],
        compiler_params=pltpu.CompilerParams(vmem_limit_bytes=40 << 20),
        cost_estimate=pl.CostEstimate(
            flops=2 * npairs * 16 * LANES * LANES, bytes_accessed=6 << 20, transcendentals=0
        ),
    )(*pin(pair_block, owner, pair_row, pair_tile, atm_state, remap_weight))


def solve_kernel(state, kappa, horiz, wet, tracer, currents_h, edge_up, edge_down, currents, sems):
    levels = kappa.shape[0]
    rows_all = kappa.shape[1]
    planes = tracer.shape[0]

    def chunk(c, carry):
        rows = pl.ds(pl.multiple_of(c * 8, 8), 8)
        column = [kappa[l, rows, :] for l in range(levels)]
        face = [0.5 * (column[l] + column[l + 1]) for l in range(levels - 1)]
        upper = []
        now = None
        for l in range(levels):
            diagonal = 1.0
            if l > 0:
                diagonal = diagonal + face[l - 1]
            if l < levels - 1:
                diagonal = diagonal + face[l]
            if l > 0:
                diagonal = diagonal + face[l - 1] * upper[-1]
            inverse = 1.0 / diagonal
            if l == 0:
                now = [state[f, 0, rows, :] * inverse for f in range(4)] + [inverse]
            else:
                pull = face[l - 1] * inverse
                now = [state[f, l, rows, :] * inverse + pull * now[f] for f in range(4)] + [pull * now[4]]
            upper.append(-face[l] * inverse if l < levels - 1 else None)
            store(l, rows, now)
        for l in range(levels - 2, -1, -1):
            here = load(l, rows)
            now = [here[f] - upper[l] * now[f] for f in range(5)]
            store(l, rows, now)
        return carry

    def store(l, rows, now):
        tracer[l, rows, :] = now[0]
        tracer[levels + l, rows, :] = now[1]
        currents[0, l, rows, :] = now[2]
        currents[1, l, rows, :] = now[3]
        tracer[2 * levels + l, rows, :] = now[4]

    def load(l, rows):
        return [
            tracer[l, rows, :],
            tracer[levels + l, rows, :],
            currents[0, l, rows, :],
            currents[1, l, rows, :],
            tracer[2 * levels + l, rows, :],
        ]

    lax.fori_loop(0, rows_all // 8, chunk, 0)
    out = start_all([(currents, currents_h)], sems)
    tracer[3 * levels] = horiz[...]
    tracer[3 * levels + 1] = wet[...].astype(F32)
    for k in range(planes):
        edge_up[k] = tracer[k, 0:8, :]
        edge_down[k] = tracer[k, rows_all - 8 : rows_all, :]
    wait_all(out)


def solve(ocean_state, vert_kappa, horiz_kappa, wet_mask):
    levels, rows, _ = vert_kappa.shape
    planes = 3 * levels + 2
    return pl.pallas_call(
        solve_kernel,
        out_shape=(
            jax.ShapeDtypeStruct((planes, rows, LANES), F32),
            pltpu.HBM((2, levels, rows, LANES), F32),
            jax.ShapeDtypeStruct((planes, 8, LANES), F32),
            jax.ShapeDtypeStruct((planes, 8, LANES), F32),
        ),
        in_specs=[vmem()] * 4,
        out_specs=(vmem(), hbm(), vmem(), vmem()),
        scratch_shapes=[pltpu.VMEM((2, levels, rows, LANES), F32), pltpu.SemaphoreType.DMA((1,))],
        compiler_params=pltpu.CompilerParams(vmem_limit_bytes=24 << 20),
        cost_estimate=pl.CostEstimate(flops=20 << 20, bytes_accessed=6 << 20, transcendentals=0),
    )(ocean_state, vert_kappa, horiz_kappa, wet_mask)


def pack_kernel(levels, tracer, above, below, wide_h, to_left, to_right, wide, sems):
    planes, rows, _ = tracer.shape
    for k in range(planes):
        wide[k, 0:HALO, :] = above[k]
        wide[k, HALO : HALO + rows, :] = tracer[k]
        wide[k, HALO + rows : 2 * HALO + rows, :] = below[k]
    out = start_all([(wide, wide_h)], sems)
    lane = iota((8, LANES), 1)

    def chunk(c, carry):
        at = pl.ds(pl.multiple_of(c * 8, 8), 8)

        def place(values, lanes):
            left, right = jnp.zeros((8, LANES), F32), jnp.zeros((8, LANES), F32)
            for k, (near, far) in zip(values, lanes):
                value = wide[k, at, :]
                left = jnp.where(lane == near, pltpu.roll(value, near, 1), left)
                left = jnp.where(lane == far, pltpu.roll(value, far - 1, 1), left)
                right = jnp.where(lane == near + 1, pltpu.roll(value, (near + 2) % LANES, 1), right)
                right = jnp.where(lane == far + 1, pltpu.roll(value, (far + 3) % LANES, 1), right)
            return left, right

        left, right = place(range(2 * levels), [(2 * k, 64 + 2 * k) for k in range(2 * levels)])
        to_left[0, at, :] = left
        to_right[0, at, :] = right
        lanes = [(2 * l, 64 + 2 * l) for l in range(levels)]
        lanes += [(2 * levels, 2 * levels + 2), (2 * levels + 4, 2 * levels + 6)]
        left, right = place(range(2 * levels, 3 * levels + 2), lanes)
        to_left[1, at, :] = left
        to_right[1, at, :] = right
        return carry

    lax.fori_loop(0, (rows + 2 * HALO) // 8, chunk, 0)
    wait_all(out)


def pack(levels, tracer, above, below):
    planes, rows, _ = tracer.shape
    tall = rows + 2 * HALO
    return pl.pallas_call(
        functools.partial(pack_kernel, levels),
        out_shape=(
            pltpu.HBM((planes, tall, LANES), F32),
            jax.ShapeDtypeStruct((2, tall, LANES), F32),
            jax.ShapeDtypeStruct((2, tall, LANES), F32),
        ),
        in_specs=[vmem()] * 3,
        out_specs=(hbm(), vmem(), vmem()),
        scratch_shapes=[pltpu.VMEM((planes, tall, LANES), F32), pltpu.SemaphoreType.DMA((1,))],
        compiler_params=pltpu.CompilerParams(vmem_limit_bytes=24 << 20),
        cost_estimate=pl.CostEstimate(flops=8 << 20, bytes_accessed=4 << 20, transcendentals=0),
    )(tracer, above, below)


def set_faces(levels, h, w, own_left, own_right, from_left, from_right, faces, packed):
    tall = h.shape[0]
    lane = iota((tall, LANES), 1)
    odd = lane % 2 == 1
    twice = lane % 64 < 2 * levels
    left, left_unit, right, right_unit = from_left[0], from_left[1], from_right[0], from_right[1]
    other = jnp.where(odd, left_unit, right_unit)
    at = 2 * levels

    def column(offset):
        return other[:, at + offset : at + offset + 1], other[:, at + offset + 1 : at + offset + 2]

    kappa_right, kappa_left = column(0)
    kappa_far_right, kappa_far_left = column(2)
    wet_right, wet_left = column(4)
    wet_far_right, wet_far_left = column(6)

    kappa_near = jnp.where(odd, kappa_left, kappa_right)
    kappa_far = jnp.where(odd, kappa_far_left, kappa_far_right)
    wet_near = jnp.where(odd, wet_left, wet_right)
    wet_far = jnp.where(odd, wet_far_left, wet_far_right)
    kappa_own = jnp.where(odd, h[:, 0:1], h[:, LANES - 1 : LANES])
    wet_own = jnp.where(odd, w[:, 0:1], w[:, LANES - 1 : LANES])

    def face(kappa_a, wet_a, kappa_b, wet_b):
        return 0.25 * (kappa_a + kappa_b) * wet_a * wet_b

    unit = jnp.where(twice, other, pltpu.roll(other, 2 * levels, 1))
    packed[0] = jnp.where(odd, left, right)
    packed[1] = unit * jnp.where(lane < 64, wet_near, wet_far)
    left, left_unit, right, right_unit = own_left[0], own_left[1], own_right[0], own_right[1]
    packed[2] = jnp.where(odd, pltpu.roll(left, 1, 1), pltpu.roll(right, LANES - 1, 1))
    own = jnp.where(odd, pltpu.roll(left_unit, 1, 1), pltpu.roll(right_unit, LANES - 1, 1))
    packed[3] = jnp.where(twice, own, pltpu.roll(own, 2 * levels, 1)) * wet_own
    north = face(kappa_near, wet_near, pltpu.roll(kappa_near, 1, 0), pltpu.roll(wet_near, 1, 0))
    packed[4] = north
    packed[5] = pltpu.roll(north, tall - 1, 0)
    packed[6] = face(kappa_near, wet_near, kappa_far, wet_far)
    packed[7] = face(kappa_near, wet_near, kappa_own, wet_own)

    north = face(h, w, pltpu.roll(h, 1, 0), pltpu.roll(w, 1, 0))
    faces[0] = north
    faces[1] = pltpu.roll(north, tall - 1, 0)
    west = face(
        h, w, jnp.where(lane == 0, kappa_left, pltpu.roll(h, 1, 1)), jnp.where(lane == 0, wet_left, pltpu.roll(w, 1, 1))
    )
    faces[2] = west
    faces[3] = jnp.where(lane == LANES - 1, face(h, w, kappa_right, wet_right), pltpu.roll(west, LANES - 1, 1))


def set_beside(levels, upright, wide, packed, beside):
    tall = upright.shape[0]
    lane = iota((tall, LANES), 1)
    odd = lane % 2 == 1
    heat = lane % 64 < 2 * levels

    def chosen(f):
        left_far, left_near, right_near, right_far = [upright[:, 4 * f + e : 4 * f + e + 1] for e in range(4)]
        near = jnp.where(odd, left_near, right_near)
        return jnp.where(lane < 64, near, jnp.where(odd, left_far, right_far))

    both = packed[0] + packed[1] * jnp.where(heat, chosen(0), chosen(1))
    far = pltpu.roll(both, 64, 1)
    ends_of = [jnp.where(odd, w[:, 0:1], w[:, LANES - 1 : LANES]) for w in wide]
    own = packed[2] + packed[3] * jnp.where(heat, ends_of[0], ends_of[1])
    near = both + packed[5] * (pltpu.roll(both, tall - 1, 0) - both)
    near = near + packed[4] * (pltpu.roll(both, 1, 0) - both)
    near = near + packed[6] * (far - both)
    near = near + packed[7] * (own - both)
    beside[0] = both
    beside[1] = near


def one_pass(value, faces, beside, shift):
    tall = value.shape[0]
    lane = iota(value.shape, 1)
    moved = pltpu.roll(beside, shift, 1)
    west = jnp.where(lane == 0, moved, pltpu.roll(value, 1, 1))
    east = jnp.where(lane == LANES - 1, moved, pltpu.roll(value, LANES - 1, 1))
    result = value + faces[1] * (pltpu.roll(value, tall - 1, 0) - value)
    result = result + faces[0] * (pltpu.roll(value, 1, 0) - value)
    result = result + faces[3] * (east - value)
    return result + faces[2] * (west - value)


def middle_kernel(
    capacity, levels, arrived, wide_h, currents_h, own_left_h, own_right_h, from_left_h, from_right_h,
    sent_h, forcing_h, near_h, faces_h,
    placing, values, number_t, top, currents, own_left, own_right, from_left, from_right,
    faces, packed, sent, forcing, near_o, sems, sent_sems,
):
    devices, message, _ = arrived.shape
    rows_all = currents.shape[1]
    tall = rows_all + 2 * HALO
    loads = start_all(
        [(wide_h.at[levels * k], top.at[k]) for k in range(3)]
        + [
            (wide_h.at[pl.ds(3 * levels, 2)], top.at[pl.ds(3, 2)]),
            (currents_h.at[0, 0], currents.at[0]),
            (currents_h.at[1, 0], currents.at[1]),
            (own_left_h, own_left),
            (own_right_h, own_right),
            (from_left_h, from_left),
            (from_right_h, from_right),
        ],
        sems,
    )
    span = 4 * capacity
    group = LANES // span
    groups = devices // group
    sub8 = iota((8, LANES), 0)
    lane8 = iota((8, LANES), 1)

    lane1 = iota((1, LANES), 1)
    spread = (iota((LANES, LANES), 0) - NUMBERS) == iota((LANES, LANES), 1) % span // 4
    every = jnp.concatenate([arrived[s, span + 8 : span + 9, :] for s in range(devices)], 0).astype(BF16)
    every = jnp.dot(every, jnp.where(spread, 1.0, 0.0).astype(BF16), preferred_element_type=F32)
    numbers = []
    for m in range(groups):
        line = jnp.zeros((1, LANES), F32)
        for g in range(group):
            s = m * group + g
            line = jnp.where(lane1 // span == g, every[s : s + 1], line)
        numbers.append(line)
    number_t[...] = jnp.transpose(
        jnp.concatenate(numbers + [jnp.zeros((LANES - groups, LANES), F32)], 0)
    )

    row_number = iota((rows_all, LANES), 0).astype(F32) + 1.0
    for m in range(groups):
        for f in range(4):
            placing[f * rows_all : (f + 1) * rows_all, m * LANES : (m + 1) * LANES] = jnp.where(
                pick(lane1 % 4 == f, numbers[m]) == row_number, 1.0, 0.0
            ).astype(BF16)
    edge_rows = jnp.zeros((8, LANES), F32)
    edge_cols = jnp.zeros((8, LANES), F32)
    for s in range(devices):
        high, low = split(arrived[s, 0:span, :])
        values[s * span : (s + 1) * span, 0:LANES] = high
        values[s * span : (s + 1) * span, LANES : 2 * LANES] = low
        edge_rows = edge_rows + arrived[s, span : span + 8, :]
        edge_cols = edge_cols + arrived[s, span + 8 : span + 16, :]
    total = jnp.dot(placing[...], values[...], preferred_element_type=F32)
    total = total[:, 0:LANES] + total[:, LANES : 2 * LANES]

    wait_all(loads)
    set_faces(levels, top[3], top[4], own_left, own_right, from_left, from_right, faces, packed)
    wet_wide = top[4]

    def plane(f):
        return total[f * rows_all : (f + 1) * rows_all]

    wide = []
    for f in range(2):
        before = pick(sub8 >= 6, edge_rows if f == 1 else pltpu.roll(edge_rows, 4, 0))
        after = pick(sub8 < 2, edge_rows if f == 0 else pltpu.roll(edge_rows, 4, 0))
        wide.append(jnp.concatenate([before, plane(f), after], 0))
        forcing[f] = wide[f]
    wet = wet_wide[HALO : HALO + rows_all]
    for f in range(2, 4):
        forcing[f, 0:HALO, :] = jnp.zeros((HALO, LANES), F32)
        forcing[f, HALO : HALO + rows_all, :] = plane(f) * wet
        forcing[f, HALO + rows_all : tall, :] = jnp.zeros((HALO, LANES), F32)

    part8 = sub8 % 4
    within = (part8 == lane8 % 4) & (lane8 >= HALO) & (lane8 < HALO + rows_all)
    upper = (part8 == 3) & (lane8 == HALO - 1)
    lower = (part8 == 0) & (lane8 == HALO + rows_all)
    halves = [[], []]
    for k in range(4):
        column = pick(within, pltpu.roll(edge_cols, HALO - k, 1))
        if k in (1, 2):
            column = column + pick(upper, pltpu.roll(edge_cols, (HALO - CORNERS - k) % LANES, 1))
            column = column + pick(lower, pltpu.roll(edge_cols, (HALO + rows_all - CORNERS - 1 - k) % LANES, 1))
        for f in range(2):
            halves[f].append(jnp.sum(column[4 * f : 4 * f + 4], axis=0, keepdims=True))
    columns = jnp.concatenate(halves[0] + halves[1], 0)
    upright = jnp.transpose(jnp.concatenate([columns, jnp.zeros((LANES - 8, LANES), F32)], 0))[0:tall]
    set_beside(levels, upright, wide, packed, near_o)
    stores = start_all([(forcing, forcing_h), (near_o, near_h), (faces, faces_h)], sems, 10)

    surface = []
    unit = top[2] * wet_wide
    for f in range(2):
        value = top[f] + unit * wide[f]
        shift = LANES - (2 * levels * f + 1)
        value = one_pass(value, faces, near_o[0], shift)
        value = one_pass(value, faces, near_o[1], shift)
        surface.append(value[HALO : HALO + rows_all] * wet)
    for f in range(2):
        surface.append(
            (currents[f] + top[2, HALO : HALO + rows_all, :] * forcing[2 + f, HALO : HALO + rows_all, :]) * wet
        )
    high, low = split(jnp.concatenate(surface, 0))
    source = jnp.concatenate([high, low], 1)
    lane_t = iota((LANES, 4 * rows_all), 1)
    sub_t = iota((LANES, 4 * rows_all), 0)
    target = jnp.where(sub_t % 4 == lane_t // rows_all, lane_t % rows_all + 1, -1).astype(F32)
    mask = jnp.concatenate([wet, jnp.zeros((LANES - rows_all, LANES), F32)], 0).astype(BF16)
    per = LANES // 4
    slot_number = number_t[pl.ds(0, per, stride=4), :]
    lane_s = (iota((per, LANES), 1) + 1).astype(F32)
    height = back_rows(capacity)
    for m in range(groups):
        chosen_rows = jnp.where(number_t[:, m : m + 1] == target, 1.0, 0.0).astype(BF16)
        rows = jnp.dot(chosen_rows, source, preferred_element_type=F32)
        rows = rows[:, 0:LANES] + rows[:, LANES : 2 * LANES]
        slots = jnp.where(slot_number[:, m : m + 1] == lane_s, 1.0, 0.0).astype(BF16)
        masks = jnp.dot(slots, mask, preferred_element_type=F32)
        for g in range(group):
            s = m * group + g
            sent[s, 0:span, :] = rows[g * span : (g + 1) * span]
            sent[s, span : span + capacity, :] = masks[g * capacity : (g + 1) * capacity]
            if height > span + capacity:
                sent[s, span + capacity : height, :] = jnp.zeros((height - span - capacity, LANES), F32)
        at = pl.ds(m * group, group)
        stores += start_all([(sent.at[at], sent_h.at[at])], sent_sems, m)
    wait_all(stores)


def middle(capacity, levels, arrived, wide, currents, *columns):
    devices = arrived.shape[0]
    rows = currents.shape[2]
    tall = rows + 2 * HALO
    height = back_rows(capacity)
    return pl.pallas_call(
        functools.partial(middle_kernel, capacity, levels),
        out_shape=(
            pltpu.HBM((devices, height, LANES), F32),
            pltpu.HBM((4, tall, LANES), F32),
            pltpu.HBM((2, tall, LANES), F32),
            pltpu.HBM((4, tall, LANES), F32),
        ),
        in_specs=[vmem()] + [hbm()] * 2 + [pl.BlockSpec(memory_space=pl.ANY)] * 4,
        out_specs=(hbm(),) * 4,
        scratch_shapes=[
            pltpu.VMEM((4 * rows, 4 * capacity * devices), BF16),
            pltpu.VMEM((4 * capacity * devices, 2 * LANES), BF16),
            pltpu.VMEM((LANES, LANES), F32),
            pltpu.VMEM((5, tall, LANES), F32),
            pltpu.VMEM((2, rows, LANES), F32),
        ]
        + [pltpu.VMEM((2, tall, LANES), F32)] * 4
        + [
            pltpu.VMEM((4, tall, LANES), F32),
            pltpu.VMEM((8, tall, LANES), F32),
            pltpu.VMEM((devices, height, LANES), F32),
            pltpu.VMEM((4, tall, LANES), F32),
            pltpu.VMEM((2, tall, LANES), F32),
            pltpu.SemaphoreType.DMA((13,)),
            pltpu.SemaphoreType.DMA((4 * capacity * devices // LANES,)),
        ],
        compiler_params=pltpu.CompilerParams(vmem_limit_bytes=24 << 20),
        cost_estimate=pl.CostEstimate(flops=200 << 20, bytes_accessed=4 << 20, transcendentals=0),
    )(arrived, *pin(wide, currents), *columns)


def finish_kernel(
    levels, wide_h, currents_h, faces_h, forcing_h, near_h, ocean, wide, currents, faces, forcing, near, sems
):
    rows_all = currents.shape[2]
    wait_all(
        start_all(
            [(wide_h, wide), (currents_h, currents), (faces_h, faces), (forcing_h, forcing), (near_h, near)], sems
        )
    )
    inner = slice(HALO, HALO + rows_all)

    def level(l, carry):
        unit = wide[2 * levels + l]
        masked = unit * wide[3 * levels + 1]
        for f in range(2):
            value = wide[f * levels + l] + masked * forcing[f]
            shift = LANES - 1 - 2 * (levels * f + l)
            value = one_pass(value, faces, near[0], shift)
            value = one_pass(value, faces, near[1], shift)
            ocean[f, l] = value[inner]
            ocean[2 + f, l] = currents[f, l] + unit[inner] * forcing[2 + f][inner]
        return carry

    lax.fori_loop(0, levels, level, 0)


def finish(levels, wide, currents, faces, forcing, near):
    rows = currents.shape[2]
    return pl.pallas_call(
        functools.partial(finish_kernel, levels),
        out_shape=jax.ShapeDtypeStruct((4, levels, rows, LANES), F32),
        in_specs=[hbm()] * 5,
        out_specs=vmem(),
        scratch_shapes=[pltpu.VMEM(a.shape, F32) for a in (wide, currents, faces, forcing, near)]
        + [pltpu.SemaphoreType.DMA((5,))],
        compiler_params=pltpu.CompilerParams(vmem_limit_bytes=24 << 20),
        cost_estimate=pl.CostEstimate(flops=40 << 20, bytes_accessed=6 << 20, transcendentals=0),
    )(*pin(wide, currents, faces, forcing, near))


def turn_kernel(weights_h, turned_h, weights, turned, sems, out_sems):
    part_tiles = weights.shape[0] // PARTS
    parts = [pl.ds(n * part_tiles, part_tiles) for n in range(PARTS)]
    loads = start_all([(weights_h.at[at], weights.at[at]) for at in parts], sems)
    stores = []
    for n, at in enumerate(parts):
        loads[n].wait()

        def tile_step(t, carry):
            turned[t] = weights[t].T
            return carry

        lax.fori_loop(n * part_tiles, (n + 1) * part_tiles, tile_step, 0, unroll=4)
        stores += start_all([(turned.at[at], turned_h.at[at])], out_sems, n)
    wait_all(stores)


def turn(remap_weight):
    return pl.pallas_call(
        turn_kernel,
        out_shape=pltpu.HBM(remap_weight.shape, BF16),
        in_specs=[hbm()],
        out_specs=hbm(),
        scratch_shapes=[pltpu.VMEM(remap_weight.shape, BF16)] * 2 + [pltpu.SemaphoreType.DMA((PARTS,))] * 2,
        compiler_params=pltpu.CompilerParams(vmem_limit_bytes=24 << 20),
        cost_estimate=pl.CostEstimate(flops=8 << 20, bytes_accessed=8 << 20, transcendentals=0),
    )(*pin(remap_weight))


def remap_back_kernel(
    block_h, tile_h, field_h, wet_h, returned, weights_h, out,
    block_s, tile_s, field_s, wet_s, weights, picked_a, picked_b, total_0, total_1, total_2, total_3, sems, weight_sems,
):
    npairs = block_s.shape[0]
    totals = [total_0, total_1, total_2, total_3]
    nblocks = total_0.shape[0]
    scalars = start_all([(field_h, field_s), (wet_h, wet_s), (block_h, block_s), (tile_h, tile_s)], sems)
    part_tiles = weights.shape[0] // PARTS
    parts = [pl.ds(n * part_tiles, part_tiles) for n in range(PARTS)]
    loads = start_all([(weights_h.at[at], weights.at[at]) for at in parts], weight_sems)
    for total in totals:
        total[...] = jnp.zeros_like(total)
    wait_all(scalars)

    def gather(p, picked, at):
        rows = returned[pl.ds(field_s[p], 4), :]
        mask = returned[pl.ds(wet_s[p] - 7, 8), :]
        high, low = split(jnp.concatenate([rows, jnp.zeros((3, LANES), F32), mask[7:8]], 0))
        picked[at] = jnp.concatenate([high, low], 0)

    def product(p, picked, at, total):
        value = jnp.dot(picked[at], weights[tile_s[p]], preferred_element_type=F32)
        b = block_s[p]
        total[b] = total[b] + (value[0:8] + value[8:16])

    half = npairs // 2
    many = len(totals)

    def first(p, carry):
        gather(p, picked_a, p)
        return carry

    def both(p, carry):
        for n in range(many):
            gather(half + many * p + n, picked_b, many * p + n)
            product(many * p + n, picked_a, many * p + n, totals[n])
        return carry

    def last(p, carry):
        for n in range(many):
            product(half + many * p + n, picked_b, many * p + n, totals[n])
        return carry

    lax.fori_loop(0, half, first, 0, unroll=64)
    wait_all(loads)
    lax.fori_loop(0, half // many, both, 0, unroll=32)
    lax.fori_loop(0, half // many, last, 0, unroll=32)
    for b in range(nblocks):
        sums = (total_0[b] + total_1[b]) + (total_2[b] + total_3[b])
        out[:, b * LANES : (b + 1) * LANES] = sums[0:4] / jnp.maximum(sums[7:8], 0.1)


def remap_back(pair_block, pair_tile, field_at, wet_at, returned, weights, nblocks):
    npairs = pair_block.shape[0]
    return pl.pallas_call(
        remap_back_kernel,
        out_shape=jax.ShapeDtypeStruct((4, nblocks * LANES), F32),
        in_specs=[hbm()] * 4 + [vmem(), hbm()],
        out_specs=vmem(),
        scratch_shapes=[pltpu.SMEM((npairs,), I32)] * 4
        + [pltpu.VMEM(weights.shape, BF16)]
        + [pltpu.VMEM((npairs // 2, 16, LANES), BF16)] * 2
        + [pltpu.VMEM((nblocks, 8, LANES), F32)] * 4
        + [pltpu.SemaphoreType.DMA((4,)), pltpu.SemaphoreType.DMA((PARTS,))],
        compiler_params=pltpu.CompilerParams(vmem_limit_bytes=24 << 20),
        cost_estimate=pl.CostEstimate(flops=2 * npairs * 16 * LANES * LANES, bytes_accessed=6 << 20, transcendentals=0),
    )(*pin(pair_block, pair_tile, field_at, wet_at), returned, *pin(weights))


def local(
    atm_state,
    pair_block,
    pair_owner,
    pair_row,
    pair_tile,
    remap_weight,
    wet_mask,
    ocean_state,
    vert_kappa,
    horiz_kappa,
):
    grid_x = lax.axis_size("gx")
    grid_y = lax.axis_size("gy")
    devices = grid_x * grid_y
    npairs = pair_block.shape[0]
    capacity = max(2, 2 * npairs // devices)
    levels, tile_rows, _ = vert_kappa.shape
    nblocks = atm_state.shape[1] // LANES
    owner = pair_owner.reshape(npairs)
    message = 4 * capacity + EDGE
    outgoing, field_at, wet_at = remap_out(
        capacity, grid_y, devices, tile_rows, atm_state, pair_block, owner, pair_row, pair_tile, remap_weight
    )
    arrived = lax.all_to_all(
        outgoing.reshape(devices, message, LANES), ("gx", "gy"), split_axis=0, concat_axis=0, tiled=True
    )
    tracer, currents, edge_up, edge_down = solve(ocean_state, vert_kappa, horiz_kappa, wet_mask)
    rise_x = [(i, i + 1) for i in range(grid_x - 1)]
    fall_x = [(b, a) for a, b in rise_x]
    rise_y = [(i, i + 1) for i in range(grid_y - 1)]
    fall_y = [(b, a) for a, b in rise_y]
    above = lax.ppermute(edge_down, "gx", rise_x)
    below = lax.ppermute(edge_up, "gx", fall_x)
    wide, to_left, to_right = pack(levels, tracer, above, below)
    from_left = lax.ppermute(to_right, "gy", rise_y)
    from_right = lax.ppermute(to_left, "gy", fall_y)
    sent, forcing, near, faces = middle(
        capacity, levels, arrived, wide, currents, to_left, to_right, from_left, from_right
    )
    returned = lax.all_to_all(sent, ("gx", "gy"), split_axis=0, concat_axis=0, tiled=True)
    ocean_next = finish(levels, wide, currents, faces, forcing, near)
    weights, _ = lax.optimization_barrier((remap_weight, near))
    atm_surface = remap_back(
        pair_block, pair_tile, field_at, wet_at, returned.reshape(-1, LANES), turn(weights), nblocks
    )
    return (ocean_next, atm_surface)


def solution(mesh):
    placed = (
        P(None, ("gx", "gy")),
        P(("gx", "gy")),
        P(("gx", "gy"), None),
        P(("gx", "gy")),
        P(("gx", "gy")),
        P(("gx", "gy"), None, None),
        P("gx", "gy"),
        P(None, None, "gx", "gy"),
        P(None, "gx", "gy"),
        P("gx", "gy"),
    )
    return jax.shard_map(
        local,
        mesh=mesh,
        in_specs=placed,
        out_specs=(P(None, None, "gx", "gy"), P(None, ("gx", "gy"))),
        check_vma=False,
    )
```

```python
import functools

import jax
import jax.numpy as jnp
from jax import lax
from jax.experimental import pallas as pl
from jax.experimental.pallas import tpu as pltpu
from jax.sharding import PartitionSpec as P

F32 = jnp.float32
BF16 = jnp.bfloat16
I32 = jnp.int32
VMEM = pltpu.VMEM
SMEM = pltpu.SMEM
LANES = 128
EDGE = 16
HALO = 8
NUMBERS = 72
CORNERS = 112
SENDS = 8
PARTS = 8


def hbm():
    return pl.BlockSpec(memory_space=pltpu.HBM)


def vmem():
    return pl.BlockSpec(memory_space=VMEM)


def pin(*arrays):
    return [pltpu.with_memory_space_constraint(a, pltpu.HBM) for a in arrays]


def start_all(pairs, sems, first=0):
    copies = [pltpu.make_async_copy(src, dst, sems.at[first + n]) for n, (src, dst) in enumerate(pairs)]
    for copy in copies:
        copy.start()
    return copies


def wait_all(copies):
    for copy in copies:
        copy.wait()


def iota(shape, dim):
    return lax.broadcasted_iota(I32, shape, dim)


def pick(mask, value):
    return jnp.where(mask, value, 0.0)


def split(value):
    high = value.astype(BF16)
    return high, (value - high.astype(F32)).astype(BF16)


def back_rows(capacity):
    return 4 * capacity + max(8, capacity)


def remap_out_kernel(
    capacity, grid_y, tile_rows, block_h, owner_h, row_h, tile_h, atm_h, weights_h, out_h, field_h, wet_h,
    out, block_s, owner_s, row_s, tile_s, slot_s, rank_s, field_s, wet_s, atm, weights, atm_rows, flux_rows, flux, fill, row_slots, col_slots, rows_acc, cols_acc, sems, weight_sems, out_sems,
):
    devices = fill.shape[0]
    npairs = block_s.shape[0]
    tiles = weights.shape[0]
    nblocks = flux.shape[0]
    message = 4 * capacity + EDGE
    copies = [
        pltpu.make_async_copy(src, dst, sems.at[n])
        for n, (src, dst) in enumerate(
            [(atm_h, atm), (block_h, block_s), (owner_h, owner_s), (row_h, row_s), (tile_h, tile_s)]
        )
    ]
    for copy in copies:
        copy.start()
    part_tiles = tiles // PARTS
    parts = [pl.ds(n * part_tiles, part_tiles) for n in range(PARTS)]
    loads = [pltpu.make_async_copy(weights_h.at[at], weights.at[at], weight_sems.at[n]) for n, at in enumerate(parts)]
    for load in loads:
        load.start()
    out[...] = jnp.zeros_like(out)
    row_slots[...] = jnp.zeros_like(row_slots)
    col_slots[...] = jnp.zeros_like(col_slots)

    def clear_fill(i, carry):
        fill[i] = 0
        return carry

    lax.fori_loop(0, devices, clear_fill, 0, unroll=16)
    flux_rows[...] = jnp.zeros_like(flux_rows)
    wait_all(copies)
    for b in range(nblocks):
        atm_rows[8 * b : 8 * b + 6, :] = atm[:, b * LANES : (b + 1) * LANES]
    wind_u, wind_v, air, dry, rain, sea = [atm_rows[pl.ds(n, nblocks, stride=8), :] for n in range(6)]
    speed = jnp.sqrt(wind_u * wind_u + wind_v * wind_v + 0.25)
    heat = 0.5 * speed * (air - sea)
    water = rain - 0.3 * speed * dry
    planes = [heat, water, 0.2 * speed * wind_u, 0.2 * speed * wind_v]
    for n, plane in list(enumerate(planes)) + [(8 + n, heat) for n in range(4)] + [(12 + n, water) for n in range(4)]:
        flux_rows[pl.ds(n, nblocks, stride=16), :] = plane
    for b in range(nblocks):
        flux[b] = flux_rows[16 * b : 16 * (b + 1), :].astype(BF16)

    height = back_rows(capacity)

    for p in range(npairs):
        owner = owner_s[p]
        rank = fill[owner]
        fill[owner] = rank + 1
        field_s[p] = owner * height + 4 * rank
        wet_s[p] = owner * height + 4 * capacity + rank
        slot_s[p] = owner * capacity + rank
        rank_s[p] = rank
    stores = start_all([(field_s, field_h), (wet_s, wet_h)], out_sems, SENDS)
    wait_all(loads)

    sub = iota((8, LANES), 0)
    lane = iota((8, LANES), 1)
    part = sub % 4
    edge_row = jnp.where(part == 0, 0, jnp.where(part == 1, 1, tile_rows - 4 + part))
    band = ((lane - part) >> 2) * 4 + part
    id_rank = jnp.where(sub == 0, lane - NUMBERS, -1)

    def pair(p, carry):
        slot = slot_s[p]
        row = row_s[p]
        rank = rank_s[p]
        value = jnp.dot(flux[block_s[p]], weights[tile_s[p]], preferred_element_type=F32)
        out[pl.ds(owner_s[p] * message + 4 * rank, 4), :] = value[0:4]
        tracer = value[8:16]
        row_slots[slot] = pick(edge_row == row, tracer)
        number = (row + 1).astype(F32)
        col_slots[slot] = pick(band == row, pltpu.roll(tracer, row + 2, 1)) + pick(id_rank == rank, number)
        return carry

    lax.fori_loop(0, npairs, pair, 0, unroll=64)

    def owner_step(d, carry):
        rows = row_slots[d * capacity]
        cols = col_slots[d * capacity]
        for r in range(1, capacity):
            rows = rows + row_slots[d * capacity + r]
            cols = cols + col_slots[d * capacity + r]
        rows_acc[d] = rows
        cols_acc[d] = cols
        return carry

    lax.fori_loop(0, devices, owner_step, 0, unroll=8)

    grid_x = devices // grid_y
    zero = jnp.zeros((8, LANES), F32)

    def columns_of(i, j):
        if not (0 <= i < grid_x and 0 <= j < grid_y):
            return zero
        return cols_acc[i * grid_y + j]

    from_left = (lane - sub) % 4 < 2
    in_band = lane < tile_rows + 4
    in_ids = (sub == 0) & (lane >= NUMBERS) & (lane < NUMBERS + capacity)
    last, first = part == 3, part == 0
    send = devices // SENDS
    for d in range(devices):
        i, j = d // grid_y, d % grid_y
        below = rows_acc[d + grid_y] if i < grid_x - 1 else zero
        above = rows_acc[d - grid_y] if i > 0 else zero
        base = d * message + 4 * capacity
        out[base : base + 8, :] = jnp.where(part < 2, below, above)
        tile = pick(in_band, jnp.where(from_left, columns_of(i, j - 1), columns_of(i, j + 1)))
        upper = pick(last & (lane == tile_rows), columns_of(i - 1, j - 1))
        upper = upper + pick(last & (lane == tile_rows + 1), columns_of(i - 1, j + 1))
        lower = pick(first & (lane == 1), columns_of(i + 1, j - 1))
        lower = lower + pick(first & (lane == 2), columns_of(i + 1, j + 1))
        tile = tile + pltpu.roll(upper, CORNERS - tile_rows, 1) + pltpu.roll(lower, CORNERS + 1, 1)
        tile = tile + pick(in_ids, cols_acc[d])
        out[base + 8 : base + 16, :] = tile
        if d % send == send - 1:
            n = d // send
            at = pl.ds(n * send * message, send * message)
            stores.append(pltpu.make_async_copy(out.at[at], out_h.at[at], out_sems.at[n]))
            stores[-1].start()
    for store in stores:
        store.wait()


def remap_out(capacity, grid_y, devices, tile_rows, atm_state, pair_block, owner, pair_row, pair_tile, remap_weight):
    npairs = pair_block.shape[0]
    nblocks = atm_state.shape[1] // LANES
    message = 4 * capacity + EDGE
    return pl.pallas_call(
        functools.partial(remap_out_kernel, capacity, grid_y, tile_rows),
        out_shape=(
            pltpu.HBM((devices * message, LANES), F32),
            pltpu.HBM((npairs,), I32),
            pltpu.HBM((npairs,), I32),
        ),
        in_specs=[hbm()] * 6,
        out_specs=(hbm(),) * 3,
        scratch_shapes=[pltpu.VMEM((devices * message, LANES), F32)]
        + [pltpu.SMEM((npairs,), I32)] * 8
        + [
            pltpu.VMEM(atm_state.shape, F32),
            pltpu.VMEM(remap_weight.shape, BF16),
            pltpu.VMEM((nblocks * 8, LANES), F32),
            pltpu.VMEM((nblocks * 16, LANES), F32),
            pltpu.VMEM((nblocks, 16, LANES), BF16),
            pltpu.SMEM((devices,), I32),
            pltpu.VMEM((devices * capacity, 8, LANES), F32),
            pltpu.VMEM((devices * capacity, 8, LANES), F32),
            pltpu.VMEM((devices, 8, LANES), F32),
            pltpu.VMEM((devices, 8, LANES), F32),
            pltpu.SemaphoreType.DMA((5,)),
            pltpu.SemaphoreType.DMA((PARTS,)),
            pltpu.SemaphoreType.DMA((SENDS + 2,)),
        ],
        compiler_params=pltpu.CompilerParams(vmem_limit_bytes=40 << 20),
        cost_estimate=pl.CostEstimate(
            flops=2 * npairs * 16 * LANES * LANES, bytes_accessed=6 << 20, transcendentals=0
        ),
    )(*pin(pair_block, owner, pair_row, pair_tile, atm_state, remap_weight))


def solve_kernel(state, kappa, horiz, wet, tracer, currents_h, edge_up, edge_down, currents, sems):
    levels = kappa.shape[0]
    rows_all = kappa.shape[1]
    planes = tracer.shape[0]

    def chunk(c, carry):
        rows = pl.ds(pl.multiple_of(c * 8, 8), 8)
        column = [kappa[l, rows, :] for l in range(levels)]
        face = [0.5 * (column[l] + column[l + 1]) for l in range(levels - 1)]
        upper = []
        now = None
        for l in range(levels):
            diagonal = 1.0
            if l > 0:
                diagonal = diagonal + face[l - 1]
            if l < levels - 1:
                diagonal = diagonal + face[l]
            if l > 0:
                diagonal = diagonal + face[l - 1] * upper[-1]
            inverse = 1.0 / diagonal
            if l == 0:
                now = [state[f, 0, rows, :] * inverse for f in range(4)] + [inverse]
            else:
                pull = face[l - 1] * inverse
                now = [state[f, l, rows, :] * inverse + pull * now[f] for f in range(4)] + [pull * now[4]]
            upper.append(-face[l] * inverse if l < levels - 1 else None)
            store(l, rows, now)
        for l in range(levels - 2, -1, -1):
            here = load(l, rows)
            now = [here[f] - upper[l] * now[f] for f in range(5)]
            store(l, rows, now)
        return carry

    def store(l, rows, now):
        tracer[l, rows, :] = now[0]
        tracer[levels + l, rows, :] = now[1]
        currents[0, l, rows, :] = now[2]
        currents[1, l, rows, :] = now[3]
        tracer[2 * levels + l, rows, :] = now[4]

    def load(l, rows):
        return [
            tracer[l, rows, :],
            tracer[levels + l, rows, :],
            currents[0, l, rows, :],
            currents[1, l, rows, :],
            tracer[2 * levels + l, rows, :],
        ]

    lax.fori_loop(0, rows_all // 8, chunk, 0)
    out = start_all([(currents, currents_h)], sems)
    tracer[3 * levels] = horiz[...]
    tracer[3 * levels + 1] = wet[...].astype(F32)
    for k in range(planes):
        edge_up[k] = tracer[k, 0:8, :]
        edge_down[k] = tracer[k, rows_all - 8 : rows_all, :]
    wait_all(out)


def solve(ocean_state, vert_kappa, horiz_kappa, wet_mask):
    levels, rows, _ = vert_kappa.shape
    planes = 3 * levels + 2
    return pl.pallas_call(
        solve_kernel,
        out_shape=(
            jax.ShapeDtypeStruct((planes, rows, LANES), F32),
            pltpu.HBM((2, levels, rows, LANES), F32),
            jax.ShapeDtypeStruct((planes, 8, LANES), F32),
            jax.ShapeDtypeStruct((planes, 8, LANES), F32),
        ),
        in_specs=[vmem()] * 4,
        out_specs=(vmem(), hbm(), vmem(), vmem()),
        scratch_shapes=[pltpu.VMEM((2, levels, rows, LANES), F32), pltpu.SemaphoreType.DMA((1,))],
        compiler_params=pltpu.CompilerParams(vmem_limit_bytes=24 << 20),
        cost_estimate=pl.CostEstimate(flops=20 << 20, bytes_accessed=6 << 20, transcendentals=0),
    )(ocean_state, vert_kappa, horiz_kappa, wet_mask)


def pack_kernel(levels, tracer, above, below, wide_h, to_left, to_right, wide, sems):
    planes, rows, _ = tracer.shape
    for k in range(planes):
        wide[k, 0:HALO, :] = above[k]
        wide[k, HALO : HALO + rows, :] = tracer[k]
        wide[k, HALO + rows : 2 * HALO + rows, :] = below[k]
    out = start_all([(wide, wide_h)], sems)
    lane = iota((8, LANES), 1)

    def chunk(c, carry):
        at = pl.ds(pl.multiple_of(c * 8, 8), 8)

        def place(values, lanes):
            left, right = jnp.zeros((8, LANES), F32), jnp.zeros((8, LANES), F32)
            for k, (near, far) in zip(values, lanes):
                value = wide[k, at, :]
                left = jnp.where(lane == near, pltpu.roll(value, near, 1), left)
                left = jnp.where(lane == far, pltpu.roll(value, far - 1, 1), left)
                right = jnp.where(lane == near + 1, pltpu.roll(value, (near + 2) % LANES, 1), right)
                right = jnp.where(lane == far + 1, pltpu.roll(value, (far + 3) % LANES, 1), right)
            return left, right

        left, right = place(range(2 * levels), [(2 * k, 64 + 2 * k) for k in range(2 * levels)])
        to_left[0, at, :] = left
        to_right[0, at, :] = right
        lanes = [(2 * l, 64 + 2 * l) for l in range(levels)]
        lanes += [(2 * levels, 2 * levels + 2), (2 * levels + 4, 2 * levels + 6)]
        left, right = place(range(2 * levels, 3 * levels + 2), lanes)
        to_left[1, at, :] = left
        to_right[1, at, :] = right
        return carry

    lax.fori_loop(0, (rows + 2 * HALO) // 8, chunk, 0)
    wait_all(out)


def pack(levels, tracer, above, below):
    planes, rows, _ = tracer.shape
    tall = rows + 2 * HALO
    return pl.pallas_call(
        functools.partial(pack_kernel, levels),
        out_shape=(
            pltpu.HBM((planes, tall, LANES), F32),
            jax.ShapeDtypeStruct((2, tall, LANES), F32),
            jax.ShapeDtypeStruct((2, tall, LANES), F32),
        ),
        in_specs=[vmem()] * 3,
        out_specs=(hbm(), vmem(), vmem()),
        scratch_shapes=[pltpu.VMEM((planes, tall, LANES), F32), pltpu.SemaphoreType.DMA((1,))],
        compiler_params=pltpu.CompilerParams(vmem_limit_bytes=24 << 20),
        cost_estimate=pl.CostEstimate(flops=8 << 20, bytes_accessed=4 << 20, transcendentals=0),
    )(tracer, above, below)


def set_faces(levels, h, w, own_left, own_right, from_left, from_right, faces, packed):
    tall = h.shape[0]
    lane = iota((tall, LANES), 1)
    odd = lane % 2 == 1
    twice = lane % 64 < 2 * levels
    left, left_unit, right, right_unit = from_left[0], from_left[1], from_right[0], from_right[1]
    other = jnp.where(odd, left_unit, right_unit)
    at = 2 * levels

    def column(offset):
        return other[:, at + offset : at + offset + 1], other[:, at + offset + 1 : at + offset + 2]

    kappa_right, kappa_left = column(0)
    kappa_far_right, kappa_far_left = column(2)
    wet_right, wet_left = column(4)
    wet_far_right, wet_far_left = column(6)

    kappa_near = jnp.where(odd, kappa_left, kappa_right)
    kappa_far = jnp.where(odd, kappa_far_left, kappa_far_right)
    wet_near = jnp.where(odd, wet_left, wet_right)
    wet_far = jnp.where(odd, wet_far_left, wet_far_right)
    kappa_own = jnp.where(odd, h[:, 0:1], h[:, LANES - 1 : LANES])
    wet_own = jnp.where(odd, w[:, 0:1], w[:, LANES - 1 : LANES])

    def face(kappa_a, wet_a, kappa_b, wet_b):
        return 0.25 * (kappa_a + kappa_b) * wet_a * wet_b

    unit = jnp.where(twice, other, pltpu.roll(other, 2 * levels, 1))
    packed[0] = jnp.where(odd, left, right)
    packed[1] = unit * jnp.where(lane < 64, wet_near, wet_far)
    left, left_unit, right, right_unit = own_left[0], own_left[1], own_right[0], own_right[1]
    packed[2] = jnp.where(odd, pltpu.roll(left, 1, 1), pltpu.roll(right, LANES - 1, 1))
    own = jnp.where(odd, pltpu.roll(left_unit, 1, 1), pltpu.roll(right_unit, LANES - 1, 1))
    packed[3] = jnp.where(twice, own, pltpu.roll(own, 2 * levels, 1)) * wet_own
    north = face(kappa_near, wet_near, pltpu.roll(kappa_near, 1, 0), pltpu.roll(wet_near, 1, 0))
    packed[4] = north
    packed[5] = pltpu.roll(north, tall - 1, 0)
    packed[6] = face(kappa_near, wet_near, kappa_far, wet_far)
    packed[7] = face(kappa_near, wet_near, kappa_own, wet_own)

    north = face(h, w, pltpu.roll(h, 1, 0), pltpu.roll(w, 1, 0))
    faces[0] = north
    faces[1] = pltpu.roll(north, tall - 1, 0)
    west = face(
        h, w, jnp.where(lane == 0, kappa_left, pltpu.roll(h, 1, 1)), jnp.where(lane == 0, wet_left, pltpu.roll(w, 1, 1))
    )
    faces[2] = west
    faces[3] = jnp.where(lane == LANES - 1, face(h, w, kappa_right, wet_right), pltpu.roll(west, LANES - 1, 1))


def set_beside(levels, upright, wide, packed, beside):
    tall = upright.shape[0]
    lane = iota((tall, LANES), 1)
    odd = lane % 2 == 1
    heat = lane % 64 < 2 * levels

    def chosen(f):
        left_far, left_near, right_near, right_far = [upright[:, 4 * f + e : 4 * f + e + 1] for e in range(4)]
        near = jnp.where(odd, left_near, right_near)
        return jnp.where(lane < 64, near, jnp.where(odd, left_far, right_far))

    both = packed[0] + packed[1] * jnp.where(heat, chosen(0), chosen(1))
    far = pltpu.roll(both, 64, 1)
    ends_of = [jnp.where(odd, w[:, 0:1], w[:, LANES - 1 : LANES]) for w in wide]
    own = packed[2] + packed[3] * jnp.where(heat, ends_of[0], ends_of[1])
    near = both + packed[5] * (pltpu.roll(both, tall - 1, 0) - both)
    near = near + packed[4] * (pltpu.roll(both, 1, 0) - both)
    near = near + packed[6] * (far - both)
    near = near + packed[7] * (own - both)
    beside[0] = both
    beside[1] = near


def one_pass(value, faces, beside, shift):
    tall = value.shape[0]
    lane = iota(value.shape, 1)
    moved = pltpu.roll(beside, shift, 1)
    west = jnp.where(lane == 0, moved, pltpu.roll(value, 1, 1))
    east = jnp.where(lane == LANES - 1, moved, pltpu.roll(value, LANES - 1, 1))
    result = value + faces[1] * (pltpu.roll(value, tall - 1, 0) - value)
    result = result + faces[0] * (pltpu.roll(value, 1, 0) - value)
    result = result + faces[3] * (east - value)
    return result + faces[2] * (west - value)


def middle_kernel(
    capacity, levels, arrived, wide_h, currents_h, own_left_h, own_right_h, from_left_h, from_right_h,
    sent_h, forcing_h, near_h, faces_h,
    placing, values, number_t, top, currents, own_left, own_right, from_left, from_right,
    faces, packed, sent, forcing, near_o, sems, sent_sems,
):
    devices, message, _ = arrived.shape
    rows_all = currents.shape[1]
    tall = rows_all + 2 * HALO
    loads = start_all(
        [(wide_h.at[levels * k], top.at[k]) for k in range(3)]
        + [
            (wide_h.at[pl.ds(3 * levels, 2)], top.at[pl.ds(3, 2)]),
            (currents_h.at[0, 0], currents.at[0]),
            (currents_h.at[1, 0], currents.at[1]),
            (own_left_h, own_left),
            (own_right_h, own_right),
            (from_left_h, from_left),
            (from_right_h, from_right),
        ],
        sems,
    )
    span = 4 * capacity
    group = LANES // span
    groups = devices // group
    sub8 = iota((8, LANES), 0)
    lane8 = iota((8, LANES), 1)

    lane1 = iota((1, LANES), 1)
    spread = (iota((LANES, LANES), 0) - NUMBERS) == iota((LANES, LANES), 1) % span // 4
    every = jnp.concatenate([arrived[s, span + 8 : span + 9, :] for s in range(devices)], 0).astype(BF16)
    every = jnp.dot(every, jnp.where(spread, 1.0, 0.0).astype(BF16), preferred_element_type=F32)
    numbers = []
    for m in range(groups):
        line = jnp.zeros((1, LANES), F32)
        for g in range(group):
            s = m * group + g
            line = jnp.where(lane1 // span == g, every[s : s + 1], line)
        numbers.append(line)
    number_t[...] = jnp.transpose(
        jnp.concatenate(numbers + [jnp.zeros((LANES - groups, LANES), F32)], 0)
    )

    row_number = iota((rows_all, LANES), 0).astype(F32) + 1.0
    for m in range(groups):
        for f in range(4):
            placing[f * rows_all : (f + 1) * rows_all, m * LANES : (m + 1) * LANES] = jnp.where(
                pick(lane1 % 4 == f, numbers[m]) == row_number, 1.0, 0.0
            ).astype(BF16)
    edge_rows = jnp.zeros((8, LANES), F32)
    edge_cols = jnp.zeros((8, LANES), F32)
    for s in range(devices):
        high, low = split(arrived[s, 0:span, :])
        values[s * span : (s + 1) * span, 0:LANES] = high
        values[s * span : (s + 1) * span, LANES : 2 * LANES] = low
        edge_rows = edge_rows + arrived[s, span : span + 8, :]
        edge_cols = edge_cols + arrived[s, span + 8 : span + 16, :]
    wait_all(loads)
    set_faces(levels, top[3], top[4], own_left, own_right, from_left, from_right, faces, packed)
    wet_wide = top[4]
    total = jnp.dot(placing[...], values[...], preferred_element_type=F32)
    total = total[:, 0:LANES] + total[:, LANES : 2 * LANES]


    def plane(f):
        return total[f * rows_all : (f + 1) * rows_all]

    wide = []
    for f in range(2):
        before = pick(sub8 >= 6, edge_rows if f == 1 else pltpu.roll(edge_rows, 4, 0))
        after = pick(sub8 < 2, edge_rows if f == 0 else pltpu.roll(edge_rows, 4, 0))
        wide.append(jnp.concatenate([before, plane(f), after], 0))
        forcing[f] = wide[f]
    wet = wet_wide[HALO : HALO + rows_all]
    for f in range(2, 4):
        forcing[f, 0:HALO, :] = jnp.zeros((HALO, LANES), F32)
        forcing[f, HALO : HALO + rows_all, :] = plane(f) * wet
        forcing[f, HALO + rows_all : tall, :] = jnp.zeros((HALO, LANES), F32)

    part8 = sub8 % 4
    within = (part8 == lane8 % 4) & (lane8 >= HALO) & (lane8 < HALO + rows_all)
    upper = (part8 == 3) & (lane8 == HALO - 1)
    lower = (part8 == 0) & (lane8 == HALO + rows_all)
    halves = [[], []]
    for k in range(4):
        column = pick(within, pltpu.roll(edge_cols, HALO - k, 1))
        if k in (1, 2):
            column = column + pick(upper, pltpu.roll(edge_cols, (HALO - CORNERS - k) % LANES, 1))
            column = column + pick(lower, pltpu.roll(edge_cols, (HALO + rows_all - CORNERS - 1 - k) % LANES, 1))
        for f in range(2):
            halves[f].append(jnp.sum(column[4 * f : 4 * f + 4], axis=0, keepdims=True))
    columns = jnp.concatenate(halves[0] + halves[1], 0)
    upright = jnp.transpose(jnp.concatenate([columns, jnp.zeros((LANES - 8, LANES), F32)], 0))[0:tall]
    set_beside(levels, upright, wide, packed, near_o)
    stores = start_all([(forcing, forcing_h), (near_o, near_h), (faces, faces_h)], sems, 10)

    surface = []
    unit = top[2] * wet_wide
    for f in range(2):
        value = top[f] + unit * wide[f]
        shift = LANES - (2 * levels * f + 1)
        value = one_pass(value, faces, near_o[0], shift)
        value = one_pass(value, faces, near_o[1], shift)
        surface.append(value[HALO : HALO + rows_all] * wet)
    for f in range(2):
        surface.append(
            (currents[f] + top[2, HALO : HALO + rows_all, :] * forcing[2 + f, HALO : HALO + rows_all, :]) * wet
        )
    high, low = split(jnp.concatenate(surface, 0))
    source = jnp.concatenate([high, low], 1)
    lane_t = iota((LANES, 4 * rows_all), 1)
    sub_t = iota((LANES, 4 * rows_all), 0)
    target = jnp.where(sub_t % 4 == lane_t // rows_all, lane_t % rows_all + 1, -1).astype(F32)
    mask = jnp.concatenate([wet, jnp.zeros((LANES - rows_all, LANES), F32)], 0).astype(BF16)
    per = LANES // 4
    slot_number = number_t[pl.ds(0, per, stride=4), :]
    lane_s = (iota((per, LANES), 1) + 1).astype(F32)
    height = back_rows(capacity)
    for m in range(groups):
        chosen_rows = jnp.where(number_t[:, m : m + 1] == target, 1.0, 0.0).astype(BF16)
        rows = jnp.dot(chosen_rows, source, preferred_element_type=F32)
        rows = rows[:, 0:LANES] + rows[:, LANES : 2 * LANES]
        slots = jnp.where(slot_number[:, m : m + 1] == lane_s, 1.0, 0.0).astype(BF16)
        masks = jnp.dot(slots, mask, preferred_element_type=F32)
        for g in range(group):
            s = m * group + g
            sent[s, 0:span, :] = rows[g * span : (g + 1) * span]
            sent[s, span : span + capacity, :] = masks[g * capacity : (g + 1) * capacity]
            if height > span + capacity:
                sent[s, span + capacity : height, :] = jnp.zeros((height - span - capacity, LANES), F32)
        at = pl.ds(m * group, group)
        stores += start_all([(sent.at[at], sent_h.at[at])], sent_sems, m)
    wait_all(stores)


def middle(capacity, levels, arrived, wide, currents, *columns):
    devices = arrived.shape[0]
    rows = currents.shape[2]
    tall = rows + 2 * HALO
    height = back_rows(capacity)
    return pl.pallas_call(
        functools.partial(middle_kernel, capacity, levels),
        out_shape=(
            pltpu.HBM((devices, height, LANES), F32),
            pltpu.HBM((4, tall, LANES), F32),
            pltpu.HBM((2, tall, LANES), F32),
            pltpu.HBM((4, tall, LANES), F32),
        ),
        in_specs=[vmem()] + [hbm()] * 2 + [pl.BlockSpec(memory_space=pl.ANY)] * 4,
        out_specs=(hbm(),) * 4,
        scratch_shapes=[
            pltpu.VMEM((4 * rows, 4 * capacity * devices), BF16),
            pltpu.VMEM((4 * capacity * devices, 2 * LANES), BF16),
            pltpu.VMEM((LANES, LANES), F32),
            pltpu.VMEM((5, tall, LANES), F32),
            pltpu.VMEM((2, rows, LANES), F32),
        ]
        + [pltpu.VMEM((2, tall, LANES), F32)] * 4
        + [
            pltpu.VMEM((4, tall, LANES), F32),
            pltpu.VMEM((8, tall, LANES), F32),
            pltpu.VMEM((devices, height, LANES), F32),
            pltpu.VMEM((4, tall, LANES), F32),
            pltpu.VMEM((2, tall, LANES), F32),
            pltpu.SemaphoreType.DMA((13,)),
            pltpu.SemaphoreType.DMA((4 * capacity * devices // LANES,)),
        ],
        compiler_params=pltpu.CompilerParams(vmem_limit_bytes=24 << 20),
        cost_estimate=pl.CostEstimate(flops=200 << 20, bytes_accessed=4 << 20, transcendentals=0),
    )(arrived, *pin(wide, currents), *columns)


def finish_kernel(
    levels, wide_h, currents_h, faces_h, forcing_h, near_h, ocean, wide, currents, faces, forcing, near, sems
):
    rows_all = currents.shape[2]
    wait_all(
        start_all(
            [(wide_h, wide), (currents_h, currents), (faces_h, faces), (forcing_h, forcing), (near_h, near)], sems
        )
    )
    inner = slice(HALO, HALO + rows_all)

    def level(l, carry):
        unit = wide[2 * levels + l]
        masked = unit * wide[3 * levels + 1]
        for f in range(2):
            value = wide[f * levels + l] + masked * forcing[f]
            shift = LANES - 1 - 2 * (levels * f + l)
            value = one_pass(value, faces, near[0], shift)
            value = one_pass(value, faces, near[1], shift)
            ocean[f, l] = value[inner]
            ocean[2 + f, l] = currents[f, l] + unit[inner] * forcing[2 + f][inner]
        return carry

    lax.fori_loop(0, levels, level, 0)


def finish(levels, wide, currents, faces, forcing, near):
    rows = currents.shape[2]
    return pl.pallas_call(
        functools.partial(finish_kernel, levels),
        out_shape=jax.ShapeDtypeStruct((4, levels, rows, LANES), F32),
        in_specs=[hbm()] * 5,
        out_specs=vmem(),
        scratch_shapes=[pltpu.VMEM(a.shape, F32) for a in (wide, currents, faces, forcing, near)]
        + [pltpu.SemaphoreType.DMA((5,))],
        compiler_params=pltpu.CompilerParams(vmem_limit_bytes=24 << 20),
        cost_estimate=pl.CostEstimate(flops=40 << 20, bytes_accessed=6 << 20, transcendentals=0),
    )(*pin(wide, currents, faces, forcing, near))


def turn_kernel(weights_h, turned_h, weights, turned, sems, out_sems):
    part_tiles = weights.shape[0] // PARTS
    parts = [pl.ds(n * part_tiles, part_tiles) for n in range(PARTS)]
    loads = start_all([(weights_h.at[at], weights.at[at]) for at in parts], sems)
    stores = []
    for n, at in enumerate(parts):
        loads[n].wait()

        def tile_step(t, carry):
            turned[t] = weights[t].T
            return carry

        lax.fori_loop(n * part_tiles, (n + 1) * part_tiles, tile_step, 0, unroll=4)
        stores += start_all([(turned.at[at], turned_h.at[at])], out_sems, n)
    wait_all(stores)


def turn(remap_weight):
    return pl.pallas_call(
        turn_kernel,
        out_shape=pltpu.HBM(remap_weight.shape, BF16),
        in_specs=[hbm()],
        out_specs=hbm(),
        scratch_shapes=[pltpu.VMEM(remap_weight.shape, BF16)] * 2 + [pltpu.SemaphoreType.DMA((PARTS,))] * 2,
        compiler_params=pltpu.CompilerParams(vmem_limit_bytes=24 << 20),
        cost_estimate=pl.CostEstimate(flops=8 << 20, bytes_accessed=8 << 20, transcendentals=0),
    )(*pin(remap_weight))


def remap_back_kernel(
    block_h, tile_h, field_h, wet_h, returned, weights_h, out,
    block_s, tile_s, field_s, wet_s, weights, picked_a, picked_b, total_0, total_1, total_2, total_3, sems, weight_sems,
):
    npairs = block_s.shape[0]
    totals = [total_0, total_1, total_2, total_3]
    nblocks = total_0.shape[0]
    scalars = start_all([(field_h, field_s), (wet_h, wet_s), (block_h, block_s), (tile_h, tile_s)], sems)
    part_tiles = weights.shape[0] // PARTS
    parts = [pl.ds(n * part_tiles, part_tiles) for n in range(PARTS)]
    loads = start_all([(weights_h.at[at], weights.at[at]) for at in parts], weight_sems)
    for total in totals:
        total[...] = jnp.zeros_like(total)
    wait_all(scalars)

    def gather(p, picked, at):
        rows = returned[pl.ds(field_s[p], 4), :]
        mask = returned[pl.ds(wet_s[p] - 7, 8), :]
        high, low = split(jnp.concatenate([rows, jnp.zeros((3, LANES), F32), mask[7:8]], 0))
        picked[at] = jnp.concatenate([high, low], 0)

    def product(p, picked, at, total):
        value = jnp.dot(picked[at], weights[tile_s[p]], preferred_element_type=F32)
        b = block_s[p]
        total[b] = total[b] + (value[0:8] + value[8:16])

    half = npairs // 2
    many = len(totals)

    def first(p, carry):
        gather(p, picked_a, p)
        return carry

    def both(p, carry):
        for n in range(many):
            gather(half + many * p + n, picked_b, many * p + n)
            product(many * p + n, picked_a, many * p + n, totals[n])
        return carry

    def last(p, carry):
        for n in range(many):
            product(half + many * p + n, picked_b, many * p + n, totals[n])
        return carry

    lax.fori_loop(0, half, first, 0, unroll=64)
    wait_all(loads)
    lax.fori_loop(0, half // many, both, 0, unroll=32)
    lax.fori_loop(0, half // many, last, 0, unroll=32)
    for b in range(nblocks):
        sums = (total_0[b] + total_1[b]) + (total_2[b] + total_3[b])
        out[:, b * LANES : (b + 1) * LANES] = sums[0:4] / jnp.maximum(sums[7:8], 0.1)


def remap_back(pair_block, pair_tile, field_at, wet_at, returned, weights, nblocks):
    npairs = pair_block.shape[0]
    return pl.pallas_call(
        remap_back_kernel,
        out_shape=jax.ShapeDtypeStruct((4, nblocks * LANES), F32),
        in_specs=[hbm()] * 4 + [vmem(), hbm()],
        out_specs=vmem(),
        scratch_shapes=[pltpu.SMEM((npairs,), I32)] * 4
        + [pltpu.VMEM(weights.shape, BF16)]
        + [pltpu.VMEM((npairs // 2, 16, LANES), BF16)] * 2
        + [pltpu.VMEM((nblocks, 8, LANES), F32)] * 4
        + [pltpu.SemaphoreType.DMA((4,)), pltpu.SemaphoreType.DMA((PARTS,))],
        compiler_params=pltpu.CompilerParams(vmem_limit_bytes=24 << 20),
        cost_estimate=pl.CostEstimate(flops=2 * npairs * 16 * LANES * LANES, bytes_accessed=6 << 20, transcendentals=0),
    )(*pin(pair_block, pair_tile, field_at, wet_at), returned, *pin(weights))


def local(
    atm_state,
    pair_block,
    pair_owner,
    pair_row,
    pair_tile,
    remap_weight,
    wet_mask,
    ocean_state,
    vert_kappa,
    horiz_kappa,
):
    grid_x = lax.axis_size("gx")
    grid_y = lax.axis_size("gy")
    devices = grid_x * grid_y
    npairs = pair_block.shape[0]
    capacity = max(2, 2 * npairs // devices)
    levels, tile_rows, _ = vert_kappa.shape
    nblocks = atm_state.shape[1] // LANES
    owner = pair_owner.reshape(npairs)
    message = 4 * capacity + EDGE
    outgoing, field_at, wet_at = remap_out(
        capacity, grid_y, devices, tile_rows, atm_state, pair_block, owner, pair_row, pair_tile, remap_weight
    )
    arrived = lax.all_to_all(
        outgoing.reshape(devices, message, LANES), ("gx", "gy"), split_axis=0, concat_axis=0, tiled=True
    )
    tracer, currents, edge_up, edge_down = solve(ocean_state, vert_kappa, horiz_kappa, wet_mask)
    rise_x = [(i, i + 1) for i in range(grid_x - 1)]
    fall_x = [(b, a) for a, b in rise_x]
    rise_y = [(i, i + 1) for i in range(grid_y - 1)]
    fall_y = [(b, a) for a, b in rise_y]
    above = lax.ppermute(edge_down, "gx", rise_x)
    below = lax.ppermute(edge_up, "gx", fall_x)
    wide, to_left, to_right = pack(levels, tracer, above, below)
    from_left = lax.ppermute(to_right, "gy", rise_y)
    from_right = lax.ppermute(to_left, "gy", fall_y)
    sent, forcing, near, faces = middle(
        capacity, levels, arrived, wide, currents, to_left, to_right, from_left, from_right
    )
    returned = lax.all_to_all(sent, ("gx", "gy"), split_axis=0, concat_axis=0, tiled=True)
    ocean_next = finish(levels, wide, currents, faces, forcing, near)
    weights, _ = lax.optimization_barrier((remap_weight, near))
    atm_surface = remap_back(
        pair_block, pair_tile, field_at, wet_at, returned.reshape(-1, LANES), turn(weights), nblocks
    )
    return (ocean_next, atm_surface)


def solution(mesh):
    placed = (
        P(None, ("gx", "gy")),
        P(("gx", "gy")),
        P(("gx", "gy"), None),
        P(("gx", "gy")),
        P(("gx", "gy")),
        P(("gx", "gy"), None, None),
        P("gx", "gy"),
        P(None, None, "gx", "gy"),
        P(None, "gx", "gy"),
        P("gx", "gy"),
    )
    return jax.shard_map(
        local,
        mesh=mesh,
        in_specs=placed,
        out_specs=(P(None, None, "gx", "gy"), P(None, ("gx", "gy"))),
        check_vma=False,
    )
```

```python
import functools

import jax
import jax.numpy as jnp
from jax import lax
from jax.experimental import pallas as pl
from jax.experimental.pallas import tpu as pltpu
from jax.sharding import PartitionSpec as P

F32 = jnp.float32
BF16 = jnp.bfloat16
I32 = jnp.int32
VMEM = pltpu.VMEM
SMEM = pltpu.SMEM
LANES = 128
EDGE = 16
HALO = 8
NUMBERS = 72
CORNERS = 112
SENDS = 8
PARTS = 8


def hbm():
    return pl.BlockSpec(memory_space=pltpu.HBM)


def vmem():
    return pl.BlockSpec(memory_space=VMEM)


def pin(*arrays):
    return [pltpu.with_memory_space_constraint(a, pltpu.HBM) for a in arrays]


def start_all(pairs, sems, first=0):
    copies = [pltpu.make_async_copy(src, dst, sems.at[first + n]) for n, (src, dst) in enumerate(pairs)]
    for copy in copies:
        copy.start()
    return copies


def wait_all(copies):
    for copy in copies:
        copy.wait()


def iota(shape, dim):
    return lax.broadcasted_iota(I32, shape, dim)


def pick(mask, value):
    return jnp.where(mask, value, 0.0)


def split(value):
    high = value.astype(BF16)
    return high, (value - high.astype(F32)).astype(BF16)


def remap_out_kernel(
    capacity, grid_y, tile_rows, block_h, owner_h, row_h, tile_h, atm_h, weights_h, out_h, field_h, wet_h,
    out, block_s, owner_s, row_s, tile_s, slot_s, rank_s, field_s, wet_s, atm, weights, atm_rows, flux_rows, flux, fill, row_slots, col_slots, rows_acc, cols_acc, sems, weight_sems, out_sems,
):
    devices = fill.shape[0]
    npairs = block_s.shape[0]
    tiles = weights.shape[0]
    nblocks = flux.shape[0]
    message = 4 * capacity + EDGE
    copies = [
        pltpu.make_async_copy(src, dst, sems.at[n])
        for n, (src, dst) in enumerate(
            [(atm_h, atm), (block_h, block_s), (owner_h, owner_s), (row_h, row_s), (tile_h, tile_s)]
        )
    ]
    for copy in copies:
        copy.start()
    part_tiles = tiles // PARTS
    parts = [pl.ds(n * part_tiles, part_tiles) for n in range(PARTS)]
    loads = [pltpu.make_async_copy(weights_h.at[at], weights.at[at], weight_sems.at[n]) for n, at in enumerate(parts)]
    for load in loads:
        load.start()
    out[...] = jnp.zeros_like(out)
    row_slots[...] = jnp.zeros_like(row_slots)
    col_slots[...] = jnp.zeros_like(col_slots)

    def clear_fill(i, carry):
        fill[i] = 0
        return carry

    lax.fori_loop(0, devices, clear_fill, 0, unroll=16)
    flux_rows[...] = jnp.zeros_like(flux_rows)
    wait_all(copies)
    for b in range(nblocks):
        atm_rows[8 * b : 8 * b + 6, :] = atm[:, b * LANES : (b + 1) * LANES]
    wind_u, wind_v, air, dry, rain, sea = [atm_rows[pl.ds(n, nblocks, stride=8), :] for n in range(6)]
    speed = jnp.sqrt(wind_u * wind_u + wind_v * wind_v + 0.25)
    heat = 0.5 * speed * (air - sea)
    water = rain - 0.3 * speed * dry
    planes = [heat, water, 0.2 * speed * wind_u, 0.2 * speed * wind_v]
    for n, plane in list(enumerate(planes)) + [(8 + n, heat) for n in range(4)] + [(12 + n, water) for n in range(4)]:
        flux_rows[pl.ds(n, nblocks, stride=16), :] = plane
    for b in range(nblocks):
        flux[b] = flux_rows[16 * b : 16 * (b + 1), :].astype(BF16)

    height = 4 * capacity

    for p in range(npairs):
        owner = owner_s[p]
        rank = fill[owner]
        fill[owner] = rank + 1
        field_s[p] = owner * height + 4 * rank
        wet_s[p] = owner * tile_rows + row_s[p]
        slot_s[p] = owner * capacity + rank
        rank_s[p] = rank
    stores = start_all([(field_s, field_h), (wet_s, wet_h)], out_sems, SENDS)
    wait_all(loads)

    sub = iota((8, LANES), 0)
    lane = iota((8, LANES), 1)
    part = sub % 4
    edge_row = jnp.where(part == 0, 0, jnp.where(part == 1, 1, tile_rows - 4 + part))
    band = ((lane - part) >> 2) * 4 + part
    id_rank = jnp.where(sub == 0, lane - NUMBERS, -1)

    def pair(p, carry):
        slot = slot_s[p]
        row = row_s[p]
        rank = rank_s[p]
        value = jnp.dot(flux[block_s[p]], weights[tile_s[p]], preferred_element_type=F32)
        out[pl.ds(owner_s[p] * message + 4 * rank, 4), :] = value[0:4]
        tracer = value[8:16]
        row_slots[slot] = pick(edge_row == row, tracer)
        number = (row + 1).astype(F32)
        col_slots[slot] = pick(band == row, pltpu.roll(tracer, row + 2, 1)) + pick(id_rank == rank, number)
        return carry

    lax.fori_loop(0, npairs, pair, 0, unroll=64)

    def owner_step(d, carry):
        rows = row_slots[d * capacity]
        cols = col_slots[d * capacity]
        for r in range(1, capacity):
            rows = rows + row_slots[d * capacity + r]
            cols = cols + col_slots[d * capacity + r]
        rows_acc[d] = rows
        cols_acc[d] = cols
        return carry

    lax.fori_loop(0, devices, owner_step, 0, unroll=8)

    grid_x = devices // grid_y
    zero = jnp.zeros((8, LANES), F32)

    def columns_of(i, j):
        if not (0 <= i < grid_x and 0 <= j < grid_y):
            return zero
        return cols_acc[i * grid_y + j]

    from_left = (lane - sub) % 4 < 2
    in_band = lane < tile_rows + 4
    in_ids = (sub == 0) & (lane >= NUMBERS) & (lane < NUMBERS + capacity)
    last, first = part == 3, part == 0
    send = devices // SENDS
    for d in range(devices):
        i, j = d // grid_y, d % grid_y
        below = rows_acc[d + grid_y] if i < grid_x - 1 else zero
        above = rows_acc[d - grid_y] if i > 0 else zero
        base = d * message + 4 * capacity
        out[base : base + 8, :] = jnp.where(part < 2, below, above)
        tile = pick(in_band, jnp.where(from_left, columns_of(i, j - 1), columns_of(i, j + 1)))
        upper = pick(last & (lane == tile_rows), columns_of(i - 1, j - 1))
        upper = upper + pick(last & (lane == tile_rows + 1), columns_of(i - 1, j + 1))
        lower = pick(first & (lane == 1), columns_of(i + 1, j - 1))
        lower = lower + pick(first & (lane == 2), columns_of(i + 1, j + 1))
        tile = tile + pltpu.roll(upper, CORNERS - tile_rows, 1) + pltpu.roll(lower, CORNERS + 1, 1)
        tile = tile + pick(in_ids, cols_acc[d])
        out[base + 8 : base + 16, :] = tile
        if d % send == send - 1:
            n = d // send
            at = pl.ds(n * send * message, send * message)
            stores.append(pltpu.make_async_copy(out.at[at], out_h.at[at], out_sems.at[n]))
            stores[-1].start()
    for store in stores:
        store.wait()


def remap_out(capacity, grid_y, devices, tile_rows, atm_state, pair_block, owner, pair_row, pair_tile, remap_weight):
    npairs = pair_block.shape[0]
    nblocks = atm_state.shape[1] // LANES
    message = 4 * capacity + EDGE
    return pl.pallas_call(
        functools.partial(remap_out_kernel, capacity, grid_y, tile_rows),
        out_shape=(
            pltpu.HBM((devices * message, LANES), F32),
            pltpu.HBM((npairs,), I32),
            pltpu.HBM((npairs,), I32),
        ),
        in_specs=[hbm()] * 6,
        out_specs=(hbm(),) * 3,
        scratch_shapes=[pltpu.VMEM((devices * message, LANES), F32)]
        + [pltpu.SMEM((npairs,), I32)] * 8
        + [
            pltpu.VMEM(atm_state.shape, F32),
            pltpu.VMEM(remap_weight.shape, BF16),
            pltpu.VMEM((nblocks * 8, LANES), F32),
            pltpu.VMEM((nblocks * 16, LANES), F32),
            pltpu.VMEM((nblocks, 16, LANES), BF16),
            pltpu.SMEM((devices,), I32),
            pltpu.VMEM((devices * capacity, 8, LANES), F32),
            pltpu.VMEM((devices * capacity, 8, LANES), F32),
            pltpu.VMEM((devices, 8, LANES), F32),
            pltpu.VMEM((devices, 8, LANES), F32),
            pltpu.SemaphoreType.DMA((5,)),
            pltpu.SemaphoreType.DMA((PARTS,)),
            pltpu.SemaphoreType.DMA((SENDS + 2,)),
        ],
        compiler_params=pltpu.CompilerParams(vmem_limit_bytes=40 << 20),
        cost_estimate=pl.CostEstimate(
            flops=2 * npairs * 16 * LANES * LANES, bytes_accessed=6 << 20, transcendentals=0
        ),
    )(*pin(pair_block, owner, pair_row, pair_tile, atm_state, remap_weight))


def solve_kernel(state, kappa, horiz, wet, tracer, currents_h, edge_up, edge_down, currents, sems):
    levels = kappa.shape[0]
    rows_all = kappa.shape[1]
    planes = tracer.shape[0]

    def chunk(c, carry):
        rows = pl.ds(pl.multiple_of(c * 8, 8), 8)
        column = [kappa[l, rows, :] for l in range(levels)]
        face = [0.5 * (column[l] + column[l + 1]) for l in range(levels - 1)]
        upper = []
        now = None
        for l in range(levels):
            diagonal = 1.0
            if l > 0:
                diagonal = diagonal + face[l - 1]
            if l < levels - 1:
                diagonal = diagonal + face[l]
            if l > 0:
                diagonal = diagonal + face[l - 1] * upper[-1]
            inverse = 1.0 / diagonal
            if l == 0:
                now = [state[f, 0, rows, :] * inverse for f in range(4)] + [inverse]
            else:
                pull = face[l - 1] * inverse
                now = [state[f, l, rows, :] * inverse + pull * now[f] for f in range(4)] + [pull * now[4]]
            upper.append(-face[l] * inverse if l < levels - 1 else None)
            store(l, rows, now)
        for l in range(levels - 2, -1, -1):
            here = load(l, rows)
            now = [here[f] - upper[l] * now[f] for f in range(5)]
            store(l, rows, now)
        return carry

    def store(l, rows, now):
        tracer[l, rows, :] = now[0]
        tracer[levels + l, rows, :] = now[1]
        currents[0, l, rows, :] = now[2]
        currents[1, l, rows, :] = now[3]
        tracer[2 * levels + l, rows, :] = now[4]

    def load(l, rows):
        return [
            tracer[l, rows, :],
            tracer[levels + l, rows, :],
            currents[0, l, rows, :],
            currents[1, l, rows, :],
            tracer[2 * levels + l, rows, :],
        ]

    lax.fori_loop(0, rows_all // 8, chunk, 0)
    out = start_all([(currents, currents_h)], sems)
    tracer[3 * levels] = horiz[...]
    tracer[3 * levels + 1] = wet[...].astype(F32)
    for k in range(planes):
        edge_up[k] = tracer[k, 0:8, :]
        edge_down[k] = tracer[k, rows_all - 8 : rows_all, :]
    wait_all(out)


def solve(ocean_state, vert_kappa, horiz_kappa, wet_mask):
    levels, rows, _ = vert_kappa.shape
    planes = 3 * levels + 2
    return pl.pallas_call(
        solve_kernel,
        out_shape=(
            jax.ShapeDtypeStruct((planes, rows, LANES), F32),
            pltpu.HBM((2, levels, rows, LANES), F32),
            jax.ShapeDtypeStruct((planes, 8, LANES), F32),
            jax.ShapeDtypeStruct((planes, 8, LANES), F32),
        ),
        in_specs=[vmem()] * 4,
        out_specs=(vmem(), hbm(), vmem(), vmem()),
        scratch_shapes=[pltpu.VMEM((2, levels, rows, LANES), F32), pltpu.SemaphoreType.DMA((1,))],
        compiler_params=pltpu.CompilerParams(vmem_limit_bytes=24 << 20),
        cost_estimate=pl.CostEstimate(flops=20 << 20, bytes_accessed=6 << 20, transcendentals=0),
    )(ocean_state, vert_kappa, horiz_kappa, wet_mask)


def pack_kernel(levels, tracer, above, below, wide_h, to_left, to_right, wide, sems):
    planes, rows, _ = tracer.shape
    for k in range(planes):
        wide[k, 0:HALO, :] = above[k]
        wide[k, HALO : HALO + rows, :] = tracer[k]
        wide[k, HALO + rows : 2 * HALO + rows, :] = below[k]
    out = start_all([(wide, wide_h)], sems)
    lane = iota((8, LANES), 1)

    def chunk(c, carry):
        at = pl.ds(pl.multiple_of(c * 8, 8), 8)

        def place(values, lanes):
            left, right = jnp.zeros((8, LANES), F32), jnp.zeros((8, LANES), F32)
            for k, (near, far) in zip(values, lanes):
                value = wide[k, at, :]
                left = jnp.where(lane == near, pltpu.roll(value, near, 1), left)
                left = jnp.where(lane == far, pltpu.roll(value, far - 1, 1), left)
                right = jnp.where(lane == near + 1, pltpu.roll(value, (near + 2) % LANES, 1), right)
                right = jnp.where(lane == far + 1, pltpu.roll(value, (far + 3) % LANES, 1), right)
            return left, right

        left, right = place(range(2 * levels), [(2 * k, 64 + 2 * k) for k in range(2 * levels)])
        to_left[0, at, :] = left
        to_right[0, at, :] = right
        lanes = [(2 * l, 64 + 2 * l) for l in range(levels)]
        lanes += [(2 * levels, 2 * levels + 2), (2 * levels + 4, 2 * levels + 6)]
        left, right = place(range(2 * levels, 3 * levels + 2), lanes)
        to_left[1, at, :] = left
        to_right[1, at, :] = right
        return carry

    lax.fori_loop(0, (rows + 2 * HALO) // 8, chunk, 0)
    wait_all(out)


def pack(levels, tracer, above, below):
    planes, rows, _ = tracer.shape
    tall = rows + 2 * HALO
    return pl.pallas_call(
        functools.partial(pack_kernel, levels),
        out_shape=(
            pltpu.HBM((planes, tall, LANES), F32),
            jax.ShapeDtypeStruct((2, tall, LANES), F32),
            jax.ShapeDtypeStruct((2, tall, LANES), F32),
        ),
        in_specs=[vmem()] * 3,
        out_specs=(hbm(), vmem(), vmem()),
        scratch_shapes=[pltpu.VMEM((planes, tall, LANES), F32), pltpu.SemaphoreType.DMA((1,))],
        compiler_params=pltpu.CompilerParams(vmem_limit_bytes=24 << 20),
        cost_estimate=pl.CostEstimate(flops=8 << 20, bytes_accessed=4 << 20, transcendentals=0),
    )(tracer, above, below)


def set_faces(levels, h, w, own_left, own_right, from_left, from_right, faces, packed):
    tall = h.shape[0]
    lane = iota((tall, LANES), 1)
    odd = lane % 2 == 1
    twice = lane % 64 < 2 * levels
    left, left_unit, right, right_unit = from_left[0], from_left[1], from_right[0], from_right[1]
    other = jnp.where(odd, left_unit, right_unit)
    at = 2 * levels

    def column(offset):
        return other[:, at + offset : at + offset + 1], other[:, at + offset + 1 : at + offset + 2]

    kappa_right, kappa_left = column(0)
    kappa_far_right, kappa_far_left = column(2)
    wet_right, wet_left = column(4)
    wet_far_right, wet_far_left = column(6)

    kappa_near = jnp.where(odd, kappa_left, kappa_right)
    kappa_far = jnp.where(odd, kappa_far_left, kappa_far_right)
    wet_near = jnp.where(odd, wet_left, wet_right)
    wet_far = jnp.where(odd, wet_far_left, wet_far_right)
    kappa_own = jnp.where(odd, h[:, 0:1], h[:, LANES - 1 : LANES])
    wet_own = jnp.where(odd, w[:, 0:1], w[:, LANES - 1 : LANES])

    def face(kappa_a, wet_a, kappa_b, wet_b):
        return 0.25 * (kappa_a + kappa_b) * wet_a * wet_b

    unit = jnp.where(twice, other, pltpu.roll(other, 2 * levels, 1))
    packed[0] = jnp.where(odd, left, right)
    packed[1] = unit * jnp.where(lane < 64, wet_near, wet_far)
    left, left_unit, right, right_unit = own_left[0], own_left[1], own_right[0], own_right[1]
    packed[2] = jnp.where(odd, pltpu.roll(left, 1, 1), pltpu.roll(right, LANES - 1, 1))
    own = jnp.where(odd, pltpu.roll(left_unit, 1, 1), pltpu.roll(right_unit, LANES - 1, 1))
    packed[3] = jnp.where(twice, own, pltpu.roll(own, 2 * levels, 1)) * wet_own
    north = face(kappa_near, wet_near, pltpu.roll(kappa_near, 1, 0), pltpu.roll(wet_near, 1, 0))
    packed[4] = north
    packed[5] = pltpu.roll(north, tall - 1, 0)
    packed[6] = face(kappa_near, wet_near, kappa_far, wet_far)
    packed[7] = face(kappa_near, wet_near, kappa_own, wet_own)

    north = face(h, w, pltpu.roll(h, 1, 0), pltpu.roll(w, 1, 0))
    faces[0] = north
    faces[1] = pltpu.roll(north, tall - 1, 0)
    west = face(
        h, w, jnp.where(lane == 0, kappa_left, pltpu.roll(h, 1, 1)), jnp.where(lane == 0, wet_left, pltpu.roll(w, 1, 1))
    )
    faces[2] = west
    faces[3] = jnp.where(lane == LANES - 1, face(h, w, kappa_right, wet_right), pltpu.roll(west, LANES - 1, 1))


def set_beside(levels, upright, wide, packed, beside):
    tall = upright.shape[0]
    lane = iota((tall, LANES), 1)
    odd = lane % 2 == 1
    heat = lane % 64 < 2 * levels

    def chosen(f):
        left_far, left_near, right_near, right_far = [upright[:, 4 * f + e : 4 * f + e + 1] for e in range(4)]
        near = jnp.where(odd, left_near, right_near)
        return jnp.where(lane < 64, near, jnp.where(odd, left_far, right_far))

    both = packed[0] + packed[1] * jnp.where(heat, chosen(0), chosen(1))
    far = pltpu.roll(both, 64, 1)
    ends_of = [jnp.where(odd, w[:, 0:1], w[:, LANES - 1 : LANES]) for w in wide]
    own = packed[2] + packed[3] * jnp.where(heat, ends_of[0], ends_of[1])
    near = both + packed[5] * (pltpu.roll(both, tall - 1, 0) - both)
    near = near + packed[4] * (pltpu.roll(both, 1, 0) - both)
    near = near + packed[6] * (far - both)
    near = near + packed[7] * (own - both)
    beside[0] = both
    beside[1] = near


def one_pass(value, faces, beside, shift):
    tall = value.shape[0]
    lane = iota(value.shape, 1)
    moved = pltpu.roll(beside, shift, 1)
    west = jnp.where(lane == 0, moved, pltpu.roll(value, 1, 1))
    east = jnp.where(lane == LANES - 1, moved, pltpu.roll(value, LANES - 1, 1))
    result = value + faces[1] * (pltpu.roll(value, tall - 1, 0) - value)
    result = result + faces[0] * (pltpu.roll(value, 1, 0) - value)
    result = result + faces[3] * (east - value)
    return result + faces[2] * (west - value)


def middle_kernel(
    capacity, levels, arrived, wide_h, currents_h, own_left_h, own_right_h, from_left_h, from_right_h,
    sent_h, forcing_h, near_h, faces_h,
    placing, values, number_t, top, currents, own_left, own_right, from_left, from_right,
    faces, packed, sent, forcing, near_o, sems, sent_sems,
):
    devices, message, _ = arrived.shape
    rows_all = currents.shape[1]
    tall = rows_all + 2 * HALO
    loads = start_all(
        [(wide_h.at[levels * k], top.at[k]) for k in range(3)]
        + [
            (wide_h.at[pl.ds(3 * levels, 2)], top.at[pl.ds(3, 2)]),
            (currents_h.at[0, 0], currents.at[0]),
            (currents_h.at[1, 0], currents.at[1]),
            (own_left_h, own_left),
            (own_right_h, own_right),
            (from_left_h, from_left),
            (from_right_h, from_right),
        ],
        sems,
    )
    span = 4 * capacity
    group = LANES // span
    groups = devices // group
    sub8 = iota((8, LANES), 0)
    lane8 = iota((8, LANES), 1)

    lane1 = iota((1, LANES), 1)
    spread = (iota((LANES, LANES), 0) - NUMBERS) == iota((LANES, LANES), 1) % span // 4
    every = jnp.concatenate([arrived[s, span + 8 : span + 9, :] for s in range(devices)], 0).astype(BF16)
    every = jnp.dot(every, jnp.where(spread, 1.0, 0.0).astype(BF16), preferred_element_type=F32)
    numbers = []
    for m in range(groups):
        line = jnp.zeros((1, LANES), F32)
        for g in range(group):
            s = m * group + g
            line = jnp.where(lane1 // span == g, every[s : s + 1], line)
        numbers.append(line)
    number_t[...] = jnp.transpose(
        jnp.concatenate(numbers + [jnp.zeros((LANES - groups, LANES), F32)], 0)
    )

    row_number = iota((rows_all, LANES), 0).astype(F32) + 1.0
    for m in range(groups):
        for f in range(4):
            placing[f * rows_all : (f + 1) * rows_all, m * LANES : (m + 1) * LANES] = jnp.where(
                pick(lane1 % 4 == f, numbers[m]) == row_number, 1.0, 0.0
            ).astype(BF16)
    edge_rows = jnp.zeros((8, LANES), F32)
    edge_cols = jnp.zeros((8, LANES), F32)
    for s in range(devices):
        high, low = split(arrived[s, 0:span, :])
        values[s * span : (s + 1) * span, 0:LANES] = high
        values[s * span : (s + 1) * span, LANES : 2 * LANES] = low
        edge_rows = edge_rows + arrived[s, span : span + 8, :]
        edge_cols = edge_cols + arrived[s, span + 8 : span + 16, :]
    wait_all(loads)
    set_faces(levels, top[3], top[4], own_left, own_right, from_left, from_right, faces, packed)
    wet_wide = top[4]
    total = jnp.dot(placing[...], values[...], preferred_element_type=F32)
    total = total[:, 0:LANES] + total[:, LANES : 2 * LANES]


    def plane(f):
        return total[f * rows_all : (f + 1) * rows_all]

    wide = []
    for f in range(2):
        before = pick(sub8 >= 6, edge_rows if f == 1 else pltpu.roll(edge_rows, 4, 0))
        after = pick(sub8 < 2, edge_rows if f == 0 else pltpu.roll(edge_rows, 4, 0))
        wide.append(jnp.concatenate([before, plane(f), after], 0))
        forcing[f] = wide[f]
    wet = wet_wide[HALO : HALO + rows_all]
    for f in range(2, 4):
        forcing[f, 0:HALO, :] = jnp.zeros((HALO, LANES), F32)
        forcing[f, HALO : HALO + rows_all, :] = plane(f) * wet
        forcing[f, HALO + rows_all : tall, :] = jnp.zeros((HALO, LANES), F32)

    part8 = sub8 % 4
    within = (part8 == lane8 % 4) & (lane8 >= HALO) & (lane8 < HALO + rows_all)
    upper = (part8 == 3) & (lane8 == HALO - 1)
    lower = (part8 == 0) & (lane8 == HALO + rows_all)
    halves = [[], []]
    for k in range(4):
        column = pick(within, pltpu.roll(edge_cols, HALO - k, 1))
        if k in (1, 2):
            column = column + pick(upper, pltpu.roll(edge_cols, (HALO - CORNERS - k) % LANES, 1))
            column = column + pick(lower, pltpu.roll(edge_cols, (HALO + rows_all - CORNERS - 1 - k) % LANES, 1))
        for f in range(2):
            halves[f].append(jnp.sum(column[4 * f : 4 * f + 4], axis=0, keepdims=True))
    columns = jnp.concatenate(halves[0] + halves[1], 0)
    upright = jnp.transpose(jnp.concatenate([columns, jnp.zeros((LANES - 8, LANES), F32)], 0))[0:tall]
    set_beside(levels, upright, wide, packed, near_o)
    stores = start_all([(forcing, forcing_h), (near_o, near_h), (faces, faces_h)], sems, 10)

    surface = []
    unit = top[2] * wet_wide
    for f in range(2):
        value = top[f] + unit * wide[f]
        shift = LANES - (2 * levels * f + 1)
        value = one_pass(value, faces, near_o[0], shift)
        value = one_pass(value, faces, near_o[1], shift)
        surface.append(value[HALO : HALO + rows_all] * wet)
    for f in range(2):
        surface.append(
            (currents[f] + top[2, HALO : HALO + rows_all, :] * forcing[2 + f, HALO : HALO + rows_all, :]) * wet
        )
    high, low = split(jnp.concatenate(surface, 0))
    source = jnp.concatenate([high, low], 1)
    lane_t = iota((LANES, 4 * rows_all), 1)
    sub_t = iota((LANES, 4 * rows_all), 0)
    target = jnp.where(sub_t % 4 == lane_t // rows_all, lane_t % rows_all + 1, -1).astype(F32)
    for m in range(groups):
        chosen_rows = jnp.where(number_t[:, m : m + 1] == target, 1.0, 0.0).astype(BF16)
        rows = jnp.dot(chosen_rows, source, preferred_element_type=F32)
        rows = rows[:, 0:LANES] + rows[:, LANES : 2 * LANES]
        for g in range(group):
            sent[m * group + g] = rows[g * span : (g + 1) * span]
        at = pl.ds(m * group, group)
        stores += start_all([(sent.at[at], sent_h.at[at])], sent_sems, m)
    wait_all(stores)


def middle(capacity, levels, arrived, wide, currents, *columns):
    devices = arrived.shape[0]
    rows = currents.shape[2]
    tall = rows + 2 * HALO
    height = 4 * capacity
    return pl.pallas_call(
        functools.partial(middle_kernel, capacity, levels),
        out_shape=(
            pltpu.HBM((devices, height, LANES), F32),
            pltpu.HBM((4, tall, LANES), F32),
            pltpu.HBM((2, tall, LANES), F32),
            pltpu.HBM((4, tall, LANES), F32),
        ),
        in_specs=[vmem()] + [hbm()] * 2 + [pl.BlockSpec(memory_space=pl.ANY)] * 4,
        out_specs=(hbm(),) * 4,
        scratch_shapes=[
            pltpu.VMEM((4 * rows, 4 * capacity * devices), BF16),
            pltpu.VMEM((4 * capacity * devices, 2 * LANES), BF16),
            pltpu.VMEM((LANES, LANES), F32),
            pltpu.VMEM((5, tall, LANES), F32),
            pltpu.VMEM((2, rows, LANES), F32),
        ]
        + [pltpu.VMEM((2, tall, LANES), F32)] * 4
        + [
            pltpu.VMEM((4, tall, LANES), F32),
            pltpu.VMEM((8, tall, LANES), F32),
            pltpu.VMEM((devices, height, LANES), F32),
            pltpu.VMEM((4, tall, LANES), F32),
            pltpu.VMEM((2, tall, LANES), F32),
            pltpu.SemaphoreType.DMA((13,)),
            pltpu.SemaphoreType.DMA((4 * capacity * devices // LANES,)),
        ],
        compiler_params=pltpu.CompilerParams(vmem_limit_bytes=24 << 20),
        cost_estimate=pl.CostEstimate(flops=200 << 20, bytes_accessed=4 << 20, transcendentals=0),
    )(arrived, *pin(wide, currents), *columns)


def finish_kernel(
    levels, wide_h, currents_h, faces_h, forcing_h, near_h, ocean, wide, currents, faces, forcing, near, sems
):
    rows_all = currents.shape[2]
    wait_all(
        start_all(
            [(wide_h, wide), (currents_h, currents), (faces_h, faces), (forcing_h, forcing), (near_h, near)], sems
        )
    )
    inner = slice(HALO, HALO + rows_all)

    def level(l, carry):
        unit = wide[2 * levels + l]
        masked = unit * wide[3 * levels + 1]
        for f in range(2):
            value = wide[f * levels + l] + masked * forcing[f]
            shift = LANES - 1 - 2 * (levels * f + l)
            value = one_pass(value, faces, near[0], shift)
            value = one_pass(value, faces, near[1], shift)
            ocean[f, l] = value[inner]
            ocean[2 + f, l] = currents[f, l] + unit[inner] * forcing[2 + f][inner]
        return carry

    lax.fori_loop(0, levels, level, 0)


def finish(levels, wide, currents, faces, forcing, near):
    rows = currents.shape[2]
    return pl.pallas_call(
        functools.partial(finish_kernel, levels),
        out_shape=jax.ShapeDtypeStruct((4, levels, rows, LANES), F32),
        in_specs=[hbm()] * 5,
        out_specs=vmem(),
        scratch_shapes=[pltpu.VMEM(a.shape, F32) for a in (wide, currents, faces, forcing, near)]
        + [pltpu.SemaphoreType.DMA((5,))],
        compiler_params=pltpu.CompilerParams(vmem_limit_bytes=24 << 20),
        cost_estimate=pl.CostEstimate(flops=40 << 20, bytes_accessed=6 << 20, transcendentals=0),
    )(*pin(wide, currents, faces, forcing, near))


def turn_kernel(weights_h, turned_h, weights, turned, sems, out_sems):
    part_tiles = weights.shape[0] // PARTS
    parts = [pl.ds(n * part_tiles, part_tiles) for n in range(PARTS)]
    loads = start_all([(weights_h.at[at], weights.at[at]) for at in parts], sems)
    stores = []
    for n, at in enumerate(parts):
        loads[n].wait()

        def tile_step(t, carry):
            turned[t] = weights[t].T
            return carry

        lax.fori_loop(n * part_tiles, (n + 1) * part_tiles, tile_step, 0, unroll=4)
        stores += start_all([(turned.at[at], turned_h.at[at])], out_sems, n)
    wait_all(stores)


def turn(remap_weight):
    return pl.pallas_call(
        turn_kernel,
        out_shape=pltpu.HBM(remap_weight.shape, BF16),
        in_specs=[hbm()],
        out_specs=hbm(),
        scratch_shapes=[pltpu.VMEM(remap_weight.shape, BF16)] * 2 + [pltpu.SemaphoreType.DMA((PARTS,))] * 2,
        compiler_params=pltpu.CompilerParams(vmem_limit_bytes=24 << 20),
        cost_estimate=pl.CostEstimate(flops=8 << 20, bytes_accessed=8 << 20, transcendentals=0),
    )(*pin(remap_weight))


def remap_back_kernel(
    block_h, tile_h, field_h, wet_h, returned, tiles_h, weights_h, out,
    block_s, tile_s, field_s, wet_s, tiles, weights, picked_a, picked_b, total_0, total_1, total_2, total_3, sems, weight_sems,
):
    npairs = block_s.shape[0]
    totals = [total_0, total_1, total_2, total_3]
    nblocks = total_0.shape[0]
    scalars = start_all([(field_h, field_s), (wet_h, wet_s), (block_h, block_s), (tile_h, tile_s), (tiles_h, tiles)], sems)
    part_tiles = weights.shape[0] // PARTS
    parts = [pl.ds(n * part_tiles, part_tiles) for n in range(PARTS)]
    loads = start_all([(weights_h.at[at], weights.at[at]) for at in parts], weight_sems)
    for total in totals:
        total[...] = jnp.zeros_like(total)
    wait_all(scalars)

    def gather(p, picked, at):
        rows = returned[pl.ds(field_s[p], 4), :]
        mask = tiles[pl.ds(wet_s[p], 1), :].astype(F32)
        high, low = split(jnp.concatenate([rows, mask, jnp.zeros((3, LANES), F32)], 0))
        picked[at] = jnp.concatenate([high, low], 0)

    def product(p, picked, at, total):
        value = jnp.dot(picked[at], weights[tile_s[p]], preferred_element_type=F32)
        b = block_s[p]
        total[b] = total[b] + (value[0:8] + value[8:16])

    half = npairs // 2
    many = len(totals)

    def first(p, carry):
        gather(p, picked_a, p)
        return carry

    def both(p, carry):
        for n in range(many):
            gather(half + many * p + n, picked_b, many * p + n)
            product(many * p + n, picked_a, many * p + n, totals[n])
        return carry

    def last(p, carry):
        for n in range(many):
            product(half + many * p + n, picked_b, many * p + n, totals[n])
        return carry

    lax.fori_loop(0, half, first, 0, unroll=64)
    wait_all(loads)
    lax.fori_loop(0, half // many, both, 0, unroll=32)
    lax.fori_loop(0, half // many, last, 0, unroll=32)
    for b in range(nblocks):
        sums = (total_0[b] + total_1[b]) + (total_2[b] + total_3[b])
        out[:, b * LANES : (b + 1) * LANES] = sums[0:4] / jnp.maximum(sums[4:5], 0.1)


def remap_back(pair_block, pair_tile, field_at, wet_at, returned, tiles, weights, nblocks):
    npairs = pair_block.shape[0]
    return pl.pallas_call(
        remap_back_kernel,
        out_shape=jax.ShapeDtypeStruct((4, nblocks * LANES), F32),
        in_specs=[hbm()] * 4 + [vmem(), hbm(), hbm()],
        out_specs=vmem(),
        scratch_shapes=[pltpu.SMEM((npairs,), I32)] * 4
        + [pltpu.VMEM(tiles.shape, I32), pltpu.VMEM(weights.shape, BF16)]
        + [pltpu.VMEM((npairs // 2, 16, LANES), BF16)] * 2
        + [pltpu.VMEM((nblocks, 8, LANES), F32)] * 4
        + [pltpu.SemaphoreType.DMA((5,)), pltpu.SemaphoreType.DMA((PARTS,))],
        compiler_params=pltpu.CompilerParams(vmem_limit_bytes=24 << 20),
        cost_estimate=pl.CostEstimate(flops=2 * npairs * 16 * LANES * LANES, bytes_accessed=6 << 20, transcendentals=0),
    )(*pin(pair_block, pair_tile, field_at, wet_at), returned, *pin(tiles, weights))


def local(
    atm_state,
    pair_block,
    pair_owner,
    pair_row,
    pair_tile,
    remap_weight,
    wet_mask,
    ocean_state,
    vert_kappa,
    horiz_kappa,
):
    grid_x = lax.axis_size("gx")
    grid_y = lax.axis_size("gy")
    devices = grid_x * grid_y
    npairs = pair_block.shape[0]
    capacity = max(2, 2 * npairs // devices)
    levels, tile_rows, _ = vert_kappa.shape
    nblocks = atm_state.shape[1] // LANES
    owner = pair_owner.reshape(npairs)
    message = 4 * capacity + EDGE
    outgoing, field_at, wet_at = remap_out(
        capacity, grid_y, devices, tile_rows, atm_state, pair_block, owner, pair_row, pair_tile, remap_weight
    )
    arrived = lax.all_to_all(
        outgoing.reshape(devices, message, LANES), ("gx", "gy"), split_axis=0, concat_axis=0, tiled=True
    )
    tracer, currents, edge_up, edge_down = solve(ocean_state, vert_kappa, horiz_kappa, wet_mask)
    rise_x = [(i, i + 1) for i in range(grid_x - 1)]
    fall_x = [(b, a) for a, b in rise_x]
    rise_y = [(i, i + 1) for i in range(grid_y - 1)]
    fall_y = [(b, a) for a, b in rise_y]
    above = lax.ppermute(edge_down, "gx", rise_x)
    below = lax.ppermute(edge_up, "gx", fall_x)
    wide, to_left, to_right = pack(levels, tracer, above, below)
    from_left = lax.ppermute(to_right, "gy", rise_y)
    from_right = lax.ppermute(to_left, "gy", fall_y)
    line = wet_mask[None]
    step = 1
    here = lax.axis_index("gy")
    while step < grid_y:
        other = lax.ppermute(line, "gy", [(j, j ^ step) for j in range(grid_y)])
        lower = (here & step) == 0
        line = jnp.concatenate([jnp.where(lower, line, other), jnp.where(lower, other, line)], 0)
        step *= 2
    arrived, _ = lax.optimization_barrier((arrived, line))
    wet_all = lax.all_gather(line.reshape(-1, LANES), "gx", axis=0, tiled=True)
    sent, forcing, near, faces = middle(
        capacity, levels, arrived, wide, currents, to_left, to_right, from_left, from_right
    )
    returned = lax.all_to_all(sent, ("gx", "gy"), split_axis=0, concat_axis=0, tiled=True)
    ocean_next = finish(levels, wide, currents, faces, forcing, near)
    weights, _ = lax.optimization_barrier((remap_weight, near))
    atm_surface = remap_back(
        pair_block, pair_tile, field_at, wet_at, returned.reshape(-1, LANES), wet_all, turn(weights), nblocks
    )
    return (ocean_next, atm_surface)


def solution(mesh):
    placed = (
        P(None, ("gx", "gy")),
        P(("gx", "gy")),
        P(("gx", "gy"), None),
        P(("gx", "gy")),
        P(("gx", "gy")),
        P(("gx", "gy"), None, None),
        P("gx", "gy"),
        P(None, None, "gx", "gy"),
        P(None, "gx", "gy"),
        P("gx", "gy"),
    )
    return jax.shard_map(
        local,
        mesh=mesh,
        in_specs=placed,
        out_specs=(P(None, None, "gx", "gy"), P(None, ("gx", "gy"))),
        check_vma=False,
    )
```

```python
import functools

import jax
import jax.numpy as jnp
from jax import lax
from jax.experimental import pallas as pl
from jax.experimental.pallas import tpu as pltpu
from jax.sharding import PartitionSpec as P

F32 = jnp.float32
BF16 = jnp.bfloat16
I32 = jnp.int32
VMEM = pltpu.VMEM
SMEM = pltpu.SMEM
LANES = 128
EDGE = 16
HALO = 8
NUMBERS = 72
CORNERS = 112
SENDS = 8
AHEAD = 64
PARTS = 8


def hbm():
    return pl.BlockSpec(memory_space=pltpu.HBM)


def vmem():
    return pl.BlockSpec(memory_space=VMEM)


def pin(*arrays):
    return [pltpu.with_memory_space_constraint(a, pltpu.HBM) for a in arrays]


def start_all(pairs, sems, first=0):
    copies = [pltpu.make_async_copy(src, dst, sems.at[first + n]) for n, (src, dst) in enumerate(pairs)]
    for copy in copies:
        copy.start()
    return copies


def wait_all(copies):
    for copy in copies:
        copy.wait()


def iota(shape, dim):
    return lax.broadcasted_iota(I32, shape, dim)


def pick(mask, value):
    return jnp.where(mask, value, 0.0)


def split(value):
    high = value.astype(BF16)
    return high, (value - high.astype(F32)).astype(BF16)


def back_rows(capacity):
    return 4 * capacity + max(8, capacity)


def remap_out_kernel(
    capacity, grid_y, tile_rows, block_h, owner_h, row_h, tile_h, atm_h, weights_h, out_h, field_h, wet_h,
    out, block_s, owner_s, row_s, tile_s, rank_s, field_s, wet_s, atm, weights, atm_rows, flux_rows, flux, fill, rows_sum, cols_sum, rows_acc, cols_acc, sems, weight_sems, out_sems,
):
    devices = fill.shape[0]
    npairs = block_s.shape[0]
    tiles = weights.shape[0]
    nblocks = flux.shape[0]
    message = 4 * capacity + EDGE
    copies = [
        pltpu.make_async_copy(src, dst, sems.at[n])
        for n, (src, dst) in enumerate(
            [(atm_h, atm), (block_h, block_s), (owner_h, owner_s), (row_h, row_s), (tile_h, tile_s)]
        )
    ]
    for copy in copies:
        copy.start()
    part_tiles = tiles // PARTS
    parts = [pl.ds(n * part_tiles, part_tiles) for n in range(PARTS)]
    loads = [pltpu.make_async_copy(weights_h.at[at], weights.at[at], weight_sems.at[n]) for n, at in enumerate(parts)]
    for load in loads:
        load.start()
    out[...] = jnp.zeros_like(out)
    rows_sum[...] = jnp.zeros_like(rows_sum)
    cols_sum[...] = jnp.zeros_like(cols_sum)

    def clear_fill(i, carry):
        fill[i] = 0
        return carry

    lax.fori_loop(0, devices, clear_fill, 0, unroll=16)
    flux_rows[...] = jnp.zeros_like(flux_rows)
    wait_all(copies)
    for b in range(nblocks):
        atm_rows[8 * b : 8 * b + 6, :] = atm[:, b * LANES : (b + 1) * LANES]
    wind_u, wind_v, air, dry, rain, sea = [atm_rows[pl.ds(n, nblocks, stride=8), :] for n in range(6)]
    speed = jnp.sqrt(wind_u * wind_u + wind_v * wind_v + 0.25)
    heat = 0.5 * speed * (air - sea)
    water = rain - 0.3 * speed * dry
    planes = [heat, water, 0.2 * speed * wind_u, 0.2 * speed * wind_v]
    for n, plane in list(enumerate(planes)) + [(8 + n, heat) for n in range(4)] + [(12 + n, water) for n in range(4)]:
        flux_rows[pl.ds(n, nblocks, stride=16), :] = plane
    for b in range(nblocks):
        flux[b] = flux_rows[16 * b : 16 * (b + 1), :].astype(BF16)

    height = back_rows(capacity)


    def place(p):
        owner = owner_s[p]
        rank = fill[owner]
        fill[owner] = rank + 1
        field_s[p] = owner * height + 4 * rank
        wet_s[p] = owner * height + 4 * capacity + rank
        rank_s[p] = rank

    for p in range(AHEAD):
        place(p)
    wait_all(loads)

    sub = iota((8, LANES), 0)
    lane = iota((8, LANES), 1)
    part = sub % 4
    edge_row = jnp.where(part == 0, 0, jnp.where(part == 1, 1, tile_rows - 4 + part))
    band = ((lane - part) >> 2) * 4 + part
    id_rank = jnp.where(sub == 0, lane - NUMBERS, -1)

    def pair(p, n):
        owner = owner_s[p]
        row = row_s[p]
        rank = rank_s[p]
        value = jnp.dot(flux[block_s[p]], weights[tile_s[p]], preferred_element_type=F32)
        out[pl.ds(owner * message + 4 * rank, 4), :] = value[0:4]
        tracer = value[8:16]
        rows_sum[n, owner] = rows_sum[n, owner] + pick(edge_row == row, tracer)
        number = (row + 1).astype(F32)
        cols_sum[n, owner] = cols_sum[n, owner] + (
            pick(band == row, pltpu.roll(tracer, row + 2, 1)) + pick(id_rank == rank, number)
        )

    many = rows_sum.shape[0]

    def pairs(more, k, carry):
        for n in range(many):
            p = many * k + n
            if more:
                place(p + AHEAD)
            pair(p, n)
        return carry

    lax.fori_loop(0, (npairs - AHEAD) // many, functools.partial(pairs, True), 0, unroll=AHEAD // many)
    stores = start_all([(field_s, field_h), (wet_s, wet_h)], out_sems, SENDS)
    lax.fori_loop((npairs - AHEAD) // many, npairs // many, functools.partial(pairs, False), 0, unroll=AHEAD // many)

    def owner_step(d, carry):
        rows_acc[d] = (rows_sum[0, d] + rows_sum[1, d]) + (rows_sum[2, d] + rows_sum[3, d])
        cols_acc[d] = (cols_sum[0, d] + cols_sum[1, d]) + (cols_sum[2, d] + cols_sum[3, d])
        return carry

    lax.fori_loop(0, devices, owner_step, 0, unroll=8)

    grid_x = devices // grid_y
    zero = jnp.zeros((8, LANES), F32)

    def columns_of(i, j):
        if not (0 <= i < grid_x and 0 <= j < grid_y):
            return zero
        return cols_acc[i * grid_y + j]

    from_left = (lane - sub) % 4 < 2
    in_band = lane < tile_rows + 4
    in_ids = (sub == 0) & (lane >= NUMBERS) & (lane < NUMBERS + capacity)
    last, first = part == 3, part == 0
    send = devices // SENDS
    for d in range(devices):
        i, j = d // grid_y, d % grid_y
        below = rows_acc[d + grid_y] if i < grid_x - 1 else zero
        above = rows_acc[d - grid_y] if i > 0 else zero
        base = d * message + 4 * capacity
        out[base : base + 8, :] = jnp.where(part < 2, below, above)
        tile = pick(in_band, jnp.where(from_left, columns_of(i, j - 1), columns_of(i, j + 1)))
        upper = pick(last & (lane == tile_rows), columns_of(i - 1, j - 1))
        upper = upper + pick(last & (lane == tile_rows + 1), columns_of(i - 1, j + 1))
        lower = pick(first & (lane == 1), columns_of(i + 1, j - 1))
        lower = lower + pick(first & (lane == 2), columns_of(i + 1, j + 1))
        tile = tile + pltpu.roll(upper, CORNERS - tile_rows, 1) + pltpu.roll(lower, CORNERS + 1, 1)
        tile = tile + pick(in_ids, cols_acc[d])
        out[base + 8 : base + 16, :] = tile
        if d % send == send - 1:
            n = d // send
            at = pl.ds(n * send * message, send * message)
            stores.append(pltpu.make_async_copy(out.at[at], out_h.at[at], out_sems.at[n]))
            stores[-1].start()
    for store in stores:
        store.wait()


def remap_out(capacity, grid_y, devices, tile_rows, atm_state, pair_block, owner, pair_row, pair_tile, remap_weight):
    npairs = pair_block.shape[0]
    nblocks = atm_state.shape[1] // LANES
    message = 4 * capacity + EDGE
    return pl.pallas_call(
        functools.partial(remap_out_kernel, capacity, grid_y, tile_rows),
        out_shape=(
            pltpu.HBM((devices * message, LANES), F32),
            pltpu.HBM((npairs,), I32),
            pltpu.HBM((npairs,), I32),
        ),
        in_specs=[hbm()] * 6,
        out_specs=(hbm(),) * 3,
        scratch_shapes=[pltpu.VMEM((devices * message, LANES), F32)]
        + [pltpu.SMEM((npairs,), I32)] * 7
        + [
            pltpu.VMEM(atm_state.shape, F32),
            pltpu.VMEM(remap_weight.shape, BF16),
            pltpu.VMEM((nblocks * 8, LANES), F32),
            pltpu.VMEM((nblocks * 16, LANES), F32),
            pltpu.VMEM((nblocks, 16, LANES), BF16),
            pltpu.SMEM((devices,), I32),
            pltpu.VMEM((4, devices, 8, LANES), F32),
            pltpu.VMEM((4, devices, 8, LANES), F32),
            pltpu.VMEM((devices, 8, LANES), F32),
            pltpu.VMEM((devices, 8, LANES), F32),
            pltpu.SemaphoreType.DMA((5,)),
            pltpu.SemaphoreType.DMA((PARTS,)),
            pltpu.SemaphoreType.DMA((SENDS + 2,)),
        ],
        compiler_params=pltpu.CompilerParams(vmem_limit_bytes=40 << 20),
        cost_estimate=pl.CostEstimate(
            flops=2 * npairs * 16 * LANES * LANES, bytes_accessed=6 << 20, transcendentals=0
        ),
    )(*pin(pair_block, owner, pair_row, pair_tile, atm_state, remap_weight))


def solve_kernel(state, kappa, horiz, wet, tracer, currents_h, edge_up, edge_down, currents, sems):
    levels = kappa.shape[0]
    rows_all = kappa.shape[1]
    planes = tracer.shape[0]

    def chunk(c, carry):
        rows = pl.ds(pl.multiple_of(c * 8, 8), 8)
        column = [kappa[l, rows, :] for l in range(levels)]
        face = [0.5 * (column[l] + column[l + 1]) for l in range(levels - 1)]
        upper = []
        now = None
        for l in range(levels):
            diagonal = 1.0
            if l > 0:
                diagonal = diagonal + face[l - 1]
            if l < levels - 1:
                diagonal = diagonal + face[l]
            if l > 0:
                diagonal = diagonal + face[l - 1] * upper[-1]
            inverse = 1.0 / diagonal
            if l == 0:
                now = [state[f, 0, rows, :] * inverse for f in range(4)] + [inverse]
            else:
                pull = face[l - 1] * inverse
                now = [state[f, l, rows, :] * inverse + pull * now[f] for f in range(4)] + [pull * now[4]]
            upper.append(-face[l] * inverse if l < levels - 1 else None)
            store(l, rows, now)
        for l in range(levels - 2, -1, -1):
            here = load(l, rows)
            now = [here[f] - upper[l] * now[f] for f in range(5)]
            store(l, rows, now)
        return carry

    def store(l, rows, now):
        tracer[l, rows, :] = now[0]
        tracer[levels + l, rows, :] = now[1]
        currents[0, l, rows, :] = now[2]
        currents[1, l, rows, :] = now[3]
        tracer[2 * levels + l, rows, :] = now[4]

    def load(l, rows):
        return [
            tracer[l, rows, :],
            tracer[levels + l, rows, :],
            currents[0, l, rows, :],
            currents[1, l, rows, :],
            tracer[2 * levels + l, rows, :],
        ]

    lax.fori_loop(0, rows_all // 8, chunk, 0)
    out = start_all([(currents, currents_h)], sems)
    tracer[3 * levels] = horiz[...]
    tracer[3 * levels + 1] = wet[...].astype(F32)
    for k in range(planes):
        edge_up[k] = tracer[k, 0:8, :]
        edge_down[k] = tracer[k, rows_all - 8 : rows_all, :]
    wait_all(out)


def solve(ocean_state, vert_kappa, horiz_kappa, wet_mask):
    levels, rows, _ = vert_kappa.shape
    planes = 3 * levels + 2
    return pl.pallas_call(
        solve_kernel,
        out_shape=(
            jax.ShapeDtypeStruct((planes, rows, LANES), F32),
            pltpu.HBM((2, levels, rows, LANES), F32),
            jax.ShapeDtypeStruct((planes, 8, LANES), F32),
            jax.ShapeDtypeStruct((planes, 8, LANES), F32),
        ),
        in_specs=[vmem()] * 4,
        out_specs=(vmem(), hbm(), vmem(), vmem()),
        scratch_shapes=[pltpu.VMEM((2, levels, rows, LANES), F32), pltpu.SemaphoreType.DMA((1,))],
        compiler_params=pltpu.CompilerParams(vmem_limit_bytes=24 << 20),
        cost_estimate=pl.CostEstimate(flops=20 << 20, bytes_accessed=6 << 20, transcendentals=0),
    )(ocean_state, vert_kappa, horiz_kappa, wet_mask)


def pack_kernel(levels, tracer, above, below, wide_h, to_left, to_right, wide, sems):
    planes, rows, _ = tracer.shape
    for k in range(planes):
        wide[k, 0:HALO, :] = above[k]
        wide[k, HALO : HALO + rows, :] = tracer[k]
        wide[k, HALO + rows : 2 * HALO + rows, :] = below[k]
    out = start_all([(wide, wide_h)], sems)
    lane = iota((8, LANES), 1)

    def chunk(c, carry):
        at = pl.ds(pl.multiple_of(c * 8, 8), 8)

        def place(values, lanes):
            left, right = jnp.zeros((8, LANES), F32), jnp.zeros((8, LANES), F32)
            for k, (near, far) in zip(values, lanes):
                value = wide[k, at, :]
                left = jnp.where(lane == near, pltpu.roll(value, near, 1), left)
                left = jnp.where(lane == far, pltpu.roll(value, far - 1, 1), left)
                right = jnp.where(lane == near + 1, pltpu.roll(value, (near + 2) % LANES, 1), right)
                right = jnp.where(lane == far + 1, pltpu.roll(value, (far + 3) % LANES, 1), right)
            return left, right

        left, right = place(range(2 * levels), [(2 * k, 64 + 2 * k) for k in range(2 * levels)])
        to_left[0, at, :] = left
        to_right[0, at, :] = right
        lanes = [(2 * l, 64 + 2 * l) for l in range(levels)]
        lanes += [(2 * levels, 2 * levels + 2), (2 * levels + 4, 2 * levels + 6)]
        left, right = place(range(2 * levels, 3 * levels + 2), lanes)
        to_left[1, at, :] = left
        to_right[1, at, :] = right
        return carry

    lax.fori_loop(0, (rows + 2 * HALO) // 8, chunk, 0)
    wait_all(out)


def pack(levels, tracer, above, below):
    planes, rows, _ = tracer.shape
    tall = rows + 2 * HALO
    return pl.pallas_call(
        functools.partial(pack_kernel, levels),
        out_shape=(
            pltpu.HBM((planes, tall, LANES), F32),
            jax.ShapeDtypeStruct((2, tall, LANES), F32),
            jax.ShapeDtypeStruct((2, tall, LANES), F32),
        ),
        in_specs=[vmem()] * 3,
        out_specs=(hbm(), vmem(), vmem()),
        scratch_shapes=[pltpu.VMEM((planes, tall, LANES), F32), pltpu.SemaphoreType.DMA((1,))],
        compiler_params=pltpu.CompilerParams(vmem_limit_bytes=24 << 20),
        cost_estimate=pl.CostEstimate(flops=8 << 20, bytes_accessed=4 << 20, transcendentals=0),
    )(tracer, above, below)


def set_faces(levels, h, w, own_left, own_right, from_left, from_right, faces, packed):
    tall = h.shape[0]
    lane = iota((tall, LANES), 1)
    odd = lane % 2 == 1
    twice = lane % 64 < 2 * levels
    left, left_unit, right, right_unit = from_left[0], from_left[1], from_right[0], from_right[1]
    other = jnp.where(odd, left_unit, right_unit)
    at = 2 * levels

    def column(offset):
        return other[:, at + offset : at + offset + 1], other[:, at + offset + 1 : at + offset + 2]

    kappa_right, kappa_left = column(0)
    kappa_far_right, kappa_far_left = column(2)
    wet_right, wet_left = column(4)
    wet_far_right, wet_far_left = column(6)

    kappa_near = jnp.where(odd, kappa_left, kappa_right)
    kappa_far = jnp.where(odd, kappa_far_left, kappa_far_right)
    wet_near = jnp.where(odd, wet_left, wet_right)
    wet_far = jnp.where(odd, wet_far_left, wet_far_right)
    kappa_own = jnp.where(odd, h[:, 0:1], h[:, LANES - 1 : LANES])
    wet_own = jnp.where(odd, w[:, 0:1], w[:, LANES - 1 : LANES])

    def face(kappa_a, wet_a, kappa_b, wet_b):
        return 0.25 * (kappa_a + kappa_b) * wet_a * wet_b

    unit = jnp.where(twice, other, pltpu.roll(other, 2 * levels, 1))
    packed[0] = jnp.where(odd, left, right)
    packed[1] = unit * jnp.where(lane < 64, wet_near, wet_far)
    left, left_unit, right, right_unit = own_left[0], own_left[1], own_right[0], own_right[1]
    packed[2] = jnp.where(odd, pltpu.roll(left, 1, 1), pltpu.roll(right, LANES - 1, 1))
    own = jnp.where(odd, pltpu.roll(left_unit, 1, 1), pltpu.roll(right_unit, LANES - 1, 1))
    packed[3] = jnp.where(twice, own, pltpu.roll(own, 2 * levels, 1)) * wet_own
    north = face(kappa_near, wet_near, pltpu.roll(kappa_near, 1, 0), pltpu.roll(wet_near, 1, 0))
    packed[4] = north
    packed[5] = pltpu.roll(north, tall - 1, 0)
    packed[6] = face(kappa_near, wet_near, kappa_far, wet_far)
    packed[7] = face(kappa_near, wet_near, kappa_own, wet_own)

    north = face(h, w, pltpu.roll(h, 1, 0), pltpu.roll(w, 1, 0))
    faces[0] = north
    faces[1] = pltpu.roll(north, tall - 1, 0)
    west = face(
        h, w, jnp.where(lane == 0, kappa_left, pltpu.roll(h, 1, 1)), jnp.where(lane == 0, wet_left, pltpu.roll(w, 1, 1))
    )
    faces[2] = west
    faces[3] = jnp.where(lane == LANES - 1, face(h, w, kappa_right, wet_right), pltpu.roll(west, LANES - 1, 1))


def set_beside(levels, upright, wide, packed, beside):
    tall = upright.shape[0]
    lane = iota((tall, LANES), 1)
    odd = lane % 2 == 1
    heat = lane % 64 < 2 * levels

    def chosen(f):
        left_far, left_near, right_near, right_far = [upright[:, 4 * f + e : 4 * f + e + 1] for e in range(4)]
        near = jnp.where(odd, left_near, right_near)
        return jnp.where(lane < 64, near, jnp.where(odd, left_far, right_far))

    both = packed[0] + packed[1] * jnp.where(heat, chosen(0), chosen(1))
    far = pltpu.roll(both, 64, 1)
    ends_of = [jnp.where(odd, w[:, 0:1], w[:, LANES - 1 : LANES]) for w in wide]
    own = packed[2] + packed[3] * jnp.where(heat, ends_of[0], ends_of[1])
    near = both + packed[5] * (pltpu.roll(both, tall - 1, 0) - both)
    near = near + packed[4] * (pltpu.roll(both, 1, 0) - both)
    near = near + packed[6] * (far - both)
    near = near + packed[7] * (own - both)
    beside[0] = both
    beside[1] = near


def one_pass(value, faces, beside, shift):
    tall = value.shape[0]
    lane = iota(value.shape, 1)
    moved = pltpu.roll(beside, shift, 1)
    west = jnp.where(lane == 0, moved, pltpu.roll(value, 1, 1))
    east = jnp.where(lane == LANES - 1, moved, pltpu.roll(value, LANES - 1, 1))
    result = value + faces[1] * (pltpu.roll(value, tall - 1, 0) - value)
    result = result + faces[0] * (pltpu.roll(value, 1, 0) - value)
    result = result + faces[3] * (east - value)
    return result + faces[2] * (west - value)


def middle_kernel(
    capacity, levels, arrived, wide_h, currents_h, own_left_h, own_right_h, from_left_h, from_right_h,
    sent_h, forcing_h, near_h, faces_h,
    placing, values, number_t, top, currents, own_left, own_right, from_left, from_right,
    faces, packed, sent, forcing, near_o, sems, sent_sems,
):
    devices, message, _ = arrived.shape
    rows_all = currents.shape[1]
    tall = rows_all + 2 * HALO
    loads = start_all(
        [(wide_h.at[levels * k], top.at[k]) for k in range(3)]
        + [
            (wide_h.at[pl.ds(3 * levels, 2)], top.at[pl.ds(3, 2)]),
            (currents_h.at[0, 0], currents.at[0]),
            (currents_h.at[1, 0], currents.at[1]),
            (own_left_h, own_left),
            (own_right_h, own_right),
            (from_left_h, from_left),
            (from_right_h, from_right),
        ],
        sems,
    )
    span = 4 * capacity
    group = LANES // span
    groups = devices // group
    sub8 = iota((8, LANES), 0)
    lane8 = iota((8, LANES), 1)

    lane1 = iota((1, LANES), 1)
    spread = (iota((LANES, LANES), 0) - NUMBERS) == iota((LANES, LANES), 1) % span // 4
    every = jnp.concatenate([arrived[s, span + 8 : span + 9, :] for s in range(devices)], 0).astype(BF16)
    every = jnp.dot(every, jnp.where(spread, 1.0, 0.0).astype(BF16), preferred_element_type=F32)
    numbers = []
    for m in range(groups):
        line = jnp.zeros((1, LANES), F32)
        for g in range(group):
            s = m * group + g
            line = jnp.where(lane1 // span == g, every[s : s + 1], line)
        numbers.append(line)
    number_t[...] = jnp.transpose(
        jnp.concatenate(numbers + [jnp.zeros((LANES - groups, LANES), F32)], 0)
    )

    row_number = iota((rows_all, LANES), 0).astype(F32) + 1.0
    for m in range(groups):
        for f in range(4):
            placing[f * rows_all : (f + 1) * rows_all, m * LANES : (m + 1) * LANES] = jnp.where(
                pick(lane1 % 4 == f, numbers[m]) == row_number, 1.0, 0.0
            ).astype(BF16)
    edge_rows = jnp.zeros((8, LANES), F32)
    edge_cols = jnp.zeros((8, LANES), F32)
    for s in range(devices):
        high, low = split(arrived[s, 0:span, :])
        values[s * span : (s + 1) * span, 0:LANES] = high
        values[s * span : (s + 1) * span, LANES : 2 * LANES] = low
        edge_rows = edge_rows + arrived[s, span : span + 8, :]
        edge_cols = edge_cols + arrived[s, span + 8 : span + 16, :]
    wait_all(loads)
    set_faces(levels, top[3], top[4], own_left, own_right, from_left, from_right, faces, packed)
    wet_wide = top[4]
    total = jnp.dot(placing[...], values[...], preferred_element_type=F32)
    total = total[:, 0:LANES] + total[:, LANES : 2 * LANES]


    def plane(f):
        return total[f * rows_all : (f + 1) * rows_all]

    wide = []
    for f in range(2):
        before = pick(sub8 >= 6, edge_rows if f == 1 else pltpu.roll(edge_rows, 4, 0))
        after = pick(sub8 < 2, edge_rows if f == 0 else pltpu.roll(edge_rows, 4, 0))
        wide.append(jnp.concatenate([before, plane(f), after], 0))
        forcing[f] = wide[f]
    wet = wet_wide[HALO : HALO + rows_all]
    for f in range(2, 4):
        forcing[f, 0:HALO, :] = jnp.zeros((HALO, LANES), F32)
        forcing[f, HALO : HALO + rows_all, :] = plane(f) * wet
        forcing[f, HALO + rows_all : tall, :] = jnp.zeros((HALO, LANES), F32)

    part8 = sub8 % 4
    within = (part8 == lane8 % 4) & (lane8 >= HALO) & (lane8 < HALO + rows_all)
    upper = (part8 == 3) & (lane8 == HALO - 1)
    lower = (part8 == 0) & (lane8 == HALO + rows_all)
    halves = [[], []]
    for k in range(4):
        column = pick(within, pltpu.roll(edge_cols, HALO - k, 1))
        if k in (1, 2):
            column = column + pick(upper, pltpu.roll(edge_cols, (HALO - CORNERS - k) % LANES, 1))
            column = column + pick(lower, pltpu.roll(edge_cols, (HALO + rows_all - CORNERS - 1 - k) % LANES, 1))
        for f in range(2):
            halves[f].append(jnp.sum(column[4 * f : 4 * f + 4], axis=0, keepdims=True))
    columns = jnp.concatenate(halves[0] + halves[1], 0)
    upright = jnp.transpose(jnp.concatenate([columns, jnp.zeros((LANES - 8, LANES), F32)], 0))[0:tall]
    set_beside(levels, upright, wide, packed, near_o)
    stores = start_all([(forcing, forcing_h), (near_o, near_h), (faces, faces_h)], sems, 10)

    surface = []
    unit = top[2] * wet_wide
    for f in range(2):
        value = top[f] + unit * wide[f]
        shift = LANES - (2 * levels * f + 1)
        value = one_pass(value, faces, near_o[0], shift)
        value = one_pass(value, faces, near_o[1], shift)
        surface.append(value[HALO : HALO + rows_all] * wet)
    for f in range(2):
        surface.append(
            (currents[f] + top[2, HALO : HALO + rows_all, :] * forcing[2 + f, HALO : HALO + rows_all, :]) * wet
        )
    high, low = split(jnp.concatenate(surface, 0))
    source = jnp.concatenate([high, low], 1)
    lane_t = iota((LANES, 4 * rows_all), 1)
    sub_t = iota((LANES, 4 * rows_all), 0)
    target = jnp.where(sub_t % 4 == lane_t // rows_all, lane_t % rows_all + 1, -1).astype(F32)
    mask = jnp.concatenate([wet, jnp.zeros((LANES - rows_all, LANES), F32)], 0).astype(BF16)
    per = LANES // 4
    slot_number = number_t[pl.ds(0, per, stride=4), :]
    lane_s = (iota((per, LANES), 1) + 1).astype(F32)
    height = back_rows(capacity)
    many = 4
    for first in range(0, groups, many):
        these = range(first, first + many)
        chosen_rows = [jnp.where(number_t[:, m : m + 1] == target, 1.0, 0.0).astype(BF16) for m in these]
        rows = jnp.dot(jnp.concatenate(chosen_rows, 0), source, preferred_element_type=F32)
        rows = rows[:, 0:LANES] + rows[:, LANES : 2 * LANES]
        slots = [jnp.where(slot_number[:, m : m + 1] == lane_s, 1.0, 0.0) for m in these]
        masks = jnp.dot(jnp.concatenate(slots, 0).astype(BF16), mask, preferred_element_type=F32)
        for g in range(many * group):
            s = first * group + g
            sent[s, 0:span, :] = rows[g * span : (g + 1) * span]
            sent[s, span : span + capacity, :] = masks[g * capacity : (g + 1) * capacity]
            if height > span + capacity:
                sent[s, span + capacity : height, :] = jnp.zeros((height - span - capacity, LANES), F32)
        at = pl.ds(first * group, many * group)
        stores += start_all([(sent.at[at], sent_h.at[at])], sent_sems, first // many)
    wait_all(stores)


def middle(capacity, levels, arrived, wide, currents, *columns):
    devices = arrived.shape[0]
    rows = currents.shape[2]
    tall = rows + 2 * HALO
    height = back_rows(capacity)
    return pl.pallas_call(
        functools.partial(middle_kernel, capacity, levels),
        out_shape=(
            pltpu.HBM((devices, height, LANES), F32),
            pltpu.HBM((4, tall, LANES), F32),
            pltpu.HBM((2, tall, LANES), F32),
            pltpu.HBM((4, tall, LANES), F32),
        ),
        in_specs=[vmem()] + [hbm()] * 2 + [pl.BlockSpec(memory_space=pl.ANY)] * 4,
        out_specs=(hbm(),) * 4,
        scratch_shapes=[
            pltpu.VMEM((4 * rows, 4 * capacity * devices), BF16),
            pltpu.VMEM((4 * capacity * devices, 2 * LANES), BF16),
            pltpu.VMEM((LANES, LANES), F32),
            pltpu.VMEM((5, tall, LANES), F32),
            pltpu.VMEM((2, rows, LANES), F32),
        ]
        + [pltpu.VMEM((2, tall, LANES), F32)] * 4
        + [
            pltpu.VMEM((4, tall, LANES), F32),
            pltpu.VMEM((8, tall, LANES), F32),
            pltpu.VMEM((devices, height, LANES), F32),
            pltpu.VMEM((4, tall, LANES), F32),
            pltpu.VMEM((2, tall, LANES), F32),
            pltpu.SemaphoreType.DMA((13,)),
            pltpu.SemaphoreType.DMA((4 * capacity * devices // LANES,)),
        ],
        compiler_params=pltpu.CompilerParams(vmem_limit_bytes=24 << 20),
        cost_estimate=pl.CostEstimate(flops=200 << 20, bytes_accessed=4 << 20, transcendentals=0),
    )(arrived, *pin(wide, currents), *columns)


def finish_kernel(
    levels, wide_h, currents_h, faces_h, forcing_h, near_h, ocean, wide, currents, faces, forcing, near, sems
):
    rows_all = currents.shape[2]
    wait_all(
        start_all(
            [(wide_h, wide), (currents_h, currents), (faces_h, faces), (forcing_h, forcing), (near_h, near)], sems
        )
    )
    inner = slice(HALO, HALO + rows_all)

    def level(l, carry):
        unit = wide[2 * levels + l]
        masked = unit * wide[3 * levels + 1]
        for f in range(2):
            value = wide[f * levels + l] + masked * forcing[f]
            shift = LANES - 1 - 2 * (levels * f + l)
            value = one_pass(value, faces, near[0], shift)
            value = one_pass(value, faces, near[1], shift)
            ocean[f, l] = value[inner]
            ocean[2 + f, l] = currents[f, l] + unit[inner] * forcing[2 + f][inner]
        return carry

    lax.fori_loop(0, levels, level, 0)


def finish(levels, wide, currents, faces, forcing, near):
    rows = currents.shape[2]
    return pl.pallas_call(
        functools.partial(finish_kernel, levels),
        out_shape=jax.ShapeDtypeStruct((4, levels, rows, LANES), F32),
        in_specs=[hbm()] * 5,
        out_specs=vmem(),
        scratch_shapes=[pltpu.VMEM(a.shape, F32) for a in (wide, currents, faces, forcing, near)]
        + [pltpu.SemaphoreType.DMA((5,))],
        compiler_params=pltpu.CompilerParams(vmem_limit_bytes=24 << 20),
        cost_estimate=pl.CostEstimate(flops=40 << 20, bytes_accessed=6 << 20, transcendentals=0),
    )(*pin(wide, currents, faces, forcing, near))


def turn_kernel(weights_h, turned_h, weights, turned, sems, out_sems):
    part_tiles = weights.shape[0] // PARTS
    parts = [pl.ds(n * part_tiles, part_tiles) for n in range(PARTS)]
    loads = start_all([(weights_h.at[at], weights.at[at]) for at in parts], sems)
    stores = []
    for n, at in enumerate(parts):
        loads[n].wait()

        def tile_step(t, carry):
            turned[t] = weights[t].T
            return carry

        lax.fori_loop(n * part_tiles, (n + 1) * part_tiles, tile_step, 0, unroll=4)
        stores += start_all([(turned.at[at], turned_h.at[at])], out_sems, n)
    wait_all(stores)


def turn(remap_weight):
    return pl.pallas_call(
        turn_kernel,
        out_shape=pltpu.HBM(remap_weight.shape, BF16),
        in_specs=[hbm()],
        out_specs=hbm(),
        scratch_shapes=[pltpu.VMEM(remap_weight.shape, BF16)] * 2 + [pltpu.SemaphoreType.DMA((PARTS,))] * 2,
        compiler_params=pltpu.CompilerParams(vmem_limit_bytes=24 << 20),
        cost_estimate=pl.CostEstimate(flops=8 << 20, bytes_accessed=8 << 20, transcendentals=0),
    )(*pin(remap_weight))


def remap_back_kernel(
    block_h, tile_h, field_h, wet_h, returned, weights_h, out,
    block_s, tile_s, field_s, wet_s, weights, picked_a, picked_b, total_0, total_1, total_2, total_3, sems, weight_sems,
):
    npairs = block_s.shape[0]
    totals = [total_0, total_1, total_2, total_3]
    nblocks = total_0.shape[0]
    scalars = start_all([(field_h, field_s), (wet_h, wet_s), (block_h, block_s), (tile_h, tile_s)], sems)
    part_tiles = weights.shape[0] // PARTS
    parts = [pl.ds(n * part_tiles, part_tiles) for n in range(PARTS)]
    loads = start_all([(weights_h.at[at], weights.at[at]) for at in parts], weight_sems)
    for total in totals:
        total[...] = jnp.zeros_like(total)
    wait_all(scalars)

    def gather(p, picked, at):
        rows = returned[pl.ds(field_s[p], 4), :]
        mask = returned[pl.ds(wet_s[p] - 7, 8), :]
        high, low = split(jnp.concatenate([rows, jnp.zeros((3, LANES), F32), mask[7:8]], 0))
        picked[at] = jnp.concatenate([high, low], 0)

    def product(p, picked, at, total):
        value = jnp.dot(picked[at], weights[tile_s[p]], preferred_element_type=F32)
        b = block_s[p]
        total[b] = total[b] + (value[0:8] + value[8:16])

    half = npairs // 2
    many = len(totals)

    def first(p, carry):
        gather(p, picked_a, p)
        return carry

    def both(p, carry):
        for n in range(many):
            gather(half + many * p + n, picked_b, many * p + n)
            product(many * p + n, picked_a, many * p + n, totals[n])
        return carry

    def last(p, carry):
        for n in range(many):
            product(half + many * p + n, picked_b, many * p + n, totals[n])
        return carry

    lax.fori_loop(0, half, first, 0, unroll=64)
    wait_all(loads)
    lax.fori_loop(0, half // many, both, 0, unroll=32)
    lax.fori_loop(0, half // many, last, 0, unroll=32)
    for b in range(nblocks):
        sums = (total_0[b] + total_1[b]) + (total_2[b] + total_3[b])
        out[:, b * LANES : (b + 1) * LANES] = sums[0:4] / jnp.maximum(sums[7:8], 0.1)


def remap_back(pair_block, pair_tile, field_at, wet_at, returned, weights, nblocks):
    npairs = pair_block.shape[0]
    return pl.pallas_call(
        remap_back_kernel,
        out_shape=jax.ShapeDtypeStruct((4, nblocks * LANES), F32),
        in_specs=[hbm()] * 4 + [vmem(), hbm()],
        out_specs=vmem(),
        scratch_shapes=[pltpu.SMEM((npairs,), I32)] * 4
        + [pltpu.VMEM(weights.shape, BF16)]
        + [pltpu.VMEM((npairs // 2, 16, LANES), BF16)] * 2
        + [pltpu.VMEM((nblocks, 8, LANES), F32)] * 4
        + [pltpu.SemaphoreType.DMA((4,)), pltpu.SemaphoreType.DMA((PARTS,))],
        compiler_params=pltpu.CompilerParams(vmem_limit_bytes=24 << 20),
        cost_estimate=pl.CostEstimate(flops=2 * npairs * 16 * LANES * LANES, bytes_accessed=6 << 20, transcendentals=0),
    )(*pin(pair_block, pair_tile, field_at, wet_at), returned, *pin(weights))


def local(
    atm_state,
    pair_block,
    pair_owner,
    pair_row,
    pair_tile,
    remap_weight,
    wet_mask,
    ocean_state,
    vert_kappa,
    horiz_kappa,
):
    grid_x = lax.axis_size("gx")
    grid_y = lax.axis_size("gy")
    devices = grid_x * grid_y
    npairs = pair_block.shape[0]
    capacity = max(2, 2 * npairs // devices)
    levels, tile_rows, _ = vert_kappa.shape
    nblocks = atm_state.shape[1] // LANES
    owner = pair_owner.reshape(npairs)
    message = 4 * capacity + EDGE
    outgoing, field_at, wet_at = remap_out(
        capacity, grid_y, devices, tile_rows, atm_state, pair_block, owner, pair_row, pair_tile, remap_weight
    )
    arrived = lax.all_to_all(
        outgoing.reshape(devices, message, LANES), ("gx", "gy"), split_axis=0, concat_axis=0, tiled=True
    )
    tracer, currents, edge_up, edge_down = solve(ocean_state, vert_kappa, horiz_kappa, wet_mask)
    rise_x = [(i, i + 1) for i in range(grid_x - 1)]
    fall_x = [(b, a) for a, b in rise_x]
    rise_y = [(i, i + 1) for i in range(grid_y - 1)]
    fall_y = [(b, a) for a, b in rise_y]
    above = lax.ppermute(edge_down, "gx", rise_x)
    below = lax.ppermute(edge_up, "gx", fall_x)
    wide, to_left, to_right = pack(levels, tracer, above, below)
    from_left = lax.ppermute(to_right, "gy", rise_y)
    from_right = lax.ppermute(to_left, "gy", fall_y)
    sent, forcing, near, faces = middle(
        capacity, levels, arrived, wide, currents, to_left, to_right, from_left, from_right
    )
    returned = lax.all_to_all(sent, ("gx", "gy"), split_axis=0, concat_axis=0, tiled=True)
    ocean_next = finish(levels, wide, currents, faces, forcing, near)
    weights, _ = lax.optimization_barrier((remap_weight, near))
    atm_surface = remap_back(
        pair_block, pair_tile, field_at, wet_at, returned.reshape(-1, LANES), turn(weights), nblocks
    )
    return (ocean_next, atm_surface)


def solution(mesh):
    placed = (
        P(None, ("gx", "gy")),
        P(("gx", "gy")),
        P(("gx", "gy"), None),
        P(("gx", "gy")),
        P(("gx", "gy")),
        P(("gx", "gy"), None, None),
        P("gx", "gy"),
        P(None, None, "gx", "gy"),
        P(None, "gx", "gy"),
        P("gx", "gy"),
    )
    return jax.shard_map(
        local,
        mesh=mesh,
        in_specs=placed,
        out_specs=(P(None, None, "gx", "gy"), P(None, ("gx", "gy"))),
        check_vma=False,
    )
```

```python
import functools

import jax
import jax.numpy as jnp
from jax import lax
from jax.experimental import pallas as pl
from jax.experimental.pallas import tpu as pltpu
from jax.sharding import PartitionSpec as P

F32 = jnp.float32
BF16 = jnp.bfloat16
I32 = jnp.int32
VMEM = pltpu.VMEM
SMEM = pltpu.SMEM
LANES = 128
EDGE = 16
HALO = 8
NUMBERS = 72
CORNERS = 112
SENDS = 8
AHEAD = 64
PARTS = 8


def hbm():
    return pl.BlockSpec(memory_space=pltpu.HBM)


def vmem():
    return pl.BlockSpec(memory_space=VMEM)


def pin(*arrays):
    return [pltpu.with_memory_space_constraint(a, pltpu.HBM) for a in arrays]


def start_all(pairs, sems, first=0):
    copies = [pltpu.make_async_copy(src, dst, sems.at[first + n]) for n, (src, dst) in enumerate(pairs)]
    for copy in copies:
        copy.start()
    return copies


def wait_all(copies):
    for copy in copies:
        copy.wait()


def iota(shape, dim):
    return lax.broadcasted_iota(I32, shape, dim)


def pick(mask, value):
    return jnp.where(mask, value, 0.0)


def split(value):
    high = value.astype(BF16)
    return high, (value - high.astype(F32)).astype(BF16)


def back_rows(capacity):
    return 4 * capacity + max(8, capacity)


def remap_out_kernel(
    capacity, grid_y, tile_rows, block_h, owner_h, row_h, tile_h, atm_h, weights_h, out_h, field_h, wet_h,
    out, block_s, owner_s, row_s, tile_s, rank_s, at_s, field_s, wet_s, atm, weights, atm_rows, flux_rows, flux, fill, rows_sum, cols_sum, rows_acc, cols_acc, sems, weight_sems, out_sems,
):
    devices = fill.shape[0]
    npairs = block_s.shape[0]
    tiles = weights.shape[0]
    nblocks = flux.shape[0]
    message = 4 * capacity + EDGE
    copies = [
        pltpu.make_async_copy(src, dst, sems.at[n])
        for n, (src, dst) in enumerate(
            [(atm_h, atm), (block_h, block_s), (owner_h, owner_s), (row_h, row_s), (tile_h, tile_s)]
        )
    ]
    for copy in copies:
        copy.start()
    part_tiles = tiles // PARTS
    parts = [pl.ds(n * part_tiles, part_tiles) for n in range(PARTS)]
    loads = [pltpu.make_async_copy(weights_h.at[at], weights.at[at], weight_sems.at[n]) for n, at in enumerate(parts)]
    for load in loads:
        load.start()
    out[...] = jnp.zeros_like(out)
    rows_sum[...] = jnp.zeros_like(rows_sum)
    cols_sum[...] = jnp.zeros_like(cols_sum)

    def clear_fill(i, carry):
        fill[i] = 0
        return carry

    lax.fori_loop(0, devices, clear_fill, 0, unroll=16)
    flux_rows[...] = jnp.zeros_like(flux_rows)
    wait_all(copies)
    for b in range(nblocks):
        atm_rows[8 * b : 8 * b + 6, :] = atm[:, b * LANES : (b + 1) * LANES]
    wind_u, wind_v, air, dry, rain, sea = [atm_rows[pl.ds(n, nblocks, stride=8), :] for n in range(6)]
    speed = jnp.sqrt(wind_u * wind_u + wind_v * wind_v + 0.25)
    heat = 0.5 * speed * (air - sea)
    water = rain - 0.3 * speed * dry
    planes = [heat, water, 0.2 * speed * wind_u, 0.2 * speed * wind_v]
    for n, plane in list(enumerate(planes)) + [(8 + n, heat) for n in range(4)] + [(12 + n, water) for n in range(4)]:
        flux_rows[pl.ds(n, nblocks, stride=16), :] = plane
    for b in range(nblocks):
        flux[b] = flux_rows[16 * b : 16 * (b + 1), :].astype(BF16)

    grid_x = devices // grid_y
    height = back_rows(capacity)


    def place(p):
        owner = owner_s[p]
        rank = fill[owner]
        fill[owner] = rank + 1
        at = lax.rem(owner, grid_y) * grid_x + lax.div(owner, grid_y)
        field_s[p] = at * height + 4 * rank
        wet_s[p] = at * height + 4 * capacity + rank
        rank_s[p] = rank
        at_s[p] = at

    for p in range(AHEAD):
        place(p)
    wait_all(loads)

    sub = iota((8, LANES), 0)
    lane = iota((8, LANES), 1)
    part = sub % 4
    edge_row = jnp.where(part == 0, 0, jnp.where(part == 1, 1, tile_rows - 4 + part))
    band = ((lane - part) >> 2) * 4 + part
    id_rank = jnp.where(sub == 0, lane - NUMBERS, -1)

    def pair(p, n):
        owner = owner_s[p]
        row = row_s[p]
        rank = rank_s[p]
        value = jnp.dot(flux[block_s[p]], weights[tile_s[p]], preferred_element_type=F32)
        out[at_s[p], pl.ds(4 * rank, 4), :] = value[0:4]
        tracer = value[8:16]
        rows_sum[n, owner] = rows_sum[n, owner] + pick(edge_row == row, tracer)
        number = (row + 1).astype(F32)
        cols_sum[n, owner] = cols_sum[n, owner] + (
            pick(band == row, pltpu.roll(tracer, row + 2, 1)) + pick(id_rank == rank, number)
        )

    many = rows_sum.shape[0]

    def pairs(more, k, carry):
        for n in range(many):
            p = many * k + n
            if more:
                place(p + AHEAD)
            pair(p, n)
        return carry

    lax.fori_loop(0, (npairs - AHEAD) // many, functools.partial(pairs, True), 0, unroll=AHEAD // many)
    stores = start_all([(field_s, field_h), (wet_s, wet_h)], out_sems, SENDS)
    lax.fori_loop((npairs - AHEAD) // many, npairs // many, functools.partial(pairs, False), 0, unroll=AHEAD // many)

    slots = (slice(None), pl.ds(0, 4 * capacity))
    stores += start_all([(out.at[slots], out_h.at[slots])], out_sems, SENDS + 2)

    def owner_step(d, carry):
        rows_acc[d] = (rows_sum[0, d] + rows_sum[1, d]) + (rows_sum[2, d] + rows_sum[3, d])
        cols_acc[d] = (cols_sum[0, d] + cols_sum[1, d]) + (cols_sum[2, d] + cols_sum[3, d])
        return carry

    lax.fori_loop(0, devices, owner_step, 0, unroll=8)

    zero = jnp.zeros((8, LANES), F32)

    def columns_of(i, j):
        if not (0 <= i < grid_x and 0 <= j < grid_y):
            return zero
        return cols_acc[i * grid_y + j]

    from_left = (lane - sub) % 4 < 2
    in_band = lane < tile_rows + 4
    in_ids = (sub == 0) & (lane >= NUMBERS) & (lane < NUMBERS + capacity)
    last, first = part == 3, part == 0
    send = devices // SENDS
    for at in range(devices):
        j, i = at // grid_x, at % grid_x
        d = i * grid_y + j
        below = rows_acc[d + grid_y] if i < grid_x - 1 else zero
        above = rows_acc[d - grid_y] if i > 0 else zero
        base = 4 * capacity
        out[at, base : base + 8, :] = jnp.where(part < 2, below, above)
        tile = pick(in_band, jnp.where(from_left, columns_of(i, j - 1), columns_of(i, j + 1)))
        upper = pick(last & (lane == tile_rows), columns_of(i - 1, j - 1))
        upper = upper + pick(last & (lane == tile_rows + 1), columns_of(i - 1, j + 1))
        lower = pick(first & (lane == 1), columns_of(i + 1, j - 1))
        lower = lower + pick(first & (lane == 2), columns_of(i + 1, j + 1))
        tile = tile + pltpu.roll(upper, CORNERS - tile_rows, 1) + pltpu.roll(lower, CORNERS + 1, 1)
        tile = tile + pick(in_ids, cols_acc[d])
        out[at, base + 8 : base + 16, :] = tile
        if at % send == send - 1:
            n = at // send
            edges = (pl.ds(n * send, send), pl.ds(base, EDGE))
            stores += start_all([(out.at[edges], out_h.at[edges])], out_sems, n)
    for store in stores:
        store.wait()


def remap_out(capacity, grid_y, devices, tile_rows, atm_state, pair_block, owner, pair_row, pair_tile, remap_weight):
    npairs = pair_block.shape[0]
    nblocks = atm_state.shape[1] // LANES
    message = 4 * capacity + EDGE
    return pl.pallas_call(
        functools.partial(remap_out_kernel, capacity, grid_y, tile_rows),
        out_shape=(
            pltpu.HBM((devices, message, LANES), F32),
            pltpu.HBM((npairs,), I32),
            pltpu.HBM((npairs,), I32),
        ),
        in_specs=[hbm()] * 6,
        out_specs=(hbm(),) * 3,
        scratch_shapes=[pltpu.VMEM((devices, message, LANES), F32)]
        + [pltpu.SMEM((npairs,), I32)] * 8
        + [
            pltpu.VMEM(atm_state.shape, F32),
            pltpu.VMEM(remap_weight.shape, BF16),
            pltpu.VMEM((nblocks * 8, LANES), F32),
            pltpu.VMEM((nblocks * 16, LANES), F32),
            pltpu.VMEM((nblocks, 16, LANES), BF16),
            pltpu.SMEM((devices,), I32),
            pltpu.VMEM((4, devices, 8, LANES), F32),
            pltpu.VMEM((4, devices, 8, LANES), F32),
            pltpu.VMEM((devices, 8, LANES), F32),
            pltpu.VMEM((devices, 8, LANES), F32),
            pltpu.SemaphoreType.DMA((5,)),
            pltpu.SemaphoreType.DMA((PARTS,)),
            pltpu.SemaphoreType.DMA((SENDS + 3,)),
        ],
        compiler_params=pltpu.CompilerParams(vmem_limit_bytes=40 << 20),
        cost_estimate=pl.CostEstimate(
            flops=2 * npairs * 16 * LANES * LANES, bytes_accessed=6 << 20, transcendentals=0
        ),
    )(*pin(pair_block, owner, pair_row, pair_tile, atm_state, remap_weight))


def solve_kernel(state, kappa, horiz, wet, tracer, currents_h, edge_up, edge_down, currents, sems):
    levels = kappa.shape[0]
    rows_all = kappa.shape[1]
    planes = tracer.shape[0]

    def chunk(c, carry):
        rows = pl.ds(pl.multiple_of(c * 8, 8), 8)
        column = [kappa[l, rows, :] for l in range(levels)]
        face = [0.5 * (column[l] + column[l + 1]) for l in range(levels - 1)]
        upper = []
        now = None
        for l in range(levels):
            diagonal = 1.0
            if l > 0:
                diagonal = diagonal + face[l - 1]
            if l < levels - 1:
                diagonal = diagonal + face[l]
            if l > 0:
                diagonal = diagonal + face[l - 1] * upper[-1]
            inverse = 1.0 / diagonal
            if l == 0:
                now = [state[f, 0, rows, :] * inverse for f in range(4)] + [inverse]
            else:
                pull = face[l - 1] * inverse
                now = [state[f, l, rows, :] * inverse + pull * now[f] for f in range(4)] + [pull * now[4]]
            upper.append(-face[l] * inverse if l < levels - 1 else None)
            store(l, rows, now)
        for l in range(levels - 2, -1, -1):
            here = load(l, rows)
            now = [here[f] - upper[l] * now[f] for f in range(5)]
            store(l, rows, now)
        return carry

    def store(l, rows, now):
        tracer[l, rows, :] = now[0]
        tracer[levels + l, rows, :] = now[1]
        currents[0, l, rows, :] = now[2]
        currents[1, l, rows, :] = now[3]
        tracer[2 * levels + l, rows, :] = now[4]

    def load(l, rows):
        return [
            tracer[l, rows, :],
            tracer[levels + l, rows, :],
            currents[0, l, rows, :],
            currents[1, l, rows, :],
            tracer[2 * levels + l, rows, :],
        ]

    lax.fori_loop(0, rows_all // 8, chunk, 0)
    out = start_all([(currents, currents_h)], sems)
    tracer[3 * levels] = horiz[...]
    tracer[3 * levels + 1] = wet[...].astype(F32)
    for k in range(planes):
        edge_up[k] = tracer[k, 0:8, :]
        edge_down[k] = tracer[k, rows_all - 8 : rows_all, :]
    wait_all(out)


def solve(ocean_state, vert_kappa, horiz_kappa, wet_mask):
    levels, rows, _ = vert_kappa.shape
    planes = 3 * levels + 2
    return pl.pallas_call(
        solve_kernel,
        out_shape=(
            jax.ShapeDtypeStruct((planes, rows, LANES), F32),
            pltpu.HBM((2, levels, rows, LANES), F32),
            jax.ShapeDtypeStruct((planes, 8, LANES), F32),
            jax.ShapeDtypeStruct((planes, 8, LANES), F32),
        ),
        in_specs=[vmem()] * 4,
        out_specs=(vmem(), hbm(), vmem(), vmem()),
        scratch_shapes=[pltpu.VMEM((2, levels, rows, LANES), F32), pltpu.SemaphoreType.DMA((1,))],
        compiler_params=pltpu.CompilerParams(vmem_limit_bytes=24 << 20),
        cost_estimate=pl.CostEstimate(flops=20 << 20, bytes_accessed=6 << 20, transcendentals=0),
    )(ocean_state, vert_kappa, horiz_kappa, wet_mask)


def pack_kernel(levels, tracer, above, below, wide_h, to_left, to_right, wide, sems):
    planes, rows, _ = tracer.shape
    for k in range(planes):
        wide[k, 0:HALO, :] = above[k]
        wide[k, HALO : HALO + rows, :] = tracer[k]
        wide[k, HALO + rows : 2 * HALO + rows, :] = below[k]
    out = start_all([(wide, wide_h)], sems)
    lane = iota((8, LANES), 1)

    def chunk(c, carry):
        at = pl.ds(pl.multiple_of(c * 8, 8), 8)

        def place(values, lanes):
            left, right = jnp.zeros((8, LANES), F32), jnp.zeros((8, LANES), F32)
            for k, (near, far) in zip(values, lanes):
                value = wide[k, at, :]
                left = jnp.where(lane == near, pltpu.roll(value, near, 1), left)
                left = jnp.where(lane == far, pltpu.roll(value, far - 1, 1), left)
                right = jnp.where(lane == near + 1, pltpu.roll(value, (near + 2) % LANES, 1), right)
                right = jnp.where(lane == far + 1, pltpu.roll(value, (far + 3) % LANES, 1), right)
            return left, right

        left, right = place(range(2 * levels), [(2 * k, 64 + 2 * k) for k in range(2 * levels)])
        to_left[0, at, :] = left
        to_right[0, at, :] = right
        lanes = [(2 * l, 64 + 2 * l) for l in range(levels)]
        lanes += [(2 * levels, 2 * levels + 2), (2 * levels + 4, 2 * levels + 6)]
        left, right = place(range(2 * levels, 3 * levels + 2), lanes)
        to_left[1, at, :] = left
        to_right[1, at, :] = right
        return carry

    lax.fori_loop(0, (rows + 2 * HALO) // 8, chunk, 0)
    wait_all(out)


def pack(levels, tracer, above, below):
    planes, rows, _ = tracer.shape
    tall = rows + 2 * HALO
    return pl.pallas_call(
        functools.partial(pack_kernel, levels),
        out_shape=(
            pltpu.HBM((planes, tall, LANES), F32),
            jax.ShapeDtypeStruct((2, tall, LANES), F32),
            jax.ShapeDtypeStruct((2, tall, LANES), F32),
        ),
        in_specs=[vmem()] * 3,
        out_specs=(hbm(), vmem(), vmem()),
        scratch_shapes=[pltpu.VMEM((planes, tall, LANES), F32), pltpu.SemaphoreType.DMA((1,))],
        compiler_params=pltpu.CompilerParams(vmem_limit_bytes=24 << 20),
        cost_estimate=pl.CostEstimate(flops=8 << 20, bytes_accessed=4 << 20, transcendentals=0),
    )(tracer, above, below)


def set_faces(levels, h, w, own_left, own_right, from_left, from_right, faces, packed):
    tall = h.shape[0]
    lane = iota((tall, LANES), 1)
    odd = lane % 2 == 1
    twice = lane % 64 < 2 * levels
    left, left_unit, right, right_unit = from_left[0], from_left[1], from_right[0], from_right[1]
    other = jnp.where(odd, left_unit, right_unit)
    at = 2 * levels

    def column(offset):
        return other[:, at + offset : at + offset + 1], other[:, at + offset + 1 : at + offset + 2]

    kappa_right, kappa_left = column(0)
    kappa_far_right, kappa_far_left = column(2)
    wet_right, wet_left = column(4)
    wet_far_right, wet_far_left = column(6)

    kappa_near = jnp.where(odd, kappa_left, kappa_right)
    kappa_far = jnp.where(odd, kappa_far_left, kappa_far_right)
    wet_near = jnp.where(odd, wet_left, wet_right)
    wet_far = jnp.where(odd, wet_far_left, wet_far_right)
    kappa_own = jnp.where(odd, h[:, 0:1], h[:, LANES - 1 : LANES])
    wet_own = jnp.where(odd, w[:, 0:1], w[:, LANES - 1 : LANES])

    def face(kappa_a, wet_a, kappa_b, wet_b):
        return 0.25 * (kappa_a + kappa_b) * wet_a * wet_b

    unit = jnp.where(twice, other, pltpu.roll(other, 2 * levels, 1))
    packed[0] = jnp.where(odd, left, right)
    packed[1] = unit * jnp.where(lane < 64, wet_near, wet_far)
    left, left_unit, right, right_unit = own_left[0], own_left[1], own_right[0], own_right[1]
    packed[2] = jnp.where(odd, pltpu.roll(left, 1, 1), pltpu.roll(right, LANES - 1, 1))
    own = jnp.where(odd, pltpu.roll(left_unit, 1, 1), pltpu.roll(right_unit, LANES - 1, 1))
    packed[3] = jnp.where(twice, own, pltpu.roll(own, 2 * levels, 1)) * wet_own
    north = face(kappa_near, wet_near, pltpu.roll(kappa_near, 1, 0), pltpu.roll(wet_near, 1, 0))
    packed[4] = north
    packed[5] = pltpu.roll(north, tall - 1, 0)
    packed[6] = face(kappa_near, wet_near, kappa_far, wet_far)
    packed[7] = face(kappa_near, wet_near, kappa_own, wet_own)

    north = face(h, w, pltpu.roll(h, 1, 0), pltpu.roll(w, 1, 0))
    faces[0] = north
    faces[1] = pltpu.roll(north, tall - 1, 0)
    west = face(
        h, w, jnp.where(lane == 0, kappa_left, pltpu.roll(h, 1, 1)), jnp.where(lane == 0, wet_left, pltpu.roll(w, 1, 1))
    )
    faces[2] = west
    faces[3] = jnp.where(lane == LANES - 1, face(h, w, kappa_right, wet_right), pltpu.roll(west, LANES - 1, 1))


def set_beside(levels, upright, wide, packed, beside):
    tall = upright.shape[0]
    lane = iota((tall, LANES), 1)
    odd = lane % 2 == 1
    heat = lane % 64 < 2 * levels

    def chosen(f):
        left_far, left_near, right_near, right_far = [upright[:, 4 * f + e : 4 * f + e + 1] for e in range(4)]
        near = jnp.where(odd, left_near, right_near)
        return jnp.where(lane < 64, near, jnp.where(odd, left_far, right_far))

    both = packed[0] + packed[1] * jnp.where(heat, chosen(0), chosen(1))
    far = pltpu.roll(both, 64, 1)
    ends_of = [jnp.where(odd, w[:, 0:1], w[:, LANES - 1 : LANES]) for w in wide]
    own = packed[2] + packed[3] * jnp.where(heat, ends_of[0], ends_of[1])
    near = both + packed[5] * (pltpu.roll(both, tall - 1, 0) - both)
    near = near + packed[4] * (pltpu.roll(both, 1, 0) - both)
    near = near + packed[6] * (far - both)
    near = near + packed[7] * (own - both)
    beside[0] = both
    beside[1] = near


def one_pass(value, faces, beside, shift):
    tall = value.shape[0]
    lane = iota(value.shape, 1)
    moved = pltpu.roll(beside, shift, 1)
    west = jnp.where(lane == 0, moved, pltpu.roll(value, 1, 1))
    east = jnp.where(lane == LANES - 1, moved, pltpu.roll(value, LANES - 1, 1))
    result = value + faces[1] * (pltpu.roll(value, tall - 1, 0) - value)
    result = result + faces[0] * (pltpu.roll(value, 1, 0) - value)
    result = result + faces[3] * (east - value)
    return result + faces[2] * (west - value)


def middle_kernel(
    capacity, levels, arrived, wide_h, currents_h, own_left_h, own_right_h, from_left_h, from_right_h,
    sent_h, forcing_h, near_h, faces_h,
    placing, values, number_t, top, currents, own_left, own_right, from_left, from_right,
    faces, packed, sent, forcing, near_o, sems, sent_sems,
):
    devices, message, _ = arrived.shape
    rows_all = currents.shape[1]
    tall = rows_all + 2 * HALO
    loads = start_all(
        [(wide_h.at[levels * k], top.at[k]) for k in range(3)]
        + [
            (wide_h.at[pl.ds(3 * levels, 2)], top.at[pl.ds(3, 2)]),
            (currents_h.at[0, 0], currents.at[0]),
            (currents_h.at[1, 0], currents.at[1]),
            (own_left_h, own_left),
            (own_right_h, own_right),
            (from_left_h, from_left),
            (from_right_h, from_right),
        ],
        sems,
    )
    span = 4 * capacity
    group = LANES // span
    groups = devices // group
    sub8 = iota((8, LANES), 0)
    lane8 = iota((8, LANES), 1)

    lane1 = iota((1, LANES), 1)
    spread = (iota((LANES, LANES), 0) - NUMBERS) == iota((LANES, LANES), 1) % span // 4
    every = jnp.concatenate([arrived[s, span + 8 : span + 9, :] for s in range(devices)], 0).astype(BF16)
    every = jnp.dot(every, jnp.where(spread, 1.0, 0.0).astype(BF16), preferred_element_type=F32)
    numbers = []
    for m in range(groups):
        line = jnp.zeros((1, LANES), F32)
        for g in range(group):
            s = m * group + g
            line = jnp.where(lane1 // span == g, every[s : s + 1], line)
        numbers.append(line)
    number_t[...] = jnp.transpose(
        jnp.concatenate(numbers + [jnp.zeros((LANES - groups, LANES), F32)], 0)
    )

    row_number = iota((rows_all, LANES), 0).astype(F32) + 1.0
    for m in range(groups):
        for f in range(4):
            placing[f * rows_all : (f + 1) * rows_all, m * LANES : (m + 1) * LANES] = jnp.where(
                pick(lane1 % 4 == f, numbers[m]) == row_number, 1.0, 0.0
            ).astype(BF16)
    edge_rows = jnp.zeros((8, LANES), F32)
    edge_cols = jnp.zeros((8, LANES), F32)
    for s in range(devices):
        high, low = split(arrived[s, 0:span, :])
        values[s * span : (s + 1) * span, 0:LANES] = high
        values[s * span : (s + 1) * span, LANES : 2 * LANES] = low
        edge_rows = edge_rows + arrived[s, span : span + 8, :]
        edge_cols = edge_cols + arrived[s, span + 8 : span + 16, :]
    wait_all(loads)
    set_faces(levels, top[3], top[4], own_left, own_right, from_left, from_right, faces, packed)
    wet_wide = top[4]
    total = jnp.dot(placing[...], values[...], preferred_element_type=F32)
    total = total[:, 0:LANES] + total[:, LANES : 2 * LANES]


    def plane(f):
        return total[f * rows_all : (f + 1) * rows_all]

    wide = []
    for f in range(2):
        before = pick(sub8 >= 6, edge_rows if f == 1 else pltpu.roll(edge_rows, 4, 0))
        after = pick(sub8 < 2, edge_rows if f == 0 else pltpu.roll(edge_rows, 4, 0))
        wide.append(jnp.concatenate([before, plane(f), after], 0))
        forcing[f] = wide[f]
    wet = wet_wide[HALO : HALO + rows_all]
    for f in range(2, 4):
        forcing[f, 0:HALO, :] = jnp.zeros((HALO, LANES), F32)
        forcing[f, HALO : HALO + rows_all, :] = plane(f) * wet
        forcing[f, HALO + rows_all : tall, :] = jnp.zeros((HALO, LANES), F32)

    part8 = sub8 % 4
    within = (part8 == lane8 % 4) & (lane8 >= HALO) & (lane8 < HALO + rows_all)
    upper = (part8 == 3) & (lane8 == HALO - 1)
    lower = (part8 == 0) & (lane8 == HALO + rows_all)
    halves = [[], []]
    for k in range(4):
        column = pick(within, pltpu.roll(edge_cols, HALO - k, 1))
        if k in (1, 2):
            column = column + pick(upper, pltpu.roll(edge_cols, (HALO - CORNERS - k) % LANES, 1))
            column = column + pick(lower, pltpu.roll(edge_cols, (HALO + rows_all - CORNERS - 1 - k) % LANES, 1))
        for f in range(2):
            halves[f].append(jnp.sum(column[4 * f : 4 * f + 4], axis=0, keepdims=True))
    columns = jnp.concatenate(halves[0] + halves[1], 0)
    upright = jnp.transpose(jnp.concatenate([columns, jnp.zeros((LANES - 8, LANES), F32)], 0))[0:tall]
    set_beside(levels, upright, wide, packed, near_o)
    stores = start_all([(forcing, forcing_h), (near_o, near_h), (faces, faces_h)], sems, 10)

    surface = []
    unit = top[2] * wet_wide
    for f in range(2):
        value = top[f] + unit * wide[f]
        shift = LANES - (2 * levels * f + 1)
        value = one_pass(value, faces, near_o[0], shift)
        value = one_pass(value, faces, near_o[1], shift)
        surface.append(value[HALO : HALO + rows_all] * wet)
    for f in range(2):
        surface.append(
            (currents[f] + top[2, HALO : HALO + rows_all, :] * forcing[2 + f, HALO : HALO + rows_all, :]) * wet
        )
    high, low = split(jnp.concatenate(surface, 0))
    source = jnp.concatenate([high, low], 1)
    lane_t = iota((LANES, 4 * rows_all), 1)
    sub_t = iota((LANES, 4 * rows_all), 0)
    target = jnp.where(sub_t % 4 == lane_t // rows_all, lane_t % rows_all + 1, -1).astype(F32)
    mask = jnp.concatenate([wet, jnp.zeros((LANES - rows_all, LANES), F32)], 0).astype(BF16)
    per = LANES // 4
    slot_number = number_t[pl.ds(0, per, stride=4), :]
    lane_s = (iota((per, LANES), 1) + 1).astype(F32)
    height = back_rows(capacity)
    many = 4
    for first in range(0, groups, many):
        these = range(first, first + many)
        chosen_rows = [jnp.where(number_t[:, m : m + 1] == target, 1.0, 0.0).astype(BF16) for m in these]
        rows = jnp.dot(jnp.concatenate(chosen_rows, 0), source, preferred_element_type=F32)
        rows = rows[:, 0:LANES] + rows[:, LANES : 2 * LANES]
        slots = [jnp.where(slot_number[:, m : m + 1] == lane_s, 1.0, 0.0) for m in these]
        masks = jnp.dot(jnp.concatenate(slots, 0).astype(BF16), mask, preferred_element_type=F32)
        for g in range(many * group):
            s = first * group + g
            sent[s, 0:span, :] = rows[g * span : (g + 1) * span]
            sent[s, span : span + capacity, :] = masks[g * capacity : (g + 1) * capacity]
            if height > span + capacity:
                sent[s, span + capacity : height, :] = jnp.zeros((height - span - capacity, LANES), F32)
        at = pl.ds(first * group, many * group)
        stores += start_all([(sent.at[at], sent_h.at[at])], sent_sems, first // many)
    wait_all(stores)


def middle(capacity, levels, arrived, wide, currents, *columns):
    devices = arrived.shape[0]
    rows = currents.shape[2]
    tall = rows + 2 * HALO
    height = back_rows(capacity)
    return pl.pallas_call(
        functools.partial(middle_kernel, capacity, levels),
        out_shape=(
            pltpu.HBM((devices, height, LANES), F32),
            pltpu.HBM((4, tall, LANES), F32),
            pltpu.HBM((2, tall, LANES), F32),
            pltpu.HBM((4, tall, LANES), F32),
        ),
        in_specs=[vmem()] + [hbm()] * 2 + [pl.BlockSpec(memory_space=pl.ANY)] * 4,
        out_specs=(hbm(),) * 4,
        scratch_shapes=[
            pltpu.VMEM((4 * rows, 4 * capacity * devices), BF16),
            pltpu.VMEM((4 * capacity * devices, 2 * LANES), BF16),
            pltpu.VMEM((LANES, LANES), F32),
            pltpu.VMEM((5, tall, LANES), F32),
            pltpu.VMEM((2, rows, LANES), F32),
        ]
        + [pltpu.VMEM((2, tall, LANES), F32)] * 4
        + [
            pltpu.VMEM((4, tall, LANES), F32),
            pltpu.VMEM((8, tall, LANES), F32),
            pltpu.VMEM((devices, height, LANES), F32),
            pltpu.VMEM((4, tall, LANES), F32),
            pltpu.VMEM((2, tall, LANES), F32),
            pltpu.SemaphoreType.DMA((13,)),
            pltpu.SemaphoreType.DMA((4 * capacity * devices // LANES,)),
        ],
        compiler_params=pltpu.CompilerParams(vmem_limit_bytes=24 << 20),
        cost_estimate=pl.CostEstimate(flops=200 << 20, bytes_accessed=4 << 20, transcendentals=0),
    )(arrived, *pin(wide, currents), *columns)


def finish_kernel(
    levels, wide_h, currents_h, faces_h, forcing_h, near_h, ocean, wide, currents, faces, forcing, near, sems
):
    rows_all = currents.shape[2]
    wait_all(
        start_all(
            [(wide_h, wide), (currents_h, currents), (faces_h, faces), (forcing_h, forcing), (near_h, near)], sems
        )
    )
    inner = slice(HALO, HALO + rows_all)

    def level(l, carry):
        unit = wide[2 * levels + l]
        masked = unit * wide[3 * levels + 1]
        for f in range(2):
            value = wide[f * levels + l] + masked * forcing[f]
            shift = LANES - 1 - 2 * (levels * f + l)
            value = one_pass(value, faces, near[0], shift)
            value = one_pass(value, faces, near[1], shift)
            ocean[f, l] = value[inner]
            ocean[2 + f, l] = currents[f, l] + unit[inner] * forcing[2 + f][inner]
        return carry

    lax.fori_loop(0, levels, level, 0)


def finish(levels, wide, currents, faces, forcing, near):
    rows = currents.shape[2]
    return pl.pallas_call(
        functools.partial(finish_kernel, levels),
        out_shape=jax.ShapeDtypeStruct((4, levels, rows, LANES), F32),
        in_specs=[hbm()] * 5,
        out_specs=vmem(),
        scratch_shapes=[pltpu.VMEM(a.shape, F32) for a in (wide, currents, faces, forcing, near)]
        + [pltpu.SemaphoreType.DMA((5,))],
        compiler_params=pltpu.CompilerParams(vmem_limit_bytes=24 << 20),
        cost_estimate=pl.CostEstimate(flops=40 << 20, bytes_accessed=6 << 20, transcendentals=0),
    )(*pin(wide, currents, faces, forcing, near))


def turn_kernel(weights_h, turned_h, weights, turned, sems, out_sems):
    part_tiles = weights.shape[0] // PARTS
    parts = [pl.ds(n * part_tiles, part_tiles) for n in range(PARTS)]
    loads = start_all([(weights_h.at[at], weights.at[at]) for at in parts], sems)
    stores = []
    for n, at in enumerate(parts):
        loads[n].wait()

        def tile_step(t, carry):
            turned[t] = weights[t].T
            return carry

        lax.fori_loop(n * part_tiles, (n + 1) * part_tiles, tile_step, 0, unroll=4)
        stores += start_all([(turned.at[at], turned_h.at[at])], out_sems, n)
    wait_all(stores)


def turn(remap_weight):
    return pl.pallas_call(
        turn_kernel,
        out_shape=pltpu.HBM(remap_weight.shape, BF16),
        in_specs=[hbm()],
        out_specs=hbm(),
        scratch_shapes=[pltpu.VMEM(remap_weight.shape, BF16)] * 2 + [pltpu.SemaphoreType.DMA((PARTS,))] * 2,
        compiler_params=pltpu.CompilerParams(vmem_limit_bytes=24 << 20),
        cost_estimate=pl.CostEstimate(flops=8 << 20, bytes_accessed=8 << 20, transcendentals=0),
    )(*pin(remap_weight))


def remap_back_kernel(
    block_h, tile_h, field_h, wet_h, returned, weights_h, out,
    block_s, tile_s, field_s, wet_s, weights, picked_a, picked_b, total_0, total_1, total_2, total_3, sems, weight_sems,
):
    npairs = block_s.shape[0]
    totals = [total_0, total_1, total_2, total_3]
    nblocks = total_0.shape[0]
    scalars = start_all([(field_h, field_s), (wet_h, wet_s), (block_h, block_s), (tile_h, tile_s)], sems)
    part_tiles = weights.shape[0] // PARTS
    parts = [pl.ds(n * part_tiles, part_tiles) for n in range(PARTS)]
    loads = start_all([(weights_h.at[at], weights.at[at]) for at in parts], weight_sems)
    for total in totals:
        total[...] = jnp.zeros_like(total)
    wait_all(scalars)

    def gather(p, picked, at):
        rows = returned[pl.ds(field_s[p], 4), :]
        mask = returned[pl.ds(wet_s[p] - 7, 8), :]
        high, low = split(jnp.concatenate([rows, jnp.zeros((3, LANES), F32), mask[7:8]], 0))
        picked[at] = jnp.concatenate([high, low], 0)

    def product(p, picked, at, total):
        value = jnp.dot(picked[at], weights[tile_s[p]], preferred_element_type=F32)
        b = block_s[p]
        total[b] = total[b] + (value[0:8] + value[8:16])

    half = npairs // 2
    many = len(totals)

    def first(p, carry):
        gather(p, picked_a, p)
        return carry

    def both(p, carry):
        for n in range(many):
            gather(half + many * p + n, picked_b, many * p + n)
            product(many * p + n, picked_a, many * p + n, totals[n])
        return carry

    def last(p, carry):
        for n in range(many):
            product(half + many * p + n, picked_b, many * p + n, totals[n])
        return carry

    lax.fori_loop(0, half, first, 0, unroll=64)
    wait_all(loads)
    lax.fori_loop(0, half // many, both, 0, unroll=32)
    lax.fori_loop(0, half // many, last, 0, unroll=32)
    for b in range(nblocks):
        sums = (total_0[b] + total_1[b]) + (total_2[b] + total_3[b])
        out[:, b * LANES : (b + 1) * LANES] = sums[0:4] / jnp.maximum(sums[7:8], 0.1)


def remap_back(pair_block, pair_tile, field_at, wet_at, returned, weights, nblocks):
    npairs = pair_block.shape[0]
    return pl.pallas_call(
        remap_back_kernel,
        out_shape=jax.ShapeDtypeStruct((4, nblocks * LANES), F32),
        in_specs=[hbm()] * 4 + [vmem(), hbm()],
        out_specs=vmem(),
        scratch_shapes=[pltpu.SMEM((npairs,), I32)] * 4
        + [pltpu.VMEM(weights.shape, BF16)]
        + [pltpu.VMEM((npairs // 2, 16, LANES), BF16)] * 2
        + [pltpu.VMEM((nblocks, 8, LANES), F32)] * 4
        + [pltpu.SemaphoreType.DMA((4,)), pltpu.SemaphoreType.DMA((PARTS,))],
        compiler_params=pltpu.CompilerParams(vmem_limit_bytes=24 << 20),
        cost_estimate=pl.CostEstimate(flops=2 * npairs * 16 * LANES * LANES, bytes_accessed=6 << 20, transcendentals=0),
    )(*pin(pair_block, pair_tile, field_at, wet_at), returned, *pin(weights))


def local(
    atm_state,
    pair_block,
    pair_owner,
    pair_row,
    pair_tile,
    remap_weight,
    wet_mask,
    ocean_state,
    vert_kappa,
    horiz_kappa,
):
    grid_x = lax.axis_size("gx")
    grid_y = lax.axis_size("gy")
    devices = grid_x * grid_y
    npairs = pair_block.shape[0]
    capacity = max(2, 2 * npairs // devices)
    levels, tile_rows, _ = vert_kappa.shape
    nblocks = atm_state.shape[1] // LANES
    owner = pair_owner.reshape(npairs)
    outgoing, field_at, wet_at = remap_out(
        capacity, grid_y, devices, tile_rows, atm_state, pair_block, owner, pair_row, pair_tile, remap_weight
    )
    arrived = lax.all_to_all(
        outgoing, ("gy", "gx"), split_axis=0, concat_axis=0, tiled=True
    )
    tracer, currents, edge_up, edge_down = solve(ocean_state, vert_kappa, horiz_kappa, wet_mask)
    rise_x = [(i, i + 1) for i in range(grid_x - 1)]
    fall_x = [(b, a) for a, b in rise_x]
    rise_y = [(i, i + 1) for i in range(grid_y - 1)]
    fall_y = [(b, a) for a, b in rise_y]
    above = lax.ppermute(edge_down, "gx", rise_x)
    below = lax.ppermute(edge_up, "gx", fall_x)
    wide, to_left, to_right = pack(levels, tracer, above, below)
    from_left = lax.ppermute(to_right, "gy", rise_y)
    from_right = lax.ppermute(to_left, "gy", fall_y)
    sent, forcing, near, faces = middle(
        capacity, levels, arrived, wide, currents, to_left, to_right, from_left, from_right
    )
    returned = lax.all_to_all(sent, ("gy", "gx"), split_axis=0, concat_axis=0, tiled=True)
    ocean_next = finish(levels, wide, currents, faces, forcing, near)
    weights, _ = lax.optimization_barrier((remap_weight, near))
    atm_surface = remap_back(
        pair_block, pair_tile, field_at, wet_at, returned.reshape(-1, LANES), turn(weights), nblocks
    )
    return (ocean_next, atm_surface)


def solution(mesh):
    placed = (
        P(None, ("gx", "gy")),
        P(("gx", "gy")),
        P(("gx", "gy"), None),
        P(("gx", "gy")),
        P(("gx", "gy")),
        P(("gx", "gy"), None, None),
        P("gx", "gy"),
        P(None, None, "gx", "gy"),
        P(None, "gx", "gy"),
        P("gx", "gy"),
    )
    return jax.shard_map(
        local,
        mesh=mesh,
        in_specs=placed,
        out_specs=(P(None, None, "gx", "gy"), P(None, ("gx", "gy"))),
        check_vma=False,
    )
```

```python
import functools

import jax
import jax.numpy as jnp
from jax import lax
from jax.experimental import pallas as pl
from jax.experimental.pallas import tpu as pltpu
from jax.sharding import PartitionSpec as P

F32 = jnp.float32
BF16 = jnp.bfloat16
I32 = jnp.int32
VMEM = pltpu.VMEM
SMEM = pltpu.SMEM
LANES = 128
EDGE = 16
HALO = 8
NUMBERS = 72
CORNERS = 112
SENDS = 8
AHEAD = 32
PARTS = 8


def hbm():
    return pl.BlockSpec(memory_space=pltpu.HBM)


def vmem():
    return pl.BlockSpec(memory_space=VMEM)


def pin(*arrays):
    return [pltpu.with_memory_space_constraint(a, pltpu.HBM) for a in arrays]


def start_all(pairs, sems, first=0):
    copies = [pltpu.make_async_copy(src, dst, sems.at[first + n]) for n, (src, dst) in enumerate(pairs)]
    for copy in copies:
        copy.start()
    return copies


def wait_all(copies):
    for copy in copies:
        copy.wait()


def iota(shape, dim):
    return lax.broadcasted_iota(I32, shape, dim)


def pick(mask, value):
    return jnp.where(mask, value, 0.0)


def split(value):
    high = value.astype(BF16)
    return high, (value - high.astype(F32)).astype(BF16)


def back_rows(capacity):
    return 4 * capacity + max(8, capacity)


def remap_out_kernel(
    capacity, grid_y, tile_rows, block_h, owner_h, row_h, tile_h, atm_h, weights_h, out_h, field_h, wet_h,
    out, block_s, owner_s, row_s, tile_s, rank_s, field_s, wet_s, atm, weights, atm_rows, flux_rows, flux, fill, rows_sum, cols_sum, rows_acc, cols_acc, sems, weight_sems, out_sems,
):
    devices = fill.shape[0]
    npairs = block_s.shape[0]
    tiles = weights.shape[0]
    nblocks = flux.shape[0]
    message = 4 * capacity + EDGE
    copies = [
        pltpu.make_async_copy(src, dst, sems.at[n])
        for n, (src, dst) in enumerate(
            [(atm_h, atm), (block_h, block_s), (owner_h, owner_s), (row_h, row_s), (tile_h, tile_s)]
        )
    ]
    for copy in copies:
        copy.start()
    part_tiles = tiles // PARTS
    parts = [pl.ds(n * part_tiles, part_tiles) for n in range(PARTS)]
    loads = [pltpu.make_async_copy(weights_h.at[at], weights.at[at], weight_sems.at[n]) for n, at in enumerate(parts)]
    for load in loads:
        load.start()
    out[...] = jnp.zeros_like(out)
    rows_sum[...] = jnp.zeros_like(rows_sum)
    rows_acc[...] = jnp.zeros_like(rows_acc)
    cols_acc[...] = jnp.zeros_like(cols_acc)
    cols_sum[...] = jnp.zeros_like(cols_sum)

    def clear_fill(i, carry):
        fill[i] = 0
        return carry

    lax.fori_loop(0, devices, clear_fill, 0, unroll=16)
    flux_rows[...] = jnp.zeros_like(flux_rows)
    wait_all(copies)
    for b in range(nblocks):
        atm_rows[8 * b : 8 * b + 6, :] = atm[:, b * LANES : (b + 1) * LANES]
    wind_u, wind_v, air, dry, rain, sea = [atm_rows[pl.ds(n, nblocks, stride=8), :] for n in range(6)]
    speed = jnp.sqrt(wind_u * wind_u + wind_v * wind_v + 0.25)
    heat = 0.5 * speed * (air - sea)
    water = rain - 0.3 * speed * dry
    planes = [heat, water, 0.2 * speed * wind_u, 0.2 * speed * wind_v]
    for n, plane in list(enumerate(planes)) + [(8 + n, heat) for n in range(4)] + [(12 + n, water) for n in range(4)]:
        flux_rows[pl.ds(n, nblocks, stride=16), :] = plane
    for b in range(nblocks):
        flux[b] = flux_rows[16 * b : 16 * (b + 1), :].astype(BF16)

    height = back_rows(capacity)


    def place(p):
        owner = owner_s[p]
        rank = fill[owner]
        fill[owner] = rank + 1
        field_s[p] = owner * height + 4 * rank
        wet_s[p] = owner * height + 4 * capacity + rank
        rank_s[p] = rank

    for p in range(AHEAD):
        place(p)
    wait_all(loads)

    sub = iota((8, LANES), 0)
    lane = iota((8, LANES), 1)
    part = sub % 4
    edge_row = jnp.where(part == 0, 0, jnp.where(part == 1, 1, tile_rows - 4 + part))
    band = ((lane - part) >> 2) * 4 + part
    id_rank = jnp.where(sub == 0, lane - NUMBERS, -1)

    def pair(p, n):
        owner = owner_s[p]
        row = row_s[p]
        rank = rank_s[p]
        value = jnp.dot(flux[block_s[p]], weights[tile_s[p]], preferred_element_type=F32)
        out[pl.ds(owner * message + 4 * rank, 4), :] = value[0:4]
        tracer = value[8:16]
        rows_sum[n, owner] = rows_sum[n, owner] + pick(edge_row == row, tracer)
        number = (row + 1).astype(F32)
        cols_sum[n, owner] = cols_sum[n, owner] + (
            pick(band == row, pltpu.roll(tracer, row + 2, 1)) + pick(id_rank == rank, number)
        )

    many = rows_sum.shape[0]

    def pairs(more, k, carry):
        for n in range(many):
            p = many * k + n
            if more:
                place(p + AHEAD)
            pair(p, n)
        return carry

    lax.fori_loop(0, (npairs - AHEAD) // many, functools.partial(pairs, True), 0, unroll=AHEAD // many)
    stores = start_all([(field_s, field_h), (wet_s, wet_h)], out_sems, SENDS)
    lax.fori_loop((npairs - AHEAD) // many, npairs // many, functools.partial(pairs, False), 0, unroll=AHEAD // many)

    across = grid_y + 2

    def inside(d):
        return (lax.div(d, grid_y) + 1) * across + lax.rem(d, grid_y) + 1

    def owner_step(d, carry):
        at = inside(d)
        rows_acc[at] = (rows_sum[0, d] + rows_sum[1, d]) + (rows_sum[2, d] + rows_sum[3, d])
        cols_acc[at] = (cols_sum[0, d] + cols_sum[1, d]) + (cols_sum[2, d] + cols_sum[3, d])
        return carry

    lax.fori_loop(0, devices, owner_step, 0, unroll=8)

    from_left = (lane - sub) % 4 < 2
    in_band = lane < tile_rows + 4
    in_ids = (sub == 0) & (lane >= NUMBERS) & (lane < NUMBERS + capacity)
    last, first = part == 3, part == 0
    upper_left, upper_right = last & (lane == tile_rows), last & (lane == tile_rows + 1)
    lower_left, lower_right = first & (lane == 1), first & (lane == 2)

    def edge_step(d, carry):
        at = inside(d)
        base = d * message + 4 * capacity
        out[pl.ds(pl.multiple_of(base, 8), 8), :] = jnp.where(part < 2, rows_acc[at + across], rows_acc[at - across])
        tile = pick(in_band, jnp.where(from_left, cols_acc[at - 1], cols_acc[at + 1]))
        upper = pick(upper_left, cols_acc[at - across - 1]) + pick(upper_right, cols_acc[at - across + 1])
        lower = pick(lower_left, cols_acc[at + across - 1]) + pick(lower_right, cols_acc[at + across + 1])
        tile = tile + pltpu.roll(upper, CORNERS - tile_rows, 1) + pltpu.roll(lower, CORNERS + 1, 1)
        out[pl.ds(pl.multiple_of(base + 8, 8), 8), :] = tile + pick(in_ids, cols_acc[at])
        return carry

    send = devices // SENDS
    for n in range(SENDS):
        lax.fori_loop(n * send, (n + 1) * send, edge_step, 0, unroll=4)
        piece = pl.ds(n * send * message, send * message)
        stores += start_all([(out.at[piece], out_h.at[piece])], out_sems, n)
    for store in stores:
        store.wait()


def remap_out(capacity, grid_y, devices, tile_rows, atm_state, pair_block, owner, pair_row, pair_tile, remap_weight):
    npairs = pair_block.shape[0]
    nblocks = atm_state.shape[1] // LANES
    message = 4 * capacity + EDGE
    border = (devices // grid_y + 2) * (grid_y + 2)
    return pl.pallas_call(
        functools.partial(remap_out_kernel, capacity, grid_y, tile_rows),
        out_shape=(
            pltpu.HBM((devices * message, LANES), F32),
            pltpu.HBM((npairs,), I32),
            pltpu.HBM((npairs,), I32),
        ),
        in_specs=[hbm()] * 6,
        out_specs=(hbm(),) * 3,
        scratch_shapes=[pltpu.VMEM((devices * message, LANES), F32)]
        + [pltpu.SMEM((npairs,), I32)] * 7
        + [
            pltpu.VMEM(atm_state.shape, F32),
            pltpu.VMEM(remap_weight.shape, BF16),
            pltpu.VMEM((nblocks * 8, LANES), F32),
            pltpu.VMEM((nblocks * 16, LANES), F32),
            pltpu.VMEM((nblocks, 16, LANES), BF16),
            pltpu.SMEM((devices,), I32),
            pltpu.VMEM((4, devices, 8, LANES), F32),
            pltpu.VMEM((4, devices, 8, LANES), F32),
            pltpu.VMEM((border, 8, LANES), F32),
            pltpu.VMEM((border, 8, LANES), F32),
            pltpu.SemaphoreType.DMA((5,)),
            pltpu.SemaphoreType.DMA((PARTS,)),
            pltpu.SemaphoreType.DMA((SENDS + 2,)),
        ],
        compiler_params=pltpu.CompilerParams(vmem_limit_bytes=40 << 20),
        cost_estimate=pl.CostEstimate(
            flops=2 * npairs * 16 * LANES * LANES, bytes_accessed=6 << 20, transcendentals=0
        ),
    )(*pin(pair_block, owner, pair_row, pair_tile, atm_state, remap_weight))


def solve_kernel(state, kappa, horiz, wet, tracer, currents_h, edge_up, edge_down, currents, sems):
    levels = kappa.shape[0]
    rows_all = kappa.shape[1]
    planes = tracer.shape[0]

    def chunk(c, carry):
        rows = pl.ds(pl.multiple_of(c * 8, 8), 8)
        column = [kappa[l, rows, :] for l in range(levels)]
        face = [0.5 * (column[l] + column[l + 1]) for l in range(levels - 1)]
        upper = []
        now = None
        for l in range(levels):
            diagonal = 1.0
            if l > 0:
                diagonal = diagonal + face[l - 1]
            if l < levels - 1:
                diagonal = diagonal + face[l]
            if l > 0:
                diagonal = diagonal + face[l - 1] * upper[-1]
            inverse = 1.0 / diagonal
            if l == 0:
                now = [state[f, 0, rows, :] * inverse for f in range(4)] + [inverse]
            else:
                pull = face[l - 1] * inverse
                now = [state[f, l, rows, :] * inverse + pull * now[f] for f in range(4)] + [pull * now[4]]
            upper.append(-face[l] * inverse if l < levels - 1 else None)
            store(l, rows, now)
        for l in range(levels - 2, -1, -1):
            here = load(l, rows)
            now = [here[f] - upper[l] * now[f] for f in range(5)]
            store(l, rows, now)
        return carry

    def store(l, rows, now):
        tracer[l, rows, :] = now[0]
        tracer[levels + l, rows, :] = now[1]
        currents[0, l, rows, :] = now[2]
        currents[1, l, rows, :] = now[3]
        tracer[2 * levels + l, rows, :] = now[4]

    def load(l, rows):
        return [
            tracer[l, rows, :],
            tracer[levels + l, rows, :],
            currents[0, l, rows, :],
            currents[1, l, rows, :],
            tracer[2 * levels + l, rows, :],
        ]

    lax.fori_loop(0, rows_all // 8, chunk, 0)
    out = start_all([(currents, currents_h)], sems)
    tracer[3 * levels] = horiz[...]
    tracer[3 * levels + 1] = wet[...].astype(F32)
    for k in range(planes):
        edge_up[k] = tracer[k, 0:8, :]
        edge_down[k] = tracer[k, rows_all - 8 : rows_all, :]
    wait_all(out)


def solve(ocean_state, vert_kappa, horiz_kappa, wet_mask):
    levels, rows, _ = vert_kappa.shape
    planes = 3 * levels + 2
    return pl.pallas_call(
        solve_kernel,
        out_shape=(
            jax.ShapeDtypeStruct((planes, rows, LANES), F32),
            pltpu.HBM((2, levels, rows, LANES), F32),
            jax.ShapeDtypeStruct((planes, 8, LANES), F32),
            jax.ShapeDtypeStruct((planes, 8, LANES), F32),
        ),
        in_specs=[vmem()] * 4,
        out_specs=(vmem(), hbm(), vmem(), vmem()),
        scratch_shapes=[pltpu.VMEM((2, levels, rows, LANES), F32), pltpu.SemaphoreType.DMA((1,))],
        compiler_params=pltpu.CompilerParams(vmem_limit_bytes=24 << 20),
        cost_estimate=pl.CostEstimate(flops=20 << 20, bytes_accessed=6 << 20, transcendentals=0),
    )(ocean_state, vert_kappa, horiz_kappa, wet_mask)


def pack_kernel(levels, tracer, above, below, wide_h, to_left, to_right, wide, sems):
    planes, rows, _ = tracer.shape
    for k in range(planes):
        wide[k, 0:HALO, :] = above[k]
        wide[k, HALO : HALO + rows, :] = tracer[k]
        wide[k, HALO + rows : 2 * HALO + rows, :] = below[k]
    out = start_all([(wide, wide_h)], sems)
    lane = iota((8, LANES), 1)

    def chunk(c, carry):
        at = pl.ds(pl.multiple_of(c * 8, 8), 8)

        def place(values, lanes):
            left, right = jnp.zeros((8, LANES), F32), jnp.zeros((8, LANES), F32)
            for k, (near, far) in zip(values, lanes):
                value = wide[k, at, :]
                left = jnp.where(lane == near, pltpu.roll(value, near, 1), left)
                left = jnp.where(lane == far, pltpu.roll(value, far - 1, 1), left)
                right = jnp.where(lane == near + 1, pltpu.roll(value, (near + 2) % LANES, 1), right)
                right = jnp.where(lane == far + 1, pltpu.roll(value, (far + 3) % LANES, 1), right)
            return left, right

        left, right = place(range(2 * levels), [(2 * k, 64 + 2 * k) for k in range(2 * levels)])
        to_left[0, at, :] = left
        to_right[0, at, :] = right
        lanes = [(2 * l, 64 + 2 * l) for l in range(levels)]
        lanes += [(2 * levels, 2 * levels + 2), (2 * levels + 4, 2 * levels + 6)]
        left, right = place(range(2 * levels, 3 * levels + 2), lanes)
        to_left[1, at, :] = left
        to_right[1, at, :] = right
        return carry

    lax.fori_loop(0, (rows + 2 * HALO) // 8, chunk, 0)
    wait_all(out)


def pack(levels, tracer, above, below):
    planes, rows, _ = tracer.shape
    tall = rows + 2 * HALO
    return pl.pallas_call(
        functools.partial(pack_kernel, levels),
        out_shape=(
            pltpu.HBM((planes, tall, LANES), F32),
            jax.ShapeDtypeStruct((2, tall, LANES), F32),
            jax.ShapeDtypeStruct((2, tall, LANES), F32),
        ),
        in_specs=[vmem()] * 3,
        out_specs=(hbm(), vmem(), vmem()),
        scratch_shapes=[pltpu.VMEM((planes, tall, LANES), F32), pltpu.SemaphoreType.DMA((1,))],
        compiler_params=pltpu.CompilerParams(vmem_limit_bytes=24 << 20),
        cost_estimate=pl.CostEstimate(flops=8 << 20, bytes_accessed=4 << 20, transcendentals=0),
    )(tracer, above, below)


def set_faces(levels, h, w, own_left, own_right, from_left, from_right, faces, packed):
    tall = h.shape[0]
    lane = iota((tall, LANES), 1)
    odd = lane % 2 == 1
    twice = lane % 64 < 2 * levels
    left, left_unit, right, right_unit = from_left[0], from_left[1], from_right[0], from_right[1]
    other = jnp.where(odd, left_unit, right_unit)
    at = 2 * levels

    def column(offset):
        return other[:, at + offset : at + offset + 1], other[:, at + offset + 1 : at + offset + 2]

    kappa_right, kappa_left = column(0)
    kappa_far_right, kappa_far_left = column(2)
    wet_right, wet_left = column(4)
    wet_far_right, wet_far_left = column(6)

    kappa_near = jnp.where(odd, kappa_left, kappa_right)
    kappa_far = jnp.where(odd, kappa_far_left, kappa_far_right)
    wet_near = jnp.where(odd, wet_left, wet_right)
    wet_far = jnp.where(odd, wet_far_left, wet_far_right)
    kappa_own = jnp.where(odd, h[:, 0:1], h[:, LANES - 1 : LANES])
    wet_own = jnp.where(odd, w[:, 0:1], w[:, LANES - 1 : LANES])

    def face(kappa_a, wet_a, kappa_b, wet_b):
        return 0.25 * (kappa_a + kappa_b) * wet_a * wet_b

    unit = jnp.where(twice, other, pltpu.roll(other, 2 * levels, 1))
    packed[0] = jnp.where(odd, left, right)
    packed[1] = unit * jnp.where(lane < 64, wet_near, wet_far)
    left, left_unit, right, right_unit = own_left[0], own_left[1], own_right[0], own_right[1]
    packed[2] = jnp.where(odd, pltpu.roll(left, 1, 1), pltpu.roll(right, LANES - 1, 1))
    own = jnp.where(odd, pltpu.roll(left_unit, 1, 1), pltpu.roll(right_unit, LANES - 1, 1))
    packed[3] = jnp.where(twice, own, pltpu.roll(own, 2 * levels, 1)) * wet_own
    north = face(kappa_near, wet_near, pltpu.roll(kappa_near, 1, 0), pltpu.roll(wet_near, 1, 0))
    packed[4] = north
    packed[5] = pltpu.roll(north, tall - 1, 0)
    packed[6] = face(kappa_near, wet_near, kappa_far, wet_far)
    packed[7] = face(kappa_near, wet_near, kappa_own, wet_own)

    north = face(h, w, pltpu.roll(h, 1, 0), pltpu.roll(w, 1, 0))
    faces[0] = north
    faces[1] = pltpu.roll(north, tall - 1, 0)
    west = face(
        h, w, jnp.where(lane == 0, kappa_left, pltpu.roll(h, 1, 1)), jnp.where(lane == 0, wet_left, pltpu.roll(w, 1, 1))
    )
    faces[2] = west
    faces[3] = jnp.where(lane == LANES - 1, face(h, w, kappa_right, wet_right), pltpu.roll(west, LANES - 1, 1))


def set_beside(levels, upright, wide, packed, beside):
    tall = upright.shape[0]
    lane = iota((tall, LANES), 1)
    odd = lane % 2 == 1
    heat = lane % 64 < 2 * levels

    def chosen(f):
        left_far, left_near, right_near, right_far = [upright[:, 4 * f + e : 4 * f + e + 1] for e in range(4)]
        near = jnp.where(odd, left_near, right_near)
        return jnp.where(lane < 64, near, jnp.where(odd, left_far, right_far))

    both = packed[0] + packed[1] * jnp.where(heat, chosen(0), chosen(1))
    far = pltpu.roll(both, 64, 1)
    ends_of = [jnp.where(odd, w[:, 0:1], w[:, LANES - 1 : LANES]) for w in wide]
    own = packed[2] + packed[3] * jnp.where(heat, ends_of[0], ends_of[1])
    near = both + packed[5] * (pltpu.roll(both, tall - 1, 0) - both)
    near = near + packed[4] * (pltpu.roll(both, 1, 0) - both)
    near = near + packed[6] * (far - both)
    near = near + packed[7] * (own - both)
    beside[0] = both
    beside[1] = near


def one_pass(value, faces, beside, shift):
    tall = value.shape[0]
    lane = iota(value.shape, 1)
    moved = pltpu.roll(beside, shift, 1)
    west = jnp.where(lane == 0, moved, pltpu.roll(value, 1, 1))
    east = jnp.where(lane == LANES - 1, moved, pltpu.roll(value, LANES - 1, 1))
    result = value + faces[1] * (pltpu.roll(value, tall - 1, 0) - value)
    result = result + faces[0] * (pltpu.roll(value, 1, 0) - value)
    result = result + faces[3] * (east - value)
    return result + faces[2] * (west - value)


def middle_kernel(
    capacity, levels, arrived, wide_h, currents_h, own_left_h, own_right_h, from_left_h, from_right_h,
    sent_h, forcing_h, near_h, faces_h,
    placing, values, number_t, top, currents, own_left, own_right, from_left, from_right,
    faces, packed, sent, forcing, near_o, sems, sent_sems,
):
    devices, message, _ = arrived.shape
    rows_all = currents.shape[1]
    tall = rows_all + 2 * HALO
    loads = start_all(
        [(wide_h.at[levels * k], top.at[k]) for k in range(3)]
        + [
            (wide_h.at[pl.ds(3 * levels, 2)], top.at[pl.ds(3, 2)]),
            (currents_h.at[0, 0], currents.at[0]),
            (currents_h.at[1, 0], currents.at[1]),
            (own_left_h, own_left),
            (own_right_h, own_right),
            (from_left_h, from_left),
            (from_right_h, from_right),
        ],
        sems,
    )
    span = 4 * capacity
    group = LANES // span
    groups = devices // group
    sub8 = iota((8, LANES), 0)
    lane8 = iota((8, LANES), 1)

    lane1 = iota((1, LANES), 1)
    spread = (iota((LANES, LANES), 0) - NUMBERS) == iota((LANES, LANES), 1) % span // 4
    every = jnp.concatenate([arrived[s, span + 8 : span + 9, :] for s in range(devices)], 0).astype(BF16)
    every = jnp.dot(every, jnp.where(spread, 1.0, 0.0).astype(BF16), preferred_element_type=F32)
    numbers = []
    for m in range(groups):
        line = jnp.zeros((1, LANES), F32)
        for g in range(group):
            s = m * group + g
            line = jnp.where(lane1 // span == g, every[s : s + 1], line)
        numbers.append(line)
    number_t[...] = jnp.transpose(
        jnp.concatenate(numbers + [jnp.zeros((LANES - groups, LANES), F32)], 0)
    )

    row_number = iota((rows_all, LANES), 0).astype(F32) + 1.0
    for m in range(groups):
        for f in range(4):
            placing[f * rows_all : (f + 1) * rows_all, m * LANES : (m + 1) * LANES] = jnp.where(
                pick(lane1 % 4 == f, numbers[m]) == row_number, 1.0, 0.0
            ).astype(BF16)
    edge_rows = jnp.zeros((8, LANES), F32)
    edge_cols = jnp.zeros((8, LANES), F32)
    for s in range(devices):
        high, low = split(arrived[s, 0:span, :])
        values[s * span : (s + 1) * span, 0:LANES] = high
        values[s * span : (s + 1) * span, LANES : 2 * LANES] = low
        edge_rows = edge_rows + arrived[s, span : span + 8, :]
        edge_cols = edge_cols + arrived[s, span + 8 : span + 16, :]
    wait_all(loads)
    set_faces(levels, top[3], top[4], own_left, own_right, from_left, from_right, faces, packed)
    wet_wide = top[4]
    total = jnp.dot(placing[...], values[...], preferred_element_type=F32)
    total = total[:, 0:LANES] + total[:, LANES : 2 * LANES]


    def plane(f):
        return total[f * rows_all : (f + 1) * rows_all]

    wide = []
    for f in range(2):
        before = pick(sub8 >= 6, edge_rows if f == 1 else pltpu.roll(edge_rows, 4, 0))
        after = pick(sub8 < 2, edge_rows if f == 0 else pltpu.roll(edge_rows, 4, 0))
        wide.append(jnp.concatenate([before, plane(f), after], 0))
        forcing[f] = wide[f]
    wet = wet_wide[HALO : HALO + rows_all]
    for f in range(2, 4):
        forcing[f, 0:HALO, :] = jnp.zeros((HALO, LANES), F32)
        forcing[f, HALO : HALO + rows_all, :] = plane(f) * wet
        forcing[f, HALO + rows_all : tall, :] = jnp.zeros((HALO, LANES), F32)

    part8 = sub8 % 4
    within = (part8 == lane8 % 4) & (lane8 >= HALO) & (lane8 < HALO + rows_all)
    upper = (part8 == 3) & (lane8 == HALO - 1)
    lower = (part8 == 0) & (lane8 == HALO + rows_all)
    halves = [[], []]
    for k in range(4):
        column = pick(within, pltpu.roll(edge_cols, HALO - k, 1))
        if k in (1, 2):
            column = column + pick(upper, pltpu.roll(edge_cols, (HALO - CORNERS - k) % LANES, 1))
            column = column + pick(lower, pltpu.roll(edge_cols, (HALO + rows_all - CORNERS - 1 - k) % LANES, 1))
        for f in range(2):
            halves[f].append(jnp.sum(column[4 * f : 4 * f + 4], axis=0, keepdims=True))
    columns = jnp.concatenate(halves[0] + halves[1], 0)
    upright = jnp.transpose(jnp.concatenate([columns, jnp.zeros((LANES - 8, LANES), F32)], 0))[0:tall]
    set_beside(levels, upright, wide, packed, near_o)
    stores = start_all([(forcing, forcing_h), (near_o, near_h), (faces, faces_h)], sems, 10)

    surface = []
    unit = top[2] * wet_wide
    for f in range(2):
        value = top[f] + unit * wide[f]
        shift = LANES - (2 * levels * f + 1)
        value = one_pass(value, faces, near_o[0], shift)
        value = one_pass(value, faces, near_o[1], shift)
        surface.append(value[HALO : HALO + rows_all] * wet)
    for f in range(2):
        surface.append(
            (currents[f] + top[2, HALO : HALO + rows_all, :] * forcing[2 + f, HALO : HALO + rows_all, :]) * wet
        )
    high, low = split(jnp.concatenate(surface, 0))
    source = jnp.concatenate([high, low], 1)
    lane_t = iota((LANES, 4 * rows_all), 1)
    sub_t = iota((LANES, 4 * rows_all), 0)
    target = jnp.where(sub_t % 4 == lane_t // rows_all, lane_t % rows_all + 1, -1).astype(F32)
    mask = jnp.concatenate([wet, jnp.zeros((LANES - rows_all, LANES), F32)], 0).astype(BF16)
    per = LANES // 4
    slot_number = number_t[pl.ds(0, per, stride=4), :]
    lane_s = (iota((per, LANES), 1) + 1).astype(F32)
    height = back_rows(capacity)
    many = 4
    for first in range(0, groups, many):
        these = range(first, first + many)
        chosen_rows = [jnp.where(number_t[:, m : m + 1] == target, 1.0, 0.0).astype(BF16) for m in these]
        rows = jnp.dot(jnp.concatenate(chosen_rows, 0), source, preferred_element_type=F32)
        rows = rows[:, 0:LANES] + rows[:, LANES : 2 * LANES]
        slots = [jnp.where(slot_number[:, m : m + 1] == lane_s, 1.0, 0.0) for m in these]
        masks = jnp.dot(jnp.concatenate(slots, 0).astype(BF16), mask, preferred_element_type=F32)
        for g in range(many * group):
            s = first * group + g
            sent[s, 0:span, :] = rows[g * span : (g + 1) * span]
            sent[s, span : span + capacity, :] = masks[g * capacity : (g + 1) * capacity]
            if height > span + capacity:
                sent[s, span + capacity : height, :] = jnp.zeros((height - span - capacity, LANES), F32)
        at = pl.ds(first * group, many * group)
        stores += start_all([(sent.at[at], sent_h.at[at])], sent_sems, first // many)
    wait_all(stores)


def middle(capacity, levels, arrived, wide, currents, *columns):
    devices = arrived.shape[0]
    rows = currents.shape[2]
    tall = rows + 2 * HALO
    height = back_rows(capacity)
    return pl.pallas_call(
        functools.partial(middle_kernel, capacity, levels),
        out_shape=(
            pltpu.HBM((devices, height, LANES), F32),
            pltpu.HBM((4, tall, LANES), F32),
            pltpu.HBM((2, tall, LANES), F32),
            pltpu.HBM((4, tall, LANES), F32),
        ),
        in_specs=[vmem()] + [hbm()] * 2 + [pl.BlockSpec(memory_space=pl.ANY)] * 4,
        out_specs=(hbm(),) * 4,
        scratch_shapes=[
            pltpu.VMEM((4 * rows, 4 * capacity * devices), BF16),
            pltpu.VMEM((4 * capacity * devices, 2 * LANES), BF16),
            pltpu.VMEM((LANES, LANES), F32),
            pltpu.VMEM((5, tall, LANES), F32),
            pltpu.VMEM((2, rows, LANES), F32),
        ]
        + [pltpu.VMEM((2, tall, LANES), F32)] * 4
        + [
            pltpu.VMEM((4, tall, LANES), F32),
            pltpu.VMEM((8, tall, LANES), F32),
            pltpu.VMEM((devices, height, LANES), F32),
            pltpu.VMEM((4, tall, LANES), F32),
            pltpu.VMEM((2, tall, LANES), F32),
            pltpu.SemaphoreType.DMA((13,)),
            pltpu.SemaphoreType.DMA((4 * capacity * devices // LANES,)),
        ],
        compiler_params=pltpu.CompilerParams(vmem_limit_bytes=24 << 20),
        cost_estimate=pl.CostEstimate(flops=200 << 20, bytes_accessed=4 << 20, transcendentals=0),
    )(arrived, *pin(wide, currents), *columns)


def finish_kernel(
    levels, wide_h, currents_h, faces_h, forcing_h, near_h, ocean, wide, currents, faces, forcing, near, sems
):
    rows_all = currents.shape[2]
    wait_all(
        start_all(
            [(wide_h, wide), (currents_h, currents), (faces_h, faces), (forcing_h, forcing), (near_h, near)], sems
        )
    )
    inner = slice(HALO, HALO + rows_all)

    def level(l, carry):
        unit = wide[2 * levels + l]
        masked = unit * wide[3 * levels + 1]
        for f in range(2):
            value = wide[f * levels + l] + masked * forcing[f]
            shift = LANES - 1 - 2 * (levels * f + l)
            value = one_pass(value, faces, near[0], shift)
            value = one_pass(value, faces, near[1], shift)
            ocean[f, l] = value[inner]
            ocean[2 + f, l] = currents[f, l] + unit[inner] * forcing[2 + f][inner]
        return carry

    lax.fori_loop(0, levels, level, 0)


def finish(levels, wide, currents, faces, forcing, near):
    rows = currents.shape[2]
    return pl.pallas_call(
        functools.partial(finish_kernel, levels),
        out_shape=jax.ShapeDtypeStruct((4, levels, rows, LANES), F32),
        in_specs=[hbm()] * 5,
        out_specs=vmem(),
        scratch_shapes=[pltpu.VMEM(a.shape, F32) for a in (wide, currents, faces, forcing, near)]
        + [pltpu.SemaphoreType.DMA((5,))],
        compiler_params=pltpu.CompilerParams(vmem_limit_bytes=24 << 20),
        cost_estimate=pl.CostEstimate(flops=40 << 20, bytes_accessed=6 << 20, transcendentals=0),
    )(*pin(wide, currents, faces, forcing, near))


def turn_kernel(weights_h, turned_h, weights, turned, sems, out_sems):
    part_tiles = weights.shape[0] // PARTS
    parts = [pl.ds(n * part_tiles, part_tiles) for n in range(PARTS)]
    loads = start_all([(weights_h.at[at], weights.at[at]) for at in parts], sems)
    stores = []
    for n, at in enumerate(parts):
        loads[n].wait()

        def tile_step(t, carry):
            turned[t] = weights[t].T
            return carry

        lax.fori_loop(n * part_tiles, (n + 1) * part_tiles, tile_step, 0, unroll=4)
        stores += start_all([(turned.at[at], turned_h.at[at])], out_sems, n)
    wait_all(stores)


def turn(remap_weight):
    return pl.pallas_call(
        turn_kernel,
        out_shape=pltpu.HBM(remap_weight.shape, BF16),
        in_specs=[hbm()],
        out_specs=hbm(),
        scratch_shapes=[pltpu.VMEM(remap_weight.shape, BF16)] * 2 + [pltpu.SemaphoreType.DMA((PARTS,))] * 2,
        compiler_params=pltpu.CompilerParams(vmem_limit_bytes=24 << 20),
        cost_estimate=pl.CostEstimate(flops=8 << 20, bytes_accessed=8 << 20, transcendentals=0),
    )(*pin(remap_weight))


def remap_back_kernel(
    block_h, tile_h, field_h, wet_h, returned, weights_h, out,
    block_s, tile_s, field_s, wet_s, weights, picked_a, picked_b, total_0, total_1, total_2, total_3, sems, weight_sems,
):
    npairs = block_s.shape[0]
    totals = [total_0, total_1, total_2, total_3]
    nblocks = total_0.shape[0]
    scalars = start_all([(field_h, field_s), (wet_h, wet_s), (block_h, block_s), (tile_h, tile_s)], sems)
    part_tiles = weights.shape[0] // PARTS
    parts = [pl.ds(n * part_tiles, part_tiles) for n in range(PARTS)]
    loads = start_all([(weights_h.at[at], weights.at[at]) for at in parts], weight_sems)
    for total in totals:
        total[...] = jnp.zeros_like(total)
    wait_all(scalars)

    def gather(p, picked, at):
        rows = returned[pl.ds(field_s[p], 4), :]
        mask = returned[pl.ds(wet_s[p] - 7, 8), :]
        high, low = split(jnp.concatenate([rows, jnp.zeros((3, LANES), F32), mask[7:8]], 0))
        picked[at] = jnp.concatenate([high, low], 0)

    def product(p, picked, at, total):
        value = jnp.dot(picked[at], weights[tile_s[p]], preferred_element_type=F32)
        b = block_s[p]
        total[b] = total[b] + (value[0:8] + value[8:16])

    half = npairs // 2
    many = len(totals)

    def first(p, carry):
        gather(p, picked_a, p)
        return carry

    def both(p, carry):
        for n in range(many):
            gather(half + many * p + n, picked_b, many * p + n)
            product(many * p + n, picked_a, many * p + n, totals[n])
        return carry

    def last(p, carry):
        for n in range(many):
            product(half + many * p + n, picked_b, many * p + n, totals[n])
        return carry

    lax.fori_loop(0, half, first, 0, unroll=32)
    wait_all(loads)
    lax.fori_loop(0, half // many, both, 0, unroll=16)
    lax.fori_loop(0, half // many, last, 0, unroll=16)
    for b in range(nblocks):
        sums = (total_0[b] + total_1[b]) + (total_2[b] + total_3[b])
        out[:, b * LANES : (b + 1) * LANES] = sums[0:4] / jnp.maximum(sums[7:8], 0.1)


def remap_back(pair_block, pair_tile, field_at, wet_at, returned, weights, nblocks):
    npairs = pair_block.shape[0]
    return pl.pallas_call(
        remap_back_kernel,
        out_shape=jax.ShapeDtypeStruct((4, nblocks * LANES), F32),
        in_specs=[hbm()] * 4 + [vmem(), hbm()],
        out_specs=vmem(),
        scratch_shapes=[pltpu.SMEM((npairs,), I32)] * 4
        + [pltpu.VMEM(weights.shape, BF16)]
        + [pltpu.VMEM((npairs // 2, 16, LANES), BF16)] * 2
        + [pltpu.VMEM((nblocks, 8, LANES), F32)] * 4
        + [pltpu.SemaphoreType.DMA((4,)), pltpu.SemaphoreType.DMA((PARTS,))],
        compiler_params=pltpu.CompilerParams(vmem_limit_bytes=24 << 20),
        cost_estimate=pl.CostEstimate(flops=2 * npairs * 16 * LANES * LANES, bytes_accessed=6 << 20, transcendentals=0),
    )(*pin(pair_block, pair_tile, field_at, wet_at), returned, *pin(weights))


def local(
    atm_state,
    pair_block,
    pair_owner,
    pair_row,
    pair_tile,
    remap_weight,
    wet_mask,
    ocean_state,
    vert_kappa,
    horiz_kappa,
):
    grid_x = lax.axis_size("gx")
    grid_y = lax.axis_size("gy")
    devices = grid_x * grid_y
    npairs = pair_block.shape[0]
    capacity = max(2, 2 * npairs // devices)
    levels, tile_rows, _ = vert_kappa.shape
    nblocks = atm_state.shape[1] // LANES
    owner = pair_owner.reshape(npairs)
    message = 4 * capacity + EDGE
    outgoing, field_at, wet_at = remap_out(
        capacity, grid_y, devices, tile_rows, atm_state, pair_block, owner, pair_row, pair_tile, remap_weight
    )
    arrived = lax.all_to_all(
        outgoing.reshape(devices, message, LANES), ("gx", "gy"), split_axis=0, concat_axis=0, tiled=True
    )
    tracer, currents, edge_up, edge_down = solve(ocean_state, vert_kappa, horiz_kappa, wet_mask)
    rise_x = [(i, i + 1) for i in range(grid_x - 1)]
    fall_x = [(b, a) for a, b in rise_x]
    rise_y = [(i, i + 1) for i in range(grid_y - 1)]
    fall_y = [(b, a) for a, b in rise_y]
    above = lax.ppermute(edge_down, "gx", rise_x)
    below = lax.ppermute(edge_up, "gx", fall_x)
    wide, to_left, to_right = pack(levels, tracer, above, below)
    from_left = lax.ppermute(to_right, "gy", rise_y)
    from_right = lax.ppermute(to_left, "gy", fall_y)
    sent, forcing, near, faces = middle(
        capacity, levels, arrived, wide, currents, to_left, to_right, from_left, from_right
    )
    returned = lax.all_to_all(sent, ("gx", "gy"), split_axis=0, concat_axis=0, tiled=True)
    ocean_next = finish(levels, wide, currents, faces, forcing, near)
    weights, _ = lax.optimization_barrier((remap_weight, near))
    atm_surface = remap_back(
        pair_block, pair_tile, field_at, wet_at, returned.reshape(-1, LANES), turn(weights), nblocks
    )
    return (ocean_next, atm_surface)


def solution(mesh):
    placed = (
        P(None, ("gx", "gy")),
        P(("gx", "gy")),
        P(("gx", "gy"), None),
        P(("gx", "gy")),
        P(("gx", "gy")),
        P(("gx", "gy"), None, None),
        P("gx", "gy"),
        P(None, None, "gx", "gy"),
        P(None, "gx", "gy"),
        P("gx", "gy"),
    )
    return jax.shard_map(
        local,
        mesh=mesh,
        in_specs=placed,
        out_specs=(P(None, None, "gx", "gy"), P(None, ("gx", "gy"))),
        check_vma=False,
    )
```

```python
import functools

import jax
import jax.numpy as jnp
from jax import lax
from jax.experimental import pallas as pl
from jax.experimental.pallas import tpu as pltpu
from jax.sharding import PartitionSpec as P

F32 = jnp.float32
BF16 = jnp.bfloat16
I32 = jnp.int32
VMEM = pltpu.VMEM
SMEM = pltpu.SMEM
LANES = 128
EDGE = 16
HALO = 8
NUMBERS = 72
CORNERS = 112
SENDS = 8
AHEAD = 64
PARTS = 8


def hbm():
    return pl.BlockSpec(memory_space=pltpu.HBM)


def vmem():
    return pl.BlockSpec(memory_space=VMEM)


def pin(*arrays):
    return [pltpu.with_memory_space_constraint(a, pltpu.HBM) for a in arrays]


def start_all(pairs, sems, first=0):
    copies = [pltpu.make_async_copy(src, dst, sems.at[first + n]) for n, (src, dst) in enumerate(pairs)]
    for copy in copies:
        copy.start()
    return copies


def wait_all(copies):
    for copy in copies:
        copy.wait()


def iota(shape, dim):
    return lax.broadcasted_iota(I32, shape, dim)


def pick(mask, value):
    return jnp.where(mask, value, 0.0)


def split(value):
    high = value.astype(BF16)
    return high, (value - high.astype(F32)).astype(BF16)


def back_rows(capacity):
    return 4 * capacity + max(8, capacity)


def remap_out_kernel(
    capacity, grid_y, tile_rows, block_h, owner_h, row_h, tile_h, atm_h, weights_h, out_h, field_h, wet_h,
    out, block_s, owner_s, row_s, tile_s, rank_s, field_s, wet_s, atm, weights, atm_rows, flux_rows, flux, fill, rows_sum, cols_sum, rows_acc, cols_acc, sems, weight_sems, out_sems,
):
    devices = fill.shape[0]
    npairs = block_s.shape[0]
    tiles = weights.shape[0]
    nblocks = flux.shape[0]
    message = 4 * capacity + EDGE
    copies = [
        pltpu.make_async_copy(src, dst, sems.at[n])
        for n, (src, dst) in enumerate(
            [(atm_h, atm), (block_h, block_s), (owner_h, owner_s), (row_h, row_s), (tile_h, tile_s)]
        )
    ]
    for copy in copies:
        copy.start()
    part_tiles = tiles // PARTS
    parts = [pl.ds(n * part_tiles, part_tiles) for n in range(PARTS)]
    loads = [pltpu.make_async_copy(weights_h.at[at], weights.at[at], weight_sems.at[n]) for n, at in enumerate(parts)]
    for load in loads:
        load.start()
    out[...] = jnp.zeros_like(out)
    rows_sum[...] = jnp.zeros_like(rows_sum)
    cols_sum[...] = jnp.zeros_like(cols_sum)

    def clear_fill(i, carry):
        fill[i] = 0
        return carry

    lax.fori_loop(0, devices, clear_fill, 0, unroll=16)
    flux_rows[...] = jnp.zeros_like(flux_rows)
    wait_all(copies)
    for b in range(nblocks):
        atm_rows[8 * b : 8 * b + 6, :] = atm[:, b * LANES : (b + 1) * LANES]
    wind_u, wind_v, air, dry, rain, sea = [atm_rows[pl.ds(n, nblocks, stride=8), :] for n in range(6)]
    speed = jnp.sqrt(wind_u * wind_u + wind_v * wind_v + 0.25)
    heat = 0.5 * speed * (air - sea)
    water = rain - 0.3 * speed * dry
    planes = [heat, water, 0.2 * speed * wind_u, 0.2 * speed * wind_v]
    for n, plane in list(enumerate(planes)) + [(8 + n, heat) for n in range(4)] + [(12 + n, water) for n in range(4)]:
        flux_rows[pl.ds(n, nblocks, stride=16), :] = plane
    for b in range(nblocks):
        flux[b] = flux_rows[16 * b : 16 * (b + 1), :].astype(BF16)

    height = back_rows(capacity)


    def place(p):
        owner = owner_s[p]
        rank = fill[owner]
        fill[owner] = rank + 1
        field_s[p] = owner * height + 4 * rank
        wet_s[p] = owner * height + 4 * capacity + rank
        rank_s[p] = rank

    for p in range(AHEAD):
        place(p)
    wait_all(loads)

    sub = iota((8, LANES), 0)
    lane = iota((8, LANES), 1)
    part = sub % 4
    edge_row = jnp.where(part == 0, 0, jnp.where(part == 1, 1, tile_rows - 4 + part))
    band = ((lane - part) >> 2) * 4 + part
    id_rank = jnp.where(sub == 0, lane - NUMBERS, -1)

    def pair(p, n):
        owner = owner_s[p]
        row = row_s[p]
        rank = rank_s[p]
        value = jnp.dot(flux[block_s[p]], weights[tile_s[p]], preferred_element_type=F32)
        out[pl.ds(owner * message + 4 * rank, 4), :] = value[0:4]
        tracer = value[8:16]
        rows_sum[n, owner] = rows_sum[n, owner] + pick(edge_row == row, tracer)
        number = (row + 1).astype(F32)
        cols_sum[n, owner] = cols_sum[n, owner] + (
            pick(band == row, pltpu.roll(tracer, row + 2, 1)) + pick(id_rank == rank, number)
        )

    many = rows_sum.shape[0]

    def pairs(more, k, carry):
        for n in range(many):
            p = many * k + n
            if more:
                place(p + AHEAD)
            pair(p, n)
        return carry

    lax.fori_loop(0, (npairs - AHEAD) // many, functools.partial(pairs, True), 0, unroll=True)
    stores = start_all([(field_s, field_h), (wet_s, wet_h)], out_sems, SENDS)
    lax.fori_loop((npairs - AHEAD) // many, npairs // many, functools.partial(pairs, False), 0, unroll=True)

    def owner_step(d, carry):
        rows_acc[d] = (rows_sum[0, d] + rows_sum[1, d]) + (rows_sum[2, d] + rows_sum[3, d])
        cols_acc[d] = (cols_sum[0, d] + cols_sum[1, d]) + (cols_sum[2, d] + cols_sum[3, d])
        return carry

    lax.fori_loop(0, devices, owner_step, 0, unroll=32)

    grid_x = devices // grid_y
    zero = jnp.zeros((8, LANES), F32)

    def columns_of(i, j):
        if not (0 <= i < grid_x and 0 <= j < grid_y):
            return zero
        return cols_acc[i * grid_y + j]

    from_left = (lane - sub) % 4 < 2
    in_band = lane < tile_rows + 4
    in_ids = (sub == 0) & (lane >= NUMBERS) & (lane < NUMBERS + capacity)
    last, first = part == 3, part == 0
    send = devices // SENDS
    for d in range(devices):
        i, j = d // grid_y, d % grid_y
        below = rows_acc[d + grid_y] if i < grid_x - 1 else zero
        above = rows_acc[d - grid_y] if i > 0 else zero
        base = d * message + 4 * capacity
        out[base : base + 8, :] = jnp.where(part < 2, below, above)
        tile = pick(in_band, jnp.where(from_left, columns_of(i, j - 1), columns_of(i, j + 1)))
        upper = pick(last & (lane == tile_rows), columns_of(i - 1, j - 1))
        upper = upper + pick(last & (lane == tile_rows + 1), columns_of(i - 1, j + 1))
        lower = pick(first & (lane == 1), columns_of(i + 1, j - 1))
        lower = lower + pick(first & (lane == 2), columns_of(i + 1, j + 1))
        tile = tile + pltpu.roll(upper, CORNERS - tile_rows, 1) + pltpu.roll(lower, CORNERS + 1, 1)
        tile = tile + pick(in_ids, cols_acc[d])
        out[base + 8 : base + 16, :] = tile
        if d % send == send - 1:
            n = d // send
            at = pl.ds(n * send * message, send * message)
            stores.append(pltpu.make_async_copy(out.at[at], out_h.at[at], out_sems.at[n]))
            stores[-1].start()
    for store in stores:
        store.wait()


def remap_out(capacity, grid_y, devices, tile_rows, atm_state, pair_block, owner, pair_row, pair_tile, remap_weight):
    npairs = pair_block.shape[0]
    nblocks = atm_state.shape[1] // LANES
    message = 4 * capacity + EDGE
    return pl.pallas_call(
        functools.partial(remap_out_kernel, capacity, grid_y, tile_rows),
        out_shape=(
            pltpu.HBM((devices * message, LANES), F32),
            pltpu.HBM((npairs,), I32),
            pltpu.HBM((npairs,), I32),
        ),
        in_specs=[hbm()] * 6,
        out_specs=(hbm(),) * 3,
        scratch_shapes=[pltpu.VMEM((devices * message, LANES), F32)]
        + [pltpu.SMEM((npairs,), I32)] * 7
        + [
            pltpu.VMEM(atm_state.shape, F32),
            pltpu.VMEM(remap_weight.shape, BF16),
            pltpu.VMEM((nblocks * 8, LANES), F32),
            pltpu.VMEM((nblocks * 16, LANES), F32),
            pltpu.VMEM((nblocks, 16, LANES), BF16),
            pltpu.SMEM((devices,), I32),
            pltpu.VMEM((4, devices, 8, LANES), F32),
            pltpu.VMEM((4, devices, 8, LANES), F32),
            pltpu.VMEM((devices, 8, LANES), F32),
            pltpu.VMEM((devices, 8, LANES), F32),
            pltpu.SemaphoreType.DMA((5,)),
            pltpu.SemaphoreType.DMA((PARTS,)),
            pltpu.SemaphoreType.DMA((SENDS + 2,)),
        ],
        compiler_params=pltpu.CompilerParams(vmem_limit_bytes=40 << 20),
        cost_estimate=pl.CostEstimate(
            flops=2 * npairs * 16 * LANES * LANES, bytes_accessed=6 << 20, transcendentals=0
        ),
    )(*pin(pair_block, owner, pair_row, pair_tile, atm_state, remap_weight))


def solve_kernel(state, kappa, horiz, wet, tracer, currents_h, edge_up, edge_down, currents, sems):
    levels = kappa.shape[0]
    rows_all = kappa.shape[1]
    planes = tracer.shape[0]

    def chunk(c, carry):
        rows = pl.ds(pl.multiple_of(c * 8, 8), 8)
        column = [kappa[l, rows, :] for l in range(levels)]
        face = [0.5 * (column[l] + column[l + 1]) for l in range(levels - 1)]
        upper = []
        now = None
        for l in range(levels):
            diagonal = 1.0
            if l > 0:
                diagonal = diagonal + face[l - 1]
            if l < levels - 1:
                diagonal = diagonal + face[l]
            if l > 0:
                diagonal = diagonal + face[l - 1] * upper[-1]
            inverse = 1.0 / diagonal
            if l == 0:
                now = [state[f, 0, rows, :] * inverse for f in range(4)] + [inverse]
            else:
                pull = face[l - 1] * inverse
                now = [state[f, l, rows, :] * inverse + pull * now[f] for f in range(4)] + [pull * now[4]]
            upper.append(-face[l] * inverse if l < levels - 1 else None)
            store(l, rows, now)
        for l in range(levels - 2, -1, -1):
            here = load(l, rows)
            now = [here[f] - upper[l] * now[f] for f in range(5)]
            store(l, rows, now)
        return carry

    def store(l, rows, now):
        tracer[l, rows, :] = now[0]
        tracer[levels + l, rows, :] = now[1]
        currents[0, l, rows, :] = now[2]
        currents[1, l, rows, :] = now[3]
        tracer[2 * levels + l, rows, :] = now[4]

    def load(l, rows):
        return [
            tracer[l, rows, :],
            tracer[levels + l, rows, :],
            currents[0, l, rows, :],
            currents[1, l, rows, :],
            tracer[2 * levels + l, rows, :],
        ]

    lax.fori_loop(0, rows_all // 8, chunk, 0)
    out = start_all([(currents, currents_h)], sems)
    tracer[3 * levels] = horiz[...]
    tracer[3 * levels + 1] = wet[...].astype(F32)
    for k in range(planes):
        edge_up[k] = tracer[k, 0:8, :]
        edge_down[k] = tracer[k, rows_all - 8 : rows_all, :]
    wait_all(out)


def solve(ocean_state, vert_kappa, horiz_kappa, wet_mask):
    levels, rows, _ = vert_kappa.shape
    planes = 3 * levels + 2
    return pl.pallas_call(
        solve_kernel,
        out_shape=(
            jax.ShapeDtypeStruct((planes, rows, LANES), F32),
            pltpu.HBM((2, levels, rows, LANES), F32),
            jax.ShapeDtypeStruct((planes, 8, LANES), F32),
            jax.ShapeDtypeStruct((planes, 8, LANES), F32),
        ),
        in_specs=[vmem()] * 4,
        out_specs=(vmem(), hbm(), vmem(), vmem()),
        scratch_shapes=[pltpu.VMEM((2, levels, rows, LANES), F32), pltpu.SemaphoreType.DMA((1,))],
        compiler_params=pltpu.CompilerParams(vmem_limit_bytes=24 << 20),
        cost_estimate=pl.CostEstimate(flops=20 << 20, bytes_accessed=6 << 20, transcendentals=0),
    )(ocean_state, vert_kappa, horiz_kappa, wet_mask)


def pack_kernel(levels, tracer, above, below, wide_h, to_left, to_right, wide, sems):
    planes, rows, _ = tracer.shape
    for k in range(planes):
        wide[k, 0:HALO, :] = above[k]
        wide[k, HALO : HALO + rows, :] = tracer[k]
        wide[k, HALO + rows : 2 * HALO + rows, :] = below[k]
    out = start_all([(wide, wide_h)], sems)
    lane = iota((8, LANES), 1)

    def chunk(c, carry):
        at = pl.ds(pl.multiple_of(c * 8, 8), 8)

        def place(values, lanes):
            left, right = jnp.zeros((8, LANES), F32), jnp.zeros((8, LANES), F32)
            for k, (near, far) in zip(values, lanes):
                value = wide[k, at, :]
                left = jnp.where(lane == near, pltpu.roll(value, near, 1), left)
                left = jnp.where(lane == far, pltpu.roll(value, far - 1, 1), left)
                right = jnp.where(lane == near + 1, pltpu.roll(value, (near + 2) % LANES, 1), right)
                right = jnp.where(lane == far + 1, pltpu.roll(value, (far + 3) % LANES, 1), right)
            return left, right

        left, right = place(range(2 * levels), [(2 * k, 64 + 2 * k) for k in range(2 * levels)])
        to_left[0, at, :] = left
        to_right[0, at, :] = right
        lanes = [(2 * l, 64 + 2 * l) for l in range(levels)]
        lanes += [(2 * levels, 2 * levels + 2), (2 * levels + 4, 2 * levels + 6)]
        left, right = place(range(2 * levels, 3 * levels + 2), lanes)
        to_left[1, at, :] = left
        to_right[1, at, :] = right
        return carry

    lax.fori_loop(0, (rows + 2 * HALO) // 8, chunk, 0)
    wait_all(out)


def pack(levels, tracer, above, below):
    planes, rows, _ = tracer.shape
    tall = rows + 2 * HALO
    return pl.pallas_call(
        functools.partial(pack_kernel, levels),
        out_shape=(
            pltpu.HBM((planes, tall, LANES), F32),
            jax.ShapeDtypeStruct((2, tall, LANES), F32),
            jax.ShapeDtypeStruct((2, tall, LANES), F32),
        ),
        in_specs=[vmem()] * 3,
        out_specs=(hbm(), vmem(), vmem()),
        scratch_shapes=[pltpu.VMEM((planes, tall, LANES), F32), pltpu.SemaphoreType.DMA((1,))],
        compiler_params=pltpu.CompilerParams(vmem_limit_bytes=24 << 20),
        cost_estimate=pl.CostEstimate(flops=8 << 20, bytes_accessed=4 << 20, transcendentals=0),
    )(tracer, above, below)


def set_faces(levels, h, w, own_left, own_right, from_left, from_right, faces, packed):
    tall = h.shape[0]
    lane = iota((tall, LANES), 1)
    odd = lane % 2 == 1
    twice = lane % 64 < 2 * levels
    left, left_unit, right, right_unit = from_left[0], from_left[1], from_right[0], from_right[1]
    other = jnp.where(odd, left_unit, right_unit)
    at = 2 * levels

    def column(offset):
        return other[:, at + offset : at + offset + 1], other[:, at + offset + 1 : at + offset + 2]

    kappa_right, kappa_left = column(0)
    kappa_far_right, kappa_far_left = column(2)
    wet_right, wet_left = column(4)
    wet_far_right, wet_far_left = column(6)

    kappa_near = jnp.where(odd, kappa_left, kappa_right)
    kappa_far = jnp.where(odd, kappa_far_left, kappa_far_right)
    wet_near = jnp.where(odd, wet_left, wet_right)
    wet_far = jnp.where(odd, wet_far_left, wet_far_right)
    kappa_own = jnp.where(odd, h[:, 0:1], h[:, LANES - 1 : LANES])
    wet_own = jnp.where(odd, w[:, 0:1], w[:, LANES - 1 : LANES])

    def face(kappa_a, wet_a, kappa_b, wet_b):
        return 0.25 * (kappa_a + kappa_b) * wet_a * wet_b

    unit = jnp.where(twice, other, pltpu.roll(other, 2 * levels, 1))
    packed[0] = jnp.where(odd, left, right)
    packed[1] = unit * jnp.where(lane < 64, wet_near, wet_far)
    left, left_unit, right, right_unit = own_left[0], own_left[1], own_right[0], own_right[1]
    packed[2] = jnp.where(odd, pltpu.roll(left, 1, 1), pltpu.roll(right, LANES - 1, 1))
    own = jnp.where(odd, pltpu.roll(left_unit, 1, 1), pltpu.roll(right_unit, LANES - 1, 1))
    packed[3] = jnp.where(twice, own, pltpu.roll(own, 2 * levels, 1)) * wet_own
    north = face(kappa_near, wet_near, pltpu.roll(kappa_near, 1, 0), pltpu.roll(wet_near, 1, 0))
    packed[4] = north
    packed[5] = pltpu.roll(north, tall - 1, 0)
    packed[6] = face(kappa_near, wet_near, kappa_far, wet_far)
    packed[7] = face(kappa_near, wet_near, kappa_own, wet_own)

    north = face(h, w, pltpu.roll(h, 1, 0), pltpu.roll(w, 1, 0))
    faces[0] = north
    faces[1] = pltpu.roll(north, tall - 1, 0)
    west = face(
        h, w, jnp.where(lane == 0, kappa_left, pltpu.roll(h, 1, 1)), jnp.where(lane == 0, wet_left, pltpu.roll(w, 1, 1))
    )
    faces[2] = west
    faces[3] = jnp.where(lane == LANES - 1, face(h, w, kappa_right, wet_right), pltpu.roll(west, LANES - 1, 1))


def set_beside(levels, upright, wide, packed, beside):
    tall = upright.shape[0]
    lane = iota((tall, LANES), 1)
    odd = lane % 2 == 1
    heat = lane % 64 < 2 * levels

    def chosen(f):
        left_far, left_near, right_near, right_far = [upright[:, 4 * f + e : 4 * f + e + 1] for e in range(4)]
        near = jnp.where(odd, left_near, right_near)
        return jnp.where(lane < 64, near, jnp.where(odd, left_far, right_far))

    both = packed[0] + packed[1] * jnp.where(heat, chosen(0), chosen(1))
    far = pltpu.roll(both, 64, 1)
    ends_of = [jnp.where(odd, w[:, 0:1], w[:, LANES - 1 : LANES]) for w in wide]
    own = packed[2] + packed[3] * jnp.where(heat, ends_of[0], ends_of[1])
    near = both + packed[5] * (pltpu.roll(both, tall - 1, 0) - both)
    near = near + packed[4] * (pltpu.roll(both, 1, 0) - both)
    near = near + packed[6] * (far - both)
    near = near + packed[7] * (own - both)
    beside[0] = both
    beside[1] = near


def one_pass(value, faces, beside, shift):
    tall = value.shape[0]
    lane = iota(value.shape, 1)
    moved = pltpu.roll(beside, shift, 1)
    west = jnp.where(lane == 0, moved, pltpu.roll(value, 1, 1))
    east = jnp.where(lane == LANES - 1, moved, pltpu.roll(value, LANES - 1, 1))
    result = value + faces[1] * (pltpu.roll(value, tall - 1, 0) - value)
    result = result + faces[0] * (pltpu.roll(value, 1, 0) - value)
    result = result + faces[3] * (east - value)
    return result + faces[2] * (west - value)


def middle_kernel(
    capacity, levels, arrived, wide_h, currents_h, own_left_h, own_right_h, from_left_h, from_right_h,
    sent_h, forcing_h, near_h, faces_h,
    placing, values, number_t, top, currents, own_left, own_right, from_left, from_right,
    faces, packed, sent, forcing, near_o, sems, sent_sems,
):
    devices, message, _ = arrived.shape
    rows_all = currents.shape[1]
    tall = rows_all + 2 * HALO
    loads = start_all(
        [(wide_h.at[levels * k], top.at[k]) for k in range(3)]
        + [
            (wide_h.at[pl.ds(3 * levels, 2)], top.at[pl.ds(3, 2)]),
            (currents_h.at[0, 0], currents.at[0]),
            (currents_h.at[1, 0], currents.at[1]),
            (own_left_h, own_left),
            (own_right_h, own_right),
            (from_left_h, from_left),
            (from_right_h, from_right),
        ],
        sems,
    )
    span = 4 * capacity
    group = LANES // span
    groups = devices // group
    sub8 = iota((8, LANES), 0)
    lane8 = iota((8, LANES), 1)

    lane1 = iota((1, LANES), 1)
    spread = (iota((LANES, LANES), 0) - NUMBERS) == iota((LANES, LANES), 1) % span // 4
    every = jnp.concatenate([arrived[s, span + 8 : span + 9, :] for s in range(devices)], 0).astype(BF16)
    every = jnp.dot(every, jnp.where(spread, 1.0, 0.0).astype(BF16), preferred_element_type=F32)
    numbers = []
    for m in range(groups):
        line = jnp.zeros((1, LANES), F32)
        for g in range(group):
            s = m * group + g
            line = jnp.where(lane1 // span == g, every[s : s + 1], line)
        numbers.append(line)
    number_t[...] = jnp.transpose(
        jnp.concatenate(numbers + [jnp.zeros((LANES - groups, LANES), F32)], 0)
    )

    row_number = iota((rows_all, LANES), 0).astype(F32) + 1.0
    for m in range(groups):
        for f in range(4):
            placing[f * rows_all : (f + 1) * rows_all, m * LANES : (m + 1) * LANES] = jnp.where(
                pick(lane1 % 4 == f, numbers[m]) == row_number, 1.0, 0.0
            ).astype(BF16)
    edge_rows = jnp.zeros((8, LANES), F32)
    edge_cols = jnp.zeros((8, LANES), F32)
    for s in range(devices):
        high, low = split(arrived[s, 0:span, :])
        values[s * span : (s + 1) * span, 0:LANES] = high
        values[s * span : (s + 1) * span, LANES : 2 * LANES] = low
        edge_rows = edge_rows + arrived[s, span : span + 8, :]
        edge_cols = edge_cols + arrived[s, span + 8 : span + 16, :]
    wait_all(loads)
    set_faces(levels, top[3], top[4], own_left, own_right, from_left, from_right, faces, packed)
    wet_wide = top[4]
    total = jnp.dot(placing[...], values[...], preferred_element_type=F32)
    total = total[:, 0:LANES] + total[:, LANES : 2 * LANES]


    def plane(f):
        return total[f * rows_all : (f + 1) * rows_all]

    wide = []
    for f in range(2):
        before = pick(sub8 >= 6, edge_rows if f == 1 else pltpu.roll(edge_rows, 4, 0))
        after = pick(sub8 < 2, edge_rows if f == 0 else pltpu.roll(edge_rows, 4, 0))
        wide.append(jnp.concatenate([before, plane(f), after], 0))
        forcing[f] = wide[f]
    wet = wet_wide[HALO : HALO + rows_all]
    for f in range(2, 4):
        forcing[f, 0:HALO, :] = jnp.zeros((HALO, LANES), F32)
        forcing[f, HALO : HALO + rows_all, :] = plane(f) * wet
        forcing[f, HALO + rows_all : tall, :] = jnp.zeros((HALO, LANES), F32)

    part8 = sub8 % 4
    within = (part8 == lane8 % 4) & (lane8 >= HALO) & (lane8 < HALO + rows_all)
    upper = (part8 == 3) & (lane8 == HALO - 1)
    lower = (part8 == 0) & (lane8 == HALO + rows_all)
    halves = [[], []]
    for k in range(4):
        column = pick(within, pltpu.roll(edge_cols, HALO - k, 1))
        if k in (1, 2):
            column = column + pick(upper, pltpu.roll(edge_cols, (HALO - CORNERS - k) % LANES, 1))
            column = column + pick(lower, pltpu.roll(edge_cols, (HALO + rows_all - CORNERS - 1 - k) % LANES, 1))
        for f in range(2):
            halves[f].append(jnp.sum(column[4 * f : 4 * f + 4], axis=0, keepdims=True))
    columns = jnp.concatenate(halves[0] + halves[1], 0)
    upright = jnp.transpose(jnp.concatenate([columns, jnp.zeros((LANES - 8, LANES), F32)], 0))[0:tall]
    set_beside(levels, upright, wide, packed, near_o)
    stores = start_all([(forcing, forcing_h), (near_o, near_h), (faces, faces_h)], sems, 10)

    surface = []
    unit = top[2] * wet_wide
    for f in range(2):
        value = top[f] + unit * wide[f]
        shift = LANES - (2 * levels * f + 1)
        value = one_pass(value, faces, near_o[0], shift)
        value = one_pass(value, faces, near_o[1], shift)
        surface.append(value[HALO : HALO + rows_all] * wet)
    for f in range(2):
        surface.append(
            (currents[f] + top[2, HALO : HALO + rows_all, :] * forcing[2 + f, HALO : HALO + rows_all, :]) * wet
        )
    high, low = split(jnp.concatenate(surface, 0))
    source = jnp.concatenate([high, low], 1)
    lane_t = iota((LANES, 4 * rows_all), 1)
    sub_t = iota((LANES, 4 * rows_all), 0)
    target = jnp.where(sub_t % 4 == lane_t // rows_all, lane_t % rows_all + 1, -1).astype(F32)
    mask = jnp.concatenate([wet, jnp.zeros((LANES - rows_all, LANES), F32)], 0).astype(BF16)
    per = LANES // 4
    slot_number = number_t[pl.ds(0, per, stride=4), :]
    lane_s = (iota((per, LANES), 1) + 1).astype(F32)
    height = back_rows(capacity)
    many = 4
    for first in range(0, groups, many):
        these = range(first, first + many)
        chosen_rows = [jnp.where(number_t[:, m : m + 1] == target, 1.0, 0.0).astype(BF16) for m in these]
        rows = jnp.dot(jnp.concatenate(chosen_rows, 0), source, preferred_element_type=F32)
        rows = rows[:, 0:LANES] + rows[:, LANES : 2 * LANES]
        slots = [jnp.where(slot_number[:, m : m + 1] == lane_s, 1.0, 0.0) for m in these]
        masks = jnp.dot(jnp.concatenate(slots, 0).astype(BF16), mask, preferred_element_type=F32)
        for g in range(many * group):
            s = first * group + g
            sent[s, 0:span, :] = rows[g * span : (g + 1) * span]
            sent[s, span : span + capacity, :] = masks[g * capacity : (g + 1) * capacity]
            if height > span + capacity:
                sent[s, span + capacity : height, :] = jnp.zeros((height - span - capacity, LANES), F32)
        at = pl.ds(first * group, many * group)
        stores += start_all([(sent.at[at], sent_h.at[at])], sent_sems, first // many)
    wait_all(stores)


def middle(capacity, levels, arrived, wide, currents, *columns):
    devices = arrived.shape[0]
    rows = currents.shape[2]
    tall = rows + 2 * HALO
    height = back_rows(capacity)
    return pl.pallas_call(
        functools.partial(middle_kernel, capacity, levels),
        out_shape=(
            pltpu.HBM((devices, height, LANES), F32),
            pltpu.HBM((4, tall, LANES), F32),
            pltpu.HBM((2, tall, LANES), F32),
            pltpu.HBM((4, tall, LANES), F32),
        ),
        in_specs=[vmem()] + [hbm()] * 2 + [pl.BlockSpec(memory_space=pl.ANY)] * 4,
        out_specs=(hbm(),) * 4,
        scratch_shapes=[
            pltpu.VMEM((4 * rows, 4 * capacity * devices), BF16),
            pltpu.VMEM((4 * capacity * devices, 2 * LANES), BF16),
            pltpu.VMEM((LANES, LANES), F32),
            pltpu.VMEM((5, tall, LANES), F32),
            pltpu.VMEM((2, rows, LANES), F32),
        ]
        + [pltpu.VMEM((2, tall, LANES), F32)] * 4
        + [
            pltpu.VMEM((4, tall, LANES), F32),
            pltpu.VMEM((8, tall, LANES), F32),
            pltpu.VMEM((devices, height, LANES), F32),
            pltpu.VMEM((4, tall, LANES), F32),
            pltpu.VMEM((2, tall, LANES), F32),
            pltpu.SemaphoreType.DMA((13,)),
            pltpu.SemaphoreType.DMA((4 * capacity * devices // LANES,)),
        ],
        compiler_params=pltpu.CompilerParams(vmem_limit_bytes=24 << 20),
        cost_estimate=pl.CostEstimate(flops=200 << 20, bytes_accessed=4 << 20, transcendentals=0),
    )(arrived, *pin(wide, currents), *columns)


def finish_kernel(
    levels, wide_h, currents_h, faces_h, forcing_h, near_h, ocean, wide, currents, faces, forcing, near, sems
):
    rows_all = currents.shape[2]
    wait_all(
        start_all(
            [(wide_h, wide), (currents_h, currents), (faces_h, faces), (forcing_h, forcing), (near_h, near)], sems
        )
    )
    inner = slice(HALO, HALO + rows_all)

    def level(l, carry):
        unit = wide[2 * levels + l]
        masked = unit * wide[3 * levels + 1]
        for f in range(2):
            value = wide[f * levels + l] + masked * forcing[f]
            shift = LANES - 1 - 2 * (levels * f + l)
            value = one_pass(value, faces, near[0], shift)
            value = one_pass(value, faces, near[1], shift)
            ocean[f, l] = value[inner]
            ocean[2 + f, l] = currents[f, l] + unit[inner] * forcing[2 + f][inner]
        return carry

    lax.fori_loop(0, levels, level, 0)


def finish(levels, wide, currents, faces, forcing, near):
    rows = currents.shape[2]
    return pl.pallas_call(
        functools.partial(finish_kernel, levels),
        out_shape=jax.ShapeDtypeStruct((4, levels, rows, LANES), F32),
        in_specs=[hbm()] * 5,
        out_specs=vmem(),
        scratch_shapes=[pltpu.VMEM(a.shape, F32) for a in (wide, currents, faces, forcing, near)]
        + [pltpu.SemaphoreType.DMA((5,))],
        compiler_params=pltpu.CompilerParams(vmem_limit_bytes=24 << 20),
        cost_estimate=pl.CostEstimate(flops=40 << 20, bytes_accessed=6 << 20, transcendentals=0),
    )(*pin(wide, currents, faces, forcing, near))


def turn_kernel(weights_h, turned_h, weights, turned, sems, out_sems):
    part_tiles = weights.shape[0] // PARTS
    parts = [pl.ds(n * part_tiles, part_tiles) for n in range(PARTS)]
    loads = start_all([(weights_h.at[at], weights.at[at]) for at in parts], sems)
    stores = []
    for n, at in enumerate(parts):
        loads[n].wait()

        def tile_step(t, carry):
            turned[t] = weights[t].T
            return carry

        lax.fori_loop(n * part_tiles, (n + 1) * part_tiles, tile_step, 0, unroll=4)
        stores += start_all([(turned.at[at], turned_h.at[at])], out_sems, n)
    wait_all(stores)


def turn(remap_weight):
    return pl.pallas_call(
        turn_kernel,
        out_shape=pltpu.HBM(remap_weight.shape, BF16),
        in_specs=[hbm()],
        out_specs=hbm(),
        scratch_shapes=[pltpu.VMEM(remap_weight.shape, BF16)] * 2 + [pltpu.SemaphoreType.DMA((PARTS,))] * 2,
        compiler_params=pltpu.CompilerParams(vmem_limit_bytes=24 << 20),
        cost_estimate=pl.CostEstimate(flops=8 << 20, bytes_accessed=8 << 20, transcendentals=0),
    )(*pin(remap_weight))


def remap_back_kernel(
    block_h, tile_h, field_h, wet_h, returned, weights_h, out,
    block_s, tile_s, field_s, wet_s, weights, picked_a, picked_b, total_0, total_1, total_2, total_3, sems, weight_sems,
):
    npairs = block_s.shape[0]
    totals = [total_0, total_1, total_2, total_3]
    nblocks = total_0.shape[0]
    scalars = start_all([(field_h, field_s), (wet_h, wet_s), (block_h, block_s), (tile_h, tile_s)], sems)
    part_tiles = weights.shape[0] // PARTS
    parts = [pl.ds(n * part_tiles, part_tiles) for n in range(PARTS)]
    loads = start_all([(weights_h.at[at], weights.at[at]) for at in parts], weight_sems)
    for total in totals:
        total[...] = jnp.zeros_like(total)
    wait_all(scalars)

    def gather(p, picked, at):
        rows = returned[pl.ds(field_s[p], 4), :]
        mask = returned[pl.ds(wet_s[p] - 7, 8), :]
        high, low = split(jnp.concatenate([rows, jnp.zeros((3, LANES), F32), mask[7:8]], 0))
        picked[at] = jnp.concatenate([high, low], 0)

    def product(p, picked, at, total):
        value = jnp.dot(picked[at], weights[tile_s[p]], preferred_element_type=F32)
        b = block_s[p]
        total[b] = total[b] + (value[0:8] + value[8:16])

    half = npairs // 2
    many = len(totals)

    def first(p, carry):
        gather(p, picked_a, p)
        return carry

    def both(p, carry):
        for n in range(many):
            gather(half + many * p + n, picked_b, many * p + n)
            product(many * p + n, picked_a, many * p + n, totals[n])
        return carry

    def last(p, carry):
        for n in range(many):
            product(half + many * p + n, picked_b, many * p + n, totals[n])
        return carry

    lax.fori_loop(0, half, first, 0, unroll=True)
    wait_all(loads)
    lax.fori_loop(0, half // many, both, 0, unroll=True)
    lax.fori_loop(0, half // many, last, 0, unroll=True)
    for b in range(nblocks):
        sums = (total_0[b] + total_1[b]) + (total_2[b] + total_3[b])
        out[:, b * LANES : (b + 1) * LANES] = sums[0:4] / jnp.maximum(sums[7:8], 0.1)


def remap_back(pair_block, pair_tile, field_at, wet_at, returned, weights, nblocks):
    npairs = pair_block.shape[0]
    return pl.pallas_call(
        remap_back_kernel,
        out_shape=jax.ShapeDtypeStruct((4, nblocks * LANES), F32),
        in_specs=[hbm()] * 4 + [vmem(), hbm()],
        out_specs=vmem(),
        scratch_shapes=[pltpu.SMEM((npairs,), I32)] * 4
        + [pltpu.VMEM(weights.shape, BF16)]
        + [pltpu.VMEM((npairs // 2, 16, LANES), BF16)] * 2
        + [pltpu.VMEM((nblocks, 8, LANES), F32)] * 4
        + [pltpu.SemaphoreType.DMA((4,)), pltpu.SemaphoreType.DMA((PARTS,))],
        compiler_params=pltpu.CompilerParams(vmem_limit_bytes=24 << 20),
        cost_estimate=pl.CostEstimate(flops=2 * npairs * 16 * LANES * LANES, bytes_accessed=6 << 20, transcendentals=0),
    )(*pin(pair_block, pair_tile, field_at, wet_at), returned, *pin(weights))


def local(
    atm_state,
    pair_block,
    pair_owner,
    pair_row,
    pair_tile,
    remap_weight,
    wet_mask,
    ocean_state,
    vert_kappa,
    horiz_kappa,
):
    grid_x = lax.axis_size("gx")
    grid_y = lax.axis_size("gy")
    devices = grid_x * grid_y
    npairs = pair_block.shape[0]
    capacity = max(2, 2 * npairs // devices)
    levels, tile_rows, _ = vert_kappa.shape
    nblocks = atm_state.shape[1] // LANES
    owner = pair_owner.reshape(npairs)
    message = 4 * capacity + EDGE
    outgoing, field_at, wet_at = remap_out(
        capacity, grid_y, devices, tile_rows, atm_state, pair_block, owner, pair_row, pair_tile, remap_weight
    )
    arrived = lax.all_to_all(
        outgoing.reshape(devices, message, LANES), ("gx", "gy"), split_axis=0, concat_axis=0, tiled=True
    )
    tracer, currents, edge_up, edge_down = solve(ocean_state, vert_kappa, horiz_kappa, wet_mask)
    rise_x = [(i, i + 1) for i in range(grid_x - 1)]
    fall_x = [(b, a) for a, b in rise_x]
    rise_y = [(i, i + 1) for i in range(grid_y - 1)]
    fall_y = [(b, a) for a, b in rise_y]
    above = lax.ppermute(edge_down, "gx", rise_x)
    below = lax.ppermute(edge_up, "gx", fall_x)
    wide, to_left, to_right = pack(levels, tracer, above, below)
    from_left = lax.ppermute(to_right, "gy", rise_y)
    from_right = lax.ppermute(to_left, "gy", fall_y)
    sent, forcing, near, faces = middle(
        capacity, levels, arrived, wide, currents, to_left, to_right, from_left, from_right
    )
    returned = lax.all_to_all(sent, ("gx", "gy"), split_axis=0, concat_axis=0, tiled=True)
    ocean_next = finish(levels, wide, currents, faces, forcing, near)
    weights, _ = lax.optimization_barrier((remap_weight, near))
    atm_surface = remap_back(
        pair_block, pair_tile, field_at, wet_at, returned.reshape(-1, LANES), turn(weights), nblocks
    )
    return (ocean_next, atm_surface)


def solution(mesh):
    placed = (
        P(None, ("gx", "gy")),
        P(("gx", "gy")),
        P(("gx", "gy"), None),
        P(("gx", "gy")),
        P(("gx", "gy")),
        P(("gx", "gy"), None, None),
        P("gx", "gy"),
        P(None, None, "gx", "gy"),
        P(None, "gx", "gy"),
        P("gx", "gy"),
    )
    return jax.shard_map(
        local,
        mesh=mesh,
        in_specs=placed,
        out_specs=(P(None, None, "gx", "gy"), P(None, ("gx", "gy"))),
        check_vma=False,
    )
```

```python
import functools

import jax
import jax.numpy as jnp
from jax import lax
from jax.experimental import pallas as pl
from jax.experimental.pallas import tpu as pltpu
from jax.sharding import PartitionSpec as P

F32 = jnp.float32
BF16 = jnp.bfloat16
I32 = jnp.int32
VMEM = pltpu.VMEM
SMEM = pltpu.SMEM
LANES = 128
EDGE = 16
HALO = 8
NUMBERS = 72
CORNERS = 112
SENDS = 8
AHEAD = 16
PARTS = 8


def hbm():
    return pl.BlockSpec(memory_space=pltpu.HBM)


def vmem():
    return pl.BlockSpec(memory_space=VMEM)


def pin(*arrays):
    return [pltpu.with_memory_space_constraint(a, pltpu.HBM) for a in arrays]


def start_all(pairs, sems, first=0):
    copies = [pltpu.make_async_copy(src, dst, sems.at[first + n]) for n, (src, dst) in enumerate(pairs)]
    for copy in copies:
        copy.start()
    return copies


def wait_all(copies):
    for copy in copies:
        copy.wait()


def iota(shape, dim):
    return lax.broadcasted_iota(I32, shape, dim)


def pick(mask, value):
    return jnp.where(mask, value, 0.0)


def split(value):
    high = value.astype(BF16)
    return high, (value - high.astype(F32)).astype(BF16)


def back_rows(capacity):
    return 4 * capacity + max(8, capacity)


def remap_out_kernel(
    capacity, grid_y, tile_rows, block_h, owner_h, row_h, tile_h, atm_h, weights_h, out_h, field_h, wet_h,
    out, block_s, owner_s, row_s, tile_s, rank_s, field_s, wet_s, atm, weights, atm_rows, flux_rows, flux, fill, rows_sum, cols_sum, rows_acc, cols_acc, sems, weight_sems, out_sems,
):
    devices = fill.shape[0]
    npairs = block_s.shape[0]
    tiles = weights.shape[0]
    nblocks = flux.shape[0]
    message = 4 * capacity + EDGE
    copies = [
        pltpu.make_async_copy(src, dst, sems.at[n])
        for n, (src, dst) in enumerate(
            [(atm_h, atm), (block_h, block_s), (owner_h, owner_s), (row_h, row_s), (tile_h, tile_s)]
        )
    ]
    for copy in copies:
        copy.start()
    part_tiles = tiles // PARTS
    parts = [pl.ds(n * part_tiles, part_tiles) for n in range(PARTS)]
    loads = [pltpu.make_async_copy(weights_h.at[at], weights.at[at], weight_sems.at[n]) for n, at in enumerate(parts)]
    for load in loads:
        load.start()
    out[...] = jnp.zeros_like(out)
    rows_sum[...] = jnp.zeros_like(rows_sum)
    cols_sum[...] = jnp.zeros_like(cols_sum)

    def clear_fill(i, carry):
        fill[i] = 0
        return carry

    lax.fori_loop(0, devices, clear_fill, 0, unroll=16)
    flux_rows[...] = jnp.zeros_like(flux_rows)
    wait_all(copies)
    for b in range(nblocks):
        atm_rows[8 * b : 8 * b + 6, :] = atm[:, b * LANES : (b + 1) * LANES]
    wind_u, wind_v, air, dry, rain, sea = [atm_rows[pl.ds(n, nblocks, stride=8), :] for n in range(6)]
    speed = jnp.sqrt(wind_u * wind_u + wind_v * wind_v + 0.25)
    heat = 0.5 * speed * (air - sea)
    water = rain - 0.3 * speed * dry
    planes = [heat, water, 0.2 * speed * wind_u, 0.2 * speed * wind_v]
    for n, plane in list(enumerate(planes)) + [(8 + n, heat) for n in range(4)] + [(12 + n, water) for n in range(4)]:
        flux_rows[pl.ds(n, nblocks, stride=16), :] = plane
    for b in range(nblocks):
        flux[b] = flux_rows[16 * b : 16 * (b + 1), :].astype(BF16)

    height = back_rows(capacity)


    def place(p):
        owner = owner_s[p]
        rank = fill[owner]
        fill[owner] = rank + 1
        field_s[p] = owner * height + 4 * rank
        wet_s[p] = owner * height + 4 * capacity + rank
        rank_s[p] = rank

    for p in range(AHEAD):
        place(p)
    wait_all(loads)

    sub = iota((8, LANES), 0)
    lane = iota((8, LANES), 1)
    part = sub % 4
    edge_row = jnp.where(part == 0, 0, jnp.where(part == 1, 1, tile_rows - 4 + part))
    band = ((lane - part) >> 2) * 4 + part
    id_rank = jnp.where(sub == 0, lane - NUMBERS, -1)

    def pair(p, n):
        owner = owner_s[p]
        row = row_s[p]
        rank = rank_s[p]
        value = jnp.dot(flux[block_s[p]], weights[tile_s[p]], preferred_element_type=F32)
        out[pl.ds(owner * message + 4 * rank, 4), :] = value[0:4]
        tracer = value[8:16]
        rows_sum[n, owner] = rows_sum[n, owner] + pick(edge_row == row, tracer)
        number = (row + 1).astype(F32)
        cols_sum[n, owner] = cols_sum[n, owner] + (
            pick(band == row, pltpu.roll(tracer, row + 2, 1)) + pick(id_rank == rank, number)
        )

    many = rows_sum.shape[0]

    def pairs(more, k, carry):
        for n in range(many):
            p = many * k + n
            if more:
                place(p + AHEAD)
            pair(p, n)
        return carry

    lax.fori_loop(0, (npairs - AHEAD) // many, functools.partial(pairs, True), 0, unroll=True)
    stores = start_all([(field_s, field_h), (wet_s, wet_h)], out_sems, SENDS)
    lax.fori_loop((npairs - AHEAD) // many, npairs // many, functools.partial(pairs, False), 0, unroll=True)

    def owner_step(d, carry):
        rows_acc[d] = (rows_sum[0, d] + rows_sum[1, d]) + (rows_sum[2, d] + rows_sum[3, d])
        cols_acc[d] = (cols_sum[0, d] + cols_sum[1, d]) + (cols_sum[2, d] + cols_sum[3, d])
        return carry

    lax.fori_loop(0, devices, owner_step, 0, unroll=32)

    grid_x = devices // grid_y
    zero = jnp.zeros((8, LANES), F32)

    def columns_of(i, j):
        if not (0 <= i < grid_x and 0 <= j < grid_y):
            return zero
        return cols_acc[i * grid_y + j]

    from_left = (lane - sub) % 4 < 2
    in_band = lane < tile_rows + 4
    in_ids = (sub == 0) & (lane >= NUMBERS) & (lane < NUMBERS + capacity)
    last, first = part == 3, part == 0
    send = devices // SENDS
    for d in range(devices):
        i, j = d // grid_y, d % grid_y
        below = rows_acc[d + grid_y] if i < grid_x - 1 else zero
        above = rows_acc[d - grid_y] if i > 0 else zero
        base = d * message + 4 * capacity
        out[base : base + 8, :] = jnp.where(part < 2, below, above)
        tile = pick(in_band, jnp.where(from_left, columns_of(i, j - 1), columns_of(i, j + 1)))
        upper = pick(last & (lane == tile_rows), columns_of(i - 1, j - 1))
        upper = upper + pick(last & (lane == tile_rows + 1), columns_of(i - 1, j + 1))
        lower = pick(first & (lane == 1), columns_of(i + 1, j - 1))
        lower = lower + pick(first & (lane == 2), columns_of(i + 1, j + 1))
        tile = tile + pltpu.roll(upper, CORNERS - tile_rows, 1) + pltpu.roll(lower, CORNERS + 1, 1)
        tile = tile + pick(in_ids, cols_acc[d])
        out[base + 8 : base + 16, :] = tile
        if d % send == send - 1:
            n = d // send
            at = pl.ds(n * send * message, send * message)
            stores.append(pltpu.make_async_copy(out.at[at], out_h.at[at], out_sems.at[n]))
            stores[-1].start()
    for store in stores:
        store.wait()


def remap_out(capacity, grid_y, devices, tile_rows, atm_state, pair_block, owner, pair_row, pair_tile, remap_weight):
    npairs = pair_block.shape[0]
    nblocks = atm_state.shape[1] // LANES
    message = 4 * capacity + EDGE
    return pl.pallas_call(
        functools.partial(remap_out_kernel, capacity, grid_y, tile_rows),
        out_shape=(
            pltpu.HBM((devices * message, LANES), F32),
            pltpu.HBM((npairs,), I32),
            pltpu.HBM((npairs,), I32),
        ),
        in_specs=[hbm()] * 6,
        out_specs=(hbm(),) * 3,
        scratch_shapes=[pltpu.VMEM((devices * message, LANES), F32)]
        + [pltpu.SMEM((npairs,), I32)] * 7
        + [
            pltpu.VMEM(atm_state.shape, F32),
            pltpu.VMEM(remap_weight.shape, BF16),
            pltpu.VMEM((nblocks * 8, LANES), F32),
            pltpu.VMEM((nblocks * 16, LANES), F32),
            pltpu.VMEM((nblocks, 16, LANES), BF16),
            pltpu.SMEM((devices,), I32),
            pltpu.VMEM((4, devices, 8, LANES), F32),
            pltpu.VMEM((4, devices, 8, LANES), F32),
            pltpu.VMEM((devices, 8, LANES), F32),
            pltpu.VMEM((devices, 8, LANES), F32),
            pltpu.SemaphoreType.DMA((5,)),
            pltpu.SemaphoreType.DMA((PARTS,)),
            pltpu.SemaphoreType.DMA((SENDS + 2,)),
        ],
        compiler_params=pltpu.CompilerParams(vmem_limit_bytes=40 << 20),
        cost_estimate=pl.CostEstimate(
            flops=2 * npairs * 16 * LANES * LANES, bytes_accessed=6 << 20, transcendentals=0
        ),
    )(*pin(pair_block, owner, pair_row, pair_tile, atm_state, remap_weight))


def solve_kernel(state, kappa, horiz, wet, tracer, currents_h, edge_up, edge_down, currents, sems):
    levels = kappa.shape[0]
    rows_all = kappa.shape[1]
    planes = tracer.shape[0]

    def chunk(c, carry):
        rows = pl.ds(pl.multiple_of(c * 8, 8), 8)
        column = [kappa[l, rows, :] for l in range(levels)]
        face = [0.5 * (column[l] + column[l + 1]) for l in range(levels - 1)]
        upper = []
        now = None
        for l in range(levels):
            diagonal = 1.0
            if l > 0:
                diagonal = diagonal + face[l - 1]
            if l < levels - 1:
                diagonal = diagonal + face[l]
            if l > 0:
                diagonal = diagonal + face[l - 1] * upper[-1]
            inverse = 1.0 / diagonal
            if l == 0:
                now = [state[f, 0, rows, :] * inverse for f in range(4)] + [inverse]
            else:
                pull = face[l - 1] * inverse
                now = [state[f, l, rows, :] * inverse + pull * now[f] for f in range(4)] + [pull * now[4]]
            upper.append(-face[l] * inverse if l < levels - 1 else None)
            store(l, rows, now)
        for l in range(levels - 2, -1, -1):
            here = load(l, rows)
            now = [here[f] - upper[l] * now[f] for f in range(5)]
            store(l, rows, now)
        return carry

    def store(l, rows, now):
        tracer[l, rows, :] = now[0]
        tracer[levels + l, rows, :] = now[1]
        currents[0, l, rows, :] = now[2]
        currents[1, l, rows, :] = now[3]
        tracer[2 * levels + l, rows, :] = now[4]

    def load(l, rows):
        return [
            tracer[l, rows, :],
            tracer[levels + l, rows, :],
            currents[0, l, rows, :],
            currents[1, l, rows, :],
            tracer[2 * levels + l, rows, :],
        ]

    lax.fori_loop(0, rows_all // 8, chunk, 0)
    out = start_all([(currents, currents_h)], sems)
    tracer[3 * levels] = horiz[...]
    tracer[3 * levels + 1] = wet[...].astype(F32)
    for k in range(planes):
        edge_up[k] = tracer[k, 0:8, :]
        edge_down[k] = tracer[k, rows_all - 8 : rows_all, :]
    wait_all(out)


def solve(ocean_state, vert_kappa, horiz_kappa, wet_mask):
    levels, rows, _ = vert_kappa.shape
    planes = 3 * levels + 2
    return pl.pallas_call(
        solve_kernel,
        out_shape=(
            jax.ShapeDtypeStruct((planes, rows, LANES), F32),
            pltpu.HBM((2, levels, rows, LANES), F32),
            jax.ShapeDtypeStruct((planes, 8, LANES), F32),
            jax.ShapeDtypeStruct((planes, 8, LANES), F32),
        ),
        in_specs=[vmem()] * 4,
        out_specs=(vmem(), hbm(), vmem(), vmem()),
        scratch_shapes=[pltpu.VMEM((2, levels, rows, LANES), F32), pltpu.SemaphoreType.DMA((1,))],
        compiler_params=pltpu.CompilerParams(vmem_limit_bytes=24 << 20),
        cost_estimate=pl.CostEstimate(flops=20 << 20, bytes_accessed=6 << 20, transcendentals=0),
    )(ocean_state, vert_kappa, horiz_kappa, wet_mask)


def pack_kernel(levels, tracer, above, below, wide_h, to_left, to_right, wide, sems):
    planes, rows, _ = tracer.shape
    for k in range(planes):
        wide[k, 0:HALO, :] = above[k]
        wide[k, HALO : HALO + rows, :] = tracer[k]
        wide[k, HALO + rows : 2 * HALO + rows, :] = below[k]
    out = start_all([(wide, wide_h)], sems)
    lane = iota((8, LANES), 1)

    def chunk(c, carry):
        at = pl.ds(pl.multiple_of(c * 8, 8), 8)

        def place(values, lanes):
            left, right = jnp.zeros((8, LANES), F32), jnp.zeros((8, LANES), F32)
            for k, (near, far) in zip(values, lanes):
                value = wide[k, at, :]
                left = jnp.where(lane == near, pltpu.roll(value, near, 1), left)
                left = jnp.where(lane == far, pltpu.roll(value, far - 1, 1), left)
                right = jnp.where(lane == near + 1, pltpu.roll(value, (near + 2) % LANES, 1), right)
                right = jnp.where(lane == far + 1, pltpu.roll(value, (far + 3) % LANES, 1), right)
            return left, right

        left, right = place(range(2 * levels), [(2 * k, 64 + 2 * k) for k in range(2 * levels)])
        to_left[0, at, :] = left
        to_right[0, at, :] = right
        lanes = [(2 * l, 64 + 2 * l) for l in range(levels)]
        lanes += [(2 * levels, 2 * levels + 2), (2 * levels + 4, 2 * levels + 6)]
        left, right = place(range(2 * levels, 3 * levels + 2), lanes)
        to_left[1, at, :] = left
        to_right[1, at, :] = right
        return carry

    lax.fori_loop(0, (rows + 2 * HALO) // 8, chunk, 0)
    wait_all(out)


def pack(levels, tracer, above, below):
    planes, rows, _ = tracer.shape
    tall = rows + 2 * HALO
    return pl.pallas_call(
        functools.partial(pack_kernel, levels),
        out_shape=(
            pltpu.HBM((planes, tall, LANES), F32),
            jax.ShapeDtypeStruct((2, tall, LANES), F32),
            jax.ShapeDtypeStruct((2, tall, LANES), F32),
        ),
        in_specs=[vmem()] * 3,
        out_specs=(hbm(), vmem(), vmem()),
        scratch_shapes=[pltpu.VMEM((planes, tall, LANES), F32), pltpu.SemaphoreType.DMA((1,))],
        compiler_params=pltpu.CompilerParams(vmem_limit_bytes=24 << 20),
        cost_estimate=pl.CostEstimate(flops=8 << 20, bytes_accessed=4 << 20, transcendentals=0),
    )(tracer, above, below)


def set_faces(levels, h, w, own_left, own_right, from_left, from_right, faces, packed):
    tall = h.shape[0]
    lane = iota((tall, LANES), 1)
    odd = lane % 2 == 1
    twice = lane % 64 < 2 * levels
    left, left_unit, right, right_unit = from_left[0], from_left[1], from_right[0], from_right[1]
    other = jnp.where(odd, left_unit, right_unit)
    at = 2 * levels

    def column(offset):
        return other[:, at + offset : at + offset + 1], other[:, at + offset + 1 : at + offset + 2]

    kappa_right, kappa_left = column(0)
    kappa_far_right, kappa_far_left = column(2)
    wet_right, wet_left = column(4)
    wet_far_right, wet_far_left = column(6)

    kappa_near = jnp.where(odd, kappa_left, kappa_right)
    kappa_far = jnp.where(odd, kappa_far_left, kappa_far_right)
    wet_near = jnp.where(odd, wet_left, wet_right)
    wet_far = jnp.where(odd, wet_far_left, wet_far_right)
    kappa_own = jnp.where(odd, h[:, 0:1], h[:, LANES - 1 : LANES])
    wet_own = jnp.where(odd, w[:, 0:1], w[:, LANES - 1 : LANES])

    def face(kappa_a, wet_a, kappa_b, wet_b):
        return 0.25 * (kappa_a + kappa_b) * wet_a * wet_b

    unit = jnp.where(twice, other, pltpu.roll(other, 2 * levels, 1))
    packed[0] = jnp.where(odd, left, right)
    packed[1] = unit * jnp.where(lane < 64, wet_near, wet_far)
    left, left_unit, right, right_unit = own_left[0], own_left[1], own_right[0], own_right[1]
    packed[2] = jnp.where(odd, pltpu.roll(left, 1, 1), pltpu.roll(right, LANES - 1, 1))
    own = jnp.where(odd, pltpu.roll(left_unit, 1, 1), pltpu.roll(right_unit, LANES - 1, 1))
    packed[3] = jnp.where(twice, own, pltpu.roll(own, 2 * levels, 1)) * wet_own
    north = face(kappa_near, wet_near, pltpu.roll(kappa_near, 1, 0), pltpu.roll(wet_near, 1, 0))
    packed[4] = north
    packed[5] = pltpu.roll(north, tall - 1, 0)
    packed[6] = face(kappa_near, wet_near, kappa_far, wet_far)
    packed[7] = face(kappa_near, wet_near, kappa_own, wet_own)

    north = face(h, w, pltpu.roll(h, 1, 0), pltpu.roll(w, 1, 0))
    faces[0] = north
    faces[1] = pltpu.roll(north, tall - 1, 0)
    west = face(
        h, w, jnp.where(lane == 0, kappa_left, pltpu.roll(h, 1, 1)), jnp.where(lane == 0, wet_left, pltpu.roll(w, 1, 1))
    )
    faces[2] = west
    faces[3] = jnp.where(lane == LANES - 1, face(h, w, kappa_right, wet_right), pltpu.roll(west, LANES - 1, 1))


def set_beside(levels, upright, wide, packed, beside):
    tall = upright.shape[0]
    lane = iota((tall, LANES), 1)
    odd = lane % 2 == 1
    heat = lane % 64 < 2 * levels

    def chosen(f):
        left_far, left_near, right_near, right_far = [upright[:, 4 * f + e : 4 * f + e + 1] for e in range(4)]
        near = jnp.where(odd, left_near, right_near)
        return jnp.where(lane < 64, near, jnp.where(odd, left_far, right_far))

    both = packed[0] + packed[1] * jnp.where(heat, chosen(0), chosen(1))
    far = pltpu.roll(both, 64, 1)
    ends_of = [jnp.where(odd, w[:, 0:1], w[:, LANES - 1 : LANES]) for w in wide]
    own = packed[2] + packed[3] * jnp.where(heat, ends_of[0], ends_of[1])
    near = both + packed[5] * (pltpu.roll(both, tall - 1, 0) - both)
    near = near + packed[4] * (pltpu.roll(both, 1, 0) - both)
    near = near + packed[6] * (far - both)
    near = near + packed[7] * (own - both)
    beside[0] = both
    beside[1] = near


def one_pass(value, faces, beside, shift):
    tall = value.shape[0]
    lane = iota(value.shape, 1)
    moved = pltpu.roll(beside, shift, 1)
    west = jnp.where(lane == 0, moved, pltpu.roll(value, 1, 1))
    east = jnp.where(lane == LANES - 1, moved, pltpu.roll(value, LANES - 1, 1))
    result = value + faces[1] * (pltpu.roll(value, tall - 1, 0) - value)
    result = result + faces[0] * (pltpu.roll(value, 1, 0) - value)
    result = result + faces[3] * (east - value)
    return result + faces[2] * (west - value)


def middle_kernel(
    capacity, levels, arrived, wide_h, currents_h, own_left_h, own_right_h, from_left_h, from_right_h,
    sent_h, forcing_h, near_h, faces_h,
    placing, values, number_t, top, currents, own_left, own_right, from_left, from_right,
    faces, packed, sent, forcing, near_o, sems, sent_sems,
):
    devices, message, _ = arrived.shape
    rows_all = currents.shape[1]
    tall = rows_all + 2 * HALO
    loads = start_all(
        [(wide_h.at[levels * k], top.at[k]) for k in range(3)]
        + [
            (wide_h.at[pl.ds(3 * levels, 2)], top.at[pl.ds(3, 2)]),
            (currents_h.at[0, 0], currents.at[0]),
            (currents_h.at[1, 0], currents.at[1]),
            (own_left_h, own_left),
            (own_right_h, own_right),
            (from_left_h, from_left),
            (from_right_h, from_right),
        ],
        sems,
    )
    span = 4 * capacity
    group = LANES // span
    groups = devices // group
    sub8 = iota((8, LANES), 0)
    lane8 = iota((8, LANES), 1)

    lane1 = iota((1, LANES), 1)
    spread = (iota((LANES, LANES), 0) - NUMBERS) == iota((LANES, LANES), 1) % span // 4
    every = jnp.concatenate([arrived[s, span + 8 : span + 9, :] for s in range(devices)], 0).astype(BF16)
    every = jnp.dot(every, jnp.where(spread, 1.0, 0.0).astype(BF16), preferred_element_type=F32)
    numbers = []
    for m in range(groups):
        line = jnp.zeros((1, LANES), F32)
        for g in range(group):
            s = m * group + g
            line = jnp.where(lane1 // span == g, every[s : s + 1], line)
        numbers.append(line)
    number_t[...] = jnp.transpose(
        jnp.concatenate(numbers + [jnp.zeros((LANES - groups, LANES), F32)], 0)
    )

    row_number = iota((rows_all, LANES), 0).astype(F32) + 1.0
    for m in range(groups):
        for f in range(4):
            placing[f * rows_all : (f + 1) * rows_all, m * LANES : (m + 1) * LANES] = jnp.where(
                pick(lane1 % 4 == f, numbers[m]) == row_number, 1.0, 0.0
            ).astype(BF16)
    edge_rows = jnp.zeros((8, LANES), F32)
    edge_cols = jnp.zeros((8, LANES), F32)
    for s in range(devices):
        high, low = split(arrived[s, 0:span, :])
        values[s * span : (s + 1) * span, 0:LANES] = high
        values[s * span : (s + 1) * span, LANES : 2 * LANES] = low
        edge_rows = edge_rows + arrived[s, span : span + 8, :]
        edge_cols = edge_cols + arrived[s, span + 8 : span + 16, :]
    wait_all(loads)
    set_faces(levels, top[3], top[4], own_left, own_right, from_left, from_right, faces, packed)
    wet_wide = top[4]
    total = jnp.dot(placing[...], values[...], preferred_element_type=F32)
    total = total[:, 0:LANES] + total[:, LANES : 2 * LANES]


    def plane(f):
        return total[f * rows_all : (f + 1) * rows_all]

    wide = []
    for f in range(2):
        before = pick(sub8 >= 6, edge_rows if f == 1 else pltpu.roll(edge_rows, 4, 0))
        after = pick(sub8 < 2, edge_rows if f == 0 else pltpu.roll(edge_rows, 4, 0))
        wide.append(jnp.concatenate([before, plane(f), after], 0))
        forcing[f] = wide[f]
    wet = wet_wide[HALO : HALO + rows_all]
    for f in range(2, 4):
        forcing[f, 0:HALO, :] = jnp.zeros((HALO, LANES), F32)
        forcing[f, HALO : HALO + rows_all, :] = plane(f) * wet
        forcing[f, HALO + rows_all : tall, :] = jnp.zeros((HALO, LANES), F32)

    part8 = sub8 % 4
    within = (part8 == lane8 % 4) & (lane8 >= HALO) & (lane8 < HALO + rows_all)
    upper = (part8 == 3) & (lane8 == HALO - 1)
    lower = (part8 == 0) & (lane8 == HALO + rows_all)
    halves = [[], []]
    for k in range(4):
        column = pick(within, pltpu.roll(edge_cols, HALO - k, 1))
        if k in (1, 2):
            column = column + pick(upper, pltpu.roll(edge_cols, (HALO - CORNERS - k) % LANES, 1))
            column = column + pick(lower, pltpu.roll(edge_cols, (HALO + rows_all - CORNERS - 1 - k) % LANES, 1))
        for f in range(2):
            halves[f].append(jnp.sum(column[4 * f : 4 * f + 4], axis=0, keepdims=True))
    columns = jnp.concatenate(halves[0] + halves[1], 0)
    upright = jnp.transpose(jnp.concatenate([columns, jnp.zeros((LANES - 8, LANES), F32)], 0))[0:tall]
    set_beside(levels, upright, wide, packed, near_o)
    stores = start_all([(forcing, forcing_h), (near_o, near_h), (faces, faces_h)], sems, 10)

    surface = []
    unit = top[2] * wet_wide
    for f in range(2):
        value = top[f] + unit * wide[f]
        shift = LANES - (2 * levels * f + 1)
        value = one_pass(value, faces, near_o[0], shift)
        value = one_pass(value, faces, near_o[1], shift)
        surface.append(value[HALO : HALO + rows_all] * wet)
    for f in range(2):
        surface.append(
            (currents[f] + top[2, HALO : HALO + rows_all, :] * forcing[2 + f, HALO : HALO + rows_all, :]) * wet
        )
    high, low = split(jnp.concatenate(surface, 0))
    source = jnp.concatenate([high, low], 1)
    lane_t = iota((LANES, 4 * rows_all), 1)
    sub_t = iota((LANES, 4 * rows_all), 0)
    target = jnp.where(sub_t % 4 == lane_t // rows_all, lane_t % rows_all + 1, -1).astype(F32)
    mask = jnp.concatenate([wet, jnp.zeros((LANES - rows_all, LANES), F32)], 0).astype(BF16)
    per = LANES // 4
    slot_number = number_t[pl.ds(0, per, stride=4), :]
    lane_s = (iota((per, LANES), 1) + 1).astype(F32)
    height = back_rows(capacity)
    many = 4
    for first in range(0, groups, many):
        these = range(first, first + many)
        chosen_rows = [jnp.where(number_t[:, m : m + 1] == target, 1.0, 0.0).astype(BF16) for m in these]
        rows = jnp.dot(jnp.concatenate(chosen_rows, 0), source, preferred_element_type=F32)
        rows = rows[:, 0:LANES] + rows[:, LANES : 2 * LANES]
        slots = [jnp.where(slot_number[:, m : m + 1] == lane_s, 1.0, 0.0) for m in these]
        masks = jnp.dot(jnp.concatenate(slots, 0).astype(BF16), mask, preferred_element_type=F32)
        for g in range(many * group):
            s = first * group + g
            sent[s, 0:span, :] = rows[g * span : (g + 1) * span]
            sent[s, span : span + capacity, :] = masks[g * capacity : (g + 1) * capacity]
            if height > span + capacity:
                sent[s, span + capacity : height, :] = jnp.zeros((height - span - capacity, LANES), F32)
        at = pl.ds(first * group, many * group)
        stores += start_all([(sent.at[at], sent_h.at[at])], sent_sems, first // many)
    wait_all(stores)


def middle(capacity, levels, arrived, wide, currents, *columns):
    devices = arrived.shape[0]
    rows = currents.shape[2]
    tall = rows + 2 * HALO
    height = back_rows(capacity)
    return pl.pallas_call(
        functools.partial(middle_kernel, capacity, levels),
        out_shape=(
            pltpu.HBM((devices, height, LANES), F32),
            pltpu.HBM((4, tall, LANES), F32),
            pltpu.HBM((2, tall, LANES), F32),
            pltpu.HBM((4, tall, LANES), F32),
        ),
        in_specs=[vmem()] + [hbm()] * 2 + [pl.BlockSpec(memory_space=pl.ANY)] * 4,
        out_specs=(hbm(),) * 4,
        scratch_shapes=[
            pltpu.VMEM((4 * rows, 4 * capacity * devices), BF16),
            pltpu.VMEM((4 * capacity * devices, 2 * LANES), BF16),
            pltpu.VMEM((LANES, LANES), F32),
            pltpu.VMEM((5, tall, LANES), F32),
            pltpu.VMEM((2, rows, LANES), F32),
        ]
        + [pltpu.VMEM((2, tall, LANES), F32)] * 4
        + [
            pltpu.VMEM((4, tall, LANES), F32),
            pltpu.VMEM((8, tall, LANES), F32),
            pltpu.VMEM((devices, height, LANES), F32),
            pltpu.VMEM((4, tall, LANES), F32),
            pltpu.VMEM((2, tall, LANES), F32),
            pltpu.SemaphoreType.DMA((13,)),
            pltpu.SemaphoreType.DMA((4 * capacity * devices // LANES,)),
        ],
        compiler_params=pltpu.CompilerParams(vmem_limit_bytes=24 << 20),
        cost_estimate=pl.CostEstimate(flops=200 << 20, bytes_accessed=4 << 20, transcendentals=0),
    )(arrived, *pin(wide, currents), *columns)


def finish_kernel(
    levels, wide_h, currents_h, faces_h, forcing_h, near_h, ocean, wide, currents, faces, forcing, near, sems
):
    rows_all = currents.shape[2]
    wait_all(
        start_all(
            [(wide_h, wide), (currents_h, currents), (faces_h, faces), (forcing_h, forcing), (near_h, near)], sems
        )
    )
    inner = slice(HALO, HALO + rows_all)

    def level(l, carry):
        unit = wide[2 * levels + l]
        masked = unit * wide[3 * levels + 1]
        for f in range(2):
            value = wide[f * levels + l] + masked * forcing[f]
            shift = LANES - 1 - 2 * (levels * f + l)
            value = one_pass(value, faces, near[0], shift)
            value = one_pass(value, faces, near[1], shift)
            ocean[f, l] = value[inner]
            ocean[2 + f, l] = currents[f, l] + unit[inner] * forcing[2 + f][inner]
        return carry

    lax.fori_loop(0, levels, level, 0)


def finish(levels, wide, currents, faces, forcing, near):
    rows = currents.shape[2]
    return pl.pallas_call(
        functools.partial(finish_kernel, levels),
        out_shape=jax.ShapeDtypeStruct((4, levels, rows, LANES), F32),
        in_specs=[hbm()] * 5,
        out_specs=vmem(),
        scratch_shapes=[pltpu.VMEM(a.shape, F32) for a in (wide, currents, faces, forcing, near)]
        + [pltpu.SemaphoreType.DMA((5,))],
        compiler_params=pltpu.CompilerParams(vmem_limit_bytes=24 << 20),
        cost_estimate=pl.CostEstimate(flops=40 << 20, bytes_accessed=6 << 20, transcendentals=0),
    )(*pin(wide, currents, faces, forcing, near))


def turn_kernel(weights_h, turned_h, weights, turned, sems, out_sems):
    part_tiles = weights.shape[0] // PARTS
    parts = [pl.ds(n * part_tiles, part_tiles) for n in range(PARTS)]
    loads = start_all([(weights_h.at[at], weights.at[at]) for at in parts], sems)
    stores = []
    for n, at in enumerate(parts):
        loads[n].wait()

        def tile_step(t, carry):
            turned[t] = weights[t].T
            return carry

        lax.fori_loop(n * part_tiles, (n + 1) * part_tiles, tile_step, 0, unroll=4)
        stores += start_all([(turned.at[at], turned_h.at[at])], out_sems, n)
    wait_all(stores)


def turn(remap_weight):
    return pl.pallas_call(
        turn_kernel,
        out_shape=pltpu.HBM(remap_weight.shape, BF16),
        in_specs=[hbm()],
        out_specs=hbm(),
        scratch_shapes=[pltpu.VMEM(remap_weight.shape, BF16)] * 2 + [pltpu.SemaphoreType.DMA((PARTS,))] * 2,
        compiler_params=pltpu.CompilerParams(vmem_limit_bytes=24 << 20),
        cost_estimate=pl.CostEstimate(flops=8 << 20, bytes_accessed=8 << 20, transcendentals=0),
    )(*pin(remap_weight))


def remap_back_kernel(
    block_h, tile_h, field_h, wet_h, returned, weights_h, out,
    block_s, tile_s, field_s, wet_s, weights, picked_a, picked_b, total_0, total_1, total_2, total_3, sems, weight_sems,
):
    npairs = block_s.shape[0]
    totals = [total_0, total_1, total_2, total_3]
    nblocks = total_0.shape[0]
    scalars = start_all([(field_h, field_s), (wet_h, wet_s), (block_h, block_s), (tile_h, tile_s)], sems)
    part_tiles = weights.shape[0] // PARTS
    parts = [pl.ds(n * part_tiles, part_tiles) for n in range(PARTS)]
    loads = start_all([(weights_h.at[at], weights.at[at]) for at in parts], weight_sems)
    for total in totals:
        total[...] = jnp.zeros_like(total)
    wait_all(scalars)

    def gather(p, picked, at):
        rows = returned[pl.ds(field_s[p], 4), :]
        mask = returned[pl.ds(wet_s[p] - 7, 8), :]
        high, low = split(jnp.concatenate([rows, jnp.zeros((3, LANES), F32), mask[7:8]], 0))
        picked[at] = jnp.concatenate([high, low], 0)

    def product(p, picked, at, total):
        value = jnp.dot(picked[at], weights[tile_s[p]], preferred_element_type=F32)
        b = block_s[p]
        total[b] = total[b] + (value[0:8] + value[8:16])

    early, late = picked_a.shape[0], picked_b.shape[0]
    many = len(totals)

    def first(p, carry):
        gather(p, picked_a, p)
        return carry

    def both(p, carry):
        for n in range(many):
            gather(early + many * p + n, picked_b, many * p + n)
            product(many * p + n, picked_a, many * p + n, totals[n])
        return carry

    def rest(p, carry):
        for n in range(many):
            product(many * p + n, picked_a, many * p + n, totals[n])
        return carry

    def last(p, carry):
        for n in range(many):
            product(early + many * p + n, picked_b, many * p + n, totals[n])
        return carry

    lax.fori_loop(0, early, first, 0, unroll=True)
    wait_all(loads)
    lax.fori_loop(0, late // many, both, 0, unroll=True)
    lax.fori_loop(late // many, early // many, rest, 0, unroll=True)
    lax.fori_loop(0, late // many, last, 0, unroll=True)
    for b in range(nblocks):
        sums = (total_0[b] + total_1[b]) + (total_2[b] + total_3[b])
        out[:, b * LANES : (b + 1) * LANES] = sums[0:4] / jnp.maximum(sums[7:8], 0.1)


def remap_back(pair_block, pair_tile, field_at, wet_at, returned, weights, nblocks):
    npairs = pair_block.shape[0]
    return pl.pallas_call(
        remap_back_kernel,
        out_shape=jax.ShapeDtypeStruct((4, nblocks * LANES), F32),
        in_specs=[hbm()] * 4 + [vmem(), hbm()],
        out_specs=vmem(),
        scratch_shapes=[pltpu.SMEM((npairs,), I32)] * 4
        + [pltpu.VMEM(weights.shape, BF16)]
        + [pltpu.VMEM((npairs // 4 * 3, 16, LANES), BF16), pltpu.VMEM((npairs // 4, 16, LANES), BF16)]
        + [pltpu.VMEM((nblocks, 8, LANES), F32)] * 4
        + [pltpu.SemaphoreType.DMA((4,)), pltpu.SemaphoreType.DMA((PARTS,))],
        compiler_params=pltpu.CompilerParams(vmem_limit_bytes=24 << 20),
        cost_estimate=pl.CostEstimate(flops=2 * npairs * 16 * LANES * LANES, bytes_accessed=6 << 20, transcendentals=0),
    )(*pin(pair_block, pair_tile, field_at, wet_at), returned, *pin(weights))


def local(
    atm_state,
    pair_block,
    pair_owner,
    pair_row,
    pair_tile,
    remap_weight,
    wet_mask,
    ocean_state,
    vert_kappa,
    horiz_kappa,
):
    grid_x = lax.axis_size("gx")
    grid_y = lax.axis_size("gy")
    devices = grid_x * grid_y
    npairs = pair_block.shape[0]
    capacity = max(2, 2 * npairs // devices)
    levels, tile_rows, _ = vert_kappa.shape
    nblocks = atm_state.shape[1] // LANES
    owner = pair_owner.reshape(npairs)
    message = 4 * capacity + EDGE
    outgoing, field_at, wet_at = remap_out(
        capacity, grid_y, devices, tile_rows, atm_state, pair_block, owner, pair_row, pair_tile, remap_weight
    )
    arrived = lax.all_to_all(
        outgoing.reshape(devices, message, LANES), ("gx", "gy"), split_axis=0, concat_axis=0, tiled=True
    )
    tracer, currents, edge_up, edge_down = solve(ocean_state, vert_kappa, horiz_kappa, wet_mask)
    rise_x = [(i, i + 1) for i in range(grid_x - 1)]
    fall_x = [(b, a) for a, b in rise_x]
    rise_y = [(i, i + 1) for i in range(grid_y - 1)]
    fall_y = [(b, a) for a, b in rise_y]
    above = lax.ppermute(edge_down, "gx", rise_x)
    below = lax.ppermute(edge_up, "gx", fall_x)
    wide, to_left, to_right = pack(levels, tracer, above, below)
    from_left = lax.ppermute(to_right, "gy", rise_y)
    from_right = lax.ppermute(to_left, "gy", fall_y)
    sent, forcing, near, faces = middle(
        capacity, levels, arrived, wide, currents, to_left, to_right, from_left, from_right
    )
    returned = lax.all_to_all(sent, ("gx", "gy"), split_axis=0, concat_axis=0, tiled=True)
    ocean_next = finish(levels, wide, currents, faces, forcing, near)
    weights, _ = lax.optimization_barrier((remap_weight, near))
    atm_surface = remap_back(
        pair_block, pair_tile, field_at, wet_at, returned.reshape(-1, LANES), turn(weights), nblocks
    )
    return (ocean_next, atm_surface)


def solution(mesh):
    placed = (
        P(None, ("gx", "gy")),
        P(("gx", "gy")),
        P(("gx", "gy"), None),
        P(("gx", "gy")),
        P(("gx", "gy")),
        P(("gx", "gy"), None, None),
        P("gx", "gy"),
        P(None, None, "gx", "gy"),
        P(None, "gx", "gy"),
        P("gx", "gy"),
    )
    return jax.shard_map(
        local,
        mesh=mesh,
        in_specs=placed,
        out_specs=(P(None, None, "gx", "gy"), P(None, ("gx", "gy"))),
        check_vma=False,
    )
```

```python
import functools

import jax
import jax.numpy as jnp
from jax import lax
from jax.experimental import pallas as pl
from jax.experimental.pallas import tpu as pltpu
from jax.sharding import PartitionSpec as P

F32 = jnp.float32
BF16 = jnp.bfloat16
I32 = jnp.int32
VMEM = pltpu.VMEM
SMEM = pltpu.SMEM
LANES = 128
EDGE = 16
HALO = 8
NUMBERS = 72
CORNERS = 112
SENDS = 16
AHEAD = 16
PARTS = 16


def hbm():
    return pl.BlockSpec(memory_space=pltpu.HBM)


def vmem():
    return pl.BlockSpec(memory_space=VMEM)


def pin(*arrays):
    return [pltpu.with_memory_space_constraint(a, pltpu.HBM) for a in arrays]


def start_all(pairs, sems, first=0):
    copies = [pltpu.make_async_copy(src, dst, sems.at[first + n]) for n, (src, dst) in enumerate(pairs)]
    for copy in copies:
        copy.start()
    return copies


def wait_all(copies):
    for copy in copies:
        copy.wait()


def iota(shape, dim):
    return lax.broadcasted_iota(I32, shape, dim)


def pick(mask, value):
    return jnp.where(mask, value, 0.0)


def split(value):
    high = value.astype(BF16)
    return high, (value - high.astype(F32)).astype(BF16)


def back_rows(capacity):
    return 4 * capacity + max(8, capacity)


def remap_out_kernel(
    capacity, grid_y, tile_rows, block_h, owner_h, row_h, tile_h, atm_h, weights_h, out_h, field_h, wet_h,
    out, block_s, owner_s, row_s, tile_s, rank_s, field_s, wet_s, atm, weights, atm_rows, flux_rows, flux, fill, rows_sum, cols_sum, rows_acc, cols_acc, sems, weight_sems, out_sems,
):
    devices = fill.shape[0]
    npairs = block_s.shape[0]
    tiles = weights.shape[0]
    nblocks = flux.shape[0]
    message = 4 * capacity + EDGE
    copies = [
        pltpu.make_async_copy(src, dst, sems.at[n])
        for n, (src, dst) in enumerate(
            [(atm_h, atm), (block_h, block_s), (owner_h, owner_s), (row_h, row_s), (tile_h, tile_s)]
        )
    ]
    for copy in copies:
        copy.start()
    part_tiles = tiles // PARTS
    parts = [pl.ds(n * part_tiles, part_tiles) for n in range(PARTS)]
    loads = [pltpu.make_async_copy(weights_h.at[at], weights.at[at], weight_sems.at[n]) for n, at in enumerate(parts)]
    for load in loads:
        load.start()
    out[...] = jnp.zeros_like(out)
    rows_sum[...] = jnp.zeros_like(rows_sum)
    cols_sum[...] = jnp.zeros_like(cols_sum)

    def clear_fill(i, carry):
        fill[i] = 0
        return carry

    lax.fori_loop(0, devices, clear_fill, 0, unroll=16)
    flux_rows[...] = jnp.zeros_like(flux_rows)
    wait_all(copies)
    for b in range(nblocks):
        atm_rows[8 * b : 8 * b + 6, :] = atm[:, b * LANES : (b + 1) * LANES]
    wind_u, wind_v, air, dry, rain, sea = [atm_rows[pl.ds(n, nblocks, stride=8), :] for n in range(6)]
    speed = jnp.sqrt(wind_u * wind_u + wind_v * wind_v + 0.25)
    heat = 0.5 * speed * (air - sea)
    water = rain - 0.3 * speed * dry
    planes = [heat, water, 0.2 * speed * wind_u, 0.2 * speed * wind_v]
    for n, plane in list(enumerate(planes)) + [(8 + n, heat) for n in range(4)] + [(12 + n, water) for n in range(4)]:
        flux_rows[pl.ds(n, nblocks, stride=16), :] = plane
    for b in range(nblocks):
        flux[b] = flux_rows[16 * b : 16 * (b + 1), :].astype(BF16)

    height = back_rows(capacity)


    def place(p):
        owner = owner_s[p]
        rank = fill[owner]
        fill[owner] = rank + 1
        field_s[p] = owner * height + 4 * rank
        wet_s[p] = owner * height + 4 * capacity + rank
        rank_s[p] = rank

    for p in range(AHEAD):
        place(p)
    wait_all(loads)

    sub = iota((8, LANES), 0)
    lane = iota((8, LANES), 1)
    part = sub % 4
    edge_row = jnp.where(part == 0, 0, jnp.where(part == 1, 1, tile_rows - 4 + part))
    band = ((lane - part) >> 2) * 4 + part
    id_rank = jnp.where(sub == 0, lane - NUMBERS, -1)

    def pair(p, n):
        owner = owner_s[p]
        row = row_s[p]
        rank = rank_s[p]
        value = jnp.dot(flux[block_s[p]], weights[tile_s[p]], preferred_element_type=F32)
        out[pl.ds(owner * message + 4 * rank, 4), :] = value[0:4]
        tracer = value[8:16]
        rows_sum[n, owner] = rows_sum[n, owner] + pick(edge_row == row, tracer)
        number = (row + 1).astype(F32)
        cols_sum[n, owner] = cols_sum[n, owner] + (
            pick(band == row, pltpu.roll(tracer, row + 2, 1)) + pick(id_rank == rank, number)
        )

    many = rows_sum.shape[0]

    def pairs(more, k, carry):
        for n in range(many):
            p = many * k + n
            if more:
                place(p + AHEAD)
            pair(p, n)
        return carry

    lax.fori_loop(0, (npairs - AHEAD) // many, functools.partial(pairs, True), 0, unroll=True)
    stores = start_all([(field_s, field_h), (wet_s, wet_h)], out_sems, SENDS)
    lax.fori_loop((npairs - AHEAD) // many, npairs // many, functools.partial(pairs, False), 0, unroll=True)

    def owner_step(d, carry):
        rows_acc[d] = (rows_sum[0, d] + rows_sum[1, d]) + (rows_sum[2, d] + rows_sum[3, d])
        cols_acc[d] = (cols_sum[0, d] + cols_sum[1, d]) + (cols_sum[2, d] + cols_sum[3, d])
        return carry

    lax.fori_loop(0, devices, owner_step, 0, unroll=32)

    grid_x = devices // grid_y
    zero = jnp.zeros((8, LANES), F32)

    def columns_of(i, j):
        if not (0 <= i < grid_x and 0 <= j < grid_y):
            return zero
        return cols_acc[i * grid_y + j]

    from_left = (lane - sub) % 4 < 2
    in_band = lane < tile_rows + 4
    in_ids = (sub == 0) & (lane >= NUMBERS) & (lane < NUMBERS + capacity)
    last, first = part == 3, part == 0
    send = devices // SENDS
    for d in range(devices):
        i, j = d // grid_y, d % grid_y
        below = rows_acc[d + grid_y] if i < grid_x - 1 else zero
        above = rows_acc[d - grid_y] if i > 0 else zero
        base = d * message + 4 * capacity
        out[base : base + 8, :] = jnp.where(part < 2, below, above)
        tile = pick(in_band, jnp.where(from_left, columns_of(i, j - 1), columns_of(i, j + 1)))
        upper = pick(last & (lane == tile_rows), columns_of(i - 1, j - 1))
        upper = upper + pick(last & (lane == tile_rows + 1), columns_of(i - 1, j + 1))
        lower = pick(first & (lane == 1), columns_of(i + 1, j - 1))
        lower = lower + pick(first & (lane == 2), columns_of(i + 1, j + 1))
        tile = tile + pltpu.roll(upper, CORNERS - tile_rows, 1) + pltpu.roll(lower, CORNERS + 1, 1)
        tile = tile + pick(in_ids, cols_acc[d])
        out[base + 8 : base + 16, :] = tile
        if d % send == send - 1:
            n = d // send
            at = pl.ds(n * send * message, send * message)
            stores.append(pltpu.make_async_copy(out.at[at], out_h.at[at], out_sems.at[n]))
            stores[-1].start()
    for store in stores:
        store.wait()


def remap_out(capacity, grid_y, devices, tile_rows, atm_state, pair_block, owner, pair_row, pair_tile, remap_weight):
    npairs = pair_block.shape[0]
    nblocks = atm_state.shape[1] // LANES
    message = 4 * capacity + EDGE
    return pl.pallas_call(
        functools.partial(remap_out_kernel, capacity, grid_y, tile_rows),
        out_shape=(
            pltpu.HBM((devices * message, LANES), F32),
            pltpu.HBM((npairs,), I32),
            pltpu.HBM((npairs,), I32),
        ),
        in_specs=[hbm()] * 6,
        out_specs=(hbm(),) * 3,
        scratch_shapes=[pltpu.VMEM((devices * message, LANES), F32)]
        + [pltpu.SMEM((npairs,), I32)] * 7
        + [
            pltpu.VMEM(atm_state.shape, F32),
            pltpu.VMEM(remap_weight.shape, BF16),
            pltpu.VMEM((nblocks * 8, LANES), F32),
            pltpu.VMEM((nblocks * 16, LANES), F32),
            pltpu.VMEM((nblocks, 16, LANES), BF16),
            pltpu.SMEM((devices,), I32),
            pltpu.VMEM((4, devices, 8, LANES), F32),
            pltpu.VMEM((4, devices, 8, LANES), F32),
            pltpu.VMEM((devices, 8, LANES), F32),
            pltpu.VMEM((devices, 8, LANES), F32),
            pltpu.SemaphoreType.DMA((5,)),
            pltpu.SemaphoreType.DMA((PARTS,)),
            pltpu.SemaphoreType.DMA((SENDS + 2,)),
        ],
        compiler_params=pltpu.CompilerParams(vmem_limit_bytes=40 << 20),
        cost_estimate=pl.CostEstimate(
            flops=2 * npairs * 16 * LANES * LANES, bytes_accessed=6 << 20, transcendentals=0
        ),
    )(*pin(pair_block, owner, pair_row, pair_tile, atm_state, remap_weight))


def solve_kernel(state, kappa, horiz, wet, tracer, currents_h, edge_up, edge_down, currents, sems):
    levels = kappa.shape[0]
    rows_all = kappa.shape[1]
    planes = tracer.shape[0]

    def chunk(c, carry):
        rows = pl.ds(pl.multiple_of(c * 8, 8), 8)
        column = [kappa[l, rows, :] for l in range(levels)]
        face = [0.5 * (column[l] + column[l + 1]) for l in range(levels - 1)]
        upper = []
        now = None
        for l in range(levels):
            diagonal = 1.0
            if l > 0:
                diagonal = diagonal + face[l - 1]
            if l < levels - 1:
                diagonal = diagonal + face[l]
            if l > 0:
                diagonal = diagonal + face[l - 1] * upper[-1]
            inverse = 1.0 / diagonal
            if l == 0:
                now = [state[f, 0, rows, :] * inverse for f in range(4)] + [inverse]
            else:
                pull = face[l - 1] * inverse
                now = [state[f, l, rows, :] * inverse + pull * now[f] for f in range(4)] + [pull * now[4]]
            upper.append(-face[l] * inverse if l < levels - 1 else None)
            store(l, rows, now)
        for l in range(levels - 2, -1, -1):
            here = load(l, rows)
            now = [here[f] - upper[l] * now[f] for f in range(5)]
            store(l, rows, now)
        return carry

    def store(l, rows, now):
        tracer[l, rows, :] = now[0]
        tracer[levels + l, rows, :] = now[1]
        currents[0, l, rows, :] = now[2]
        currents[1, l, rows, :] = now[3]
        tracer[2 * levels + l, rows, :] = now[4]

    def load(l, rows):
        return [
            tracer[l, rows, :],
            tracer[levels + l, rows, :],
            currents[0, l, rows, :],
            currents[1, l, rows, :],
            tracer[2 * levels + l, rows, :],
        ]

    lax.fori_loop(0, rows_all // 8, chunk, 0)
    out = start_all([(currents, currents_h)], sems)
    tracer[3 * levels] = horiz[...]
    tracer[3 * levels + 1] = wet[...].astype(F32)
    for k in range(planes):
        edge_up[k] = tracer[k, 0:8, :]
        edge_down[k] = tracer[k, rows_all - 8 : rows_all, :]
    wait_all(out)


def solve(ocean_state, vert_kappa, horiz_kappa, wet_mask):
    levels, rows, _ = vert_kappa.shape
    planes = 3 * levels + 2
    return pl.pallas_call(
        solve_kernel,
        out_shape=(
            jax.ShapeDtypeStruct((planes, rows, LANES), F32),
            pltpu.HBM((2, levels, rows, LANES), F32),
            jax.ShapeDtypeStruct((planes, 8, LANES), F32),
            jax.ShapeDtypeStruct((planes, 8, LANES), F32),
        ),
        in_specs=[vmem()] * 4,
        out_specs=(vmem(), hbm(), vmem(), vmem()),
        scratch_shapes=[pltpu.VMEM((2, levels, rows, LANES), F32), pltpu.SemaphoreType.DMA((1,))],
        compiler_params=pltpu.CompilerParams(vmem_limit_bytes=24 << 20),
        cost_estimate=pl.CostEstimate(flops=20 << 20, bytes_accessed=6 << 20, transcendentals=0),
    )(ocean_state, vert_kappa, horiz_kappa, wet_mask)


def pack_kernel(levels, tracer, above, below, wide_h, to_left, to_right, wide, sems):
    planes, rows, _ = tracer.shape
    for k in range(planes):
        wide[k, 0:HALO, :] = above[k]
        wide[k, HALO : HALO + rows, :] = tracer[k]
        wide[k, HALO + rows : 2 * HALO + rows, :] = below[k]
    out = start_all([(wide, wide_h)], sems)
    lane = iota((8, LANES), 1)

    def chunk(c, carry):
        at = pl.ds(pl.multiple_of(c * 8, 8), 8)

        def place(values, lanes):
            left, right = jnp.zeros((8, LANES), F32), jnp.zeros((8, LANES), F32)
            for k, (near, far) in zip(values, lanes):
                value = wide[k, at, :]
                left = jnp.where(lane == near, pltpu.roll(value, near, 1), left)
                left = jnp.where(lane == far, pltpu.roll(value, far - 1, 1), left)
                right = jnp.where(lane == near + 1, pltpu.roll(value, (near + 2) % LANES, 1), right)
                right = jnp.where(lane == far + 1, pltpu.roll(value, (far + 3) % LANES, 1), right)
            return left, right

        left, right = place(range(2 * levels), [(2 * k, 64 + 2 * k) for k in range(2 * levels)])
        to_left[0, at, :] = left
        to_right[0, at, :] = right
        lanes = [(2 * l, 64 + 2 * l) for l in range(levels)]
        lanes += [(2 * levels, 2 * levels + 2), (2 * levels + 4, 2 * levels + 6)]
        left, right = place(range(2 * levels, 3 * levels + 2), lanes)
        to_left[1, at, :] = left
        to_right[1, at, :] = right
        return carry

    lax.fori_loop(0, (rows + 2 * HALO) // 8, chunk, 0)
    wait_all(out)


def pack(levels, tracer, above, below):
    planes, rows, _ = tracer.shape
    tall = rows + 2 * HALO
    return pl.pallas_call(
        functools.partial(pack_kernel, levels),
        out_shape=(
            pltpu.HBM((planes, tall, LANES), F32),
            jax.ShapeDtypeStruct((2, tall, LANES), F32),
            jax.ShapeDtypeStruct((2, tall, LANES), F32),
        ),
        in_specs=[vmem()] * 3,
        out_specs=(hbm(), vmem(), vmem()),
        scratch_shapes=[pltpu.VMEM((planes, tall, LANES), F32), pltpu.SemaphoreType.DMA((1,))],
        compiler_params=pltpu.CompilerParams(vmem_limit_bytes=24 << 20),
        cost_estimate=pl.CostEstimate(flops=8 << 20, bytes_accessed=4 << 20, transcendentals=0),
    )(tracer, above, below)


def set_faces(levels, h, w, own_left, own_right, from_left, from_right, faces, packed):
    tall = h.shape[0]
    lane = iota((tall, LANES), 1)
    odd = lane % 2 == 1
    twice = lane % 64 < 2 * levels
    left, left_unit, right, right_unit = from_left[0], from_left[1], from_right[0], from_right[1]
    other = jnp.where(odd, left_unit, right_unit)
    at = 2 * levels

    def column(offset):
        return other[:, at + offset : at + offset + 1], other[:, at + offset + 1 : at + offset + 2]

    kappa_right, kappa_left = column(0)
    kappa_far_right, kappa_far_left = column(2)
    wet_right, wet_left = column(4)
    wet_far_right, wet_far_left = column(6)

    kappa_near = jnp.where(odd, kappa_left, kappa_right)
    kappa_far = jnp.where(odd, kappa_far_left, kappa_far_right)
    wet_near = jnp.where(odd, wet_left, wet_right)
    wet_far = jnp.where(odd, wet_far_left, wet_far_right)
    kappa_own = jnp.where(odd, h[:, 0:1], h[:, LANES - 1 : LANES])
    wet_own = jnp.where(odd, w[:, 0:1], w[:, LANES - 1 : LANES])

    def face(kappa_a, wet_a, kappa_b, wet_b):
        return 0.25 * (kappa_a + kappa_b) * wet_a * wet_b

    unit = jnp.where(twice, other, pltpu.roll(other, 2 * levels, 1))
    packed[0] = jnp.where(odd, left, right)
    packed[1] = unit * jnp.where(lane < 64, wet_near, wet_far)
    left, left_unit, right, right_unit = own_left[0], own_left[1], own_right[0], own_right[1]
    packed[2] = jnp.where(odd, pltpu.roll(left, 1, 1), pltpu.roll(right, LANES - 1, 1))
    own = jnp.where(odd, pltpu.roll(left_unit, 1, 1), pltpu.roll(right_unit, LANES - 1, 1))
    packed[3] = jnp.where(twice, own, pltpu.roll(own, 2 * levels, 1)) * wet_own
    north = face(kappa_near, wet_near, pltpu.roll(kappa_near, 1, 0), pltpu.roll(wet_near, 1, 0))
    packed[4] = north
    packed[5] = pltpu.roll(north, tall - 1, 0)
    packed[6] = face(kappa_near, wet_near, kappa_far, wet_far)
    packed[7] = face(kappa_near, wet_near, kappa_own, wet_own)

    north = face(h, w, pltpu.roll(h, 1, 0), pltpu.roll(w, 1, 0))
    faces[0] = north
    faces[1] = pltpu.roll(north, tall - 1, 0)
    west = face(
        h, w, jnp.where(lane == 0, kappa_left, pltpu.roll(h, 1, 1)), jnp.where(lane == 0, wet_left, pltpu.roll(w, 1, 1))
    )
    faces[2] = west
    faces[3] = jnp.where(lane == LANES - 1, face(h, w, kappa_right, wet_right), pltpu.roll(west, LANES - 1, 1))


def set_beside(levels, upright, wide, packed, beside):
    tall = upright.shape[0]
    lane = iota((tall, LANES), 1)
    odd = lane % 2 == 1
    heat = lane % 64 < 2 * levels

    def chosen(f):
        left_far, left_near, right_near, right_far = [upright[:, 4 * f + e : 4 * f + e + 1] for e in range(4)]
        near = jnp.where(odd, left_near, right_near)
        return jnp.where(lane < 64, near, jnp.where(odd, left_far, right_far))

    both = packed[0] + packed[1] * jnp.where(heat, chosen(0), chosen(1))
    far = pltpu.roll(both, 64, 1)
    ends_of = [jnp.where(odd, w[:, 0:1], w[:, LANES - 1 : LANES]) for w in wide]
    own = packed[2] + packed[3] * jnp.where(heat, ends_of[0], ends_of[1])
    near = both + packed[5] * (pltpu.roll(both, tall - 1, 0) - both)
    near = near + packed[4] * (pltpu.roll(both, 1, 0) - both)
    near = near + packed[6] * (far - both)
    near = near + packed[7] * (own - both)
    beside[0] = both
    beside[1] = near


def one_pass(value, faces, beside, shift):
    tall = value.shape[0]
    lane = iota(value.shape, 1)
    moved = pltpu.roll(beside, shift, 1)
    west = jnp.where(lane == 0, moved, pltpu.roll(value, 1, 1))
    east = jnp.where(lane == LANES - 1, moved, pltpu.roll(value, LANES - 1, 1))
    result = value + faces[1] * (pltpu.roll(value, tall - 1, 0) - value)
    result = result + faces[0] * (pltpu.roll(value, 1, 0) - value)
    result = result + faces[3] * (east - value)
    return result + faces[2] * (west - value)


def middle_kernel(
    capacity, levels, arrived, wide_h, currents_h, own_left_h, own_right_h, from_left_h, from_right_h,
    sent_h, forcing_h, near_h, faces_h,
    placing, values, number_t, top, currents, own_left, own_right, from_left, from_right,
    faces, packed, sent, forcing, near_o, sems, sent_sems,
):
    devices, message, _ = arrived.shape
    rows_all = currents.shape[1]
    tall = rows_all + 2 * HALO
    loads = start_all(
        [(wide_h.at[levels * k], top.at[k]) for k in range(3)]
        + [
            (wide_h.at[pl.ds(3 * levels, 2)], top.at[pl.ds(3, 2)]),
            (currents_h.at[0, 0], currents.at[0]),
            (currents_h.at[1, 0], currents.at[1]),
            (own_left_h, own_left),
            (own_right_h, own_right),
            (from_left_h, from_left),
            (from_right_h, from_right),
        ],
        sems,
    )
    span = 4 * capacity
    group = LANES // span
    groups = devices // group
    sub8 = iota((8, LANES), 0)
    lane8 = iota((8, LANES), 1)

    lane1 = iota((1, LANES), 1)
    spread = (iota((LANES, LANES), 0) - NUMBERS) == iota((LANES, LANES), 1) % span // 4
    every = jnp.concatenate([arrived[s, span + 8 : span + 9, :] for s in range(devices)], 0).astype(BF16)
    every = jnp.dot(every, jnp.where(spread, 1.0, 0.0).astype(BF16), preferred_element_type=F32)
    numbers = []
    for m in range(groups):
        line = jnp.zeros((1, LANES), F32)
        for g in range(group):
            s = m * group + g
            line = jnp.where(lane1 // span == g, every[s : s + 1], line)
        numbers.append(line)
    number_t[...] = jnp.transpose(
        jnp.concatenate(numbers + [jnp.zeros((LANES - groups, LANES), F32)], 0)
    )

    row_number = iota((rows_all, LANES), 0).astype(F32) + 1.0
    for m in range(groups):
        for f in range(4):
            placing[f * rows_all : (f + 1) * rows_all, m * LANES : (m + 1) * LANES] = jnp.where(
                pick(lane1 % 4 == f, numbers[m]) == row_number, 1.0, 0.0
            ).astype(BF16)
    edge_rows = jnp.zeros((8, LANES), F32)
    edge_cols = jnp.zeros((8, LANES), F32)
    for s in range(devices):
        high, low = split(arrived[s, 0:span, :])
        values[s * span : (s + 1) * span, 0:LANES] = high
        values[s * span : (s + 1) * span, LANES : 2 * LANES] = low
        edge_rows = edge_rows + arrived[s, span : span + 8, :]
        edge_cols = edge_cols + arrived[s, span + 8 : span + 16, :]
    wait_all(loads)
    set_faces(levels, top[3], top[4], own_left, own_right, from_left, from_right, faces, packed)
    wet_wide = top[4]
    total = jnp.dot(placing[...], values[...], preferred_element_type=F32)
    total = total[:, 0:LANES] + total[:, LANES : 2 * LANES]


    def plane(f):
        return total[f * rows_all : (f + 1) * rows_all]

    wide = []
    for f in range(2):
        before = pick(sub8 >= 6, edge_rows if f == 1 else pltpu.roll(edge_rows, 4, 0))
        after = pick(sub8 < 2, edge_rows if f == 0 else pltpu.roll(edge_rows, 4, 0))
        wide.append(jnp.concatenate([before, plane(f), after], 0))
        forcing[f] = wide[f]
    wet = wet_wide[HALO : HALO + rows_all]
    for f in range(2, 4):
        forcing[f, 0:HALO, :] = jnp.zeros((HALO, LANES), F32)
        forcing[f, HALO : HALO + rows_all, :] = plane(f) * wet
        forcing[f, HALO + rows_all : tall, :] = jnp.zeros((HALO, LANES), F32)

    part8 = sub8 % 4
    within = (part8 == lane8 % 4) & (lane8 >= HALO) & (lane8 < HALO + rows_all)
    upper = (part8 == 3) & (lane8 == HALO - 1)
    lower = (part8 == 0) & (lane8 == HALO + rows_all)
    halves = [[], []]
    for k in range(4):
        column = pick(within, pltpu.roll(edge_cols, HALO - k, 1))
        if k in (1, 2):
            column = column + pick(upper, pltpu.roll(edge_cols, (HALO - CORNERS - k) % LANES, 1))
            column = column + pick(lower, pltpu.roll(edge_cols, (HALO + rows_all - CORNERS - 1 - k) % LANES, 1))
        for f in range(2):
            halves[f].append(jnp.sum(column[4 * f : 4 * f + 4], axis=0, keepdims=True))
    columns = jnp.concatenate(halves[0] + halves[1], 0)
    upright = jnp.transpose(jnp.concatenate([columns, jnp.zeros((LANES - 8, LANES), F32)], 0))[0:tall]
    set_beside(levels, upright, wide, packed, near_o)
    stores = start_all([(forcing, forcing_h), (near_o, near_h), (faces, faces_h)], sems, 10)

    surface = []
    unit = top[2] * wet_wide
    for f in range(2):
        value = top[f] + unit * wide[f]
        shift = LANES - (2 * levels * f + 1)
        value = one_pass(value, faces, near_o[0], shift)
        value = one_pass(value, faces, near_o[1], shift)
        surface.append(value[HALO : HALO + rows_all] * wet)
    for f in range(2):
        surface.append(
            (currents[f] + top[2, HALO : HALO + rows_all, :] * forcing[2 + f, HALO : HALO + rows_all, :]) * wet
        )
    high, low = split(jnp.concatenate(surface, 0))
    source = jnp.concatenate([high, low], 1)
    lane_t = iota((LANES, 4 * rows_all), 1)
    sub_t = iota((LANES, 4 * rows_all), 0)
    target = jnp.where(sub_t % 4 == lane_t // rows_all, lane_t % rows_all + 1, -1).astype(F32)
    mask = jnp.concatenate([wet, jnp.zeros((LANES - rows_all, LANES), F32)], 0).astype(BF16)
    per = LANES // 4
    slot_number = number_t[pl.ds(0, per, stride=4), :]
    lane_s = (iota((per, LANES), 1) + 1).astype(F32)
    height = back_rows(capacity)
    many = 4
    for first in range(0, groups, many):
        these = range(first, first + many)
        chosen_rows = [jnp.where(number_t[:, m : m + 1] == target, 1.0, 0.0).astype(BF16) for m in these]
        rows = jnp.dot(jnp.concatenate(chosen_rows, 0), source, preferred_element_type=F32)
        rows = rows[:, 0:LANES] + rows[:, LANES : 2 * LANES]
        slots = [jnp.where(slot_number[:, m : m + 1] == lane_s, 1.0, 0.0) for m in these]
        masks = jnp.dot(jnp.concatenate(slots, 0).astype(BF16), mask, preferred_element_type=F32)
        for g in range(many * group):
            s = first * group + g
            sent[s, 0:span, :] = rows[g * span : (g + 1) * span]
            sent[s, span : span + capacity, :] = masks[g * capacity : (g + 1) * capacity]
            if height > span + capacity:
                sent[s, span + capacity : height, :] = jnp.zeros((height - span - capacity, LANES), F32)
        at = pl.ds(first * group, many * group)
        stores += start_all([(sent.at[at], sent_h.at[at])], sent_sems, first // many)
    wait_all(stores)


def middle(capacity, levels, arrived, wide, currents, *columns):
    devices = arrived.shape[0]
    rows = currents.shape[2]
    tall = rows + 2 * HALO
    height = back_rows(capacity)
    return pl.pallas_call(
        functools.partial(middle_kernel, capacity, levels),
        out_shape=(
            pltpu.HBM((devices, height, LANES), F32),
            pltpu.HBM((4, tall, LANES), F32),
            pltpu.HBM((2, tall, LANES), F32),
            pltpu.HBM((4, tall, LANES), F32),
        ),
        in_specs=[vmem()] + [hbm()] * 2 + [pl.BlockSpec(memory_space=pl.ANY)] * 4,
        out_specs=(hbm(),) * 4,
        scratch_shapes=[
            pltpu.VMEM((4 * rows, 4 * capacity * devices), BF16),
            pltpu.VMEM((4 * capacity * devices, 2 * LANES), BF16),
            pltpu.VMEM((LANES, LANES), F32),
            pltpu.VMEM((5, tall, LANES), F32),
            pltpu.VMEM((2, rows, LANES), F32),
        ]
        + [pltpu.VMEM((2, tall, LANES), F32)] * 4
        + [
            pltpu.VMEM((4, tall, LANES), F32),
            pltpu.VMEM((8, tall, LANES), F32),
            pltpu.VMEM((devices, height, LANES), F32),
            pltpu.VMEM((4, tall, LANES), F32),
            pltpu.VMEM((2, tall, LANES), F32),
            pltpu.SemaphoreType.DMA((13,)),
            pltpu.SemaphoreType.DMA((4 * capacity * devices // LANES,)),
        ],
        compiler_params=pltpu.CompilerParams(vmem_limit_bytes=24 << 20),
        cost_estimate=pl.CostEstimate(flops=200 << 20, bytes_accessed=4 << 20, transcendentals=0),
    )(arrived, *pin(wide, currents), *columns)


def finish_kernel(
    levels, wide_h, currents_h, faces_h, forcing_h, near_h, ocean, wide, currents, faces, forcing, near, sems
):
    rows_all = currents.shape[2]
    wait_all(
        start_all(
            [(wide_h, wide), (currents_h, currents), (faces_h, faces), (forcing_h, forcing), (near_h, near)], sems
        )
    )
    inner = slice(HALO, HALO + rows_all)

    def level(l, carry):
        unit = wide[2 * levels + l]
        masked = unit * wide[3 * levels + 1]
        for f in range(2):
            value = wide[f * levels + l] + masked * forcing[f]
            shift = LANES - 1 - 2 * (levels * f + l)
            value = one_pass(value, faces, near[0], shift)
            value = one_pass(value, faces, near[1], shift)
            ocean[f, l] = value[inner]
            ocean[2 + f, l] = currents[f, l] + unit[inner] * forcing[2 + f][inner]
        return carry

    lax.fori_loop(0, levels, level, 0)


def finish(levels, wide, currents, faces, forcing, near):
    rows = currents.shape[2]
    return pl.pallas_call(
        functools.partial(finish_kernel, levels),
        out_shape=jax.ShapeDtypeStruct((4, levels, rows, LANES), F32),
        in_specs=[hbm()] * 5,
        out_specs=vmem(),
        scratch_shapes=[pltpu.VMEM(a.shape, F32) for a in (wide, currents, faces, forcing, near)]
        + [pltpu.SemaphoreType.DMA((5,))],
        compiler_params=pltpu.CompilerParams(vmem_limit_bytes=24 << 20),
        cost_estimate=pl.CostEstimate(flops=40 << 20, bytes_accessed=6 << 20, transcendentals=0),
    )(*pin(wide, currents, faces, forcing, near))


def turn_kernel(weights_h, turned_h, weights, turned, sems, out_sems):
    part_tiles = weights.shape[0] // PARTS
    parts = [pl.ds(n * part_tiles, part_tiles) for n in range(PARTS)]
    loads = start_all([(weights_h.at[at], weights.at[at]) for at in parts], sems)
    stores = []
    for n, at in enumerate(parts):
        loads[n].wait()

        def tile_step(t, carry):
            turned[t] = weights[t].T
            return carry

        lax.fori_loop(n * part_tiles, (n + 1) * part_tiles, tile_step, 0, unroll=4)
        stores += start_all([(turned.at[at], turned_h.at[at])], out_sems, n)
    wait_all(stores)


def turn(remap_weight):
    return pl.pallas_call(
        turn_kernel,
        out_shape=pltpu.HBM(remap_weight.shape, BF16),
        in_specs=[hbm()],
        out_specs=hbm(),
        scratch_shapes=[pltpu.VMEM(remap_weight.shape, BF16)] * 2 + [pltpu.SemaphoreType.DMA((PARTS,))] * 2,
        compiler_params=pltpu.CompilerParams(vmem_limit_bytes=24 << 20),
        cost_estimate=pl.CostEstimate(flops=8 << 20, bytes_accessed=8 << 20, transcendentals=0),
    )(*pin(remap_weight))


def remap_back_kernel(
    block_h, tile_h, field_h, wet_h, returned, weights_h, out,
    block_s, tile_s, field_s, wet_s, weights, picked_a, picked_b, total_0, total_1, total_2, total_3, sems, weight_sems,
):
    npairs = block_s.shape[0]
    totals = [total_0, total_1, total_2, total_3]
    nblocks = total_0.shape[0]
    scalars = start_all([(field_h, field_s), (wet_h, wet_s), (block_h, block_s), (tile_h, tile_s)], sems)
    part_tiles = weights.shape[0] // PARTS
    parts = [pl.ds(n * part_tiles, part_tiles) for n in range(PARTS)]
    loads = start_all([(weights_h.at[at], weights.at[at]) for at in parts], weight_sems)
    for total in totals:
        total[...] = jnp.zeros_like(total)
    wait_all(scalars)

    def gather(p, picked, at):
        rows = returned[pl.ds(field_s[p], 4), :]
        mask = returned[pl.ds(wet_s[p] - 7, 8), :]
        high, low = split(jnp.concatenate([rows, jnp.zeros((3, LANES), F32), mask[7:8]], 0))
        picked[at] = jnp.concatenate([high, low], 0)

    def product(p, picked, at, total):
        value = jnp.dot(picked[at], weights[tile_s[p]], preferred_element_type=F32)
        b = block_s[p]
        total[b] = total[b] + (value[0:8] + value[8:16])

    early, late = picked_a.shape[0], picked_b.shape[0]
    many = len(totals)

    def first(p, carry):
        gather(p, picked_a, p)
        return carry

    def both(p, carry):
        for n in range(many):
            gather(early + many * p + n, picked_b, many * p + n)
            product(many * p + n, picked_a, many * p + n, totals[n])
        return carry

    def rest(p, carry):
        for n in range(many):
            product(many * p + n, picked_a, many * p + n, totals[n])
        return carry

    def last(p, carry):
        for n in range(many):
            product(early + many * p + n, picked_b, many * p + n, totals[n])
        return carry

    lax.fori_loop(0, early, first, 0, unroll=True)
    wait_all(loads)
    lax.fori_loop(0, late // many, both, 0, unroll=True)
    lax.fori_loop(late // many, early // many, rest, 0, unroll=True)
    lax.fori_loop(0, late // many, last, 0, unroll=True)
    for b in range(nblocks):
        sums = (total_0[b] + total_1[b]) + (total_2[b] + total_3[b])
        out[:, b * LANES : (b + 1) * LANES] = sums[0:4] / jnp.maximum(sums[7:8], 0.1)


def remap_back(pair_block, pair_tile, field_at, wet_at, returned, weights, nblocks):
    npairs = pair_block.shape[0]
    return pl.pallas_call(
        remap_back_kernel,
        out_shape=jax.ShapeDtypeStruct((4, nblocks * LANES), F32),
        in_specs=[hbm()] * 4 + [vmem(), hbm()],
        out_specs=vmem(),
        scratch_shapes=[pltpu.SMEM((npairs,), I32)] * 4
        + [pltpu.VMEM(weights.shape, BF16)]
        + [pltpu.VMEM((npairs // 4 * 3, 16, LANES), BF16), pltpu.VMEM((npairs // 4, 16, LANES), BF16)]
        + [pltpu.VMEM((nblocks, 8, LANES), F32)] * 4
        + [pltpu.SemaphoreType.DMA((4,)), pltpu.SemaphoreType.DMA((PARTS,))],
        compiler_params=pltpu.CompilerParams(vmem_limit_bytes=24 << 20),
        cost_estimate=pl.CostEstimate(flops=2 * npairs * 16 * LANES * LANES, bytes_accessed=6 << 20, transcendentals=0),
    )(*pin(pair_block, pair_tile, field_at, wet_at), returned, *pin(weights))


def local(
    atm_state,
    pair_block,
    pair_owner,
    pair_row,
    pair_tile,
    remap_weight,
    wet_mask,
    ocean_state,
    vert_kappa,
    horiz_kappa,
):
    grid_x = lax.axis_size("gx")
    grid_y = lax.axis_size("gy")
    devices = grid_x * grid_y
    npairs = pair_block.shape[0]
    capacity = max(2, 2 * npairs // devices)
    levels, tile_rows, _ = vert_kappa.shape
    nblocks = atm_state.shape[1] // LANES
    owner = pair_owner.reshape(npairs)
    message = 4 * capacity + EDGE
    outgoing, field_at, wet_at = remap_out(
        capacity, grid_y, devices, tile_rows, atm_state, pair_block, owner, pair_row, pair_tile, remap_weight
    )
    arrived = lax.all_to_all(
        outgoing.reshape(devices, message, LANES), ("gx", "gy"), split_axis=0, concat_axis=0, tiled=True
    )
    tracer, currents, edge_up, edge_down = solve(ocean_state, vert_kappa, horiz_kappa, wet_mask)
    rise_x = [(i, i + 1) for i in range(grid_x - 1)]
    fall_x = [(b, a) for a, b in rise_x]
    rise_y = [(i, i + 1) for i in range(grid_y - 1)]
    fall_y = [(b, a) for a, b in rise_y]
    above = lax.ppermute(edge_down, "gx", rise_x)
    below = lax.ppermute(edge_up, "gx", fall_x)
    wide, to_left, to_right = pack(levels, tracer, above, below)
    from_left = lax.ppermute(to_right, "gy", rise_y)
    from_right = lax.ppermute(to_left, "gy", fall_y)
    sent, forcing, near, faces = middle(
        capacity, levels, arrived, wide, currents, to_left, to_right, from_left, from_right
    )
    returned = lax.all_to_all(sent, ("gx", "gy"), split_axis=0, concat_axis=0, tiled=True)
    ocean_next = finish(levels, wide, currents, faces, forcing, near)
    weights, _ = lax.optimization_barrier((remap_weight, near))
    atm_surface = remap_back(
        pair_block, pair_tile, field_at, wet_at, returned.reshape(-1, LANES), turn(weights), nblocks
    )
    return (ocean_next, atm_surface)


def solution(mesh):
    placed = (
        P(None, ("gx", "gy")),
        P(("gx", "gy")),
        P(("gx", "gy"), None),
        P(("gx", "gy")),
        P(("gx", "gy")),
        P(("gx", "gy"), None, None),
        P("gx", "gy"),
        P(None, None, "gx", "gy"),
        P(None, "gx", "gy"),
        P("gx", "gy"),
    )
    return jax.shard_map(
        local,
        mesh=mesh,
        in_specs=placed,
        out_specs=(P(None, None, "gx", "gy"), P(None, ("gx", "gy"))),
        check_vma=False,
    )
```
